32 devices in a mesh: dp: 4 (over y, core), fsdp: 8 (over z, x).
Axes of the slice: x: 2, y: 2, z: 4, core: 2. Of those that a mesh axis runs over, the one named last changes fastest.
Arguments:
- layer_input: bfloat16 [8192, 4096], P(('dp', 'fsdp')), may hold values from -6 to 6
- query_states: bfloat16 [8192, 2048], P(('dp', 'fsdp')), may hold values from -120 to 120
- key_states: bfloat16 [8192, 512], P(('dp', 'fsdp')), may hold values from -6 to 6
- output_grad: bfloat16 [8192, 2048], P(('dp', 'fsdp')), may hold values from -0.0625 to 0.0625
- document_ids: int32 [8192], P(('dp', 'fsdp')), may hold values from 0 to 255, as said below
- weight_index: int32 [8192], P(('dp', 'fsdp')), may hold values from 0 to 15, as said below
- loss_weights: float32 [16], replicated, may hold values from 0.25 to 4
- scale_exponent: int32 [32], P(('dp', 'fsdp')), may hold values from 0 to 3
- swap_start: int32 [32, 2], P(('dp', 'fsdp')), may hold values from 128 to 224, as said below
- swap_rows: int32 [32, 2], P(('dp', 'fsdp')), may hold values from 16 to 32, as said below
Outputs:
- grad_value: float32 [4096, 512], P('fsdp')
- value_grad: bfloat16 [8192, 512], P(('dp', 'fsdp'))
The draws below stay inside these ranges and needn't reach their ends.
Inputs may be any that keep to these rules, and one draw needn't show every extreme that they name: `document_ids`: each row holds the index, within its device's 256 rows, of its document's first row; a document lies inside one device, either within its first 128 rows or within one of its last 8 aligned blocks of 16 rows. `weight_index`: equal on all rows of a document. `swap_start`: 128 plus a multiple of 16. `swap_rows`: 16 or 32; equal on the two devices whose dp indices differ in bit level.
All inputs are finite; a program needn't handle non-finite values.
Results may differ from the reference program's by a relative error of at most 0.0065.
Values may be sent and summed in bfloat16 or wider, within the bound.
No kernel may reach another device: no remote copies, remote signals or barrier semaphores. Data moves between devices by JAX's collectives and lax.ppermute only.
A program may use at most 64 MiB of HBM per device.

```python
import math
import jax
import jax.numpy as jnp
from jax import lax

D = 4096
HD = 128
HQ = 16
KVH = 4
TOK_DEV = 256
SEG = 16
SHORT_SEGS = 8
NWEIGHT = 16
CAP = 32
GQ = 4
QW = 2048
KVW = 512
BITS = 2
TOKENS = 8192
OWN = 512
N_DP = 4
N_FSDP = 8


def doc_layout(key):
    devices = N_DP * N_FSDP
    long_rows = TOK_DEV - SHORT_SEGS * SEG
    positions = jnp.arange(TOK_DEV)
    flags_long = jax.random.randint(jax.random.fold_in(key, 101), (devices, TOK_DEV), 0, 40) == 0
    flags_short = jax.random.randint(jax.random.fold_in(key, 102), (devices, TOK_DEV), 0, 5) == 0
    in_short = positions >= long_rows
    flags = jnp.where(in_short[None, :], flags_short, flags_long)
    forced = (positions == 0) | in_short & ((positions - long_rows) % SEG == 0) | (positions == TOK_DEV - 1)
    flags = flags | forced[None, :]
    local = lax.cummax(jnp.where(flags, positions[None, :], 0), axis=1)
    return local.astype(jnp.int32)


def key_table(key):
    return jnp.clip(jax.random.normal(jax.random.fold_in(key, 103), (TOKENS, KVH * HD), jnp.float32), -6.0, 6.0)


def draw_document_ids(key, part):
    local = doc_layout(key)
    return local.reshape(-1).astype(jnp.int32)


def draw_weight_index(key, part):
    local = doc_layout(key)
    device = jnp.arange(N_DP * N_FSDP)[:, None]
    starts = (device * TOK_DEV + local).reshape(-1)
    key = jax.random.fold_in(key, 4)
    entries = jax.random.randint(key, (TOKENS,), 0, NWEIGHT)
    return jnp.take(entries, starts).astype(jnp.int32)


def draw_key_states(key, part):
    shared = key_table(key)
    return shared.astype(jnp.bfloat16)


def draw_query_states(key, part):
    key = jax.random.fold_in(key, 6)
    return jnp.clip(jax.random.normal(key, (TOKENS, HQ * HD), jnp.float32), -6.0, 6.0).astype(jnp.bfloat16)


def draw_swap_start(key, part):
    key = jax.random.fold_in(key, 7)
    blocks = jax.random.randint(key, (N_DP * N_FSDP, BITS), 0, SHORT_SEGS - 1)
    blocks = blocks.at[0, 0].set(SHORT_SEGS - 2)
    blocks = blocks.at[N_DP * N_FSDP - 1, 0].set(0)
    return (TOK_DEV - SHORT_SEGS * SEG + blocks * SEG).astype(jnp.int32)


def draw_swap_rows(key, part):
    key = jax.random.fold_in(key, 8)
    counts = jax.random.randint(key, (N_DP, N_FSDP, BITS), 1, 3)
    counts = counts.at[0, 0, :].set(2)
    counts = counts.at[0, N_FSDP - 1, :].set(1)
    rank = jnp.arange(N_DP)
    columns = []
    for level in range(BITS):
        lower = rank - jnp.bitwise_and(rank, 1 << level)
        columns.append(counts[lower, :, level])
    stacked = jnp.stack(columns, axis=-1) * SEG
    return stacked.reshape(N_DP * N_FSDP, BITS).astype(jnp.int32)


def plant(result, key, smallest, high):
    index_at = [jax.random.randint(jax.random.fold_in(key, axis), (), 0, length) for axis, length in enumerate(result.shape)]
    widest = result.shape.index(max(result.shape))
    next_to = index_at[:widest] + [(index_at[widest] + 1) % result.shape[widest]] + index_at[widest + 1:]
    return result.at[tuple(index_at)].set(smallest).at[tuple(next_to)].set(high)


def strengthened(values, rng, source, target, blocks, factor):
    def block_of(dim):
        return (jnp.arange(values.shape[dim]) // (values.shape[dim] // blocks)).reshape((-1,) + (1,) * (values.ndim - 1 - dim))

    one_side = jax.random.permutation(rng, blocks)[block_of(target)]
    other_side = (block_of(target) + blocks // 2) % blocks
    return jnp.where((block_of(source) == one_side) | (block_of(source) == other_side), factor * values, values)


def block_levels(key, shape, split, low, top_value):
    factor_of = 1.0
    for axis_at, parts in split:
        steps = jax.random.uniform(jax.random.fold_in(jax.random.fold_in(key, 6), axis_at), (parts,), jnp.float32, low / len(split), top_value / len(split))
        factor_of = factor_of * jnp.repeat(jnp.exp(steps), shape[axis_at] // parts).reshape((-1,) + (1,) * (len(shape) - 1 - axis_at))
    return factor_of


def noise(key, shape, spread, most, shards=(), kind=jnp.bfloat16):
    loudness = block_levels(key, shape, shards, -0.22, 0.18) if shards else 1.0
    array = jax.random.normal(key, shape, jnp.float32) * spread * loudness
    return jnp.minimum(jnp.maximum(array, -most), most).astype(kind)


def bell_draw_with(rng, shape, width, most, pieces, heavy, held_as=jnp.bfloat16):
    result = width * jax.random.normal(rng, shape, jnp.float32)
    if pieces:
        result = result * block_levels(rng, shape, pieces, -0.22, 0.18)
    return jnp.clip(strengthened(result, jax.random.fold_in(rng, 3), *heavy), -most, most).astype(held_as)


def setup_inputs(seed: int = 0) -> dict:
    seeds = jax.random.split(jax.random.key(seed), 11)
    layer_input = bell_draw_with(seeds[0], (TOKENS, D), 1.0, 6.0, ((0, 32),), (0, 1, 32, 2.75))
    query_states = draw_query_states(jax.random.fold_in(seeds[10], 71), 0)
    key_states = draw_key_states(jax.random.fold_in(seeds[10], 71), 0)
    output_grad = noise(seeds[3], (TOKENS, QW), TOKENS ** -0.5, 0.0625, ((0, 32),))
    document_ids = draw_document_ids(jax.random.fold_in(seeds[10], 71), 0)
    weight_index = draw_weight_index(jax.random.fold_in(seeds[10], 71), 0)
    loss_weights = jnp.clip(jnp.exp(jax.random.uniform(seeds[6], (NWEIGHT,), jnp.float32, math.log(0.25), math.log(4.0))), 0.25, 4.0)
    scale_exponent = plant(jax.random.randint(seeds[7], (N_DP * N_FSDP,), 0, 4), jax.random.fold_in(seeds[7], 1), 0, 3).astype(jnp.int32)
    swap_start = draw_swap_start(jax.random.fold_in(seeds[10], 71), 0)
    swap_rows = draw_swap_rows(jax.random.fold_in(seeds[10], 71), 0)
    return {"layer_input": layer_input, "query_states": query_states, "key_states": key_states, "output_grad": output_grad, "document_ids": document_ids, "weight_index": weight_index, "loss_weights": loss_weights, "scale_exponent": scale_exponent, "swap_start": swap_start, "swap_rows": swap_rows}


def cut_rows(item, offset):
    return lax.dynamic_slice_in_dim(item, offset, CAP, 0)


def blend_rows(item, incoming, offset, extent):
    inside = jnp.arange(CAP) < extent
    shaped = inside.reshape((CAP,) + (1,) * (item.ndim - 1))
    chosen = jnp.where(shaped, incoming, lax.dynamic_slice_in_dim(item, offset, CAP, 0))
    return lax.dynamic_update_slice_in_dim(item, chosen, offset, 0)


def swap_level(item, offsets, extents, level):
    windows = jax.vmap(jax.vmap(cut_rows))(item, offsets)
    partner = jnp.bitwise_xor(jnp.arange(N_DP), 1 << level)
    arrived = windows[partner]
    return jax.vmap(jax.vmap(blend_rows))(item, arrived, offsets, extents)


def attend(query_rows, key_rows, grad_rows, doc_rows):
    tokens = query_rows.shape[0]
    q_four = query_rows.astype(jnp.float32).reshape(tokens, KVH, GQ, HD)
    k_three = key_rows.astype(jnp.float32).reshape(tokens, KVH, HD)
    scores = jnp.einsum("ignd,jgd->gnij", q_four, k_three) * (HD ** -0.5)
    positions = jnp.arange(tokens)
    allowed = (doc_rows[:, None] == doc_rows[None, :]) & (positions[None, :] <= positions[:, None])
    scores = jnp.where(allowed, scores, -1e30)
    highest = jnp.max(scores, axis=-1, keepdims=True)
    expo = jnp.exp(scores - highest)
    probs = (expo / jnp.sum(expo, axis=-1, keepdims=True)).astype(jnp.bfloat16)
    g_four = grad_rows.astype(jnp.float32).reshape(tokens, KVH, GQ, HD)
    values = jnp.einsum("gnij,ignd->jgd", probs.astype(jnp.float32), g_four)
    return values.reshape(tokens, KVW).astype(jnp.bfloat16)


def reference(layer_input, query_states, key_states, output_grad, document_ids, weight_index, loss_weights, scale_exponent, swap_start, swap_rows):
    onehot = (weight_index[:, None] == jnp.arange(NWEIGHT)[None, :]).astype(jnp.float32)
    unscale = jnp.exp2(-scale_exponent.astype(jnp.float32))
    factor = jnp.sum(onehot * loss_weights[None, :], axis=1) * jnp.repeat(unscale, TOK_DEV)
    count = N_DP * N_FSDP
    shape_two = (N_DP, N_FSDP, TOK_DEV)
    queries = query_states.reshape(shape_two + (QW,))
    key_rows = key_states.reshape(shape_two + (KVW,))
    grads = output_grad.reshape(shape_two + (QW,))
    factors = factor.reshape(shape_two)
    device_first = (jnp.arange(count, dtype=jnp.int32) * TOK_DEV).reshape(N_DP, N_FSDP, 1)
    doc_rows = document_ids.reshape(shape_two) + device_first
    offsets = swap_start.reshape(N_DP, N_FSDP, BITS)
    extents = swap_rows.reshape(N_DP, N_FSDP, BITS)
    for level in range(BITS):
        queries = swap_level(queries, offsets[:, :, level], extents[:, :, level], level)
        key_rows = swap_level(key_rows, offsets[:, :, level], extents[:, :, level], level)
        grads = swap_level(grads, offsets[:, :, level], extents[:, :, level], level)
        factors = swap_level(factors, offsets[:, :, level], extents[:, :, level], level)
        doc_rows = swap_level(doc_rows, offsets[:, :, level], extents[:, :, level], level)

    def one_device(items):
        query_rows, key_part, grad_rows, factor_rows, doc_part = items
        weighted = (grad_rows.astype(jnp.float32) * factor_rows[:, None]).astype(jnp.bfloat16)
        return attend(query_rows, key_part, weighted, doc_part)

    values = lax.map(one_device, (queries.reshape(count, TOK_DEV, QW), key_rows.reshape(count, TOK_DEV, KVW), grads.reshape(count, TOK_DEV, QW), factors.reshape(count, TOK_DEV), doc_rows.reshape(count, TOK_DEV)))
    balanced_values = values.reshape(TOKENS, KVW)
    values = values.reshape(shape_two + (KVW,))
    for level in reversed(range(BITS)):
        values = swap_level(values, offsets[:, :, level], extents[:, :, level], level)
    gradient = lax.dot_general(layer_input, values.reshape(TOKENS, KVW), (((0,), (0,)), ((), ())), preferred_element_type=jnp.float32)
    return jnp.pad(gradient, ((0, OWN * N_FSDP - D), (0, 0))), balanced_values
```

```python
import functools

import jax
import jax.numpy as jnp
from jax import lax
from jax.experimental import pallas as pl
from jax.experimental.pallas import tpu as pltpu
from jax.sharding import PartitionSpec as P

D = 4096
HD = 128
CAP = 32
HALF = 128
LANE = 128
INFO = 16
MIB = 1 << 20
BF16 = jnp.bfloat16
F32 = jnp.float32

VMEM = pl.BlockSpec(memory_space=pltpu.VMEM)
SMEM = pl.BlockSpec(memory_space=pltpu.SMEM)
ANY = pl.BlockSpec(memory_space=pl.ANY)


def attend_kernel(per_group, loss_ref, exponent_ref, start_ref, rows_ref, q_ref, k_ref, g_ref, doc_ref, index_ref, v_ref):
    exponent = exponent_ref[0]
    unscale = jnp.float32(1.0)
    for bit in range(5):
        unscale = unscale * jnp.where((exponent >> bit) & 1 == 1, jnp.float32(2.0 ** -(1 << bit)), 1.0)
    row = lax.broadcasted_iota(jnp.int32, (HALF, HALF), 0)
    col = lax.broadcasted_iota(jnp.int32, (HALF, HALF), 1)
    for half in range(2):
        span = pl.ds(half * HALF, HALF)
        doc_i = jnp.broadcast_to(doc_ref[:, span], (HALF, HALF))
        allowed = (doc_i == doc_i.T) & (row <= col)
        index = index_ref[:, span]
        factor = jnp.zeros((1, HALF), F32)
        for entry in range(loss_ref.shape[0]):
            factor = jnp.where(index == entry, loss_ref[entry], factor)
        factor = jnp.broadcast_to(factor * unscale, (HALF, HALF)).T
        q_all = jnp.concatenate([q_ref[span, pl.ds(n * HD, HD)] for n in range(per_group)], axis=0)
        scores = lax.dot_general(
            k_ref[span, :], q_all, (((1,), (1,)), ((), ())), preferred_element_type=F32
        ) * HD ** (-0.5)
        probs = []
        weighted = []
        for n in range(per_group):
            own = jnp.where(allowed, scores[:, n * HALF:(n + 1) * HALF], -1e30)
            expo = jnp.exp(own - jnp.max(own, axis=0, keepdims=True))
            probs.append((expo / jnp.sum(expo, axis=0, keepdims=True)).astype(BF16))
            weighted.append((g_ref[span, pl.ds(n * HD, HD)].astype(F32) * factor).astype(BF16))
        values = jnp.dot(
            jnp.concatenate(probs, axis=1), jnp.concatenate(weighted, axis=0), preferred_element_type=F32
        )
        v_ref[span, :] = values.astype(BF16)
    info_row = lax.broadcasted_iota(jnp.int32, (INFO, HD), 0)
    info = jnp.zeros((INFO, HD), jnp.int32)
    for level in range(min(start_ref.shape[1], INFO // 2)):
        info = jnp.where(info_row == 2 * level, start_ref[0, level], info)
        info = jnp.where(info_row == 2 * level + 1, rows_ref[0, level], info)
    v_ref[pl.ds(2 * HALF, INFO), :] = info.astype(F32).astype(BF16)


def attend(query, key, grad, ids, index, loss, exponent, start, rows):
    tokens, key_width = key.shape
    groups = key_width // HD
    per_group = query.shape[1] // key_width
    wide = per_group * HD
    return pl.pallas_call(
        functools.partial(attend_kernel, per_group),
        grid=(groups,),
        in_specs=[SMEM] * 4 + [
            pl.BlockSpec((tokens, wide), lambda g: (0, g)),
            pl.BlockSpec((tokens, HD), lambda g: (0, g)),
            pl.BlockSpec((tokens, wide), lambda g: (0, g)),
            pl.BlockSpec((1, tokens), lambda g: (0, 0)),
            pl.BlockSpec((1, tokens), lambda g: (0, 0)),
        ],
        out_specs=pl.BlockSpec((tokens + INFO, HD), lambda g: (0, g)),
        out_shape=jax.ShapeDtypeStruct((tokens + INFO, key_width), BF16),
        compiler_params=pltpu.CompilerParams(vmem_limit_bytes=32 * MIB),
        cost_estimate=pl.CostEstimate(flops=600_000_000, bytes_accessed=3 * MIB, transcendentals=500_000),
        name="attend",
    )(loss, exponent, start, rows, query, key, grad, ids.reshape(1, tokens), index.reshape(1, tokens))


CORE, Y, X = 8, 16, 1


def xor_permute(value, mask):
    count = lax.axis_size("dp") * lax.axis_size("fsdp")
    return lax.ppermute(value, ("dp", "fsdp"), [(i, i ^ mask) for i in range(count)])


def pieces_kernel(x_ref, near_ref, a2_ref, a3_ref, b2_ref, b3_ref, own_ref, sems):
    dp = lax.axis_index("dp")
    fsdp = lax.axis_index("fsdp")

    def column(dp_flip, fsdp_flip):
        owner = fsdp ^ fsdp_flip
        return pl.multiple_of(owner * 512 + (dp ^ dp_flip) * LANE, LANE)

    copies = []

    def put(target, at, dp_flip, fsdp_flip):
        copy = pltpu.make_async_copy(
            x_ref.at[:, pl.ds(column(dp_flip, fsdp_flip), LANE)], target.at[:, pl.ds(at, LANE)], sems.at[len(copies)]
        )
        copy.start()
        copies.append(copy)

    a_targets = {3: a3_ref, 2: a2_ref, 1: near_ref.at[0], 0: own_ref.at[0]}
    b_targets = {3: b3_ref, 2: b2_ref, 1: near_ref.at[1], 0: own_ref.at[1]}
    for m in (2, 3, 1, 0):
        for far in range(2):
            for z in range(2):
                at = (far * 2 + z) * LANE
                put(a_targets[m], at, m, (z << 1) | far)
                put(b_targets[m], at, (m & 1) | (far << 1), ((2 + z) << 1) | (m >> 1))
    for copy in copies:
        copy.wait()


def make_pieces(layer_input):
    tokens = layer_input.shape[0]
    one = jax.ShapeDtypeStruct((tokens, 512), BF16)
    two = jax.ShapeDtypeStruct((2, tokens, 512), BF16)
    return pl.pallas_call(
        pieces_kernel,
        in_specs=[ANY],
        out_specs=[ANY] * 6,
        out_shape=[two, one, one, one, one, two],
        scratch_shapes=[pltpu.SemaphoreType.DMA((32,))],
        cost_estimate=pl.CostEstimate(flops=0, bytes_accessed=4 * MIB, transcendentals=0),
        name="pieces",
    )(layer_input)


def partial_kernel(which, own_ref, near_ref, far_ref, diagonal_ref, v0_ref, v1_ref, v2_ref, v3_ref, keep_ref, send_ref):
    total = None
    tokens = far_ref.shape[0]
    for x, v in (
        (own_ref[which], v0_ref), (near_ref[which], v1_ref), (far_ref[...], v2_ref), (diagonal_ref[...], v3_ref)
    ):
        term = lax.dot_general(x, v[:tokens, :], (((0,), (0,)), ((), ())), preferred_element_type=F32)
        total = term if total is None else total + term
    keep_ref[...] = total[:256]
    send_ref[...] = total[256:].astype(BF16)


def partial_sums(which, own, near, far, diagonal, values):
    return pl.pallas_call(
        functools.partial(partial_kernel, which),
        in_specs=[VMEM] * 8,
        out_specs=[VMEM] * 2,
        out_shape=[jax.ShapeDtypeStruct((256, 512), F32), jax.ShapeDtypeStruct((256, 512), BF16)],
        compiler_params=pltpu.CompilerParams(vmem_limit_bytes=32 * MIB),
        cost_estimate=pl.CostEstimate(flops=540_000_000, bytes_accessed=4 * MIB, transcendentals=0),
        name="partial_sums",
    )(own, near, far, diagonal, *values)


def balance_kernel(v0_ref, v1_ref, v2_ref, v3_ref, out_ref):
    refs = (v0_ref, v1_ref, v2_ref, v3_ref)
    tokens = out_ref.shape[0]
    infos = [ref[pl.ds(tokens, INFO), pl.ds(0, HALF)].astype(F32).astype(jnp.int32) for ref in refs]

    def table(device, entry):
        return jnp.broadcast_to(infos[device][entry:entry + 1, :], (HALF, HALF))

    place = lax.broadcasted_iota(jnp.int32, (HALF, HALF), 0) + HALF
    inner = lax.broadcasted_iota(jnp.int32, (HALF, HALF), 1) + HALF

    def source(device, at):
        first = table(device, 0)
        swapped = (at >= first) & (at < first + table(device, 1))
        return swapped, jnp.where(swapped, table(device ^ 1, 0) + at - first, at)

    first = table(0, 2)
    outer = (place >= first) & (place < first + table(0, 3))
    swapped_here, here = source(0, place)
    swapped_there, there = source(2, table(2, 2) + place - first)
    position = jnp.where(outer, there, here)
    device = jnp.where(outer, jnp.where(swapped_there, 3, 2), jnp.where(swapped_here, 1, 0))
    total = None
    for number, ref in enumerate(refs):
        pick = jnp.where((device == number) & (position == inner), 1.0, 0.0).astype(BF16)
        term = jnp.dot(pick, ref[pl.ds(HALF, HALF), :], preferred_element_type=F32)
        total = term if total is None else total + term
    out_ref[pl.ds(0, HALF), :] = v0_ref[pl.ds(0, HALF), :]
    out_ref[pl.ds(HALF, HALF), :] = total.astype(BF16)


def balance(values):
    return pl.pallas_call(
        balance_kernel,
        in_specs=[VMEM] * 4,
        out_specs=VMEM,
        out_shape=jax.ShapeDtypeStruct((2 * HALF, values[0].shape[1]), BF16),
        compiler_params=pltpu.CompilerParams(vmem_limit_bytes=32 * MIB),
        cost_estimate=pl.CostEstimate(flops=70_000_000, bytes_accessed=MIB, transcendentals=0),
        name="balance",
    )(*values)


def place_kernel(pair_ref, near_ref, out_ref):
    dp = lax.axis_index("dp")
    for ref, core in ((pair_ref, 0), (near_ref, 1)):
        for y in range(2):
            quarter = dp ^ (core | y << 1)
            out_ref[pl.ds(pl.multiple_of(quarter * LANE, LANE), LANE), :] = ref[y].astype(F32)


def place(pair, near):
    return pl.pallas_call(
        place_kernel,
        in_specs=[VMEM] * 2,
        out_specs=VMEM,
        out_shape=jax.ShapeDtypeStruct((512, pair.shape[2]), F32),
        cost_estimate=pl.CostEstimate(flops=0, bytes_accessed=2 * MIB, transcendentals=0),
        name="place",
    )(pair, near)


def reduce_by_axis(layer_input, values):
    near, a2, a3, b2, b3, own = make_pieces(layer_input)
    a2 = xor_permute(a2, Y)
    b2 = xor_permute(b2, X)
    a3 = xor_permute(a3, Y | CORE)
    b3 = xor_permute(b3, X | CORE)
    near = xor_permute(near, CORE)
    values = values()
    v_core = xor_permute(values, CORE)
    v_y = xor_permute(values, Y)
    v_x = xor_permute(values, X)
    v_y_core = xor_permute(v_y, CORE)
    v_x_core = xor_permute(v_x, CORE)
    b_keep, b_send = partial_sums(1, own, near, b2, b3, (values, v_core, v_x, v_x_core))
    a_keep, a_send = partial_sums(0, own, near, a2, a3, (values, v_core, v_y, v_y_core))
    b_total = b_keep + xor_permute(b_send, Y).astype(F32)
    a_total = a_keep + xor_permute(a_send, X).astype(F32)
    z2 = xor_permute(b_total[:LANE].astype(BF16), 4)
    z3 = xor_permute(b_total[LANE:].astype(BF16), 6)
    z1 = xor_permute(a_total[LANE:].astype(BF16), 2)
    mine = (a_total[:LANE] + z1.astype(F32) + (z2.astype(F32) + z3.astype(F32))).astype(BF16)
    pair = jnp.stack([mine, xor_permute(mine, Y)])
    grad_value = place(pair, xor_permute(pair, CORE))
    return grad_value, balance((values, v_core, v_y, v_y_core))


def swapped(block, axis, distance):
    count = lax.axis_size(axis)
    route = []
    for low in range(count):
        high = low | 1 << distance
        if high != low and high < count:
            route += [(low, high), (high, low)]
    return lax.ppermute(block, axis, route)


def blend_rows(item, incoming, offset, extent):
    inside = (jnp.arange(CAP) < extent)[:, None]
    chosen = jnp.where(inside, incoming, lax.dynamic_slice_in_dim(item, offset, CAP, 0))
    return lax.dynamic_update_slice_in_dim(item, chosen, offset, 0)


def reduce_by_owner(layer_input, values, swap_start, swap_rows):
    tokens = layer_input.shape[0]
    values = values()[:tokens]
    balanced = values
    for level in range(lax.axis_size("dp").bit_length() - 1):
        offset = swap_start[0, level]
        window = lax.dynamic_slice_in_dim(balanced, offset, CAP, 0)
        balanced = blend_rows(balanced, swapped(window, "dp", level), offset, swap_rows[0, level])
    owners = lax.axis_size("fsdp")
    owned = (D + owners - 1) // owners
    padded = jnp.pad(layer_input, ((0, 0), (0, owned * owners - D)))
    arranged = lax.all_to_all(
        padded.reshape(tokens, owners, owned), "fsdp", split_axis=1, concat_axis=0, tiled=True
    )
    block = lax.dot_general(
        arranged.reshape(-1, owned),
        lax.all_gather(values, "fsdp", axis=0, tiled=True),
        (((0,), (0,)), ((), ())),
        preferred_element_type=F32,
    )
    return lax.psum(block, "dp"), balanced


def on_device(
    layer_input,
    query_states,
    key_states,
    output_grad,
    document_ids,
    weight_index,
    loss_weights,
    scale_exponent,
    swap_start,
    swap_rows,
):
    def values():
        return attend(
            query_states, key_states, output_grad, document_ids, weight_index,
            loss_weights, scale_exponent, swap_start, swap_rows,
        )

    if lax.axis_size("dp") == 4 and lax.axis_size("fsdp") == 8:
        return reduce_by_axis(layer_input, values)
    return reduce_by_owner(layer_input, values, swap_start, swap_rows)


def solution(mesh):
    return jax.shard_map(
        on_device,
        mesh=mesh,
        in_specs=(
            P(("dp", "fsdp"), None),
            P(("dp", "fsdp"), None),
            P(("dp", "fsdp"), None),
            P(("dp", "fsdp"), None),
            P(("dp", "fsdp")),
            P(("dp", "fsdp")),
            P(),
            P(("dp", "fsdp")),
            P(("dp", "fsdp"), None),
            P(("dp", "fsdp"), None),
        ),
        out_specs=(P("fsdp", None), P(("dp", "fsdp"), None)),
        check_vma=False,
    )
```

```python
import functools

import jax
import jax.numpy as jnp
from jax import lax
from jax.experimental import pallas as pl
from jax.experimental.pallas import tpu as pltpu
from jax.sharding import PartitionSpec as P

D = 4096
HD = 128
CAP = 32
HALF = 128
LANE = 128
INFO = 16
MIB = 1 << 20
BF16 = jnp.bfloat16
F32 = jnp.float32

VMEM = pl.BlockSpec(memory_space=pltpu.VMEM)
HBM = pl.BlockSpec(memory_space=pltpu.HBM)


def attend_group(per_group, span, q, k, g, allowed, factor):
    q_all = jnp.concatenate([q[span, n * HD:(n + 1) * HD] for n in range(per_group)], axis=0)
    scores = lax.dot_general(
        k[span, :], q_all, (((1,), (1,)), ((), ())), preferred_element_type=F32
    ) * HD ** (-0.5)
    probs = []
    weighted = []
    for n in range(per_group):
        own = jnp.where(allowed, scores[:, n * HALF:(n + 1) * HALF], -1e30)
        expo = jnp.exp(own - jnp.max(own, axis=0, keepdims=True))
        probs.append((expo / jnp.sum(expo, axis=0, keepdims=True)).astype(BF16))
        weighted.append((g[span, n * HD:(n + 1) * HD].astype(F32) * factor).astype(BF16))
    return jnp.dot(
        jnp.concatenate(probs, axis=1), jnp.concatenate(weighted, axis=0), preferred_element_type=F32
    ).astype(BF16)


def mask_and_factor(span, loss_ref, exponent_ref, ids_ref, index_ref):
    exponent = exponent_ref[0]
    unscale = jnp.float32(1.0)
    for bit in range(5):
        unscale = unscale * jnp.where((exponent >> bit) & 1 == 1, jnp.float32(2.0 ** -(1 << bit)), 1.0)
    row = lax.broadcasted_iota(jnp.int32, (HALF, HALF), 0)
    col = lax.broadcasted_iota(jnp.int32, (HALF, HALF), 1)
    doc_i = jnp.broadcast_to(ids_ref[:, span], (HALF, HALF))
    allowed = (doc_i == doc_i.T) & (row <= col)
    index = index_ref[:, span]
    factor = jnp.zeros((1, HALF), F32)
    for entry in range(loss_ref.shape[0]):
        factor = jnp.where(index == entry, loss_ref[entry], factor)
    return allowed, jnp.broadcast_to(factor * unscale, (HALF, HALF)).T


def front_kernel(
    split, per_group, loss_hbm, exponent_hbm, start_hbm, rows_hbm, q_hbm, k_hbm, g_hbm, ids_hbm, index_hbm, *rest
):
    if split:
        x_hbm, own_ref, near_ref, y1_ref, x1_ref, *pieces = rest[:11]
        rest = rest[11:]
        v_refs = (own_ref, near_ref, y1_ref, x1_ref)
    else:
        v_refs = rest[:1]
        rest = rest[1:]
    loss_ref, exponent_ref, start_ref, rows_ref, q_ref, k_ref, g_ref, ids_ref, index_ref, sems = rest
    count = 0

    def begin(source, target):
        nonlocal count
        copy = pltpu.make_async_copy(source, target, sems.at[count])
        copy.start()
        count += 1
        return copy

    small = [
        begin(source, target)
        for source, target in (
            (ids_hbm, ids_ref), (index_hbm, index_ref), (loss_hbm, loss_ref), (exponent_hbm, exponent_ref),
            (start_hbm, start_ref), (rows_hbm, rows_ref),
        )
    ]
    groups = k_ref.shape[1] // HD
    wide = per_group * HD
    loads = []
    for group in range(groups):
        some = pl.ds(group * wide, wide)
        one = pl.ds(group * HD, HD)
        loads.append([
            begin(q_hbm.at[:, some], q_ref.at[:, some]),
            begin(k_hbm.at[:, one], k_ref.at[:, one]),
            begin(g_hbm.at[:, some], g_ref.at[:, some]),
        ])
    cuts = []
    if split:
        dp = lax.axis_index("dp")
        fsdp = lax.axis_index("fsdp")

        def cut(target, row, dp_flips, fsdp_flips):
            for far in range(2):
                owner = fsdp ^ fsdp_flips[far]
                column = pl.multiple_of(owner * (4 * LANE) + (dp ^ dp_flips[far]) * LANE, LANE)
                cuts.append(begin(
                    x_hbm.at[:, pl.ds(column, LANE)],
                    target.at[pl.ds(row, 2 * HALF), pl.ds(far * LANE, LANE)],
                ))

        def cut_a(target, row, m, z):
            cut(target, row, (m, m), (z << 1, z << 1 | 1))

        def cut_b(target, row, m, z):
            cut(target, row, (m & 1, m & 1 | 2), (z << 1 | m >> 1, z << 1 | m >> 1))

        a3_1, b3_1, a2_2, a3_2, b2_2, b3_2 = pieces
        cut_a(y1_ref, VROWS, 2, 2)
        cut_b(x1_ref, VROWS, 2, 3)
        cut_a(a3_1, 0, 3, 2)
        cut_b(b3_1, 0, 3, 3)
        for m, ref in ((1, near_ref), (0, own_ref)):
            cut_a(ref, VROWS, m, 2)
            cut_b(ref, VROWS + 256, m, 3)
            cut_a(ref, VROWS + 512, m, 0)
            cut_b(ref, VROWS + 768, m, 1)
        cut_a(a2_2, 0, 2, 0)
        cut_b(b2_2, 0, 2, 1)
        cut_a(a3_2, 0, 3, 0)
        cut_b(b3_2, 0, 3, 1)
    for copy in small:
        copy.wait()
    masks = [
        mask_and_factor(pl.ds(half * HALF, HALF), loss_ref, exponent_ref, ids_ref, index_ref) for half in range(2)
    ]

    def put(group, row, value):
        for ref in v_refs:
            ref[pl.ds((group // 2) * (2 * HALF + INFO) + row, value.shape[0]), pl.ds(group % 2 * HD, HD)] = value

    info_row = lax.broadcasted_iota(jnp.int32, (INFO, HD), 0)
    info = jnp.zeros((INFO, HD), jnp.int32)
    for level in range(min(start_ref.shape[1], INFO // 2)):
        info = jnp.where(info_row == 2 * level, start_ref[0, level], info)
        info = jnp.where(info_row == 2 * level + 1, rows_ref[0, level], info)
    info = info.astype(F32).astype(BF16)
    for group in range(groups):
        for copy in loads[group]:
            copy.wait()
        some = pl.ds(group * wide, wide)
        for half in range(2):
            span = pl.ds(half * HALF, HALF)
            value = attend_group(
                per_group, slice(None), q_ref[span, some], k_ref[span, pl.ds(group * HD, HD)], g_ref[span, some],
                *masks[half],
            )
            put(group, half * HALF, value)
        put(group, 2 * HALF, info)
    for copy in cuts:
        copy.wait()


def front(split, layer_input, query, key, grad, ids, index, loss, exponent, start, rows):
    tokens, key_width = key.shape
    per_group = query.shape[1] // key_width
    groups = key_width // HD
    v_rows = (tokens + INFO) * (groups // 2)
    heights = [v_rows + 4 * tokens, v_rows + 4 * tokens, v_rows + tokens, v_rows + tokens] + [tokens] * 6
    args = [
        loss, exponent, start, rows, query, key, grad, ids.reshape(1, tokens), index.reshape(1, tokens)
    ]
    return pl.pallas_call(
        functools.partial(front_kernel, split, per_group),
        in_specs=[HBM] * (10 if split else 9),
        out_specs=[VMEM] * (10 if split else 1),
        out_shape=[jax.ShapeDtypeStruct((height, 2 * HD), BF16) for height in (heights if split else [v_rows])],
        scratch_shapes=[
            pltpu.SMEM(loss.shape, F32), pltpu.SMEM(exponent.shape, jnp.int32),
            pltpu.SMEM(start.shape, jnp.int32), pltpu.SMEM(rows.shape, jnp.int32),
            pltpu.VMEM(query.shape, BF16), pltpu.VMEM(key.shape, BF16), pltpu.VMEM(grad.shape, BF16),
            pltpu.VMEM((1, tokens), jnp.int32), pltpu.VMEM((1, tokens), jnp.int32),
            pltpu.SemaphoreType.DMA((6 + 3 * groups + 32,)),
        ],
        compiler_params=pltpu.CompilerParams(vmem_limit_bytes=32 * MIB),
        cost_estimate=pl.CostEstimate(flops=600_000_000, bytes_accessed=8 * MIB, transcendentals=500_000),
        name="front",
    )(*(args + [layer_input] if split else args))


CORE, Y, X = 8, 16, 1
VROWS = 2 * (2 * HALF + INFO)


def xor_permute(value, mask):
    count = lax.axis_size("dp") * lax.axis_size("fsdp")
    return lax.ppermute(value, ("dp", "fsdp"), [(i, i ^ mask) for i in range(count)])


def partial_kernel(number, own_ref, near_ref, v2_ref, v3_ref, *rest):
    *far_refs, diagonal_ref, keep_ref, send_ref = rest
    row = VROWS + 256 * number
    far = far_refs[0][...] if far_refs else v2_ref[pl.ds(VROWS, 256), :]
    x = jnp.concatenate([own_ref[pl.ds(row, 256), :], near_ref[pl.ds(row, 256), :], far, diagonal_ref[...]], axis=0)
    for part in range(2):
        v = jnp.concatenate(
            [ref[pl.ds(part * (256 + INFO), 256), :] for ref in (own_ref, near_ref, v2_ref, v3_ref)], axis=0
        )
        total = lax.dot_general(x, v, (((0,), (0,)), ((), ())), preferred_element_type=F32)
        keep_ref[:, pl.ds(256 * part, 256)] = total[:LANE]
        send_ref[:, pl.ds(256 * part, 256)] = total[LANE:].astype(BF16)


def partial_sums(number, *args):
    return pl.pallas_call(
        functools.partial(partial_kernel, number),
        in_specs=[VMEM] * len(args),
        out_specs=[VMEM] * 2,
        out_shape=[jax.ShapeDtypeStruct((LANE, 512), F32), jax.ShapeDtypeStruct((LANE, 512), BF16)],
        compiler_params=pltpu.CompilerParams(vmem_limit_bytes=32 * MIB),
        cost_estimate=pl.CostEstimate(flops=270_000_000, bytes_accessed=2 * MIB, transcendentals=0),
        name="partial_sums",
    )(*args)


def balance_kernel(v0_ref, v1_ref, v2_ref, v3_ref, out_ref):
    refs = (v0_ref, v1_ref, v2_ref, v3_ref)
    tokens = out_ref.shape[0]
    infos = [ref[pl.ds(tokens, INFO), pl.ds(0, HALF)].astype(F32).astype(jnp.int32) for ref in refs]

    def table(device, entry):
        return jnp.broadcast_to(infos[device][entry:entry + 1, :], (HALF, HALF))

    place = lax.broadcasted_iota(jnp.int32, (HALF, HALF), 0) + HALF
    inner = lax.broadcasted_iota(jnp.int32, (HALF, HALF), 1) + HALF

    def source(device, at):
        first = table(device, 0)
        swapped = (at >= first) & (at < first + table(device, 1))
        return swapped, jnp.where(swapped, table(device ^ 1, 0) + at - first, at)

    first = table(0, 2)
    outer = (place >= first) & (place < first + table(0, 3))
    swapped_here, here = source(0, place)
    swapped_there, there = source(2, table(2, 2) + place - first)
    position = jnp.where(outer, there, here)
    device = jnp.where(outer, jnp.where(swapped_there, 3, 2), jnp.where(swapped_here, 1, 0))
    for part in range(2):
        base = part * (tokens + INFO)
        some = pl.ds(256 * part, 256)
        total = None
        for number, ref in enumerate(refs):
            pick = jnp.where((device == number) & (position == inner), 1.0, 0.0).astype(BF16)
            term = jnp.dot(pick, ref[pl.ds(base + HALF, HALF), :], preferred_element_type=F32)
            total = term if total is None else total + term
        out_ref[pl.ds(0, HALF), some] = v0_ref[pl.ds(base, HALF), :]
        out_ref[pl.ds(HALF, HALF), some] = total.astype(BF16)


def balance(values):
    return pl.pallas_call(
        balance_kernel,
        in_specs=[VMEM] * 4,
        out_specs=VMEM,
        out_shape=jax.ShapeDtypeStruct((2 * HALF, 512), BF16),
        compiler_params=pltpu.CompilerParams(vmem_limit_bytes=32 * MIB),
        cost_estimate=pl.CostEstimate(flops=70_000_000, bytes_accessed=MIB, transcendentals=0),
        name="balance",
    )(*values)


def place_kernel(mine_ref, y_ref, near_ref, out_ref):
    dp = lax.axis_index("dp")
    for flip, block in ((0, mine_ref), (2, y_ref), (1, near_ref.at[0]), (3, near_ref.at[1])):
        out_ref[pl.ds(pl.multiple_of((dp ^ flip) * LANE, LANE), LANE), :] = block[...].astype(F32)


def place(mine, from_y, near):
    return pl.pallas_call(
        place_kernel,
        in_specs=[VMEM] * 3,
        out_specs=VMEM,
        out_shape=jax.ShapeDtypeStruct((512, 512), F32),
        compiler_params=pltpu.CompilerParams(vmem_limit_bytes=8 * MIB),
        cost_estimate=pl.CostEstimate(flops=0, bytes_accessed=2 * MIB, transcendentals=0),
        name="place",
    )(mine, from_y, near)


def reduce_by_axis(*args):
    own, near, y1, x1, a3_1, b3_1, a2_2, a3_2, b2_2, b3_2 = front(True, *args)
    y1 = xor_permute(y1, Y)
    x1 = xor_permute(x1, X)
    near = xor_permute(near, CORE)
    a3_1 = xor_permute(a3_1, Y | CORE)
    b3_1 = xor_permute(b3_1, X | CORE)
    a2_2 = xor_permute(a2_2, Y)
    b2_2 = xor_permute(b2_2, X)
    a3_2 = xor_permute(a3_2, Y | CORE)
    b3_2 = xor_permute(b3_2, X | CORE)
    y_core = xor_permute(y1[:VROWS], CORE)
    x_core = xor_permute(x1[:VROWS], CORE)
    keep_a1, send_a1 = partial_sums(0, own, near, y1, y_core, a3_1)
    keep_b1, send_b1 = partial_sums(1, own, near, x1, x_core, b3_1)
    keep_a2, send_a2 = partial_sums(2, own, near, y1, y_core, a2_2, a3_2)
    keep_b2, send_b2 = partial_sums(3, own, near, x1, x_core, b2_2, b3_2)
    z2 = xor_permute((keep_a1 + xor_permute(send_a1, X).astype(F32)).astype(BF16), 4)
    z3 = xor_permute((keep_b1 + xor_permute(send_b1, Y).astype(F32)).astype(BF16), 6)
    total = keep_a2 + xor_permute(send_a2, X).astype(F32)
    z1 = xor_permute((keep_b2 + xor_permute(send_b2, Y).astype(F32)).astype(BF16), 2)
    mine = (total + z1.astype(F32) + (z2.astype(F32) + z3.astype(F32))).astype(BF16)
    from_y = xor_permute(mine, Y)
    grad_value = place(mine, from_y, xor_permute(jnp.stack([mine, from_y]), CORE))
    return grad_value, balance((own, near, y1, y_core))


def swapped(block, axis, distance):
    count = lax.axis_size(axis)
    route = []
    for low in range(count):
        high = low | 1 << distance
        if high != low and high < count:
            route += [(low, high), (high, low)]
    return lax.ppermute(block, axis, route)


def blend_rows(item, incoming, offset, extent):
    inside = (jnp.arange(CAP) < extent)[:, None]
    chosen = jnp.where(inside, incoming, lax.dynamic_slice_in_dim(item, offset, CAP, 0))
    return lax.dynamic_update_slice_in_dim(item, chosen, offset, 0)


def reduce_by_owner(layer_input, *args):
    swap_start, swap_rows = args[-2:]
    tokens = layer_input.shape[0]
    halves = front(False, layer_input, *args)[0].reshape(2, tokens + INFO, 2 * HD)[:, :tokens]
    values = jnp.concatenate([halves[0], halves[1]], axis=1)
    balanced = values
    for level in range(lax.axis_size("dp").bit_length() - 1):
        offset = swap_start[0, level]
        window = lax.dynamic_slice_in_dim(balanced, offset, CAP, 0)
        balanced = blend_rows(balanced, swapped(window, "dp", level), offset, swap_rows[0, level])
    owners = lax.axis_size("fsdp")
    owned = (D + owners - 1) // owners
    padded = jnp.pad(layer_input, ((0, 0), (0, owned * owners - D)))
    arranged = lax.all_to_all(
        padded.reshape(tokens, owners, owned), "fsdp", split_axis=1, concat_axis=0, tiled=True
    )
    block = lax.dot_general(
        arranged.reshape(-1, owned),
        lax.all_gather(values, "fsdp", axis=0, tiled=True),
        (((0,), (0,)), ((), ())),
        preferred_element_type=F32,
    )
    return lax.psum(block, "dp"), balanced


def on_device(layer_input, *args):
    if lax.axis_size("dp") == 4 and lax.axis_size("fsdp") == 8:
        return reduce_by_axis(layer_input, *args)
    return reduce_by_owner(layer_input, *args)


def solution(mesh):
    return jax.shard_map(
        on_device,
        mesh=mesh,
        in_specs=(
            P(("dp", "fsdp"), None),
            P(("dp", "fsdp"), None),
            P(("dp", "fsdp"), None),
            P(("dp", "fsdp"), None),
            P(("dp", "fsdp")),
            P(("dp", "fsdp")),
            P(),
            P(("dp", "fsdp")),
            P(("dp", "fsdp"), None),
            P(("dp", "fsdp"), None),
        ),
        out_specs=(P("fsdp", None), P(("dp", "fsdp"), None)),
        check_vma=False,
    )
```

```python
import functools

import jax
import jax.numpy as jnp
from jax import lax
from jax.experimental import pallas as pl
from jax.experimental.pallas import tpu as pltpu
from jax.sharding import PartitionSpec as P

D = 4096
HD = 128
CAP = 32
HALF = 128
LANE = 128
INFO = 16
MIB = 1 << 20
FREE = pl.CostEstimate(flops=0, bytes_accessed=0, transcendentals=0)
BF16 = jnp.bfloat16
F32 = jnp.float32

VMEM = pl.BlockSpec(memory_space=pltpu.VMEM)
HBM = pl.BlockSpec(memory_space=pltpu.HBM)


def attend_group(per_group, span, q, k, g, allowed, factor):
    q_all = jnp.concatenate([q[span, n * HD:(n + 1) * HD] for n in range(per_group)], axis=0)
    scores = lax.dot_general(
        k[span, :], q_all, (((1,), (1,)), ((), ())), preferred_element_type=F32
    ) * HD ** (-0.5)
    probs = []
    weighted = []
    for n in range(per_group):
        own = jnp.where(allowed, scores[:, n * HALF:(n + 1) * HALF], -1e30)
        expo = jnp.exp(own - jnp.max(own, axis=0, keepdims=True))
        probs.append((expo / jnp.sum(expo, axis=0, keepdims=True)).astype(BF16))
        weighted.append((g[span, n * HD:(n + 1) * HD].astype(F32) * factor).astype(BF16))
    return jnp.dot(
        jnp.concatenate(probs, axis=1), jnp.concatenate(weighted, axis=0), preferred_element_type=F32
    ).astype(BF16)


def mask_and_factor(span, loss_ref, exponent_ref, ids_ref, index_ref):
    exponent = exponent_ref[0]
    unscale = jnp.float32(1.0)
    for bit in range(5):
        unscale = unscale * jnp.where((exponent >> bit) & 1 == 1, jnp.float32(2.0 ** -(1 << bit)), 1.0)
    row = lax.broadcasted_iota(jnp.int32, (HALF, HALF), 0)
    col = lax.broadcasted_iota(jnp.int32, (HALF, HALF), 1)
    doc_i = jnp.broadcast_to(ids_ref[:, span], (HALF, HALF))
    allowed = (doc_i == doc_i.T) & (row <= col)
    index = index_ref[:, span]
    factor = jnp.zeros((1, HALF), F32)
    for entry in range(loss_ref.shape[0]):
        factor = jnp.where(index == entry, loss_ref[entry], factor)
    return allowed, jnp.broadcast_to(factor * unscale, (HALF, HALF)).T


def front_kernel(
    split, per_group, loss_hbm, exponent_hbm, start_hbm, rows_hbm, q_hbm, k_hbm, g_hbm, ids_hbm, index_hbm, *rest
):
    if split:
        x_hbm, own1_ref, near1_ref, own2_ref, near2_ref = rest[:5]
        rest = rest[5:]
        v_refs = (own1_ref, near1_ref)
    else:
        v_refs = rest[:1]
        rest = rest[1:]
    loss_ref, exponent_ref, start_ref, rows_ref, q_ref, k_ref, g_ref, ids_ref, index_ref, sems = rest
    count = 0

    def begin(source, target):
        nonlocal count
        copy = pltpu.make_async_copy(source, target, sems.at[count])
        copy.start()
        count += 1
        return copy

    small = [
        begin(source, target)
        for source, target in (
            (ids_hbm, ids_ref), (index_hbm, index_ref), (loss_hbm, loss_ref), (exponent_hbm, exponent_ref),
            (start_hbm, start_ref), (rows_hbm, rows_ref),
        )
    ]
    groups = k_ref.shape[1] // HD
    wide = per_group * HD
    loads = []
    for group in range(groups):
        some = pl.ds(group * wide, wide)
        one = pl.ds(group * HD, HD)
        loads.append([
            begin(q_hbm.at[:, some], q_ref.at[:, some]),
            begin(k_hbm.at[:, one], k_ref.at[:, one]),
            begin(g_hbm.at[:, some], g_ref.at[:, some]),
        ])
    cuts = []
    if split:
        dp = lax.axis_index("dp")
        fsdp = lax.axis_index("fsdp")

        def cut(target, row, core, z, flips):
            for at, (y, x) in enumerate(flips):
                owner = fsdp ^ (z << 1 | x)
                column = pl.multiple_of(owner * (4 * LANE) + (dp ^ (y << 1 | core)) * LANE, LANE)
                cuts.append(begin(
                    x_hbm.at[:, pl.ds(column, LANE)],
                    target.at[pl.ds(row, 2 * HALF), pl.ds(at * LANE, LANE)],
                ))

        for core, row, z_a, z_b, target in (
            (1, VROWS, 2, 3, near1_ref), (0, VROWS, 2, 3, own1_ref), (1, 0, 0, 1, near2_ref), (0, 0, 0, 1, own2_ref)
        ):
            cut(target, row, core, z_a, ((1, 1), (1, 0)))
            cut(target, row + 256, core, z_b, ((1, 1), (0, 1)))
            cut(target, row + 512, core, z_a, ((0, 1), (0, 0)))
            cut(target, row + 768, core, z_b, ((1, 0), (0, 0)))
    for copy in small:
        copy.wait()
    masks = [
        mask_and_factor(pl.ds(half * HALF, HALF), loss_ref, exponent_ref, ids_ref, index_ref) for half in range(2)
    ]

    def put(group, row, value):
        for ref in v_refs:
            ref[pl.ds((group // 2) * (2 * HALF + INFO) + row, value.shape[0]), pl.ds(group % 2 * HD, HD)] = value

    info_row = lax.broadcasted_iota(jnp.int32, (INFO, HD), 0)
    info = jnp.zeros((INFO, HD), jnp.int32)
    for level in range(min(start_ref.shape[1], INFO // 2)):
        info = jnp.where(info_row == 2 * level, start_ref[0, level], info)
        info = jnp.where(info_row == 2 * level + 1, rows_ref[0, level], info)
    info = info.astype(F32).astype(BF16)
    for group in range(groups):
        for copy in loads[group]:
            copy.wait()
        some = pl.ds(group * wide, wide)
        for half in range(2):
            span = pl.ds(half * HALF, HALF)
            value = attend_group(
                per_group, slice(None), q_ref[span, some], k_ref[span, pl.ds(group * HD, HD)], g_ref[span, some],
                *masks[half],
            )
            put(group, half * HALF, value)
        put(group, 2 * HALF, info)
    for copy in cuts:
        copy.wait()


def front(split, layer_input, query, key, grad, ids, index, loss, exponent, start, rows):
    tokens, key_width = key.shape
    per_group = query.shape[1] // key_width
    groups = key_width // HD
    v_rows = (tokens + INFO) * (groups // 2)
    heights = [v_rows + 4 * tokens, v_rows + 4 * tokens, 4 * tokens, 4 * tokens]
    args = [
        loss, exponent, start, rows, query, key, grad, ids.reshape(1, tokens), index.reshape(1, tokens)
    ]
    return pl.pallas_call(
        functools.partial(front_kernel, split, per_group),
        in_specs=[HBM] * (10 if split else 9),
        out_specs=[VMEM] * (4 if split else 1),
        out_shape=[jax.ShapeDtypeStruct((height, 2 * HD), BF16) for height in (heights if split else [v_rows])],
        scratch_shapes=[
            pltpu.SMEM(loss.shape, F32), pltpu.SMEM(exponent.shape, jnp.int32),
            pltpu.SMEM(start.shape, jnp.int32), pltpu.SMEM(rows.shape, jnp.int32),
            pltpu.VMEM(query.shape, BF16), pltpu.VMEM(key.shape, BF16), pltpu.VMEM(grad.shape, BF16),
            pltpu.VMEM((1, tokens), jnp.int32), pltpu.VMEM((1, tokens), jnp.int32),
            pltpu.SemaphoreType.DMA((6 + 3 * groups + 32,)),
        ],
        compiler_params=pltpu.CompilerParams(vmem_limit_bytes=32 * MIB),
        cost_estimate=FREE,
        name="front",
    )(*[
        arg if arg is exponent else pltpu.with_memory_space_constraint(arg, pltpu.HBM)
        for arg in (args + [layer_input] if split else args)
    ])


CORE, Y, X = 8, 16, 1
VROWS = 2 * (2 * HALF + INFO)


def xor_permute(value, mask):
    count = lax.axis_size("dp") * lax.axis_size("fsdp")
    return lax.ppermute(value, ("dp", "fsdp"), [(i, i ^ mask) for i in range(count)])


def partial_kernel(row, own_ref, near_ref, v0_ref, v1_ref, a_ref, b_ref):
    for number, out_ref in enumerate((a_ref, b_ref)):
        some = pl.ds(row + 256 * number, 256)
        x = jnp.concatenate([own_ref[some, :], near_ref[some, :]], axis=0)
        for part in range(2):
            v = jnp.concatenate([ref[pl.ds(part * (256 + INFO), 256), :] for ref in (v0_ref, v1_ref)], axis=0)
            total = lax.dot_general(x, v, (((0,), (0,)), ((), ())), preferred_element_type=F32)
            out_ref[:, pl.ds(256 * part, 256)] = total.astype(out_ref.dtype)


def partial_sums(row, dtype, own, near, v0, v1):
    return pl.pallas_call(
        functools.partial(partial_kernel, row),
        in_specs=[VMEM] * 4,
        out_specs=[VMEM] * 2,
        out_shape=[jax.ShapeDtypeStruct((256, 512), dtype)] * 2,
        compiler_params=pltpu.CompilerParams(vmem_limit_bytes=32 * MIB),
        cost_estimate=FREE,
        name="partial_sums",
    )(own, near, v0, v1)


def inner_swap_kernel(v0_ref, v1_ref, out_ref, window_ref):
    tokens = out_ref.shape[0]
    infos = [ref[pl.ds(tokens, INFO), pl.ds(0, HALF)].astype(F32).astype(jnp.int32) for ref in (v0_ref, v1_ref)]

    def table(device, entry):
        return jnp.broadcast_to(infos[device][entry:entry + 1, :], (HALF, HALF))

    place = lax.broadcasted_iota(jnp.int32, (HALF, HALF), 0) + HALF
    inner = lax.broadcasted_iota(jnp.int32, (HALF, HALF), 1) + HALF
    first = table(0, 0)
    moved = (place >= first) & (place < first + table(0, 1))
    stays = jnp.where(~moved & (place == inner), 1.0, 0.0).astype(BF16)
    comes = jnp.where(moved & (place + table(1, 0) - first == inner), 1.0, 0.0).astype(BF16)
    taken = jnp.where(place - HALF + table(0, 2) == inner, 1.0, 0.0).astype(BF16)[:CAP]
    for part in range(2):
        base = part * (tokens + INFO)
        some = pl.ds(256 * part, 256)
        rows = (
            jnp.dot(stays, v0_ref[pl.ds(base + HALF, HALF), :], preferred_element_type=F32)
            + jnp.dot(comes, v1_ref[pl.ds(base + HALF, HALF), :], preferred_element_type=F32)
        ).astype(BF16)
        out_ref[pl.ds(0, HALF), some] = v0_ref[pl.ds(base, HALF), :]
        out_ref[pl.ds(HALF, HALF), some] = rows
        window_ref[:, some] = jnp.dot(taken, rows, preferred_element_type=F32).astype(BF16)


def inner_swap(v0, v1):
    return pl.pallas_call(
        inner_swap_kernel,
        in_specs=[VMEM] * 2,
        out_specs=[VMEM] * 2,
        out_shape=[jax.ShapeDtypeStruct((2 * HALF, 512), BF16), jax.ShapeDtypeStruct((CAP, 512), BF16)],
        compiler_params=pltpu.CompilerParams(vmem_limit_bytes=8 * MIB),
        cost_estimate=FREE,
        name="inner_swap",
    )(v0, v1)


def outer_swap_kernel(v0_ref, rows_ref, window_ref, out_ref):
    tokens = out_ref.shape[0]
    info = v0_ref[pl.ds(tokens, INFO), pl.ds(0, HALF)].astype(F32).astype(jnp.int32)
    first = jnp.broadcast_to(info[2:3, :], (HALF, HALF))
    extent = jnp.broadcast_to(info[3:4, :], (HALF, HALF))
    place = lax.broadcasted_iota(jnp.int32, (HALF, HALF), 0) + HALF
    inner = lax.broadcasted_iota(jnp.int32, (HALF, HALF), 1)
    moved = (place >= first) & (place < first + extent)
    stays = jnp.where(~moved & (place == inner + HALF), 1.0, 0.0).astype(BF16)
    comes = jnp.where(moved & (place - first == inner), 1.0, 0.0).astype(BF16)[:, :CAP]
    out_ref[pl.ds(0, HALF), :] = rows_ref[pl.ds(0, HALF), :]
    out_ref[pl.ds(HALF, HALF), :] = (
        jnp.dot(stays, rows_ref[pl.ds(HALF, HALF), :], preferred_element_type=F32)
        + jnp.dot(comes, window_ref[...], preferred_element_type=F32)
    ).astype(BF16)


def outer_swap(v0, rows, window):
    return pl.pallas_call(
        outer_swap_kernel,
        in_specs=[VMEM] * 3,
        out_specs=VMEM,
        out_shape=jax.ShapeDtypeStruct(rows.shape, BF16),
        compiler_params=pltpu.CompilerParams(vmem_limit_bytes=8 * MIB),
        cost_estimate=FREE,
        name="outer_swap",
    )(v0, rows, window)


def place_kernel(mine_ref, y_ref, near_ref, out_ref):
    dp = lax.axis_index("dp")
    for flip, block in ((0, mine_ref), (2, y_ref), (1, near_ref.at[0]), (3, near_ref.at[1])):
        out_ref[pl.ds(pl.multiple_of((dp ^ flip) * LANE, LANE), LANE), :] = block[...].astype(F32)


def place(mine, from_y, near):
    return pl.pallas_call(
        place_kernel,
        in_specs=[VMEM] * 3,
        out_specs=VMEM,
        out_shape=jax.ShapeDtypeStruct((512, 512), F32),
        compiler_params=pltpu.CompilerParams(vmem_limit_bytes=8 * MIB),
        cost_estimate=FREE,
        name="place",
    )(mine, from_y, near)


def reduce_by_axis(*args):
    own1, near1, own2, near2 = front(True, *args)
    near1 = xor_permute(near1, CORE)
    near2 = xor_permute(near2, CORE)
    send_a1, send_b1 = partial_sums(VROWS, BF16, own1, near1, own1, near1)
    send_a2, send_b2 = partial_sums(0, BF16, own2, near2, own1, near1)
    keep_a1, keep_b1 = partial_sums(VROWS + 512, F32, own1, near1, own1, near1)
    keep_a2, keep_b2 = partial_sums(512, F32, own2, near2, own1, near1)
    half_a1 = keep_a1 + xor_permute(send_a1, Y).astype(F32)
    half_b1 = keep_b1 + xor_permute(send_b1, X).astype(F32)
    half_a2 = keep_a2 + xor_permute(send_a2, Y).astype(F32)
    half_b2 = keep_b2 + xor_permute(send_b2, X).astype(F32)

    def other(half, mask):
        return half[LANE:] + xor_permute(half[:LANE].astype(BF16), mask).astype(F32)

    z2 = xor_permute(other(half_a1, X).astype(BF16), 4)
    z3 = xor_permute(other(half_b1, Y).astype(BF16), 6)
    z1 = xor_permute(other(half_b2, Y).astype(BF16), 2)
    z0 = other(half_a2, X)
    rows, window = inner_swap(own1, near1)
    value_grad = outer_swap(own1, rows, xor_permute(window, Y))
    z1, value_grad = lax.optimization_barrier((z1, value_grad))
    mine = (z0 + z1.astype(F32) + (z2.astype(F32) + z3.astype(F32))).astype(BF16)
    from_y = xor_permute(mine, Y)
    grad_value = place(mine, from_y, xor_permute(jnp.stack([mine, from_y]), CORE))
    return grad_value, value_grad


def swapped(block, axis, distance):
    count = lax.axis_size(axis)
    route = []
    for low in range(count):
        high = low | 1 << distance
        if high != low and high < count:
            route += [(low, high), (high, low)]
    return lax.ppermute(block, axis, route)


def blend_rows(item, incoming, offset, extent):
    inside = (jnp.arange(CAP) < extent)[:, None]
    chosen = jnp.where(inside, incoming, lax.dynamic_slice_in_dim(item, offset, CAP, 0))
    return lax.dynamic_update_slice_in_dim(item, chosen, offset, 0)


def reduce_by_owner(layer_input, *args):
    swap_start, swap_rows = args[-2:]
    tokens = layer_input.shape[0]
    halves = front(False, layer_input, *args)[0].reshape(2, tokens + INFO, 2 * HD)[:, :tokens]
    values = jnp.concatenate([halves[0], halves[1]], axis=1)
    balanced = values
    for level in range(lax.axis_size("dp").bit_length() - 1):
        offset = swap_start[0, level]
        window = lax.dynamic_slice_in_dim(balanced, offset, CAP, 0)
        balanced = blend_rows(balanced, swapped(window, "dp", level), offset, swap_rows[0, level])
    owners = lax.axis_size("fsdp")
    owned = (D + owners - 1) // owners
    padded = jnp.pad(layer_input, ((0, 0), (0, owned * owners - D)))
    arranged = lax.all_to_all(
        padded.reshape(tokens, owners, owned), "fsdp", split_axis=1, concat_axis=0, tiled=True
    )
    block = lax.dot_general(
        arranged.reshape(-1, owned),
        lax.all_gather(values, "fsdp", axis=0, tiled=True),
        (((0,), (0,)), ((), ())),
        preferred_element_type=F32,
    )
    return lax.psum(block, "dp"), balanced


def on_device(layer_input, *args):
    if lax.axis_size("dp") == 4 and lax.axis_size("fsdp") == 8:
        return reduce_by_axis(layer_input, *args)
    return reduce_by_owner(layer_input, *args)


def solution(mesh):
    return jax.shard_map(
        on_device,
        mesh=mesh,
        in_specs=(
            P(("dp", "fsdp"), None),
            P(("dp", "fsdp"), None),
            P(("dp", "fsdp"), None),
            P(("dp", "fsdp"), None),
            P(("dp", "fsdp")),
            P(("dp", "fsdp")),
            P(),
            P(("dp", "fsdp")),
            P(("dp", "fsdp"), None),
            P(("dp", "fsdp"), None),
        ),
        out_specs=(P("fsdp", None), P(("dp", "fsdp"), None)),
        check_vma=False,
    )
```

```python
import functools

import jax
import jax.numpy as jnp
from jax import lax
from jax.experimental import pallas as pl
from jax.experimental.pallas import tpu as pltpu
from jax.sharding import PartitionSpec as P

D = 4096
HD = 128
CAP = 32
HALF = 128
LANE = 128
INFO = 16
MIB = 1 << 20
FREE = pl.CostEstimate(flops=0, bytes_accessed=0, transcendentals=0)
BF16 = jnp.bfloat16
F32 = jnp.float32

VMEM = pl.BlockSpec(memory_space=pltpu.VMEM)
HBM = pl.BlockSpec(memory_space=pltpu.HBM)


def attend_group(per_group, span, q, k, g, allowed, factor):
    q_all = jnp.concatenate([q[span, n * HD:(n + 1) * HD] for n in range(per_group)], axis=0)
    scores = lax.dot_general(
        k[span, :], q_all, (((1,), (1,)), ((), ())), preferred_element_type=F32
    ) * HD ** (-0.5)
    probs = []
    weighted = []
    for n in range(per_group):
        own = jnp.where(allowed, scores[:, n * HALF:(n + 1) * HALF], -1e30)
        expo = jnp.exp(own - jnp.max(own, axis=0, keepdims=True))
        probs.append((expo / jnp.sum(expo, axis=0, keepdims=True)).astype(BF16))
        weighted.append((g[span, n * HD:(n + 1) * HD].astype(F32) * factor).astype(BF16))
    return jnp.dot(
        jnp.concatenate(probs, axis=1), jnp.concatenate(weighted, axis=0), preferred_element_type=F32
    ).astype(BF16)


def mask_and_factor(span, loss_ref, exponent_ref, ids_ref, index_ref):
    exponent = exponent_ref[0]
    unscale = jnp.float32(1.0)
    for bit in range(5):
        unscale = unscale * jnp.where((exponent >> bit) & 1 == 1, jnp.float32(2.0 ** -(1 << bit)), 1.0)
    row = lax.broadcasted_iota(jnp.int32, (HALF, HALF), 0)
    col = lax.broadcasted_iota(jnp.int32, (HALF, HALF), 1)
    doc_i = jnp.broadcast_to(ids_ref[:, span], (HALF, HALF))
    allowed = (doc_i == doc_i.T) & (row <= col)
    index = index_ref[:, span]
    factor = jnp.zeros((1, HALF), F32)
    for entry in range(loss_ref.shape[0]):
        factor = jnp.where(index == entry, loss_ref[entry], factor)
    return allowed, jnp.broadcast_to(factor * unscale, (HALF, HALF)).T


def front_kernel(
    per_group, loss_hbm, exponent_hbm, start_hbm, rows_hbm, q_hbm, k_hbm, g_hbm, ids_hbm, index_hbm, *rest
):
    v_ref, loss_ref, exponent_ref, start_ref, rows_ref, q_ref, k_ref, g_ref, ids_ref, index_ref, sems = rest
    count = 0

    def begin(source, target):
        nonlocal count
        copy = pltpu.make_async_copy(source, target, sems.at[count])
        copy.start()
        count += 1
        return copy

    small = [
        begin(source, target)
        for source, target in (
            (ids_hbm, ids_ref), (index_hbm, index_ref), (loss_hbm, loss_ref), (exponent_hbm, exponent_ref),
            (start_hbm, start_ref), (rows_hbm, rows_ref),
        )
    ]
    groups = k_ref.shape[1] // HD
    wide = per_group * HD
    loads = []
    for group in range(groups):
        some = pl.ds(group * wide, wide)
        one = pl.ds(group * HD, HD)
        loads.append([
            begin(q_hbm.at[:, some], q_ref.at[:, some]),
            begin(k_hbm.at[:, one], k_ref.at[:, one]),
            begin(g_hbm.at[:, some], g_ref.at[:, some]),
        ])
    for copy in small:
        copy.wait()
    masks = [
        mask_and_factor(pl.ds(half * HALF, HALF), loss_ref, exponent_ref, ids_ref, index_ref) for half in range(2)
    ]

    def put(group, row, value):
        v_ref[pl.ds(row, value.shape[0]), pl.ds(group * HD, HD)] = value

    info_row = lax.broadcasted_iota(jnp.int32, (INFO, HD), 0)
    info = jnp.zeros((INFO, HD), jnp.int32)
    for level in range(min(start_ref.shape[1], INFO // 2)):
        info = jnp.where(info_row == 2 * level, start_ref[0, level], info)
        info = jnp.where(info_row == 2 * level + 1, rows_ref[0, level], info)
    info = info.astype(F32).astype(BF16)
    for group in range(groups):
        for copy in loads[group]:
            copy.wait()
        some = pl.ds(group * wide, wide)
        for half in range(2):
            span = pl.ds(half * HALF, HALF)
            value = attend_group(
                per_group, slice(None), q_ref[span, some], k_ref[span, pl.ds(group * HD, HD)], g_ref[span, some],
                *masks[half],
            )
            put(group, half * HALF, value)
        put(group, 2 * HALF, info)


def front(query, key, grad, ids, index, loss, exponent, start, rows):
    tokens, key_width = key.shape
    per_group = query.shape[1] // key_width
    groups = key_width // HD
    args = [
        loss, exponent, start, rows, query, key, grad, ids.reshape(1, tokens), index.reshape(1, tokens)
    ]
    return pl.pallas_call(
        functools.partial(front_kernel, per_group),
        in_specs=[HBM] * 9,
        out_specs=VMEM,
        out_shape=jax.ShapeDtypeStruct((tokens + INFO, key_width), BF16),
        scratch_shapes=[
            pltpu.SMEM(loss.shape, F32), pltpu.SMEM(exponent.shape, jnp.int32),
            pltpu.SMEM(start.shape, jnp.int32), pltpu.SMEM(rows.shape, jnp.int32),
            pltpu.VMEM(query.shape, BF16), pltpu.VMEM(key.shape, BF16), pltpu.VMEM(grad.shape, BF16),
            pltpu.VMEM((1, tokens), jnp.int32), pltpu.VMEM((1, tokens), jnp.int32),
            pltpu.SemaphoreType.DMA((6 + 3 * groups,)),
        ],
        compiler_params=pltpu.CompilerParams(vmem_limit_bytes=24 * MIB),
        cost_estimate=FREE,
        name="front",
    )(*[arg if arg is exponent else pltpu.with_memory_space_constraint(arg, pltpu.HBM) for arg in args])


CORE, Y, X = 8, 16, 1


def xor_permute(value, mask):
    count = lax.axis_size("dp") * lax.axis_size("fsdp")
    return lax.ppermute(value, ("dp", "fsdp"), [(i, i ^ mask) for i in range(count)])


def partial_kernel(parts, own_ref, near_ref, v0_ref, v1_ref, *out_refs):
    dp = lax.axis_index("dp")
    fsdp = lax.axis_index("fsdp")
    v = jnp.concatenate([ref[pl.ds(0, 2 * HALF), :] for ref in (v0_ref, v1_ref)], axis=0)
    for blocks, out_ref in zip(parts, out_refs):
        columns = []
        for z, y, x in blocks:
            owner = fsdp ^ (z << 1 | x)
            column = pl.multiple_of(owner * (4 * LANE) + (dp ^ (y << 1)) * LANE, LANE)
            columns.append(jnp.concatenate([ref[:, pl.ds(column, LANE)] for ref in (own_ref, near_ref)], axis=0))
        total = lax.dot_general(
            jnp.concatenate(columns, axis=1), v, (((0,), (0,)), ((), ())), preferred_element_type=F32
        )
        out_ref[...] = total.astype(out_ref.dtype)


def partial_sums(parts, dtype, own, near, v0, v1):
    return pl.pallas_call(
        functools.partial(partial_kernel, parts),
        in_specs=[VMEM] * 4,
        out_specs=[VMEM] * len(parts),
        out_shape=[jax.ShapeDtypeStruct((len(blocks) * LANE, 512), dtype) for blocks in parts],
        compiler_params=pltpu.CompilerParams(vmem_limit_bytes=24 * MIB),
        cost_estimate=FREE,
        name="partial_sums",
    )(own, near, v0, v1)


def inner_swap_kernel(v0_ref, v1_ref, out_ref, window_ref):
    tokens = out_ref.shape[0]
    infos = [ref[pl.ds(tokens, INFO), pl.ds(0, HALF)].astype(F32).astype(jnp.int32) for ref in (v0_ref, v1_ref)]

    def table(device, entry):
        return jnp.broadcast_to(infos[device][entry:entry + 1, :], (HALF, HALF))

    place = lax.broadcasted_iota(jnp.int32, (HALF, HALF), 0) + HALF
    inner = lax.broadcasted_iota(jnp.int32, (HALF, HALF), 1) + HALF
    first = table(0, 0)
    moved = (place >= first) & (place < first + table(0, 1))
    stays = jnp.where(~moved & (place == inner), 1.0, 0.0).astype(BF16)
    comes = jnp.where(moved & (place + table(1, 0) - first == inner), 1.0, 0.0).astype(BF16)
    taken = jnp.where(place - HALF + table(0, 2) == inner, 1.0, 0.0).astype(BF16)[:CAP]
    rows = (
        jnp.dot(stays, v0_ref[pl.ds(HALF, HALF), :], preferred_element_type=F32)
        + jnp.dot(comes, v1_ref[pl.ds(HALF, HALF), :], preferred_element_type=F32)
    ).astype(BF16)
    out_ref[pl.ds(0, HALF), :] = v0_ref[pl.ds(0, HALF), :]
    out_ref[pl.ds(HALF, HALF), :] = rows
    window_ref[...] = jnp.dot(taken, rows, preferred_element_type=F32).astype(BF16)


def inner_swap(v0, v1):
    return pl.pallas_call(
        inner_swap_kernel,
        in_specs=[VMEM] * 2,
        out_specs=[VMEM] * 2,
        out_shape=[jax.ShapeDtypeStruct((2 * HALF, 512), BF16), jax.ShapeDtypeStruct((CAP, 512), BF16)],
        compiler_params=pltpu.CompilerParams(vmem_limit_bytes=8 * MIB),
        cost_estimate=FREE,
        name="inner_swap",
    )(v0, v1)


def outer_swap_kernel(v0_ref, rows_ref, window_ref, out_ref):
    tokens = out_ref.shape[0]
    info = v0_ref[pl.ds(tokens, INFO), pl.ds(0, HALF)].astype(F32).astype(jnp.int32)
    first = jnp.broadcast_to(info[2:3, :], (HALF, HALF))
    extent = jnp.broadcast_to(info[3:4, :], (HALF, HALF))
    place = lax.broadcasted_iota(jnp.int32, (HALF, HALF), 0) + HALF
    inner = lax.broadcasted_iota(jnp.int32, (HALF, HALF), 1)
    moved = (place >= first) & (place < first + extent)
    stays = jnp.where(~moved & (place == inner + HALF), 1.0, 0.0).astype(BF16)
    comes = jnp.where(moved & (place - first == inner), 1.0, 0.0).astype(BF16)[:, :CAP]
    out_ref[pl.ds(0, HALF), :] = rows_ref[pl.ds(0, HALF), :]
    out_ref[pl.ds(HALF, HALF), :] = (
        jnp.dot(stays, rows_ref[pl.ds(HALF, HALF), :], preferred_element_type=F32)
        + jnp.dot(comes, window_ref[...], preferred_element_type=F32)
    ).astype(BF16)


def outer_swap(v0, rows, window):
    return pl.pallas_call(
        outer_swap_kernel,
        in_specs=[VMEM] * 3,
        out_specs=VMEM,
        out_shape=jax.ShapeDtypeStruct(rows.shape, BF16),
        compiler_params=pltpu.CompilerParams(vmem_limit_bytes=8 * MIB),
        cost_estimate=FREE,
        name="outer_swap",
    )(v0, rows, window)


def place_kernel(mine_ref, y_ref, near_ref, out_ref):
    dp = lax.axis_index("dp")
    for flip, block in ((0, mine_ref), (2, y_ref), (1, near_ref.at[0]), (3, near_ref.at[1])):
        out_ref[pl.ds(pl.multiple_of((dp ^ flip) * LANE, LANE), LANE), :] = block[...].astype(F32)


def place(mine, from_y, near):
    return pl.pallas_call(
        place_kernel,
        in_specs=[VMEM] * 3,
        out_specs=VMEM,
        out_shape=jax.ShapeDtypeStruct((512, 512), F32),
        compiler_params=pltpu.CompilerParams(vmem_limit_bytes=8 * MIB),
        cost_estimate=FREE,
        name="place",
    )(mine, from_y, near)


def reduce_by_axis(layer_input, *args):
    near = xor_permute(layer_input, CORE)
    v0 = front(*args)
    v1 = xor_permute(v0, CORE)

    def sums(parts, dtype):
        return partial_sums(parts, dtype, layer_input, near, v0, v1)

    far_a, far_b = sums((((2, 1, 1),), ((3, 1, 1),)), BF16)
    side_a, side_b = sums((((2, 1, 0),), ((3, 0, 1),)), BF16)
    late_a, late_b = sums((((0, 1, 1), (0, 1, 0)), ((1, 1, 1), (1, 0, 1))), BF16)
    keep_far_a, keep_far_b = sums((((2, 0, 1),), ((3, 1, 0),)), F32)
    keep_a, keep_b = sums((((2, 0, 0),), ((3, 0, 0),)), F32)
    keep_late_a, keep_late_b = sums((((0, 0, 1), (0, 0, 0)), ((1, 1, 0), (1, 0, 0))), F32)

    far_a = xor_permute(far_a, Y)
    far_b = xor_permute(far_b, X)
    side_a = xor_permute(side_a, Y)
    side_b = xor_permute(side_b, X)
    on_a = (keep_far_a + far_a.astype(F32)).astype(BF16)
    on_b = (keep_far_b + far_b.astype(F32)).astype(BF16)
    on_a, on_b, late_a, late_b = lax.optimization_barrier((on_a, on_b, late_a, late_b))
    on_a = xor_permute(on_a, X)
    on_b = xor_permute(on_b, Y)
    late_a = xor_permute(late_a, Y)
    late_b = xor_permute(late_b, X)
    z2 = xor_permute((keep_a + side_a.astype(F32) + on_a.astype(F32)).astype(BF16), 4)
    z3 = xor_permute((keep_b + side_b.astype(F32) + on_b.astype(F32)).astype(BF16), 6)
    half_a = keep_late_a + late_a.astype(F32)
    half_b = keep_late_b + late_b.astype(F32)
    on_late_a = xor_permute(half_a[:LANE].astype(BF16), X)
    on_late_b = xor_permute(half_b[:LANE].astype(BF16), Y)
    z0 = half_a[LANE:] + on_late_a.astype(F32)
    z1 = xor_permute((half_b[LANE:] + on_late_b.astype(F32)).astype(BF16), 2)
    rows, window = inner_swap(v0, v1)
    value_grad = outer_swap(v0, rows, xor_permute(window, Y))
    z1, value_grad = lax.optimization_barrier((z1, value_grad))
    mine = (z0 + z1.astype(F32) + (z2.astype(F32) + z3.astype(F32))).astype(BF16)
    from_y = xor_permute(mine, Y)
    return place(mine, from_y, xor_permute(jnp.stack([mine, from_y]), CORE)), value_grad


def swapped(block, axis, distance):
    count = lax.axis_size(axis)
    route = []
    for low in range(count):
        high = low | 1 << distance
        if high != low and high < count:
            route += [(low, high), (high, low)]
    return lax.ppermute(block, axis, route)


def blend_rows(item, incoming, offset, extent):
    inside = (jnp.arange(CAP) < extent)[:, None]
    chosen = jnp.where(inside, incoming, lax.dynamic_slice_in_dim(item, offset, CAP, 0))
    return lax.dynamic_update_slice_in_dim(item, chosen, offset, 0)


def reduce_by_owner(layer_input, *args):
    swap_start, swap_rows = args[-2:]
    tokens = layer_input.shape[0]
    values = front(*args)[:tokens]
    balanced = values
    for level in range(lax.axis_size("dp").bit_length() - 1):
        offset = swap_start[0, level]
        window = lax.dynamic_slice_in_dim(balanced, offset, CAP, 0)
        balanced = blend_rows(balanced, swapped(window, "dp", level), offset, swap_rows[0, level])
    owners = lax.axis_size("fsdp")
    owned = (D + owners - 1) // owners
    padded = jnp.pad(layer_input, ((0, 0), (0, owned * owners - D)))
    arranged = lax.all_to_all(
        padded.reshape(tokens, owners, owned), "fsdp", split_axis=1, concat_axis=0, tiled=True
    )
    block = lax.dot_general(
        arranged.reshape(-1, owned),
        lax.all_gather(values, "fsdp", axis=0, tiled=True),
        (((0,), (0,)), ((), ())),
        preferred_element_type=F32,
    )
    return lax.psum(block, "dp"), balanced


def on_device(layer_input, *args):
    if lax.axis_size("dp") == 4 and lax.axis_size("fsdp") == 8:
        return reduce_by_axis(layer_input, *args)
    return reduce_by_owner(layer_input, *args)


def solution(mesh):
    return jax.shard_map(
        on_device,
        mesh=mesh,
        in_specs=(
            P(("dp", "fsdp"), None),
            P(("dp", "fsdp"), None),
            P(("dp", "fsdp"), None),
            P(("dp", "fsdp"), None),
            P(("dp", "fsdp")),
            P(("dp", "fsdp")),
            P(),
            P(("dp", "fsdp")),
            P(("dp", "fsdp"), None),
            P(("dp", "fsdp"), None),
        ),
        out_specs=(P("fsdp", None), P(("dp", "fsdp"), None)),
        check_vma=False,
    )
```

```python
import functools

import jax
import jax.numpy as jnp
from jax import lax
from jax.experimental import pallas as pl
from jax.experimental.pallas import tpu as pltpu
from jax.sharding import PartitionSpec as P

D = 4096
HD = 128
CAP = 32
HALF = 128
LANE = 128
INFO = 16
MIB = 1 << 20
FREE = pl.CostEstimate(flops=0, bytes_accessed=0, transcendentals=0)
BF16 = jnp.bfloat16
F32 = jnp.float32

VMEM = pl.BlockSpec(memory_space=pltpu.VMEM)
HBM = pl.BlockSpec(memory_space=pltpu.HBM)


def attend_group(per_group, span, q, k, g, allowed, factor):
    q_all = jnp.concatenate([q[span, n * HD:(n + 1) * HD] for n in range(per_group)], axis=0)
    scores = lax.dot_general(
        k[span, :], q_all, (((1,), (1,)), ((), ())), preferred_element_type=F32
    ) * HD ** (-0.5)
    probs = []
    weighted = []
    for n in range(per_group):
        own = jnp.where(allowed, scores[:, n * HALF:(n + 1) * HALF], -1e30)
        expo = jnp.exp(own - jnp.max(own, axis=0, keepdims=True))
        probs.append((expo / jnp.sum(expo, axis=0, keepdims=True)).astype(BF16))
        weighted.append((g[span, n * HD:(n + 1) * HD].astype(F32) * factor).astype(BF16))
    return jnp.dot(
        jnp.concatenate(probs, axis=1), jnp.concatenate(weighted, axis=0), preferred_element_type=F32
    ).astype(BF16)


def mask_and_factor(span, loss_ref, exponent_ref, ids_ref, index_ref):
    exponent = exponent_ref[0]
    unscale = jnp.float32(1.0)
    for bit in range(5):
        unscale = unscale * jnp.where((exponent >> bit) & 1 == 1, jnp.float32(2.0 ** -(1 << bit)), 1.0)
    row = lax.broadcasted_iota(jnp.int32, (HALF, HALF), 0)
    col = lax.broadcasted_iota(jnp.int32, (HALF, HALF), 1)
    doc_i = jnp.broadcast_to(ids_ref[:, span], (HALF, HALF))
    allowed = (doc_i == doc_i.T) & (row <= col)
    index = index_ref[:, span]
    factor = jnp.zeros((1, HALF), F32)
    for entry in range(loss_ref.shape[0]):
        factor = jnp.where(index == entry, loss_ref[entry], factor)
    return allowed, jnp.broadcast_to(factor * unscale, (HALF, HALF)).T


def front_kernel(
    per_group, loss_hbm, exponent_hbm, start_hbm, rows_hbm, q_hbm, k_hbm, g_hbm, ids_hbm, index_hbm, *rest
):
    v_ref, loss_ref, exponent_ref, start_ref, rows_ref, q_ref, k_ref, g_ref, ids_ref, index_ref, sems = rest
    count = 0

    def begin(source, target):
        nonlocal count
        copy = pltpu.make_async_copy(source, target, sems.at[count])
        copy.start()
        count += 1
        return copy

    small = [
        begin(source, target)
        for source, target in (
            (ids_hbm, ids_ref), (index_hbm, index_ref), (loss_hbm, loss_ref), (exponent_hbm, exponent_ref),
            (start_hbm, start_ref), (rows_hbm, rows_ref),
        )
    ]
    groups = k_ref.shape[1] // HD
    wide = per_group * HD
    loads = []
    for group in range(groups):
        some = pl.ds(group * wide, wide)
        one = pl.ds(group * HD, HD)
        loads.append([
            begin(q_hbm.at[:, some], q_ref.at[:, some]),
            begin(k_hbm.at[:, one], k_ref.at[:, one]),
            begin(g_hbm.at[:, some], g_ref.at[:, some]),
        ])
    for copy in small:
        copy.wait()
    masks = [
        mask_and_factor(pl.ds(half * HALF, HALF), loss_ref, exponent_ref, ids_ref, index_ref) for half in range(2)
    ]

    def put(group, row, value):
        v_ref[pl.ds(row, value.shape[0]), pl.ds(group * HD, HD)] = value

    info_row = lax.broadcasted_iota(jnp.int32, (INFO, HD), 0)
    info = jnp.zeros((INFO, HD), jnp.int32)
    for level in range(min(start_ref.shape[1], INFO // 2)):
        info = jnp.where(info_row == 2 * level, start_ref[0, level], info)
        info = jnp.where(info_row == 2 * level + 1, rows_ref[0, level], info)
    info = info.astype(F32).astype(BF16)
    for group in range(groups):
        for copy in loads[group]:
            copy.wait()
        some = pl.ds(group * wide, wide)
        for half in range(2):
            span = pl.ds(half * HALF, HALF)
            value = attend_group(
                per_group, slice(None), q_ref[span, some], k_ref[span, pl.ds(group * HD, HD)], g_ref[span, some],
                *masks[half],
            )
            put(group, half * HALF, value)
        put(group, 2 * HALF, info)


def front(query, key, grad, ids, index, loss, exponent, start, rows):
    tokens, key_width = key.shape
    per_group = query.shape[1] // key_width
    groups = key_width // HD
    args = [
        loss, exponent, start, rows, query, key, grad, ids.reshape(1, tokens), index.reshape(1, tokens)
    ]
    return pl.pallas_call(
        functools.partial(front_kernel, per_group),
        in_specs=[HBM] * 9,
        out_specs=VMEM,
        out_shape=jax.ShapeDtypeStruct((tokens + INFO, key_width), BF16),
        scratch_shapes=[
            pltpu.SMEM(loss.shape, F32), pltpu.SMEM(exponent.shape, jnp.int32),
            pltpu.SMEM(start.shape, jnp.int32), pltpu.SMEM(rows.shape, jnp.int32),
            pltpu.VMEM(query.shape, BF16), pltpu.VMEM(key.shape, BF16), pltpu.VMEM(grad.shape, BF16),
            pltpu.VMEM((1, tokens), jnp.int32), pltpu.VMEM((1, tokens), jnp.int32),
            pltpu.SemaphoreType.DMA((6 + 3 * groups,)),
        ],
        compiler_params=pltpu.CompilerParams(vmem_limit_bytes=24 * MIB),
        cost_estimate=FREE,
        name="front",
    )(*[arg if arg is exponent else pltpu.with_memory_space_constraint(arg, pltpu.HBM) for arg in args])


CORE, Y, X, Z1, Z2 = 8, 16, 1, 2, 4


def xor_permute(value, mask):
    count = lax.axis_size("dp") * lax.axis_size("fsdp")
    return lax.ppermute(value, ("dp", "fsdp"), [(i, i ^ mask) for i in range(count)])


def partial_kernel(parts, own_ref, near_ref, v0_ref, v1_ref, *out_refs):
    dp = lax.axis_index("dp")
    fsdp = lax.axis_index("fsdp")
    v = jnp.concatenate([ref[pl.ds(0, 2 * HALF), :] for ref in (v0_ref, v1_ref)], axis=0)
    for blocks, out_ref in zip(parts, out_refs):
        columns = []
        for z, y, x in blocks:
            owner = fsdp ^ (z << 1 | x)
            column = pl.multiple_of(owner * (4 * LANE) + (dp ^ (y << 1)) * LANE, LANE)
            columns.append(jnp.concatenate([ref[:, pl.ds(column, LANE)] for ref in (own_ref, near_ref)], axis=0))
        total = lax.dot_general(
            jnp.concatenate(columns, axis=1), v, (((0,), (0,)), ((), ())), preferred_element_type=F32
        )
        out_ref[...] = total.astype(out_ref.dtype)


def partial_sums(parts, dtype, own, near, v0, v1):
    return pl.pallas_call(
        functools.partial(partial_kernel, parts),
        in_specs=[VMEM] * 4,
        out_specs=[VMEM] * len(parts),
        out_shape=[jax.ShapeDtypeStruct((len(blocks) * LANE, 512), dtype) for blocks in parts],
        compiler_params=pltpu.CompilerParams(vmem_limit_bytes=24 * MIB),
        cost_estimate=FREE,
        name="partial_sums",
    )(own, near, v0, v1)


def inner_swap_kernel(v0_ref, v1_ref, out_ref, window_ref):
    tokens = out_ref.shape[0]
    infos = [ref[pl.ds(tokens, INFO), pl.ds(0, HALF)].astype(F32).astype(jnp.int32) for ref in (v0_ref, v1_ref)]

    def table(device, entry):
        return jnp.broadcast_to(infos[device][entry:entry + 1, :], (HALF, HALF))

    place = lax.broadcasted_iota(jnp.int32, (HALF, HALF), 0) + HALF
    inner = lax.broadcasted_iota(jnp.int32, (HALF, HALF), 1) + HALF
    first = table(0, 0)
    moved = (place >= first) & (place < first + table(0, 1))
    stays = jnp.where(~moved & (place == inner), 1.0, 0.0).astype(BF16)
    comes = jnp.where(moved & (place + table(1, 0) - first == inner), 1.0, 0.0).astype(BF16)
    taken = jnp.where(place - HALF + table(0, 2) == inner, 1.0, 0.0).astype(BF16)[:CAP]
    rows = (
        jnp.dot(stays, v0_ref[pl.ds(HALF, HALF), :], preferred_element_type=F32)
        + jnp.dot(comes, v1_ref[pl.ds(HALF, HALF), :], preferred_element_type=F32)
    ).astype(BF16)
    out_ref[pl.ds(0, HALF), :] = v0_ref[pl.ds(0, HALF), :]
    out_ref[pl.ds(HALF, HALF), :] = rows
    window_ref[...] = jnp.dot(taken, rows, preferred_element_type=F32).astype(BF16)


def inner_swap(v0, v1):
    return pl.pallas_call(
        inner_swap_kernel,
        in_specs=[VMEM] * 2,
        out_specs=[VMEM] * 2,
        out_shape=[jax.ShapeDtypeStruct((2 * HALF, 512), BF16), jax.ShapeDtypeStruct((CAP, 512), BF16)],
        compiler_params=pltpu.CompilerParams(vmem_limit_bytes=8 * MIB),
        cost_estimate=FREE,
        name="inner_swap",
    )(v0, v1)


def outer_swap_kernel(v0_ref, rows_ref, window_ref, out_ref):
    tokens = out_ref.shape[0]
    info = v0_ref[pl.ds(tokens, INFO), pl.ds(0, HALF)].astype(F32).astype(jnp.int32)
    first = jnp.broadcast_to(info[2:3, :], (HALF, HALF))
    extent = jnp.broadcast_to(info[3:4, :], (HALF, HALF))
    place = lax.broadcasted_iota(jnp.int32, (HALF, HALF), 0) + HALF
    inner = lax.broadcasted_iota(jnp.int32, (HALF, HALF), 1)
    moved = (place >= first) & (place < first + extent)
    stays = jnp.where(~moved & (place == inner + HALF), 1.0, 0.0).astype(BF16)
    comes = jnp.where(moved & (place - first == inner), 1.0, 0.0).astype(BF16)[:, :CAP]
    out_ref[pl.ds(0, HALF), :] = rows_ref[pl.ds(0, HALF), :]
    out_ref[pl.ds(HALF, HALF), :] = (
        jnp.dot(stays, rows_ref[pl.ds(HALF, HALF), :], preferred_element_type=F32)
        + jnp.dot(comes, window_ref[...], preferred_element_type=F32)
    ).astype(BF16)


def outer_swap(v0, rows, window):
    return pl.pallas_call(
        outer_swap_kernel,
        in_specs=[VMEM] * 3,
        out_specs=VMEM,
        out_shape=jax.ShapeDtypeStruct(rows.shape, BF16),
        compiler_params=pltpu.CompilerParams(vmem_limit_bytes=8 * MIB),
        cost_estimate=FREE,
        name="outer_swap",
    )(v0, rows, window)


def place_kernel(mine_ref, y_ref, near_ref, out_ref):
    dp = lax.axis_index("dp")
    for flip, block in ((0, mine_ref), (2, y_ref), (1, near_ref.at[0]), (3, near_ref.at[1])):
        out_ref[pl.ds(pl.multiple_of((dp ^ flip) * LANE, LANE), LANE), :] = block[...].astype(F32)


def place(mine, from_y, near):
    return pl.pallas_call(
        place_kernel,
        in_specs=[VMEM] * 3,
        out_specs=VMEM,
        out_shape=jax.ShapeDtypeStruct((512, 512), F32),
        compiler_params=pltpu.CompilerParams(vmem_limit_bytes=8 * MIB),
        cost_estimate=FREE,
        name="place",
    )(mine, from_y, near)


def fold_kernel(base_ref, arrived_ref, out_ref):
    out_ref[...] = base_ref[...] + arrived_ref[...].astype(F32)


def fold(base, arrived):
    return pl.pallas_call(
        fold_kernel,
        in_specs=[VMEM] * 2,
        out_specs=VMEM,
        out_shape=jax.ShapeDtypeStruct(base.shape, F32),
        compiler_params=pltpu.CompilerParams(vmem_limit_bytes=8 * MIB),
        cost_estimate=pl.CostEstimate(flops=6_000_000_000, bytes_accessed=0, transcendentals=0),
        name="fold",
    )(base, arrived)


def reduce_by_axis(layer_input, *args):
    near = xor_permute(layer_input, CORE)
    v0 = front(*args)
    v1 = xor_permute(v0, CORE)

    def sums(parts, dtype):
        return partial_sums(parts, dtype, layer_input, near, v0, v1)

    def after_all(*values):
        return lax.optimization_barrier(values)

    def add(*terms):
        total = terms[0]
        for term in terms[1:]:
            total = total + term.astype(F32)
        return total

    far_b, far_a = sums((((3, 1, 1),), ((2, 1, 1),)), BF16)
    side_b, side_a = sums((((3, 0, 1),), ((2, 1, 0),)), BF16)
    pair, = sums((((1, 1, 1), (1, 1, 0), (1, 0, 1), (1, 0, 0)),), BF16)
    keep_far_b, keep_far_a = sums((((3, 1, 0),), ((2, 0, 1),)), F32)
    keep_b, keep_a = sums((((3, 0, 0),), ((2, 0, 0),)), F32)
    own, = sums((((0, 1, 1), (0, 1, 0), (0, 0, 1), (0, 0, 0)),), F32)
    far_b = xor_permute(far_b, X)
    far_a = xor_permute(far_a, Y)
    side_b = xor_permute(side_b, X)
    pair = xor_permute(pair, Z1)
    on_b = add(keep_far_b, far_b).astype(BF16)
    rows, window = inner_swap(v0, v1)
    side_a = after_all(jnp.concatenate([side_a, window]), on_b)[0]
    on_b = xor_permute(on_b, Y)
    side_a = xor_permute(side_a, Y)
    side_a, window = side_a[:LANE], side_a[LANE:]
    on_a = xor_permute(add(keep_far_a, far_a).astype(BF16), X)
    z3 = add(keep_b, side_b, on_b).astype(BF16)
    pair, window = after_all(pair, window, z3)[:2]
    z3 = xor_permute(z3, Z1)
    value_grad = outer_swap(v0, rows, window)
    on_a, value_grad = after_all(on_a, value_grad)
    z2 = add(keep_a, side_a, on_a, z3).astype(BF16)

    total = add(own, pair)
    some, rest = total[:, :256], total[:, 256:]
    rest_far, rest_y, rest_x, rest_own = (rest[row:row + LANE] for row in range(0, 4 * LANE, LANE))
    some_in = xor_permute(some[:2 * LANE].astype(BF16), Y)
    rest_in = xor_permute(jnp.concatenate([rest_far, rest_x]).astype(BF16), X)
    some_in, rest_in = after_all(some_in, rest_in, z2)[:2]
    z2 = xor_permute(z2, Z2)
    some_on = xor_permute(add(some[2 * LANE:3 * LANE], some_in[:LANE]).astype(BF16), X)
    rest_on = xor_permute(add(rest_y, rest_in[:LANE]).astype(BF16), Y)
    base = jnp.concatenate([add(some[3 * LANE:], some_in[LANE:]), add(rest_own, rest_in[LANE:])], axis=1)
    mine = add(fold(base, z2), jnp.concatenate([some_on, rest_on], axis=1)).astype(BF16)
    from_y = xor_permute(mine, Y)
    return place(mine, from_y, xor_permute(jnp.stack([mine, from_y]), CORE)), value_grad


def swapped(block, axis, distance):
    count = lax.axis_size(axis)
    route = []
    for low in range(count):
        high = low | 1 << distance
        if high != low and high < count:
            route += [(low, high), (high, low)]
    return lax.ppermute(block, axis, route)


def blend_rows(item, incoming, offset, extent):
    inside = (jnp.arange(CAP) < extent)[:, None]
    chosen = jnp.where(inside, incoming, lax.dynamic_slice_in_dim(item, offset, CAP, 0))
    return lax.dynamic_update_slice_in_dim(item, chosen, offset, 0)


def reduce_by_owner(layer_input, *args):
    swap_start, swap_rows = args[-2:]
    tokens = layer_input.shape[0]
    values = front(*args)[:tokens]
    balanced = values
    for level in range(lax.axis_size("dp").bit_length() - 1):
        offset = swap_start[0, level]
        window = lax.dynamic_slice_in_dim(balanced, offset, CAP, 0)
        balanced = blend_rows(balanced, swapped(window, "dp", level), offset, swap_rows[0, level])
    owners = lax.axis_size("fsdp")
    owned = (D + owners - 1) // owners
    padded = jnp.pad(layer_input, ((0, 0), (0, owned * owners - D)))
    arranged = lax.all_to_all(
        padded.reshape(tokens, owners, owned), "fsdp", split_axis=1, concat_axis=0, tiled=True
    )
    block = lax.dot_general(
        arranged.reshape(-1, owned),
        lax.all_gather(values, "fsdp", axis=0, tiled=True),
        (((0,), (0,)), ((), ())),
        preferred_element_type=F32,
    )
    return lax.psum(block, "dp"), balanced


def on_device(layer_input, *args):
    if lax.axis_size("dp") == 4 and lax.axis_size("fsdp") == 8:
        return reduce_by_axis(layer_input, *args)
    return reduce_by_owner(layer_input, *args)


def solution(mesh):
    return jax.shard_map(
        on_device,
        mesh=mesh,
        in_specs=(
            P(("dp", "fsdp"), None),
            P(("dp", "fsdp"), None),
            P(("dp", "fsdp"), None),
            P(("dp", "fsdp"), None),
            P(("dp", "fsdp")),
            P(("dp", "fsdp")),
            P(),
            P(("dp", "fsdp")),
            P(("dp", "fsdp"), None),
            P(("dp", "fsdp"), None),
        ),
        out_specs=(P("fsdp", None), P(("dp", "fsdp"), None)),
        check_vma=False,
    )
```

```python
import functools

import jax
import jax.numpy as jnp
from jax import lax
from jax.experimental import pallas as pl
from jax.experimental.pallas import tpu as pltpu
from jax.sharding import PartitionSpec as P

D = 4096
HD = 128
CAP = 32
HALF = 128
LANE = 128
INFO = 16
MIB = 1 << 20
FREE = pl.CostEstimate(flops=0, bytes_accessed=0, transcendentals=0)
BF16 = jnp.bfloat16
F32 = jnp.float32

VMEM = pl.BlockSpec(memory_space=pltpu.VMEM)
HBM = pl.BlockSpec(memory_space=pltpu.HBM)


def attend_group(per_group, span, q, k, g, allowed, factor):
    q_all = jnp.concatenate([q[span, n * HD:(n + 1) * HD] for n in range(per_group)], axis=0)
    scores = lax.dot_general(
        k[span, :], q_all, (((1,), (1,)), ((), ())), preferred_element_type=F32
    ) * HD ** (-0.5)
    probs = []
    weighted = []
    for n in range(per_group):
        own = jnp.where(allowed, scores[:, n * HALF:(n + 1) * HALF], -1e30)
        expo = jnp.exp(own - jnp.max(own, axis=0, keepdims=True))
        probs.append((expo / jnp.sum(expo, axis=0, keepdims=True)).astype(BF16))
        weighted.append((g[span, n * HD:(n + 1) * HD].astype(F32) * factor).astype(BF16))
    return jnp.dot(
        jnp.concatenate(probs, axis=1), jnp.concatenate(weighted, axis=0), preferred_element_type=F32
    ).astype(BF16)


def mask_and_factor(span, loss_ref, exponent_ref, ids_ref, index_ref):
    exponent = exponent_ref[0]
    unscale = jnp.float32(1.0)
    for bit in range(5):
        unscale = unscale * jnp.where((exponent >> bit) & 1 == 1, jnp.float32(2.0 ** -(1 << bit)), 1.0)
    row = lax.broadcasted_iota(jnp.int32, (HALF, HALF), 0)
    col = lax.broadcasted_iota(jnp.int32, (HALF, HALF), 1)
    doc_i = jnp.broadcast_to(ids_ref[:, span], (HALF, HALF))
    allowed = (doc_i == doc_i.T) & (row <= col)
    index = index_ref[:, span]
    factor = jnp.zeros((1, HALF), F32)
    for entry in range(loss_ref.shape[0]):
        factor = jnp.where(index == entry, loss_ref[entry], factor)
    return allowed, jnp.broadcast_to(factor * unscale, (HALF, HALF)).T


def front_kernel(
    per_group, loss_hbm, exponent_hbm, start_hbm, rows_hbm, q_hbm, k_hbm, g_hbm, ids_hbm, index_hbm, *rest
):
    v_ref, loss_ref, exponent_ref, start_ref, rows_ref, q_ref, k_ref, g_ref, ids_ref, index_ref, sems = rest
    count = 0

    def begin(source, target):
        nonlocal count
        copy = pltpu.make_async_copy(source, target, sems.at[count])
        copy.start()
        count += 1
        return copy

    small = [
        begin(source, target)
        for source, target in (
            (ids_hbm, ids_ref), (index_hbm, index_ref), (loss_hbm, loss_ref), (exponent_hbm, exponent_ref),
            (start_hbm, start_ref), (rows_hbm, rows_ref),
        )
    ]
    groups = k_ref.shape[1] // HD
    wide = per_group * HD
    loads = []
    for group in range(groups):
        some = pl.ds(group * wide, wide)
        one = pl.ds(group * HD, HD)
        loads.append([
            begin(q_hbm.at[:, some], q_ref.at[:, some]),
            begin(k_hbm.at[:, one], k_ref.at[:, one]),
            begin(g_hbm.at[:, some], g_ref.at[:, some]),
        ])
    for copy in small:
        copy.wait()
    masks = [
        mask_and_factor(pl.ds(half * HALF, HALF), loss_ref, exponent_ref, ids_ref, index_ref) for half in range(2)
    ]

    def put(group, row, value):
        v_ref[pl.ds(row, value.shape[0]), pl.ds(group * HD, HD)] = value

    info_row = lax.broadcasted_iota(jnp.int32, (INFO, HD), 0)
    info = jnp.zeros((INFO, HD), jnp.int32)
    for level in range(min(start_ref.shape[1], INFO // 2)):
        info = jnp.where(info_row == 2 * level, start_ref[0, level], info)
        info = jnp.where(info_row == 2 * level + 1, rows_ref[0, level], info)
    info = info.astype(F32).astype(BF16)
    for group in range(groups):
        for copy in loads[group]:
            copy.wait()
        some = pl.ds(group * wide, wide)
        for half in range(2):
            span = pl.ds(half * HALF, HALF)
            value = attend_group(
                per_group, slice(None), q_ref[span, some], k_ref[span, pl.ds(group * HD, HD)], g_ref[span, some],
                *masks[half],
            )
            put(group, half * HALF, value)
        put(group, 2 * HALF, info)


def front(query, key, grad, ids, index, loss, exponent, start, rows):
    tokens, key_width = key.shape
    per_group = query.shape[1] // key_width
    groups = key_width // HD
    args = [
        loss, exponent, start, rows, query, key, grad, ids.reshape(1, tokens), index.reshape(1, tokens)
    ]
    return pl.pallas_call(
        functools.partial(front_kernel, per_group),
        in_specs=[HBM] * 9,
        out_specs=VMEM,
        out_shape=jax.ShapeDtypeStruct((tokens + INFO, key_width), BF16),
        scratch_shapes=[
            pltpu.SMEM(loss.shape, F32), pltpu.SMEM(exponent.shape, jnp.int32),
            pltpu.SMEM(start.shape, jnp.int32), pltpu.SMEM(rows.shape, jnp.int32),
            pltpu.VMEM(query.shape, BF16), pltpu.VMEM(key.shape, BF16), pltpu.VMEM(grad.shape, BF16),
            pltpu.VMEM((1, tokens), jnp.int32), pltpu.VMEM((1, tokens), jnp.int32),
            pltpu.SemaphoreType.DMA((6 + 3 * groups,)),
        ],
        compiler_params=pltpu.CompilerParams(vmem_limit_bytes=24 * MIB),
        cost_estimate=FREE,
        name="front",
    )(*[arg if arg is exponent else pltpu.with_memory_space_constraint(arg, pltpu.HBM) for arg in args])


CORE, Y, X, Z1, Z2 = 8, 16, 1, 2, 4


def xor_permute(value, mask):
    count = lax.axis_size("dp") * lax.axis_size("fsdp")
    return lax.ppermute(value, ("dp", "fsdp"), [(i, i ^ mask) for i in range(count)])


def partial_kernel(parts, own_ref, near_ref, v0_ref, v1_ref, *out_refs):
    dp = lax.axis_index("dp")
    fsdp = lax.axis_index("fsdp")
    v = jnp.concatenate([ref[pl.ds(0, 2 * HALF), :] for ref in (v0_ref, v1_ref)], axis=0)
    for blocks, out_ref in zip(parts, out_refs):
        columns = []
        for z, y, x in blocks:
            owner = fsdp ^ (z << 1 | x)
            column = pl.multiple_of(owner * (4 * LANE) + (dp ^ (y << 1)) * LANE, LANE)
            columns.append(jnp.concatenate([ref[:, pl.ds(column, LANE)] for ref in (own_ref, near_ref)], axis=0))
        total = lax.dot_general(
            jnp.concatenate(columns, axis=1), v, (((0,), (0,)), ((), ())), preferred_element_type=F32
        )
        out_ref[...] = total.astype(out_ref.dtype)


def partial_sums(parts, dtype, own, near, v0, v1):
    return pl.pallas_call(
        functools.partial(partial_kernel, parts),
        in_specs=[VMEM] * 4,
        out_specs=[VMEM] * len(parts),
        out_shape=[jax.ShapeDtypeStruct((len(blocks) * LANE, 512), dtype) for blocks in parts],
        compiler_params=pltpu.CompilerParams(vmem_limit_bytes=24 * MIB),
        cost_estimate=FREE,
        name="partial_sums",
    )(own, near, v0, v1)


def inner_swap_kernel(v0_ref, v1_ref, out_ref, window_ref):
    tokens = out_ref.shape[0]
    infos = [ref[pl.ds(tokens, INFO), pl.ds(0, HALF)].astype(F32).astype(jnp.int32) for ref in (v0_ref, v1_ref)]

    def table(device, entry):
        return jnp.broadcast_to(infos[device][entry:entry + 1, :], (HALF, HALF))

    place = lax.broadcasted_iota(jnp.int32, (HALF, HALF), 0) + HALF
    inner = lax.broadcasted_iota(jnp.int32, (HALF, HALF), 1) + HALF
    first = table(0, 0)
    moved = (place >= first) & (place < first + table(0, 1))
    stays = jnp.where(~moved & (place == inner), 1.0, 0.0).astype(BF16)
    comes = jnp.where(moved & (place + table(1, 0) - first == inner), 1.0, 0.0).astype(BF16)
    taken = jnp.where(place - HALF + table(0, 2) == inner, 1.0, 0.0).astype(BF16)[:CAP]
    rows = (
        jnp.dot(stays, v0_ref[pl.ds(HALF, HALF), :], preferred_element_type=F32)
        + jnp.dot(comes, v1_ref[pl.ds(HALF, HALF), :], preferred_element_type=F32)
    ).astype(BF16)
    out_ref[pl.ds(0, HALF), :] = v0_ref[pl.ds(0, HALF), :]
    out_ref[pl.ds(HALF, HALF), :] = rows
    window_ref[...] = jnp.dot(taken, rows, preferred_element_type=F32).astype(BF16)


def inner_swap(v0, v1):
    return pl.pallas_call(
        inner_swap_kernel,
        in_specs=[VMEM] * 2,
        out_specs=[VMEM] * 2,
        out_shape=[jax.ShapeDtypeStruct((2 * HALF, 512), BF16), jax.ShapeDtypeStruct((CAP, 512), BF16)],
        compiler_params=pltpu.CompilerParams(vmem_limit_bytes=8 * MIB),
        cost_estimate=FREE,
        name="inner_swap",
    )(v0, v1)


def outer_swap_kernel(v0_ref, rows_ref, window_ref, out_ref):
    tokens = out_ref.shape[0]
    info = v0_ref[pl.ds(tokens, INFO), pl.ds(0, HALF)].astype(F32).astype(jnp.int32)
    first = jnp.broadcast_to(info[2:3, :], (HALF, HALF))
    extent = jnp.broadcast_to(info[3:4, :], (HALF, HALF))
    place = lax.broadcasted_iota(jnp.int32, (HALF, HALF), 0) + HALF
    inner = lax.broadcasted_iota(jnp.int32, (HALF, HALF), 1)
    moved = (place >= first) & (place < first + extent)
    stays = jnp.where(~moved & (place == inner + HALF), 1.0, 0.0).astype(BF16)
    comes = jnp.where(moved & (place - first == inner), 1.0, 0.0).astype(BF16)[:, :CAP]
    out_ref[pl.ds(0, HALF), :] = rows_ref[pl.ds(0, HALF), :]
    out_ref[pl.ds(HALF, HALF), :] = (
        jnp.dot(stays, rows_ref[pl.ds(HALF, HALF), :], preferred_element_type=F32)
        + jnp.dot(comes, window_ref[...], preferred_element_type=F32)
    ).astype(BF16)


def outer_swap(v0, rows, window):
    return pl.pallas_call(
        outer_swap_kernel,
        in_specs=[VMEM] * 3,
        out_specs=VMEM,
        out_shape=jax.ShapeDtypeStruct(rows.shape, BF16),
        compiler_params=pltpu.CompilerParams(vmem_limit_bytes=8 * MIB),
        cost_estimate=FREE,
        name="outer_swap",
    )(v0, rows, window)


def place_kernel(mine_ref, y_ref, near_ref, out_ref):
    dp = lax.axis_index("dp")
    for flip, block in ((0, mine_ref), (2, y_ref), (1, near_ref.at[0]), (3, near_ref.at[1])):
        out_ref[pl.ds(pl.multiple_of((dp ^ flip) * LANE, LANE), LANE), :] = block[...].astype(F32)


def place(mine, from_y, near):
    return pl.pallas_call(
        place_kernel,
        in_specs=[VMEM] * 3,
        out_specs=VMEM,
        out_shape=jax.ShapeDtypeStruct((512, 512), F32),
        compiler_params=pltpu.CompilerParams(vmem_limit_bytes=8 * MIB),
        cost_estimate=FREE,
        name="place",
    )(mine, from_y, near)


def fold_kernel(base_ref, arrived_ref, out_ref):
    out_ref[...] = base_ref[...] + arrived_ref[...].astype(F32)


def fold(base, arrived):
    return pl.pallas_call(
        fold_kernel,
        in_specs=[VMEM] * 2,
        out_specs=VMEM,
        out_shape=jax.ShapeDtypeStruct(base.shape, F32),
        compiler_params=pltpu.CompilerParams(vmem_limit_bytes=8 * MIB),
        cost_estimate=pl.CostEstimate(flops=6_000_000_000, bytes_accessed=0, transcendentals=0),
        name="fold",
    )(base, arrived)


def reduce_by_axis(layer_input, *args):
    near = xor_permute(layer_input, CORE)
    v0 = front(*args)
    v1 = xor_permute(v0, CORE)

    def sums(parts, dtype):
        return partial_sums(parts, dtype, layer_input, near, v0, v1)

    def after_all(*values):
        return lax.optimization_barrier(values)

    def add(*terms):
        total = terms[0]
        for term in terms[1:]:
            total = total + term.astype(F32)
        return total

    first_b, first_a = sums((((3, 1, 1), (3, 0, 1)), ((2, 1, 1), (2, 1, 0))), BF16)
    rows, window = inner_swap(v0, v1)
    pair, = sums((((1, 1, 1), (1, 1, 0), (1, 0, 1), (1, 0, 0)),), BF16)
    keep_b, keep_a = sums((((3, 1, 0), (3, 0, 0)), ((2, 0, 1), (2, 0, 0))), F32)
    own, = sums((((0, 1, 1), (0, 1, 0), (0, 0, 1), (0, 0, 0)),), F32)
    first_b = xor_permute(first_b, X)
    first_a = xor_permute(jnp.concatenate([first_a, window]), Y)
    pair = xor_permute(pair, Z1)
    on_b = xor_permute(add(keep_b[:LANE], first_b[:LANE]).astype(BF16), Y)
    on_a = xor_permute(add(keep_a[:LANE], first_a[:LANE]).astype(BF16), X)
    z3 = add(keep_b[LANE:], first_b[LANE:], on_b).astype(BF16)
    pair = after_all(pair, z3)[0]
    z3 = xor_permute(z3, Z1)
    z2 = add(keep_a[LANE:], first_a[LANE:2 * LANE], on_a, z3).astype(BF16)

    total = add(own, pair)
    some, rest = total[:, :256], total[:, 256:]
    rest_far, rest_y, rest_x, rest_own = (rest[row:row + LANE] for row in range(0, 4 * LANE, LANE))
    some_in = xor_permute(some[:2 * LANE].astype(BF16), Y)
    rest_in = xor_permute(jnp.concatenate([rest_far, rest_x]).astype(BF16), X)
    some_in, rest_in, window = after_all(some_in, rest_in, first_a[2 * LANE:], z2)[:3]
    z2 = xor_permute(z2, Z2)
    some_on = xor_permute(add(some[2 * LANE:3 * LANE], some_in[:LANE]).astype(BF16), X)
    rest_on = xor_permute(add(rest_y, rest_in[:LANE]).astype(BF16), Y)
    value_grad = outer_swap(v0, rows, window)
    base = jnp.concatenate([add(some[3 * LANE:], some_in[LANE:]), add(rest_own, rest_in[LANE:])], axis=1)
    base, value_grad = after_all(base, value_grad)
    mine = add(fold(base, z2), jnp.concatenate([some_on, rest_on], axis=1)).astype(BF16)
    from_y = xor_permute(mine, Y)
    return place(mine, from_y, xor_permute(jnp.stack([mine, from_y]), CORE)), value_grad


def swapped(block, axis, distance):
    count = lax.axis_size(axis)
    route = []
    for low in range(count):
        high = low | 1 << distance
        if high != low and high < count:
            route += [(low, high), (high, low)]
    return lax.ppermute(block, axis, route)


def blend_rows(item, incoming, offset, extent):
    inside = (jnp.arange(CAP) < extent)[:, None]
    chosen = jnp.where(inside, incoming, lax.dynamic_slice_in_dim(item, offset, CAP, 0))
    return lax.dynamic_update_slice_in_dim(item, chosen, offset, 0)


def reduce_by_owner(layer_input, *args):
    swap_start, swap_rows = args[-2:]
    tokens = layer_input.shape[0]
    values = front(*args)[:tokens]
    balanced = values
    for level in range(lax.axis_size("dp").bit_length() - 1):
        offset = swap_start[0, level]
        window = lax.dynamic_slice_in_dim(balanced, offset, CAP, 0)
        balanced = blend_rows(balanced, swapped(window, "dp", level), offset, swap_rows[0, level])
    owners = lax.axis_size("fsdp")
    owned = (D + owners - 1) // owners
    padded = jnp.pad(layer_input, ((0, 0), (0, owned * owners - D)))
    arranged = lax.all_to_all(
        padded.reshape(tokens, owners, owned), "fsdp", split_axis=1, concat_axis=0, tiled=True
    )
    block = lax.dot_general(
        arranged.reshape(-1, owned),
        lax.all_gather(values, "fsdp", axis=0, tiled=True),
        (((0,), (0,)), ((), ())),
        preferred_element_type=F32,
    )
    return lax.psum(block, "dp"), balanced


def on_device(layer_input, *args):
    if lax.axis_size("dp") == 4 and lax.axis_size("fsdp") == 8:
        return reduce_by_axis(layer_input, *args)
    return reduce_by_owner(layer_input, *args)


def solution(mesh):
    return jax.shard_map(
        on_device,
        mesh=mesh,
        in_specs=(
            P(("dp", "fsdp"), None),
            P(("dp", "fsdp"), None),
            P(("dp", "fsdp"), None),
            P(("dp", "fsdp"), None),
            P(("dp", "fsdp")),
            P(("dp", "fsdp")),
            P(),
            P(("dp", "fsdp")),
            P(("dp", "fsdp"), None),
            P(("dp", "fsdp"), None),
        ),
        out_specs=(P("fsdp", None), P(("dp", "fsdp"), None)),
        check_vma=False,
    )
```

```python
import functools
import math

import jax
import jax.numpy as jnp
from jax import lax
from jax.experimental import pallas as pl
from jax.experimental.pallas import tpu as pltpu
from jax.sharding import PartitionSpec as P

D = 4096
HD = 128
CAP = 32
HALF = 128
SEG = 16
LANE = 128
INFO = 16
MIB = 1 << 20
FREE = pl.CostEstimate(flops=0, bytes_accessed=0, transcendentals=0)
BF16 = jnp.bfloat16
F32 = jnp.float32

VMEM = pl.BlockSpec(memory_space=pltpu.VMEM)
HBM = pl.BlockSpec(memory_space=pltpu.HBM)


def attend_half(per_group, folded, span, q_ref, k_ref, g_ref, allowed, factor):
    heads = q_ref.shape[1] // HD
    groups = heads // per_group
    scores = [
        lax.dot_general(
            k_ref[span, pl.ds(group * HD, HD)],
            jnp.concatenate(
                [q_ref[span, pl.ds((group * per_group + n) * HD, HD)] for n in range(per_group)], axis=0
            ),
            (((1,), (1,)), ((), ())),
            preferred_element_type=F32,
        )
        for group in range(groups)
    ]
    weighted = [
        (g_ref[span, pl.ds(head * HD, HD)].astype(F32) * factor).astype(BF16) for head in range(heads)
    ]
    if folded:
        block = lax.broadcasted_iota(jnp.int32, (SEG, HALF), 1) // SEG
    probs = []
    for head in range(heads):
        n = head % per_group
        own = scores[head // per_group][:, n * HALF:(n + 1) * HALF]
        if folded:
            own = fold_blocks(own, block)
        own = jnp.where(allowed, own, -1e30)
        expo = jnp.exp2((own - jnp.max(own, axis=0, keepdims=True)) * (HD ** (-0.5) * math.log2(math.e)))
        prob = (expo * (1.0 / jnp.sum(expo, axis=0, keepdims=True))).astype(BF16)
        if folded:
            prob = jnp.concatenate(
                [jnp.where(block == b, prob, jnp.zeros_like(prob)) for b in range(HALF // SEG)], axis=0
            )
        probs.append(prob)
    return [
        jnp.dot(
            jnp.concatenate(probs[head:head + per_group], axis=1),
            jnp.concatenate(weighted[head:head + per_group], axis=0),
            preferred_element_type=F32,
        ).astype(BF16)
        for head in range(0, heads, per_group)
    ]


def fold_blocks(square, block):
    total = square[:SEG]
    for b in range(1, HALF // SEG):
        total = jnp.where(block == b, square[b * SEG:(b + 1) * SEG], total)
    return total


def mask_and_factor(folded, span, loss_ref, exponent_ref, ids_ref, index_ref):
    exponent = exponent_ref[0]
    unscale = jnp.float32(1.0)
    for bit in range(5):
        unscale = unscale * jnp.where((exponent >> bit) & 1 == 1, jnp.float32(2.0 ** -(1 << bit)), 1.0)
    row = lax.broadcasted_iota(jnp.int32, (HALF, HALF), 0)
    col = lax.broadcasted_iota(jnp.int32, (HALF, HALF), 1)
    doc_i = jnp.broadcast_to(ids_ref[:, span], (HALF, HALF))
    allowed = (doc_i == doc_i.T) & (row <= col)
    if folded:
        allowed = fold_blocks(
            jnp.where(allowed, 1, 0), lax.broadcasted_iota(jnp.int32, (SEG, HALF), 1) // SEG
        ) == 1
    index = index_ref[:, span]
    factor = jnp.zeros((1, HALF), F32)
    for entry in range(loss_ref.shape[0]):
        factor = jnp.where(index == entry, loss_ref[entry], factor)
    return allowed, jnp.broadcast_to(factor * unscale, (HALF, HALF)).T


def front_kernel(
    per_group, loss_hbm, exponent_hbm, start_hbm, rows_hbm, q_hbm, k_hbm, g_hbm, ids_hbm, index_hbm, *rest
):
    v_ref, loss_ref, exponent_ref, start_ref, rows_ref, q_ref, k_ref, g_ref, ids_ref, index_ref, sems = rest
    count = 0

    def begin(source, target):
        nonlocal count
        copy = pltpu.make_async_copy(source, target, sems.at[count])
        copy.start()
        count += 1
        return copy

    small = [
        begin(source, target)
        for source, target in (
            (ids_hbm, ids_ref), (index_hbm, index_ref), (loss_hbm, loss_ref), (exponent_hbm, exponent_ref),
            (start_hbm, start_ref), (rows_hbm, rows_ref),
        )
    ]
    groups = k_ref.shape[1] // HD
    wide = per_group * HD
    loads = []
    for half in range(2):
        span = pl.ds(half * HALF, HALF)
        loads.append([
            begin(source.at[span, :], target.at[span, :])
            for source, target in ((q_hbm, q_ref), (k_hbm, k_ref), (g_hbm, g_ref))
        ])
    for copy in small:
        copy.wait()
    masks = [
        mask_and_factor(half == 1, pl.ds(half * HALF, HALF), loss_ref, exponent_ref, ids_ref, index_ref)
        for half in range(2)
    ]
    info_row = lax.broadcasted_iota(jnp.int32, (INFO, k_ref.shape[1]), 0)
    info = jnp.zeros(info_row.shape, jnp.int32)
    for level in range(min(start_ref.shape[1], INFO // 2)):
        info = jnp.where(info_row == 2 * level, start_ref[0, level], info)
        info = jnp.where(info_row == 2 * level + 1, rows_ref[0, level], info)
    v_ref[pl.ds(2 * HALF, INFO), :] = info.astype(F32).astype(BF16)
    for half in range(2):
        for copy in loads[half]:
            copy.wait()
        span = pl.ds(half * HALF, HALF)
        values = attend_half(per_group, half == 1, span, q_ref, k_ref, g_ref, *masks[half])
        for group, value in enumerate(values):
            v_ref[span, pl.ds(group * HD, HD)] = value


def front(query, key, grad, ids, index, loss, exponent, start, rows):
    tokens, key_width = key.shape
    per_group = query.shape[1] // key_width
    args = [
        loss, exponent, start, rows, query, key, grad, ids.reshape(1, tokens), index.reshape(1, tokens)
    ]
    return pl.pallas_call(
        functools.partial(front_kernel, per_group),
        in_specs=[HBM] * 9,
        out_specs=VMEM,
        out_shape=jax.ShapeDtypeStruct((tokens + INFO, key_width), BF16),
        scratch_shapes=[
            pltpu.SMEM(loss.shape, F32), pltpu.SMEM(exponent.shape, jnp.int32),
            pltpu.SMEM(start.shape, jnp.int32), pltpu.SMEM(rows.shape, jnp.int32),
            pltpu.VMEM(query.shape, BF16), pltpu.VMEM(key.shape, BF16), pltpu.VMEM(grad.shape, BF16),
            pltpu.VMEM((1, tokens), jnp.int32), pltpu.VMEM((1, tokens), jnp.int32),
            pltpu.SemaphoreType.DMA((12,)),
        ],
        compiler_params=pltpu.CompilerParams(vmem_limit_bytes=24 * MIB),
        cost_estimate=FREE,
        name="front",
    )(*[arg if arg is exponent else pltpu.with_memory_space_constraint(arg, pltpu.HBM) for arg in args])


CORE, Y, X, Z1, Z2 = 8, 16, 1, 2, 4


def xor_permute(value, mask):
    count = lax.axis_size("dp") * lax.axis_size("fsdp")
    return lax.ppermute(value, ("dp", "fsdp"), [(i, i ^ mask) for i in range(count)])


def partial_kernel(parts, own_ref, near_ref, v0_ref, v1_ref, *out_refs):
    dp = lax.axis_index("dp")
    fsdp = lax.axis_index("fsdp")
    v = jnp.concatenate([ref[pl.ds(0, 2 * HALF), :] for ref in (v0_ref, v1_ref)], axis=0)
    for blocks, out_ref in zip(parts, out_refs):
        columns = []
        for z, y, x in blocks:
            owner = fsdp ^ (z << 1 | x)
            column = pl.multiple_of(owner * (4 * LANE) + (dp ^ (y << 1)) * LANE, LANE)
            columns.append(jnp.concatenate([ref[:, pl.ds(column, LANE)] for ref in (own_ref, near_ref)], axis=0))
        total = lax.dot_general(
            jnp.concatenate(columns, axis=1), v, (((0,), (0,)), ((), ())), preferred_element_type=F32
        )
        out_ref[...] = total.astype(out_ref.dtype)


def partial_sums(parts, dtype, own, near, v0, v1):
    return pl.pallas_call(
        functools.partial(partial_kernel, parts),
        in_specs=[VMEM] * 4,
        out_specs=[VMEM] * len(parts),
        out_shape=[jax.ShapeDtypeStruct((len(blocks) * LANE, 512), dtype) for blocks in parts],
        compiler_params=pltpu.CompilerParams(vmem_limit_bytes=24 * MIB),
        cost_estimate=FREE,
        name="partial_sums",
    )(own, near, v0, v1)


def inner_swap_kernel(v0_ref, v1_ref, out_ref, window_ref):
    tokens = out_ref.shape[0]
    infos = [ref[pl.ds(tokens, INFO), pl.ds(0, HALF)].astype(F32).astype(jnp.int32) for ref in (v0_ref, v1_ref)]

    def table(device, entry):
        return jnp.broadcast_to(infos[device][entry:entry + 1, :], (HALF, HALF))

    place = lax.broadcasted_iota(jnp.int32, (HALF, HALF), 0) + HALF
    inner = lax.broadcasted_iota(jnp.int32, (HALF, HALF), 1) + HALF
    first = table(0, 0)
    moved = (place >= first) & (place < first + table(0, 1))
    stays = jnp.where(~moved & (place == inner), 1.0, 0.0).astype(BF16)
    comes = jnp.where(moved & (place + table(1, 0) - first == inner), 1.0, 0.0).astype(BF16)
    taken = jnp.where(place - HALF + table(0, 2) == inner, 1.0, 0.0).astype(BF16)[:CAP]
    rows = (
        jnp.dot(stays, v0_ref[pl.ds(HALF, HALF), :], preferred_element_type=F32)
        + jnp.dot(comes, v1_ref[pl.ds(HALF, HALF), :], preferred_element_type=F32)
    ).astype(BF16)
    out_ref[pl.ds(0, HALF), :] = v0_ref[pl.ds(0, HALF), :]
    out_ref[pl.ds(HALF, HALF), :] = rows
    window_ref[...] = jnp.dot(taken, rows, preferred_element_type=F32).astype(BF16)


def inner_swap(v0, v1):
    return pl.pallas_call(
        inner_swap_kernel,
        in_specs=[VMEM] * 2,
        out_specs=[VMEM] * 2,
        out_shape=[jax.ShapeDtypeStruct((2 * HALF, 512), BF16), jax.ShapeDtypeStruct((CAP, 512), BF16)],
        compiler_params=pltpu.CompilerParams(vmem_limit_bytes=8 * MIB),
        cost_estimate=FREE,
        name="inner_swap",
    )(v0, v1)


def outer_swap_kernel(v0_ref, rows_ref, window_ref, out_ref):
    tokens = out_ref.shape[0]
    info = v0_ref[pl.ds(tokens, INFO), pl.ds(0, HALF)].astype(F32).astype(jnp.int32)
    first = jnp.broadcast_to(info[2:3, :], (HALF, HALF))
    extent = jnp.broadcast_to(info[3:4, :], (HALF, HALF))
    place = lax.broadcasted_iota(jnp.int32, (HALF, HALF), 0) + HALF
    inner = lax.broadcasted_iota(jnp.int32, (HALF, HALF), 1)
    moved = (place >= first) & (place < first + extent)
    stays = jnp.where(~moved & (place == inner + HALF), 1.0, 0.0).astype(BF16)
    comes = jnp.where(moved & (place - first == inner), 1.0, 0.0).astype(BF16)[:, :CAP]
    out_ref[pl.ds(0, HALF), :] = rows_ref[pl.ds(0, HALF), :]
    out_ref[pl.ds(HALF, HALF), :] = (
        jnp.dot(stays, rows_ref[pl.ds(HALF, HALF), :], preferred_element_type=F32)
        + jnp.dot(comes, window_ref[...], preferred_element_type=F32)
    ).astype(BF16)


def outer_swap(v0, rows, window):
    return pl.pallas_call(
        outer_swap_kernel,
        in_specs=[VMEM] * 3,
        out_specs=VMEM,
        out_shape=jax.ShapeDtypeStruct(rows.shape, BF16),
        compiler_params=pltpu.CompilerParams(vmem_limit_bytes=8 * MIB),
        cost_estimate=FREE,
        name="outer_swap",
    )(v0, rows, window)


def place_kernel(mine_ref, y_ref, near_ref, out_ref):
    dp = lax.axis_index("dp")
    for flip, block in ((0, mine_ref), (2, y_ref), (1, near_ref.at[0]), (3, near_ref.at[1])):
        out_ref[pl.ds(pl.multiple_of((dp ^ flip) * LANE, LANE), LANE), :] = block[...].astype(F32)


def place(mine, from_y, near):
    return pl.pallas_call(
        place_kernel,
        in_specs=[VMEM] * 3,
        out_specs=VMEM,
        out_shape=jax.ShapeDtypeStruct((512, 512), F32),
        compiler_params=pltpu.CompilerParams(vmem_limit_bytes=8 * MIB),
        cost_estimate=FREE,
        name="place",
    )(mine, from_y, near)


def fold_kernel(base_ref, arrived_ref, out_ref):
    out_ref[...] = base_ref[...] + arrived_ref[...].astype(F32)


def fold(base, arrived):
    return pl.pallas_call(
        fold_kernel,
        in_specs=[VMEM] * 2,
        out_specs=VMEM,
        out_shape=jax.ShapeDtypeStruct(base.shape, F32),
        compiler_params=pltpu.CompilerParams(vmem_limit_bytes=8 * MIB),
        cost_estimate=pl.CostEstimate(flops=6_000_000_000, bytes_accessed=0, transcendentals=0),
        name="fold",
    )(base, arrived)


def reduce_by_axis(layer_input, *args):
    near = xor_permute(layer_input, CORE)
    v0 = front(*args)
    v1 = xor_permute(v0, CORE)

    def sums(parts, dtype):
        return partial_sums(parts, dtype, layer_input, near, v0, v1)

    def after_all(*values):
        return lax.optimization_barrier(values)

    def add(*terms):
        total = terms[0]
        for term in terms[1:]:
            total = total + term.astype(F32)
        return total

    first_b, first_a = sums((((3, 1, 1), (3, 0, 1)), ((2, 1, 1), (2, 1, 0))), BF16)
    pair, = sums((((1, 1, 1), (1, 1, 0), (1, 0, 1), (1, 0, 0)),), BF16)
    keep_b, keep_a = sums((((3, 1, 0), (3, 0, 0)), ((2, 0, 1), (2, 0, 0))), F32)
    own, = sums((((0, 1, 1), (0, 1, 0), (0, 0, 1), (0, 0, 0)),), F32)
    first_b = xor_permute(first_b, X)
    first_a = xor_permute(first_a, Y)
    pair = xor_permute(pair, Z1)
    on_b = add(keep_b[:LANE], first_b[:LANE]).astype(BF16)
    rows, window = inner_swap(after_all(v0, own)[0], v1)
    window = xor_permute(after_all(window, on_b)[0], Y)
    on_b = xor_permute(on_b, Y)
    on_a = xor_permute(add(keep_a[:LANE], first_a[:LANE]).astype(BF16), X)
    z3 = add(keep_b[LANE:], first_b[LANE:], on_b).astype(BF16)
    pair, window = after_all(pair, window, z3)[:2]
    z3 = xor_permute(z3, Z1)
    z2 = add(keep_a[LANE:], first_a[LANE:], on_a, z3).astype(BF16)

    total = add(own, pair)
    some, rest = total[:, :256], total[:, 256:]
    rest_far, rest_y, rest_x, rest_own = (rest[row:row + LANE] for row in range(0, 4 * LANE, LANE))
    some_in = xor_permute(some[:2 * LANE].astype(BF16), Y)
    rest_in = xor_permute(jnp.concatenate([rest_far, rest_x]).astype(BF16), X)
    some_in, rest_in = after_all(some_in, rest_in, z2)[:2]
    z2 = xor_permute(z2, Z2)
    some_on = xor_permute(add(some[2 * LANE:3 * LANE], some_in[:LANE]).astype(BF16), X)
    rest_on = xor_permute(add(rest_y, rest_in[:LANE]).astype(BF16), Y)
    base = jnp.concatenate([add(some[3 * LANE:], some_in[LANE:]), add(rest_own, rest_in[LANE:])], axis=1)
    mine = add(fold(base, z2), jnp.concatenate([some_on, rest_on], axis=1)).astype(BF16)
    from_y = xor_permute(mine, Y)
    value_grad = outer_swap(v0, rows, after_all(window, from_y)[0])
    return place(mine, from_y, xor_permute(jnp.stack([mine, from_y]), CORE)), value_grad


def swapped(block, axis, distance):
    count = lax.axis_size(axis)
    route = []
    for low in range(count):
        high = low | 1 << distance
        if high != low and high < count:
            route += [(low, high), (high, low)]
    return lax.ppermute(block, axis, route)


def blend_rows(item, incoming, offset, extent):
    inside = (jnp.arange(CAP) < extent)[:, None]
    chosen = jnp.where(inside, incoming, lax.dynamic_slice_in_dim(item, offset, CAP, 0))
    return lax.dynamic_update_slice_in_dim(item, chosen, offset, 0)


def reduce_by_owner(layer_input, *args):
    swap_start, swap_rows = args[-2:]
    tokens = layer_input.shape[0]
    values = front(*args)[:tokens]
    balanced = values
    for level in range(lax.axis_size("dp").bit_length() - 1):
        offset = swap_start[0, level]
        window = lax.dynamic_slice_in_dim(balanced, offset, CAP, 0)
        balanced = blend_rows(balanced, swapped(window, "dp", level), offset, swap_rows[0, level])
    owners = lax.axis_size("fsdp")
    owned = (D + owners - 1) // owners
    padded = jnp.pad(layer_input, ((0, 0), (0, owned * owners - D)))
    arranged = lax.all_to_all(
        padded.reshape(tokens, owners, owned), "fsdp", split_axis=1, concat_axis=0, tiled=True
    )
    block = lax.dot_general(
        arranged.reshape(-1, owned),
        lax.all_gather(values, "fsdp", axis=0, tiled=True),
        (((0,), (0,)), ((), ())),
        preferred_element_type=F32,
    )
    return lax.psum(block, "dp"), balanced


def on_device(layer_input, *args):
    if lax.axis_size("dp") == 4 and lax.axis_size("fsdp") == 8:
        return reduce_by_axis(layer_input, *args)
    return reduce_by_owner(layer_input, *args)


def solution(mesh):
    return jax.shard_map(
        on_device,
        mesh=mesh,
        in_specs=(
            P(("dp", "fsdp"), None),
            P(("dp", "fsdp"), None),
            P(("dp", "fsdp"), None),
            P(("dp", "fsdp"), None),
            P(("dp", "fsdp")),
            P(("dp", "fsdp")),
            P(),
            P(("dp", "fsdp")),
            P(("dp", "fsdp"), None),
            P(("dp", "fsdp"), None),
        ),
        out_specs=(P("fsdp", None), P(("dp", "fsdp"), None)),
        check_vma=False,
    )
```

```python
import functools
import math

import jax
import jax.numpy as jnp
from jax import lax
from jax.experimental import pallas as pl
from jax.experimental.pallas import tpu as pltpu
from jax.sharding import PartitionSpec as P

D = 4096
HD = 128
CAP = 32
HALF = 128
SEG = 16
LANE = 128
INFO = 16
MIB = 1 << 20
FREE = pl.CostEstimate(flops=0, bytes_accessed=0, transcendentals=0)
BF16 = jnp.bfloat16
F32 = jnp.float32

VMEM = pl.BlockSpec(memory_space=pltpu.VMEM)
HBM = pl.BlockSpec(memory_space=pltpu.HBM)


def attend_half(per_group, folded, span, q_ref, k_ref, g_ref, allowed, factor):
    heads = q_ref.shape[1] // HD
    groups = heads // per_group
    scores = [
        lax.dot_general(
            k_ref[span, pl.ds(group * HD, HD)],
            jnp.concatenate(
                [q_ref[span, pl.ds((group * per_group + n) * HD, HD)] for n in range(per_group)], axis=0
            ),
            (((1,), (1,)), ((), ())),
            preferred_element_type=F32,
        )
        for group in range(groups)
    ]
    weighted = [
        (g_ref[span, pl.ds(head * HD, HD)].astype(F32) * factor).astype(BF16) for head in range(heads)
    ]
    if folded:
        block = lax.broadcasted_iota(jnp.int32, (SEG, HALF), 1) // SEG
    probs = []
    for head in range(heads):
        n = head % per_group
        own = scores[head // per_group][:, n * HALF:(n + 1) * HALF]
        if folded:
            own = fold_blocks(own, block)
        own = jnp.where(allowed, own, -1e30)
        expo = jnp.exp2((own - jnp.max(own, axis=0, keepdims=True)) * (HD ** (-0.5) * math.log2(math.e)))
        prob = (expo * (1.0 / jnp.sum(expo, axis=0, keepdims=True))).astype(BF16)
        if folded:
            prob = jnp.concatenate(
                [jnp.where(block == b, prob, jnp.zeros_like(prob)) for b in range(HALF // SEG)], axis=0
            )
        probs.append(prob)
    return [
        jnp.dot(
            jnp.concatenate(probs[head:head + per_group], axis=1),
            jnp.concatenate(weighted[head:head + per_group], axis=0),
            preferred_element_type=F32,
        ).astype(BF16)
        for head in range(0, heads, per_group)
    ]


def fold_blocks(square, block):
    total = square[:SEG]
    for b in range(1, HALF // SEG):
        total = jnp.where(block == b, square[b * SEG:(b + 1) * SEG], total)
    return total


def mask_and_factor(folded, span, loss_ref, exponent_ref, ids_ref, index_ref):
    exponent = exponent_ref[0]
    unscale = jnp.float32(1.0)
    for bit in range(5):
        unscale = unscale * jnp.where((exponent >> bit) & 1 == 1, jnp.float32(2.0 ** -(1 << bit)), 1.0)
    row = lax.broadcasted_iota(jnp.int32, (HALF, HALF), 0)
    col = lax.broadcasted_iota(jnp.int32, (HALF, HALF), 1)
    doc_i = jnp.broadcast_to(ids_ref[:, span], (HALF, HALF))
    allowed = (doc_i == doc_i.T) & (row <= col)
    if folded:
        allowed = fold_blocks(
            jnp.where(allowed, 1, 0), lax.broadcasted_iota(jnp.int32, (SEG, HALF), 1) // SEG
        ) == 1
    index = index_ref[:, span]
    factor = jnp.zeros((1, HALF), F32)
    for entry in range(loss_ref.shape[0]):
        factor = jnp.where(index == entry, loss_ref[entry], factor)
    return allowed, jnp.broadcast_to(factor * unscale, (HALF, HALF)).T


def front_kernel(
    per_group, loss_hbm, exponent_hbm, start_hbm, rows_hbm, q_hbm, k_hbm, g_hbm, ids_hbm, index_hbm, *rest
):
    v_ref, loss_ref, exponent_ref, start_ref, rows_ref, q_ref, k_ref, g_ref, ids_ref, index_ref, sems = rest
    count = 0

    def begin(source, target):
        nonlocal count
        copy = pltpu.make_async_copy(source, target, sems.at[count])
        copy.start()
        count += 1
        return copy

    small = [
        begin(source, target)
        for source, target in (
            (ids_hbm, ids_ref), (index_hbm, index_ref), (loss_hbm, loss_ref), (exponent_hbm, exponent_ref),
            (start_hbm, start_ref), (rows_hbm, rows_ref),
        )
    ]
    groups = k_ref.shape[1] // HD
    wide = per_group * HD
    loads = []
    for half in range(2):
        span = pl.ds(half * HALF, HALF)
        loads.append([
            begin(source.at[span, :], target.at[span, :])
            for source, target in ((q_hbm, q_ref), (k_hbm, k_ref), (g_hbm, g_ref))
        ])
    for copy in small:
        copy.wait()
    masks = [
        mask_and_factor(half == 1, pl.ds(half * HALF, HALF), loss_ref, exponent_ref, ids_ref, index_ref)
        for half in range(2)
    ]
    info_row = lax.broadcasted_iota(jnp.int32, (INFO, k_ref.shape[1]), 0)
    info = jnp.zeros(info_row.shape, jnp.int32)
    for level in range(min(start_ref.shape[1], INFO // 2)):
        info = jnp.where(info_row == 2 * level, start_ref[0, level], info)
        info = jnp.where(info_row == 2 * level + 1, rows_ref[0, level], info)
    v_ref[pl.ds(2 * HALF, INFO), :] = info.astype(F32).astype(BF16)
    for half in range(2):
        for copy in loads[half]:
            copy.wait()
        span = pl.ds(half * HALF, HALF)
        values = attend_half(per_group, half == 1, span, q_ref, k_ref, g_ref, *masks[half])
        for group, value in enumerate(values):
            v_ref[span, pl.ds(group * HD, HD)] = value


def front(query, key, grad, ids, index, loss, exponent, start, rows):
    tokens, key_width = key.shape
    per_group = query.shape[1] // key_width
    args = [
        loss, exponent, start, rows, query, key, grad, ids.reshape(1, tokens), index.reshape(1, tokens)
    ]
    return pl.pallas_call(
        functools.partial(front_kernel, per_group),
        in_specs=[HBM] * 9,
        out_specs=VMEM,
        out_shape=jax.ShapeDtypeStruct((tokens + INFO, key_width), BF16),
        scratch_shapes=[
            pltpu.SMEM(loss.shape, F32), pltpu.SMEM(exponent.shape, jnp.int32),
            pltpu.SMEM(start.shape, jnp.int32), pltpu.SMEM(rows.shape, jnp.int32),
            pltpu.VMEM(query.shape, BF16), pltpu.VMEM(key.shape, BF16), pltpu.VMEM(grad.shape, BF16),
            pltpu.VMEM((1, tokens), jnp.int32), pltpu.VMEM((1, tokens), jnp.int32),
            pltpu.SemaphoreType.DMA((12,)),
        ],
        compiler_params=pltpu.CompilerParams(vmem_limit_bytes=24 * MIB),
        cost_estimate=FREE,
        name="front",
    )(*[arg if arg is exponent else pltpu.with_memory_space_constraint(arg, pltpu.HBM) for arg in args])


CORE, Y, X, Z1, Z2 = 8, 16, 1, 2, 4


def xor_permute(value, mask):
    count = lax.axis_size("dp") * lax.axis_size("fsdp")
    return lax.ppermute(value, ("dp", "fsdp"), [(i, i ^ mask) for i in range(count)])


def partial_kernel(parts, own_ref, near_ref, v0_ref, v1_ref, *out_refs):
    dp = lax.axis_index("dp")
    fsdp = lax.axis_index("fsdp")
    v = jnp.concatenate([ref[pl.ds(0, 2 * HALF), :] for ref in (v0_ref, v1_ref)], axis=0)
    for blocks, out_ref in zip(parts, out_refs):
        columns = []
        for z, y, x in blocks:
            owner = fsdp ^ (z << 1 | x)
            column = pl.multiple_of(owner * (4 * LANE) + (dp ^ (y << 1)) * LANE, LANE)
            columns.append(jnp.concatenate([ref[:, pl.ds(column, LANE)] for ref in (own_ref, near_ref)], axis=0))
        total = lax.dot_general(
            jnp.concatenate(columns, axis=1), v, (((0,), (0,)), ((), ())), preferred_element_type=F32
        )
        out_ref[...] = total.astype(out_ref.dtype)


def partial_sums(parts, dtype, own, near, v0, v1):
    return pl.pallas_call(
        functools.partial(partial_kernel, parts),
        in_specs=[VMEM] * 4,
        out_specs=[VMEM] * len(parts),
        out_shape=[jax.ShapeDtypeStruct((len(blocks) * LANE, 512), dtype) for blocks in parts],
        compiler_params=pltpu.CompilerParams(vmem_limit_bytes=24 * MIB),
        cost_estimate=FREE,
        name="partial_sums",
    )(own, near, v0, v1)


def inner_swap_kernel(v0_ref, v1_ref, out_ref, window_ref):
    tokens = out_ref.shape[0]
    infos = [ref[pl.ds(tokens, INFO), pl.ds(0, HALF)].astype(F32).astype(jnp.int32) for ref in (v0_ref, v1_ref)]

    def table(device, entry):
        return jnp.broadcast_to(infos[device][entry:entry + 1, :], (HALF, HALF))

    place = lax.broadcasted_iota(jnp.int32, (HALF, HALF), 0) + HALF
    inner = lax.broadcasted_iota(jnp.int32, (HALF, HALF), 1) + HALF
    first = table(0, 0)
    moved = (place >= first) & (place < first + table(0, 1))
    stays = jnp.where(~moved & (place == inner), 1.0, 0.0).astype(BF16)
    comes = jnp.where(moved & (place + table(1, 0) - first == inner), 1.0, 0.0).astype(BF16)
    taken = jnp.where(place - HALF + table(0, 2) == inner, 1.0, 0.0).astype(BF16)[:CAP]
    rows = (
        jnp.dot(stays, v0_ref[pl.ds(HALF, HALF), :], preferred_element_type=F32)
        + jnp.dot(comes, v1_ref[pl.ds(HALF, HALF), :], preferred_element_type=F32)
    ).astype(BF16)
    out_ref[pl.ds(0, HALF), :] = v0_ref[pl.ds(0, HALF), :]
    out_ref[pl.ds(HALF, HALF), :] = rows
    window_ref[...] = jnp.dot(taken, rows, preferred_element_type=F32).astype(BF16)


def inner_swap(v0, v1):
    return pl.pallas_call(
        inner_swap_kernel,
        in_specs=[VMEM] * 2,
        out_specs=[VMEM] * 2,
        out_shape=[jax.ShapeDtypeStruct((2 * HALF, 512), BF16), jax.ShapeDtypeStruct((CAP, 512), BF16)],
        compiler_params=pltpu.CompilerParams(vmem_limit_bytes=8 * MIB),
        cost_estimate=FREE,
        name="inner_swap",
    )(v0, v1)


def outer_swap_kernel(v0_ref, rows_ref, window_ref, out_ref):
    tokens = out_ref.shape[0]
    info = v0_ref[pl.ds(tokens, INFO), pl.ds(0, HALF)].astype(F32).astype(jnp.int32)
    first = jnp.broadcast_to(info[2:3, :], (HALF, HALF))
    extent = jnp.broadcast_to(info[3:4, :], (HALF, HALF))
    place = lax.broadcasted_iota(jnp.int32, (HALF, HALF), 0) + HALF
    inner = lax.broadcasted_iota(jnp.int32, (HALF, HALF), 1)
    moved = (place >= first) & (place < first + extent)
    stays = jnp.where(~moved & (place == inner + HALF), 1.0, 0.0).astype(BF16)
    comes = jnp.where(moved & (place - first == inner), 1.0, 0.0).astype(BF16)[:, :CAP]
    out_ref[pl.ds(0, HALF), :] = rows_ref[pl.ds(0, HALF), :]
    out_ref[pl.ds(HALF, HALF), :] = (
        jnp.dot(stays, rows_ref[pl.ds(HALF, HALF), :], preferred_element_type=F32)
        + jnp.dot(comes, window_ref[...], preferred_element_type=F32)
    ).astype(BF16)


def outer_swap(v0, rows, window):
    return pl.pallas_call(
        outer_swap_kernel,
        in_specs=[VMEM] * 3,
        out_specs=VMEM,
        out_shape=jax.ShapeDtypeStruct(rows.shape, BF16),
        compiler_params=pltpu.CompilerParams(vmem_limit_bytes=8 * MIB),
        cost_estimate=FREE,
        name="outer_swap",
    )(v0, rows, window)


def place_kernel(mine_ref, y_ref, near_ref, out_ref):
    dp = lax.axis_index("dp")
    for flip, block in ((0, mine_ref), (2, y_ref), (1, near_ref.at[0]), (3, near_ref.at[1])):
        out_ref[pl.ds(pl.multiple_of((dp ^ flip) * LANE, LANE), LANE), :] = block[...].astype(F32)


def place(mine, from_y, near):
    return pl.pallas_call(
        place_kernel,
        in_specs=[VMEM] * 3,
        out_specs=VMEM,
        out_shape=jax.ShapeDtypeStruct((512, 512), F32),
        compiler_params=pltpu.CompilerParams(vmem_limit_bytes=8 * MIB),
        cost_estimate=FREE,
        name="place",
    )(mine, from_y, near)


def fold_kernel(base_ref, arrived_ref, out_ref):
    out_ref[...] = base_ref[...] + arrived_ref[...].astype(F32)


def fold(base, arrived):
    return pl.pallas_call(
        fold_kernel,
        in_specs=[VMEM] * 2,
        out_specs=VMEM,
        out_shape=jax.ShapeDtypeStruct(base.shape, F32),
        compiler_params=pltpu.CompilerParams(vmem_limit_bytes=8 * MIB),
        cost_estimate=pl.CostEstimate(flops=6_000_000_000, bytes_accessed=0, transcendentals=0),
        name="fold",
    )(base, arrived)


def reduce_by_axis(layer_input, *args):
    near = xor_permute(layer_input, CORE)
    v0 = front(*args)
    v1 = xor_permute(v0, CORE)

    def sums(parts, dtype):
        return partial_sums(parts, dtype, layer_input, near, v0, v1)

    def after_all(*values):
        return lax.optimization_barrier(values)

    def add(*terms):
        total = terms[0]
        for term in terms[1:]:
            total = total + term.astype(F32)
        return total

    first_b, first_a = sums((((3, 1, 1), (3, 0, 1)), ((2, 1, 1), (2, 1, 0))), BF16)
    late_b, late_a = sums((((1, 1, 1), (1, 0, 1)), ((0, 1, 1), (0, 1, 0))), BF16)
    keep_b, keep_a = sums((((3, 1, 0), (3, 0, 0)), ((2, 0, 1), (2, 0, 0))), F32)
    rest_b, rest_a = sums((((1, 1, 0), (1, 0, 0)), ((0, 0, 1), (0, 0, 0))), F32)
    rows, window = inner_swap(after_all(v0, rest_b)[0], v1)
    first_b = xor_permute(first_b, X)
    first_a = xor_permute(first_a, Y)
    late_b = xor_permute(late_b, X)
    on_b = add(keep_b[:LANE], first_b[:LANE]).astype(BF16)
    window, late_a = after_all(window, late_a, on_b)[:2]
    on_b = xor_permute(on_b, Y)
    on_a = xor_permute(add(keep_a[:LANE], first_a[:LANE]).astype(BF16), X)
    late_a = xor_permute(late_a, Y)
    window = xor_permute(window, Y)
    z3 = add(keep_b[LANE:], first_b[LANE:], on_b).astype(BF16)
    late_b = after_all(late_b, z3)[0]
    z3 = xor_permute(z3, Z1)
    z2 = add(keep_a[LANE:], first_a[LANE:], on_a, z3).astype(BF16)
    late_a = after_all(late_a, z2)[0]
    z2 = xor_permute(z2, Z2)
    late_on_b = xor_permute(add(rest_b[:LANE], late_b[:LANE]).astype(BF16), Y)
    late_on_a = xor_permute(add(rest_a[:LANE], late_a[:LANE]).astype(BF16), X)
    z1 = add(rest_b[LANE:], late_b[LANE:], late_on_b).astype(BF16)
    z1, window = after_all(z1, window)
    z1 = xor_permute(z1, Z1)
    mine = add(fold(add(rest_a[LANE:], late_a[LANE:], late_on_a), z2), z1).astype(BF16)
    from_y = xor_permute(mine, Y)
    value_grad = outer_swap(v0, rows, after_all(window, from_y)[0])
    return place(mine, from_y, xor_permute(jnp.stack([mine, from_y]), CORE)), value_grad


def swapped(block, axis, distance):
    count = lax.axis_size(axis)
    route = []
    for low in range(count):
        high = low | 1 << distance
        if high != low and high < count:
            route += [(low, high), (high, low)]
    return lax.ppermute(block, axis, route)


def blend_rows(item, incoming, offset, extent):
    inside = (jnp.arange(CAP) < extent)[:, None]
    chosen = jnp.where(inside, incoming, lax.dynamic_slice_in_dim(item, offset, CAP, 0))
    return lax.dynamic_update_slice_in_dim(item, chosen, offset, 0)


def reduce_by_owner(layer_input, *args):
    swap_start, swap_rows = args[-2:]
    tokens = layer_input.shape[0]
    values = front(*args)[:tokens]
    balanced = values
    for level in range(lax.axis_size("dp").bit_length() - 1):
        offset = swap_start[0, level]
        window = lax.dynamic_slice_in_dim(balanced, offset, CAP, 0)
        balanced = blend_rows(balanced, swapped(window, "dp", level), offset, swap_rows[0, level])
    owners = lax.axis_size("fsdp")
    owned = (D + owners - 1) // owners
    padded = jnp.pad(layer_input, ((0, 0), (0, owned * owners - D)))
    arranged = lax.all_to_all(
        padded.reshape(tokens, owners, owned), "fsdp", split_axis=1, concat_axis=0, tiled=True
    )
    block = lax.dot_general(
        arranged.reshape(-1, owned),
        lax.all_gather(values, "fsdp", axis=0, tiled=True),
        (((0,), (0,)), ((), ())),
        preferred_element_type=F32,
    )
    return lax.psum(block, "dp"), balanced


def on_device(layer_input, *args):
    if lax.axis_size("dp") == 4 and lax.axis_size("fsdp") == 8:
        return reduce_by_axis(layer_input, *args)
    return reduce_by_owner(layer_input, *args)


def solution(mesh):
    return jax.shard_map(
        on_device,
        mesh=mesh,
        in_specs=(
            P(("dp", "fsdp"), None),
            P(("dp", "fsdp"), None),
            P(("dp", "fsdp"), None),
            P(("dp", "fsdp"), None),
            P(("dp", "fsdp")),
            P(("dp", "fsdp")),
            P(),
            P(("dp", "fsdp")),
            P(("dp", "fsdp"), None),
            P(("dp", "fsdp"), None),
        ),
        out_specs=(P("fsdp", None), P(("dp", "fsdp"), None)),
        check_vma=False,
    )
```

```python
import functools
import math

import jax
import jax.numpy as jnp
from jax import lax
from jax.experimental import pallas as pl
from jax.experimental.pallas import tpu as pltpu
from jax.sharding import PartitionSpec as P

D = 4096
HD = 128
CAP = 32
HALF = 128
SEG = 16
LANE = 128
INFO = 16
MIB = 1 << 20
FREE = pl.CostEstimate(flops=0, bytes_accessed=0, transcendentals=0)
BF16 = jnp.bfloat16
F32 = jnp.float32

VMEM = pl.BlockSpec(memory_space=pltpu.VMEM)
HBM = pl.BlockSpec(memory_space=pltpu.HBM)


def attend_half(per_group, folded, span, q_ref, k_ref, g_ref, allowed, factor):
    heads = q_ref.shape[1] // HD
    groups = heads // per_group
    scores = [
        lax.dot_general(
            k_ref[span, pl.ds(group * HD, HD)],
            jnp.concatenate(
                [q_ref[span, pl.ds((group * per_group + n) * HD, HD)] for n in range(per_group)], axis=0
            ),
            (((1,), (1,)), ((), ())),
            preferred_element_type=F32,
        )
        for group in range(groups)
    ]
    weighted = [
        (g_ref[span, pl.ds(head * HD, HD)].astype(F32) * factor).astype(BF16) for head in range(heads)
    ]
    if folded:
        block = lax.broadcasted_iota(jnp.int32, (SEG, HALF), 1) // SEG
    probs = []
    for head in range(heads):
        n = head % per_group
        own = scores[head // per_group][:, n * HALF:(n + 1) * HALF]
        if folded:
            own = fold_blocks(own, block)
        own = jnp.where(allowed, own, -1e30)
        expo = jnp.exp2((own - jnp.max(own, axis=0, keepdims=True)) * (HD ** (-0.5) * math.log2(math.e)))
        prob = (expo * (1.0 / jnp.sum(expo, axis=0, keepdims=True))).astype(BF16)
        if folded:
            prob = jnp.concatenate(
                [jnp.where(block == b, prob, jnp.zeros_like(prob)) for b in range(HALF // SEG)], axis=0
            )
        probs.append(prob)
    return [
        jnp.dot(
            jnp.concatenate(probs[head:head + per_group], axis=1),
            jnp.concatenate(weighted[head:head + per_group], axis=0),
            preferred_element_type=F32,
        ).astype(BF16)
        for head in range(0, heads, per_group)
    ]


def fold_blocks(square, block):
    total = square[:SEG]
    for b in range(1, HALF // SEG):
        total = jnp.where(block == b, square[b * SEG:(b + 1) * SEG], total)
    return total


def mask_and_factor(folded, span, loss_ref, exponent_ref, ids_ref, index_ref):
    exponent = exponent_ref[0]
    unscale = jnp.float32(1.0)
    for bit in range(5):
        unscale = unscale * jnp.where((exponent >> bit) & 1 == 1, jnp.float32(2.0 ** -(1 << bit)), 1.0)
    row = lax.broadcasted_iota(jnp.int32, (HALF, HALF), 0)
    col = lax.broadcasted_iota(jnp.int32, (HALF, HALF), 1)
    doc_i = jnp.broadcast_to(ids_ref[:, span], (HALF, HALF))
    allowed = (doc_i == doc_i.T) & (row <= col)
    if folded:
        allowed = fold_blocks(
            jnp.where(allowed, 1, 0), lax.broadcasted_iota(jnp.int32, (SEG, HALF), 1) // SEG
        ) == 1
    index = index_ref[:, span]
    factor = jnp.zeros((1, HALF), F32)
    for entry in range(loss_ref.shape[0]):
        factor = jnp.where(index == entry, loss_ref[entry], factor)
    return allowed, jnp.broadcast_to(factor * unscale, (HALF, HALF)).T


def front_kernel(
    per_group, loss_hbm, exponent_hbm, start_hbm, rows_hbm, q_hbm, k_hbm, g_hbm, ids_hbm, index_hbm, *rest
):
    v_ref, loss_ref, exponent_ref, start_ref, rows_ref, q_ref, k_ref, g_ref, ids_ref, index_ref, sems = rest
    count = 0

    def begin(source, target):
        nonlocal count
        copy = pltpu.make_async_copy(source, target, sems.at[count])
        copy.start()
        count += 1
        return copy

    small = [
        begin(source, target)
        for source, target in (
            (ids_hbm, ids_ref), (index_hbm, index_ref), (loss_hbm, loss_ref), (exponent_hbm, exponent_ref),
            (start_hbm, start_ref), (rows_hbm, rows_ref),
        )
    ]
    groups = k_ref.shape[1] // HD
    wide = per_group * HD
    loads = []
    for half in range(2):
        span = pl.ds(half * HALF, HALF)
        loads.append([
            begin(source.at[span, :], target.at[span, :])
            for source, target in ((q_hbm, q_ref), (k_hbm, k_ref), (g_hbm, g_ref))
        ])
    for copy in small:
        copy.wait()
    masks = [
        mask_and_factor(half == 1, pl.ds(half * HALF, HALF), loss_ref, exponent_ref, ids_ref, index_ref)
        for half in range(2)
    ]
    info_row = lax.broadcasted_iota(jnp.int32, (INFO, k_ref.shape[1]), 0)
    info = jnp.zeros(info_row.shape, jnp.int32)
    for level in range(min(start_ref.shape[1], INFO // 2)):
        info = jnp.where(info_row == 2 * level, start_ref[0, level], info)
        info = jnp.where(info_row == 2 * level + 1, rows_ref[0, level], info)
    v_ref[pl.ds(2 * HALF, INFO), :] = info.astype(F32).astype(BF16)
    for half in range(2):
        for copy in loads[half]:
            copy.wait()
        span = pl.ds(half * HALF, HALF)
        values = attend_half(per_group, half == 1, span, q_ref, k_ref, g_ref, *masks[half])
        for group, value in enumerate(values):
            v_ref[span, pl.ds(group * HD, HD)] = value


def front(query, key, grad, ids, index, loss, exponent, start, rows):
    tokens, key_width = key.shape
    per_group = query.shape[1] // key_width
    args = [
        loss, exponent, start, rows, query, key, grad, ids.reshape(1, tokens), index.reshape(1, tokens)
    ]
    return pl.pallas_call(
        functools.partial(front_kernel, per_group),
        in_specs=[HBM] * 9,
        out_specs=VMEM,
        out_shape=jax.ShapeDtypeStruct((tokens + INFO, key_width), BF16),
        scratch_shapes=[
            pltpu.SMEM(loss.shape, F32), pltpu.SMEM(exponent.shape, jnp.int32),
            pltpu.SMEM(start.shape, jnp.int32), pltpu.SMEM(rows.shape, jnp.int32),
            pltpu.VMEM(query.shape, BF16), pltpu.VMEM(key.shape, BF16), pltpu.VMEM(grad.shape, BF16),
            pltpu.VMEM((1, tokens), jnp.int32), pltpu.VMEM((1, tokens), jnp.int32),
            pltpu.SemaphoreType.DMA((12,)),
        ],
        compiler_params=pltpu.CompilerParams(vmem_limit_bytes=24 * MIB),
        cost_estimate=FREE,
        name="front",
    )(*[arg if arg is exponent else pltpu.with_memory_space_constraint(arg, pltpu.HBM) for arg in args])


CORE, Y, X, Z1, Z2 = 8, 16, 1, 2, 4


def xor_permute(value, mask):
    count = lax.axis_size("dp") * lax.axis_size("fsdp")
    return lax.ppermute(value, ("dp", "fsdp"), [(i, i ^ mask) for i in range(count)])


def partial_kernel(parts, own_ref, near_ref, v0_ref, v1_ref, *out_refs):
    dp = lax.axis_index("dp")
    fsdp = lax.axis_index("fsdp")
    loaded = {}

    def block(z, y, x):
        if (z, y, x) not in loaded:
            owner = fsdp ^ (z << 1 | x)
            column = pl.multiple_of(owner * (4 * LANE) + (dp ^ (y << 1)) * LANE, LANE)
            loaded[z, y, x] = jnp.concatenate([ref[:, pl.ds(column, LANE)] for ref in (own_ref, near_ref)], axis=0)
        return loaded[z, y, x]

    for (blocks, start, width), out_ref in zip(parts, out_refs):
        v = jnp.concatenate([ref[pl.ds(0, 2 * HALF), pl.ds(start, width)] for ref in (v0_ref, v1_ref)], axis=0)
        total = lax.dot_general(
            jnp.concatenate([block(*place) for place in blocks], axis=1), v, (((0,), (0,)), ((), ())),
            preferred_element_type=F32,
        )
        out_ref[...] = total.astype(out_ref.dtype)


def partial_sums(parts, dtype, own, near, v0, v1):
    return pl.pallas_call(
        functools.partial(partial_kernel, parts),
        in_specs=[VMEM] * 4,
        out_specs=[VMEM] * len(parts),
        out_shape=[jax.ShapeDtypeStruct((len(blocks) * LANE, width), dtype) for blocks, _, width in parts],
        compiler_params=pltpu.CompilerParams(vmem_limit_bytes=24 * MIB),
        cost_estimate=FREE,
        name="partial_sums",
    )(own, near, v0, v1)


def inner_swap_kernel(v0_ref, v1_ref, out_ref, window_ref):
    tokens = out_ref.shape[0]
    infos = [ref[pl.ds(tokens, INFO), pl.ds(0, HALF)].astype(F32).astype(jnp.int32) for ref in (v0_ref, v1_ref)]

    def table(device, entry):
        return jnp.broadcast_to(infos[device][entry:entry + 1, :], (HALF, HALF))

    place = lax.broadcasted_iota(jnp.int32, (HALF, HALF), 0) + HALF
    inner = lax.broadcasted_iota(jnp.int32, (HALF, HALF), 1) + HALF
    first = table(0, 0)
    moved = (place >= first) & (place < first + table(0, 1))
    stays = jnp.where(~moved & (place == inner), 1.0, 0.0).astype(BF16)
    comes = jnp.where(moved & (place + table(1, 0) - first == inner), 1.0, 0.0).astype(BF16)
    taken = jnp.where(place - HALF + table(0, 2) == inner, 1.0, 0.0).astype(BF16)[:CAP]
    rows = (
        jnp.dot(stays, v0_ref[pl.ds(HALF, HALF), :], preferred_element_type=F32)
        + jnp.dot(comes, v1_ref[pl.ds(HALF, HALF), :], preferred_element_type=F32)
    ).astype(BF16)
    out_ref[pl.ds(0, HALF), :] = v0_ref[pl.ds(0, HALF), :]
    out_ref[pl.ds(HALF, HALF), :] = rows
    window_ref[...] = jnp.dot(taken, rows, preferred_element_type=F32).astype(BF16)


def inner_swap(v0, v1):
    return pl.pallas_call(
        inner_swap_kernel,
        in_specs=[VMEM] * 2,
        out_specs=[VMEM] * 2,
        out_shape=[jax.ShapeDtypeStruct((2 * HALF, 512), BF16), jax.ShapeDtypeStruct((CAP, 512), BF16)],
        compiler_params=pltpu.CompilerParams(vmem_limit_bytes=8 * MIB),
        cost_estimate=FREE,
        name="inner_swap",
    )(v0, v1)


def outer_swap_kernel(v0_ref, rows_ref, window_ref, out_ref):
    tokens = out_ref.shape[0]
    info = v0_ref[pl.ds(tokens, INFO), pl.ds(0, HALF)].astype(F32).astype(jnp.int32)
    first = jnp.broadcast_to(info[2:3, :], (HALF, HALF))
    extent = jnp.broadcast_to(info[3:4, :], (HALF, HALF))
    place = lax.broadcasted_iota(jnp.int32, (HALF, HALF), 0) + HALF
    inner = lax.broadcasted_iota(jnp.int32, (HALF, HALF), 1)
    moved = (place >= first) & (place < first + extent)
    stays = jnp.where(~moved & (place == inner + HALF), 1.0, 0.0).astype(BF16)
    comes = jnp.where(moved & (place - first == inner), 1.0, 0.0).astype(BF16)[:, :CAP]
    out_ref[pl.ds(0, HALF), :] = rows_ref[pl.ds(0, HALF), :]
    out_ref[pl.ds(HALF, HALF), :] = (
        jnp.dot(stays, rows_ref[pl.ds(HALF, HALF), :], preferred_element_type=F32)
        + jnp.dot(comes, window_ref[...], preferred_element_type=F32)
    ).astype(BF16)


def outer_swap(v0, rows, window):
    return pl.pallas_call(
        outer_swap_kernel,
        in_specs=[VMEM] * 3,
        out_specs=VMEM,
        out_shape=jax.ShapeDtypeStruct(rows.shape, BF16),
        compiler_params=pltpu.CompilerParams(vmem_limit_bytes=8 * MIB),
        cost_estimate=FREE,
        name="outer_swap",
    )(v0, rows, window)


def place_kernel(mine_ref, y_ref, near_ref, out_ref):
    dp = lax.axis_index("dp")
    for flip, block in ((0, mine_ref), (2, y_ref), (1, near_ref.at[0]), (3, near_ref.at[1])):
        out_ref[pl.ds(pl.multiple_of((dp ^ flip) * LANE, LANE), LANE), :] = block[...].astype(F32)


def place(mine, from_y, near):
    return pl.pallas_call(
        place_kernel,
        in_specs=[VMEM] * 3,
        out_specs=VMEM,
        out_shape=jax.ShapeDtypeStruct((512, 512), F32),
        compiler_params=pltpu.CompilerParams(vmem_limit_bytes=8 * MIB),
        cost_estimate=FREE,
        name="place",
    )(mine, from_y, near)


def fold_kernel(base_ref, arrived_ref, out_ref):
    out_ref[...] = base_ref[...] + arrived_ref[...].astype(F32)


def fold(base, arrived):
    return pl.pallas_call(
        fold_kernel,
        in_specs=[VMEM] * 2,
        out_specs=VMEM,
        out_shape=jax.ShapeDtypeStruct(base.shape, F32),
        compiler_params=pltpu.CompilerParams(vmem_limit_bytes=8 * MIB),
        cost_estimate=pl.CostEstimate(flops=6_000_000_000, bytes_accessed=0, transcendentals=0),
        name="fold",
    )(base, arrived)


def reduce_by_axis(layer_input, *args):
    near = xor_permute(layer_input, CORE)
    v0 = front(*args)
    v1 = xor_permute(v0, CORE)

    def sums(parts, dtype):
        return partial_sums(parts, dtype, layer_input, near, v0, v1)

    def after_all(*values):
        return lax.optimization_barrier(values)

    def add(*terms):
        total = terms[0]
        for term in terms[1:]:
            total = total + term.astype(F32)
        return total

    first_b, first_a = sums([(((3, 1, 1), (3, 0, 1)), 0, 512), (((2, 1, 1), (2, 1, 0)), 0, 512)], BF16)
    every = ((1, 1), (1, 0), (0, 1), (0, 0))
    pair_some, pair_rest = sums([(tuple((1, *at) for at in every), start, 256) for start in (0, 256)], BF16)
    keep_b, keep_a = sums([(((3, 1, 0), (3, 0, 0)), 0, 512), (((2, 0, 1), (2, 0, 0)), 0, 512)], F32)
    own_some, own_rest = sums([(tuple((0, *at) for at in every), start, 256) for start in (0, 256)], F32)
    first_b = xor_permute(first_b, X)
    first_a = xor_permute(first_a, Y)
    pair_sent = pair_rest
    pair_some = xor_permute(pair_some, Z1)
    pair_rest = xor_permute(pair_rest, Z1)
    on_b = add(keep_b[:LANE], first_b[:LANE]).astype(BF16)
    rows, window = inner_swap(after_all(v0, pair_sent)[0], v1)
    window = xor_permute(after_all(window, on_b)[0], Y)
    on_b = xor_permute(on_b, Y)
    on_a = xor_permute(add(keep_a[:LANE], first_a[:LANE]).astype(BF16), X)
    z3 = add(keep_b[LANE:], first_b[LANE:], on_b).astype(BF16)
    pair_some, window = after_all(pair_some, window, z3)[:2]
    z3 = xor_permute(z3, Z1)
    z2 = add(keep_a[LANE:], first_a[LANE:], on_a, z3).astype(BF16)

    some = add(own_some, pair_some)
    some_in = xor_permute(some[:2 * LANE].astype(BF16), Y)
    rest = add(own_rest, after_all(pair_rest, some)[0])
    rest_far, rest_y, rest_x, rest_own = (rest[row:row + LANE] for row in range(0, 4 * LANE, LANE))
    rest_in = xor_permute(jnp.concatenate([rest_far, rest_x]).astype(BF16), X)
    some_in = after_all(some_in, z2)[0]
    z2 = xor_permute(z2, Z2)
    some_on = add(some[2 * LANE:3 * LANE], some_in[:LANE]).astype(BF16)
    rest_in = after_all(rest_in, some_on)[0]
    some_on = xor_permute(some_on, X)
    rest_on = xor_permute(add(rest_y, rest_in[:LANE]).astype(BF16), Y)
    base = jnp.concatenate([add(some[3 * LANE:], some_in[LANE:]), add(rest_own, rest_in[LANE:])], axis=1)
    mine = add(fold(base, z2), jnp.concatenate([some_on, rest_on], axis=1)).astype(BF16)
    from_y = xor_permute(mine, Y)
    value_grad = outer_swap(v0, rows, after_all(window, from_y)[0])
    return place(mine, from_y, xor_permute(jnp.stack([mine, from_y]), CORE)), value_grad


def swapped(block, axis, distance):
    count = lax.axis_size(axis)
    route = []
    for low in range(count):
        high = low | 1 << distance
        if high != low and high < count:
            route += [(low, high), (high, low)]
    return lax.ppermute(block, axis, route)


def blend_rows(item, incoming, offset, extent):
    inside = (jnp.arange(CAP) < extent)[:, None]
    chosen = jnp.where(inside, incoming, lax.dynamic_slice_in_dim(item, offset, CAP, 0))
    return lax.dynamic_update_slice_in_dim(item, chosen, offset, 0)


def reduce_by_owner(layer_input, *args):
    swap_start, swap_rows = args[-2:]
    tokens = layer_input.shape[0]
    values = front(*args)[:tokens]
    balanced = values
    for level in range(lax.axis_size("dp").bit_length() - 1):
        offset = swap_start[0, level]
        window = lax.dynamic_slice_in_dim(balanced, offset, CAP, 0)
        balanced = blend_rows(balanced, swapped(window, "dp", level), offset, swap_rows[0, level])
    owners = lax.axis_size("fsdp")
    owned = (D + owners - 1) // owners
    padded = jnp.pad(layer_input, ((0, 0), (0, owned * owners - D)))
    arranged = lax.all_to_all(
        padded.reshape(tokens, owners, owned), "fsdp", split_axis=1, concat_axis=0, tiled=True
    )
    block = lax.dot_general(
        arranged.reshape(-1, owned),
        lax.all_gather(values, "fsdp", axis=0, tiled=True),
        (((0,), (0,)), ((), ())),
        preferred_element_type=F32,
    )
    return lax.psum(block, "dp"), balanced


def on_device(layer_input, *args):
    if lax.axis_size("dp") == 4 and lax.axis_size("fsdp") == 8:
        return reduce_by_axis(layer_input, *args)
    return reduce_by_owner(layer_input, *args)


def solution(mesh):
    return jax.shard_map(
        on_device,
        mesh=mesh,
        in_specs=(
            P(("dp", "fsdp"), None),
            P(("dp", "fsdp"), None),
            P(("dp", "fsdp"), None),
            P(("dp", "fsdp"), None),
            P(("dp", "fsdp")),
            P(("dp", "fsdp")),
            P(),
            P(("dp", "fsdp")),
            P(("dp", "fsdp"), None),
            P(("dp", "fsdp"), None),
        ),
        out_specs=(P("fsdp", None), P(("dp", "fsdp"), None)),
        check_vma=False,
    )
```

```python
import functools
import math

import jax
import jax.numpy as jnp
from jax import lax
from jax.experimental import pallas as pl
from jax.experimental.pallas import tpu as pltpu
from jax.sharding import PartitionSpec as P

D = 4096
HD = 128
CAP = 32
HALF = 128
SEG = 16
LANE = 128
INFO = 16
MIB = 1 << 20
FREE = pl.CostEstimate(flops=0, bytes_accessed=0, transcendentals=0)
BF16 = jnp.bfloat16
F32 = jnp.float32

VMEM = pl.BlockSpec(memory_space=pltpu.VMEM)
HBM = pl.BlockSpec(memory_space=pltpu.HBM)


def attend_half(per_group, folded, span, q_ref, k_ref, g_ref, allowed, factor):
    heads = q_ref.shape[1] // HD
    groups = heads // per_group
    scores = [
        lax.dot_general(
            k_ref[span, pl.ds(group * HD, HD)],
            jnp.concatenate(
                [q_ref[span, pl.ds((group * per_group + n) * HD, HD)] for n in range(per_group)], axis=0
            ),
            (((1,), (1,)), ((), ())),
            preferred_element_type=F32,
        )
        for group in range(groups)
    ]
    weighted = [
        (g_ref[span, pl.ds(head * HD, HD)].astype(F32) * factor).astype(BF16) for head in range(heads)
    ]
    if folded:
        block = lax.broadcasted_iota(jnp.int32, (SEG, HALF), 1) // SEG
    probs = []
    for head in range(heads):
        n = head % per_group
        own = scores[head // per_group][:, n * HALF:(n + 1) * HALF]
        if folded:
            own = fold_blocks(own, block)
        own = jnp.where(allowed, own, -1e30)
        expo = jnp.exp2((own - jnp.max(own, axis=0, keepdims=True)) * (HD ** (-0.5) * math.log2(math.e)))
        prob = (expo * (1.0 / jnp.sum(expo, axis=0, keepdims=True))).astype(BF16)
        if folded:
            prob = jnp.concatenate(
                [jnp.where(block == b, prob, jnp.zeros_like(prob)) for b in range(HALF // SEG)], axis=0
            )
        probs.append(prob)
    return [
        jnp.dot(
            jnp.concatenate(probs[head:head + per_group], axis=1),
            jnp.concatenate(weighted[head:head + per_group], axis=0),
            preferred_element_type=F32,
        ).astype(BF16)
        for head in range(0, heads, per_group)
    ]


def fold_blocks(square, block):
    total = square[:SEG]
    for b in range(1, HALF // SEG):
        total = jnp.where(block == b, square[b * SEG:(b + 1) * SEG], total)
    return total


def mask_and_factor(folded, span, loss_ref, exponent_ref, ids_ref, index_ref):
    exponent = exponent_ref[0]
    unscale = jnp.float32(1.0)
    for bit in range(5):
        unscale = unscale * jnp.where((exponent >> bit) & 1 == 1, jnp.float32(2.0 ** -(1 << bit)), 1.0)
    row = lax.broadcasted_iota(jnp.int32, (HALF, HALF), 0)
    col = lax.broadcasted_iota(jnp.int32, (HALF, HALF), 1)
    doc_i = jnp.broadcast_to(ids_ref[:, span], (HALF, HALF))
    allowed = (doc_i == doc_i.T) & (row <= col)
    if folded:
        allowed = fold_blocks(
            jnp.where(allowed, 1, 0), lax.broadcasted_iota(jnp.int32, (SEG, HALF), 1) // SEG
        ) == 1
    index = index_ref[:, span]
    factor = jnp.zeros((1, HALF), F32)
    for entry in range(loss_ref.shape[0]):
        factor = jnp.where(index == entry, loss_ref[entry], factor)
    return allowed, jnp.broadcast_to(factor * unscale, (HALF, HALF)).T


def front_kernel(
    per_group, loss_hbm, exponent_hbm, start_hbm, rows_hbm, q_hbm, k_hbm, g_hbm, ids_hbm, index_hbm, *rest
):
    v_ref, loss_ref, exponent_ref, start_ref, rows_ref, q_ref, k_ref, g_ref, ids_ref, index_ref, sems = rest
    count = 0

    def begin(source, target):
        nonlocal count
        copy = pltpu.make_async_copy(source, target, sems.at[count])
        copy.start()
        count += 1
        return copy

    small = [
        begin(source, target)
        for source, target in (
            (ids_hbm, ids_ref), (index_hbm, index_ref), (loss_hbm, loss_ref), (exponent_hbm, exponent_ref),
            (start_hbm, start_ref), (rows_hbm, rows_ref),
        )
    ]
    groups = k_ref.shape[1] // HD
    wide = per_group * HD
    loads = []
    for half in range(2):
        span = pl.ds(half * HALF, HALF)
        loads.append([
            begin(source.at[span, :], target.at[span, :])
            for source, target in ((q_hbm, q_ref), (k_hbm, k_ref), (g_hbm, g_ref))
        ])
    for copy in small:
        copy.wait()
    masks = [
        mask_and_factor(half == 1, pl.ds(half * HALF, HALF), loss_ref, exponent_ref, ids_ref, index_ref)
        for half in range(2)
    ]
    info_row = lax.broadcasted_iota(jnp.int32, (INFO, k_ref.shape[1]), 0)
    info = jnp.zeros(info_row.shape, jnp.int32)
    for level in range(min(start_ref.shape[1], INFO // 2)):
        info = jnp.where(info_row == 2 * level, start_ref[0, level], info)
        info = jnp.where(info_row == 2 * level + 1, rows_ref[0, level], info)
    v_ref[pl.ds(2 * HALF, INFO), :] = info.astype(F32).astype(BF16)
    for half in range(2):
        for copy in loads[half]:
            copy.wait()
        span = pl.ds(half * HALF, HALF)
        values = attend_half(per_group, half == 1, span, q_ref, k_ref, g_ref, *masks[half])
        for group, value in enumerate(values):
            v_ref[span, pl.ds(group * HD, HD)] = value


def front(query, key, grad, ids, index, loss, exponent, start, rows):
    tokens, key_width = key.shape
    per_group = query.shape[1] // key_width
    args = [
        loss, exponent, start, rows, query, key, grad, ids.reshape(1, tokens), index.reshape(1, tokens)
    ]
    return pl.pallas_call(
        functools.partial(front_kernel, per_group),
        in_specs=[HBM] * 9,
        out_specs=VMEM,
        out_shape=jax.ShapeDtypeStruct((tokens + INFO, key_width), BF16),
        scratch_shapes=[
            pltpu.SMEM(loss.shape, F32), pltpu.SMEM(exponent.shape, jnp.int32),
            pltpu.SMEM(start.shape, jnp.int32), pltpu.SMEM(rows.shape, jnp.int32),
            pltpu.VMEM(query.shape, BF16), pltpu.VMEM(key.shape, BF16), pltpu.VMEM(grad.shape, BF16),
            pltpu.VMEM((1, tokens), jnp.int32), pltpu.VMEM((1, tokens), jnp.int32),
            pltpu.SemaphoreType.DMA((12,)),
        ],
        compiler_params=pltpu.CompilerParams(vmem_limit_bytes=24 * MIB),
        cost_estimate=FREE,
        name="front",
    )(*[arg if arg is exponent else pltpu.with_memory_space_constraint(arg, pltpu.HBM) for arg in args])


CORE, Y, X, Z1, Z2 = 8, 16, 1, 2, 4


def routed(value, odd, even):
    owners = lax.axis_size("fsdp")
    count = lax.axis_size("dp") * owners
    return lax.ppermute(
        value, ("dp", "fsdp"), [(i, i ^ (odd if i // owners % 2 else even)) for i in range(count)]
    )


def xor_permute(value, mask):
    return routed(value, mask, mask)


def partial_kernel(parts, own_ref, near_ref, v0_ref, v1_ref, *out_refs):
    dp = lax.axis_index("dp")
    fsdp = lax.axis_index("fsdp")
    odd = dp & 1

    def pick(choices):
        return choices[0] + odd * (choices[1] - choices[0])

    for units, out_ref in zip(parts, out_refs):
        for number, (odd_unit, even_unit) in enumerate(units):
            z, y, x, part = (pick(pair) for pair in zip(even_unit, odd_unit))
            owner = fsdp ^ (z * 2 + x)
            quarter = (dp - odd) ^ (y * 2)
            column = pl.ds(pl.multiple_of(owner * (4 * LANE) + quarter * LANE, 2 * LANE), 2 * LANE)
            some = pl.ds(pl.multiple_of(part * (2 * LANE), 2 * LANE), 2 * LANE)
            total = lax.dot_general(
                jnp.concatenate([own_ref[:, column], near_ref[:, column]], axis=0),
                jnp.concatenate([ref[pl.ds(0, 2 * HALF), some] for ref in (v0_ref, v1_ref)], axis=0),
                (((0,), (0,)), ((), ())),
                preferred_element_type=F32,
            )
            out_ref[pl.ds(number * (2 * LANE), 2 * LANE), :] = total.astype(out_ref.dtype)


def partial_sums(parts, dtype, own, near, v0, v1):
    return pl.pallas_call(
        functools.partial(partial_kernel, parts),
        in_specs=[VMEM] * 4,
        out_specs=[VMEM] * len(parts),
        out_shape=[jax.ShapeDtypeStruct((2 * HALF * len(units), 2 * HALF), dtype) for units in parts],
        compiler_params=pltpu.CompilerParams(vmem_limit_bytes=24 * MIB),
        cost_estimate=FREE,
        name="partial_sums",
    )(own, near, v0, v1)


def inner_swap_kernel(v0_ref, v1_ref, out_ref, window_ref):
    tokens = out_ref.shape[0]
    infos = [ref[pl.ds(tokens, INFO), pl.ds(0, HALF)].astype(F32).astype(jnp.int32) for ref in (v0_ref, v1_ref)]

    def table(device, entry):
        return jnp.broadcast_to(infos[device][entry:entry + 1, :], (HALF, HALF))

    place = lax.broadcasted_iota(jnp.int32, (HALF, HALF), 0) + HALF
    inner = lax.broadcasted_iota(jnp.int32, (HALF, HALF), 1) + HALF
    first = table(0, 0)
    moved = (place >= first) & (place < first + table(0, 1))
    stays = jnp.where(~moved & (place == inner), 1.0, 0.0).astype(BF16)
    comes = jnp.where(moved & (place + table(1, 0) - first == inner), 1.0, 0.0).astype(BF16)
    taken = jnp.where(place - HALF + table(0, 2) == inner, 1.0, 0.0).astype(BF16)[:CAP]
    rows = (
        jnp.dot(stays, v0_ref[pl.ds(HALF, HALF), :], preferred_element_type=F32)
        + jnp.dot(comes, v1_ref[pl.ds(HALF, HALF), :], preferred_element_type=F32)
    ).astype(BF16)
    out_ref[pl.ds(0, HALF), :] = v0_ref[pl.ds(0, HALF), :]
    out_ref[pl.ds(HALF, HALF), :] = rows
    window_ref[...] = jnp.dot(taken, rows, preferred_element_type=F32).astype(BF16)


def inner_swap(v0, v1):
    return pl.pallas_call(
        inner_swap_kernel,
        in_specs=[VMEM] * 2,
        out_specs=[VMEM] * 2,
        out_shape=[jax.ShapeDtypeStruct((2 * HALF, 512), BF16), jax.ShapeDtypeStruct((CAP, 512), BF16)],
        compiler_params=pltpu.CompilerParams(vmem_limit_bytes=8 * MIB),
        cost_estimate=FREE,
        name="inner_swap",
    )(v0, v1)


def outer_swap_kernel(v0_ref, rows_ref, window_ref, out_ref):
    tokens = out_ref.shape[0]
    info = v0_ref[pl.ds(tokens, INFO), pl.ds(0, HALF)].astype(F32).astype(jnp.int32)
    first = jnp.broadcast_to(info[2:3, :], (HALF, HALF))
    extent = jnp.broadcast_to(info[3:4, :], (HALF, HALF))
    place = lax.broadcasted_iota(jnp.int32, (HALF, HALF), 0) + HALF
    inner = lax.broadcasted_iota(jnp.int32, (HALF, HALF), 1)
    moved = (place >= first) & (place < first + extent)
    stays = jnp.where(~moved & (place == inner + HALF), 1.0, 0.0).astype(BF16)
    comes = jnp.where(moved & (place - first == inner), 1.0, 0.0).astype(BF16)[:, :CAP]
    out_ref[pl.ds(0, HALF), :] = rows_ref[pl.ds(0, HALF), :]
    out_ref[pl.ds(HALF, HALF), :] = (
        jnp.dot(stays, rows_ref[pl.ds(HALF, HALF), :], preferred_element_type=F32)
        + jnp.dot(comes, window_ref[...], preferred_element_type=F32)
    ).astype(BF16)


def outer_swap(v0, rows, window):
    return pl.pallas_call(
        outer_swap_kernel,
        in_specs=[VMEM] * 3,
        out_specs=VMEM,
        out_shape=jax.ShapeDtypeStruct(rows.shape, BF16),
        compiler_params=pltpu.CompilerParams(vmem_limit_bytes=8 * MIB),
        cost_estimate=FREE,
        name="outer_swap",
    )(v0, rows, window)


def place_kernel(pair_ref, near_ref, out_ref):
    dp = lax.axis_index("dp")
    for ref, part in ((pair_ref, dp & 1), (near_ref, 1 - (dp & 1))):
        some = pl.ds(pl.multiple_of(part * (2 * LANE), 2 * LANE), 2 * LANE)
        for flip in range(2):
            rows = pl.ds(pl.multiple_of(((dp >> 1) ^ flip) * (2 * LANE), 2 * LANE), 2 * LANE)
            out_ref[rows, some] = ref[flip].astype(F32)


def place(pair, near):
    return pl.pallas_call(
        place_kernel,
        in_specs=[VMEM] * 2,
        out_specs=VMEM,
        out_shape=jax.ShapeDtypeStruct((512, 512), F32),
        compiler_params=pltpu.CompilerParams(vmem_limit_bytes=8 * MIB),
        cost_estimate=FREE,
        name="place",
    )(pair, near)


def reduce_by_axis(layer_input, *args):
    near = xor_permute(layer_input, CORE)
    v0 = front(*args)
    v1 = xor_permute(v0, CORE)
    odd = (lax.axis_index("dp") & 1) == 1
    both = 2 * LANE

    def sums(parts, dtype):
        return partial_sums(parts, dtype, layer_input, near, v0, v1)

    def after_all(*values):
        return lax.optimization_barrier(values)

    def add(*terms):
        total = terms[0]
        for term in terms[1:]:
            total = total + term.astype(F32)
        return total

    def chain(z, y, x):
        return ((z, y, x, 0), (z, y, x, 1))

    def own(z, y, part):
        return ((z, y, 1, part), (z, y, 0, part))

    def parts(*pairs):
        return [tuple(zip(*pair)) for pair in pairs]

    first, second = sums(parts((chain(3, 1, 1), own(1, 1, 0)), (chain(2, 1, 1), own(1, 0, 0))), BF16)
    third, fourth = sums(parts((chain(3, 0, 1), own(1, 1, 1)), (chain(2, 1, 0), own(1, 0, 1))), BF16)
    keep1, keep2 = sums(parts((chain(3, 1, 0), own(0, 1, 0)), (chain(2, 0, 1), own(0, 0, 0))), F32)
    keep3, keep4 = sums(parts((chain(3, 0, 0), own(0, 1, 1)), (chain(2, 0, 0), own(0, 0, 1))), F32)
    side = fourth
    first = routed(first, X, Z1)
    second = routed(second, Y, Z1)
    third = routed(third, X, Z1)
    total1 = add(keep1, first)
    fourth = routed(jnp.where(odd, total1.astype(BF16), fourth), Y, Z1)
    total2 = add(keep2, second)
    fifth = jnp.where(odd, total2, total1).astype(BF16)
    rows, window = inner_swap(after_all(v0, third)[0], v1)
    side = after_all(side, fifth)[0]
    fifth = routed(fifth, X, Y)
    side = routed(side, Y, 0)
    total3 = add(keep3, third)
    sixth = jnp.where(odd, add(total3, fourth), total3).astype(BF16)
    window = xor_permute(after_all(window, sixth)[0], Y)
    sixth = routed(sixth, Z1, Y)
    some = add(total2, fifth)
    rest = add(keep4, jnp.where(odd, side, fourth), sixth)
    last = jnp.where(odd, add(rest, fifth), jnp.concatenate([some[:both], rest[:both]])).astype(BF16)
    last, window = after_all(last, window)
    last = routed(last, Z2, X)
    base = jnp.concatenate([add(some[both:], last[:both]), add(rest[both:], last[both:])])
    mine = jnp.where(odd, last.astype(F32), base)
    crossed = xor_permute(jnp.where(odd, last[:both], base[both:].astype(BF16)), CORE)
    mine = add(jnp.where(odd, mine[both:], mine[:both]), crossed).astype(BF16)
    from_y = xor_permute(mine, Y)
    value_grad = outer_swap(v0, rows, after_all(window, from_y)[0])
    pair = jnp.stack([mine, from_y])
    return place(pair, xor_permute(pair, CORE)), value_grad


def swapped(block, axis, distance):
    count = lax.axis_size(axis)
    route = []
    for low in range(count):
        high = low | 1 << distance
        if high != low and high < count:
            route += [(low, high), (high, low)]
    return lax.ppermute(block, axis, route)


def blend_rows(item, incoming, offset, extent):
    inside = (jnp.arange(CAP) < extent)[:, None]
    chosen = jnp.where(inside, incoming, lax.dynamic_slice_in_dim(item, offset, CAP, 0))
    return lax.dynamic_update_slice_in_dim(item, chosen, offset, 0)


def reduce_by_owner(layer_input, *args):
    swap_start, swap_rows = args[-2:]
    tokens = layer_input.shape[0]
    values = front(*args)[:tokens]
    balanced = values
    for level in range(lax.axis_size("dp").bit_length() - 1):
        offset = swap_start[0, level]
        window = lax.dynamic_slice_in_dim(balanced, offset, CAP, 0)
        balanced = blend_rows(balanced, swapped(window, "dp", level), offset, swap_rows[0, level])
    owners = lax.axis_size("fsdp")
    owned = (D + owners - 1) // owners
    padded = jnp.pad(layer_input, ((0, 0), (0, owned * owners - D)))
    arranged = lax.all_to_all(
        padded.reshape(tokens, owners, owned), "fsdp", split_axis=1, concat_axis=0, tiled=True
    )
    block = lax.dot_general(
        arranged.reshape(-1, owned),
        lax.all_gather(values, "fsdp", axis=0, tiled=True),
        (((0,), (0,)), ((), ())),
        preferred_element_type=F32,
    )
    return lax.psum(block, "dp"), balanced


def on_device(layer_input, *args):
    if lax.axis_size("dp") == 4 and lax.axis_size("fsdp") == 8:
        return reduce_by_axis(layer_input, *args)
    return reduce_by_owner(layer_input, *args)


def solution(mesh):
    return jax.shard_map(
        on_device,
        mesh=mesh,
        in_specs=(
            P(("dp", "fsdp"), None),
            P(("dp", "fsdp"), None),
            P(("dp", "fsdp"), None),
            P(("dp", "fsdp"), None),
            P(("dp", "fsdp")),
            P(("dp", "fsdp")),
            P(),
            P(("dp", "fsdp")),
            P(("dp", "fsdp"), None),
            P(("dp", "fsdp"), None),
        ),
        out_specs=(P("fsdp", None), P(("dp", "fsdp"), None)),
        check_vma=False,
    )
```

```python
import functools
import math

import jax
import jax.numpy as jnp
from jax import lax
from jax.experimental import pallas as pl
from jax.experimental.pallas import tpu as pltpu
from jax.sharding import PartitionSpec as P

D = 4096
HD = 128
CAP = 32
HALF = 128
SEG = 16
LANE = 128
INFO = 16
MIB = 1 << 20
FREE = pl.CostEstimate(flops=0, bytes_accessed=0, transcendentals=0)
BF16 = jnp.bfloat16
F32 = jnp.float32

VMEM = pl.BlockSpec(memory_space=pltpu.VMEM)
HBM = pl.BlockSpec(memory_space=pltpu.HBM)


def attend_half(per_group, folded, span, q_ref, k_ref, g_ref, allowed, factor):
    heads = q_ref.shape[1] // HD
    groups = heads // per_group
    scores = [
        lax.dot_general(
            k_ref[span, pl.ds(group * HD, HD)],
            jnp.concatenate(
                [q_ref[span, pl.ds((group * per_group + n) * HD, HD)] for n in range(per_group)], axis=0
            ),
            (((1,), (1,)), ((), ())),
            preferred_element_type=F32,
        )
        for group in range(groups)
    ]
    weighted = [
        (g_ref[span, pl.ds(head * HD, HD)].astype(F32) * factor).astype(BF16) for head in range(heads)
    ]
    if folded:
        block = lax.broadcasted_iota(jnp.int32, (SEG, HALF), 1) // SEG
    probs = []
    for head in range(heads):
        n = head % per_group
        own = scores[head // per_group][:, n * HALF:(n + 1) * HALF]
        if folded:
            own = fold_blocks(own, block)
        own = jnp.where(allowed, own, -1e30)
        expo = jnp.exp2((own - jnp.max(own, axis=0, keepdims=True)) * (HD ** (-0.5) * math.log2(math.e)))
        prob = (expo * (1.0 / jnp.sum(expo, axis=0, keepdims=True))).astype(BF16)
        if folded:
            prob = jnp.concatenate(
                [jnp.where(block == b, prob, jnp.zeros_like(prob)) for b in range(HALF // SEG)], axis=0
            )
        probs.append(prob)
    return [
        jnp.dot(
            jnp.concatenate(probs[head:head + per_group], axis=1),
            jnp.concatenate(weighted[head:head + per_group], axis=0),
            preferred_element_type=F32,
        ).astype(BF16)
        for head in range(0, heads, per_group)
    ]


def fold_blocks(square, block):
    total = square[:SEG]
    for b in range(1, HALF // SEG):
        total = jnp.where(block == b, square[b * SEG:(b + 1) * SEG], total)
    return total


def mask_and_factor(folded, span, loss_ref, exponent_ref, ids_ref, index_ref):
    exponent = exponent_ref[0]
    unscale = jnp.float32(1.0)
    for bit in range(5):
        unscale = unscale * jnp.where((exponent >> bit) & 1 == 1, jnp.float32(2.0 ** -(1 << bit)), 1.0)
    row = lax.broadcasted_iota(jnp.int32, (HALF, HALF), 0)
    col = lax.broadcasted_iota(jnp.int32, (HALF, HALF), 1)
    doc_i = jnp.broadcast_to(ids_ref[:, span], (HALF, HALF))
    allowed = (doc_i == doc_i.T) & (row <= col)
    if folded:
        allowed = fold_blocks(
            jnp.where(allowed, 1, 0), lax.broadcasted_iota(jnp.int32, (SEG, HALF), 1) // SEG
        ) == 1
    index = index_ref[:, span]
    factor = jnp.zeros((1, HALF), F32)
    for entry in range(loss_ref.shape[0]):
        factor = jnp.where(index == entry, loss_ref[entry], factor)
    return allowed, jnp.broadcast_to(factor * unscale, (HALF, HALF)).T


def front_kernel(
    per_group, loss_hbm, exponent_hbm, start_hbm, rows_hbm, q_hbm, k_hbm, g_hbm, ids_hbm, index_hbm, *rest
):
    v_ref, odd_ref, loss_ref, exponent_ref, start_ref, rows_ref, q_ref, k_ref, g_ref, ids_ref, index_ref, sems = rest
    count = 0

    def begin(source, target):
        nonlocal count
        copy = pltpu.make_async_copy(source, target, sems.at[count])
        copy.start()
        count += 1
        return copy

    small = [
        begin(source, target)
        for source, target in (
            (ids_hbm, ids_ref), (index_hbm, index_ref), (loss_hbm, loss_ref), (exponent_hbm, exponent_ref),
            (start_hbm, start_ref), (rows_hbm, rows_ref),
        )
    ]
    groups = k_ref.shape[1] // HD
    wide = per_group * HD
    loads = []
    for half in range(2):
        span = pl.ds(half * HALF, HALF)
        loads.append([
            begin(source.at[span, :], target.at[span, :])
            for source, target in ((q_hbm, q_ref), (k_hbm, k_ref), (g_hbm, g_ref))
        ])
    odd_ref[...] = jnp.broadcast_to((lax.axis_index("dp") & 1).astype(F32), odd_ref.shape)
    for copy in small:
        copy.wait()
    masks = [
        mask_and_factor(half == 1, pl.ds(half * HALF, HALF), loss_ref, exponent_ref, ids_ref, index_ref)
        for half in range(2)
    ]
    info_row = lax.broadcasted_iota(jnp.int32, (INFO, k_ref.shape[1]), 0)
    info = jnp.zeros(info_row.shape, jnp.int32)
    for level in range(min(start_ref.shape[1], INFO // 2)):
        info = jnp.where(info_row == 2 * level, start_ref[0, level], info)
        info = jnp.where(info_row == 2 * level + 1, rows_ref[0, level], info)
    v_ref[pl.ds(2 * HALF, INFO), :] = info.astype(F32).astype(BF16)
    for half in range(2):
        for copy in loads[half]:
            copy.wait()
        span = pl.ds(half * HALF, HALF)
        values = attend_half(per_group, half == 1, span, q_ref, k_ref, g_ref, *masks[half])
        for group, value in enumerate(values):
            v_ref[span, pl.ds(group * HD, HD)] = value


def front(query, key, grad, ids, index, loss, exponent, start, rows):
    tokens, key_width = key.shape
    per_group = query.shape[1] // key_width
    args = [
        loss, exponent, start, rows, query, key, grad, ids.reshape(1, tokens), index.reshape(1, tokens)
    ]
    return pl.pallas_call(
        functools.partial(front_kernel, per_group),
        in_specs=[HBM] * 9,
        out_specs=[VMEM] * 2,
        out_shape=[
            jax.ShapeDtypeStruct((tokens + INFO, key_width), BF16), jax.ShapeDtypeStruct((8, 2 * HALF), F32)
        ],
        scratch_shapes=[
            pltpu.SMEM(loss.shape, F32), pltpu.SMEM(exponent.shape, jnp.int32),
            pltpu.SMEM(start.shape, jnp.int32), pltpu.SMEM(rows.shape, jnp.int32),
            pltpu.VMEM(query.shape, BF16), pltpu.VMEM(key.shape, BF16), pltpu.VMEM(grad.shape, BF16),
            pltpu.VMEM((1, tokens), jnp.int32), pltpu.VMEM((1, tokens), jnp.int32),
            pltpu.SemaphoreType.DMA((12,)),
        ],
        compiler_params=pltpu.CompilerParams(vmem_limit_bytes=24 * MIB),
        cost_estimate=FREE,
        name="front",
    )(*[arg if arg is exponent else pltpu.with_memory_space_constraint(arg, pltpu.HBM) for arg in args])


CORE, Y, X, Z1, Z2 = 8, 16, 1, 2, 4


def routed(value, odd, even):
    owners = lax.axis_size("fsdp")
    count = lax.axis_size("dp") * owners
    return lax.ppermute(
        value, ("dp", "fsdp"), [(i, i ^ (odd if i // owners % 2 else even)) for i in range(count)]
    )


def xor_permute(value, mask):
    return routed(value, mask, mask)


def partial_kernel(parts, own_ref, near_ref, v0_ref, v1_ref, *out_refs):
    dp = lax.axis_index("dp")
    fsdp = lax.axis_index("fsdp")
    odd = dp & 1

    def pick(choices):
        return choices[0] + odd * (choices[1] - choices[0])

    for units, out_ref in zip(parts, out_refs):
        for number, (odd_unit, even_unit) in enumerate(units):
            z, y, x, part = (pick(pair) for pair in zip(even_unit, odd_unit))
            owner = fsdp ^ (z * 2 + x)
            quarter = (dp - odd) ^ (y * 2)
            column = pl.ds(pl.multiple_of(owner * (4 * LANE) + quarter * LANE, 2 * LANE), 2 * LANE)
            some = pl.ds(pl.multiple_of(part * (2 * LANE), 2 * LANE), 2 * LANE)
            total = lax.dot_general(
                jnp.concatenate([own_ref[:, column], near_ref[:, column]], axis=0),
                jnp.concatenate([ref[pl.ds(0, 2 * HALF), some] for ref in (v0_ref, v1_ref)], axis=0),
                (((0,), (0,)), ((), ())),
                preferred_element_type=F32,
            )
            out_ref[pl.ds(number * (2 * LANE), 2 * LANE), :] = total.astype(out_ref.dtype)


def partial_sums(parts, dtype, own, near, v0, v1):
    return pl.pallas_call(
        functools.partial(partial_kernel, parts),
        in_specs=[VMEM] * 4,
        out_specs=[VMEM] * len(parts),
        out_shape=[jax.ShapeDtypeStruct((2 * HALF * len(units), 2 * HALF), dtype) for units in parts],
        compiler_params=pltpu.CompilerParams(vmem_limit_bytes=24 * MIB),
        cost_estimate=FREE,
        name="partial_sums",
    )(own, near, v0, v1)


def inner_swap_kernel(v0_ref, v1_ref, out_ref, window_ref):
    tokens = out_ref.shape[0]
    infos = [ref[pl.ds(tokens, INFO), pl.ds(0, HALF)].astype(F32).astype(jnp.int32) for ref in (v0_ref, v1_ref)]

    def table(device, entry):
        return jnp.broadcast_to(infos[device][entry:entry + 1, :], (HALF, HALF))

    place = lax.broadcasted_iota(jnp.int32, (HALF, HALF), 0) + HALF
    inner = lax.broadcasted_iota(jnp.int32, (HALF, HALF), 1) + HALF
    first = table(0, 0)
    moved = (place >= first) & (place < first + table(0, 1))
    stays = jnp.where(~moved & (place == inner), 1.0, 0.0).astype(BF16)
    comes = jnp.where(moved & (place + table(1, 0) - first == inner), 1.0, 0.0).astype(BF16)
    taken = jnp.where(place - HALF + table(0, 2) == inner, 1.0, 0.0).astype(BF16)[:CAP]
    rows = (
        jnp.dot(stays, v0_ref[pl.ds(HALF, HALF), :], preferred_element_type=F32)
        + jnp.dot(comes, v1_ref[pl.ds(HALF, HALF), :], preferred_element_type=F32)
    ).astype(BF16)
    out_ref[pl.ds(0, HALF), :] = v0_ref[pl.ds(0, HALF), :]
    out_ref[pl.ds(HALF, HALF), :] = rows
    window_ref[...] = jnp.dot(taken, rows, preferred_element_type=F32).astype(BF16)


def inner_swap(v0, v1):
    return pl.pallas_call(
        inner_swap_kernel,
        in_specs=[VMEM] * 2,
        out_specs=[VMEM] * 2,
        out_shape=[jax.ShapeDtypeStruct((2 * HALF, 512), BF16), jax.ShapeDtypeStruct((CAP, 512), BF16)],
        compiler_params=pltpu.CompilerParams(vmem_limit_bytes=8 * MIB),
        cost_estimate=FREE,
        name="inner_swap",
    )(v0, v1)


def outer_swap_kernel(v0_ref, rows_ref, window_ref, out_ref):
    tokens = out_ref.shape[0]
    info = v0_ref[pl.ds(tokens, INFO), pl.ds(0, HALF)].astype(F32).astype(jnp.int32)
    first = jnp.broadcast_to(info[2:3, :], (HALF, HALF))
    extent = jnp.broadcast_to(info[3:4, :], (HALF, HALF))
    place = lax.broadcasted_iota(jnp.int32, (HALF, HALF), 0) + HALF
    inner = lax.broadcasted_iota(jnp.int32, (HALF, HALF), 1)
    moved = (place >= first) & (place < first + extent)
    stays = jnp.where(~moved & (place == inner + HALF), 1.0, 0.0).astype(BF16)
    comes = jnp.where(moved & (place - first == inner), 1.0, 0.0).astype(BF16)[:, :CAP]
    out_ref[pl.ds(0, HALF), :] = rows_ref[pl.ds(0, HALF), :]
    out_ref[pl.ds(HALF, HALF), :] = (
        jnp.dot(stays, rows_ref[pl.ds(HALF, HALF), :], preferred_element_type=F32)
        + jnp.dot(comes, window_ref[...], preferred_element_type=F32)
    ).astype(BF16)


def outer_swap(v0, rows, window):
    return pl.pallas_call(
        outer_swap_kernel,
        in_specs=[VMEM] * 3,
        out_specs=VMEM,
        out_shape=jax.ShapeDtypeStruct(rows.shape, BF16),
        compiler_params=pltpu.CompilerParams(vmem_limit_bytes=8 * MIB),
        cost_estimate=FREE,
        name="outer_swap",
    )(v0, rows, window)


def place_kernel(pair_ref, near_ref, out_ref):
    dp = lax.axis_index("dp")
    for ref, part in ((pair_ref, dp & 1), (near_ref, 1 - (dp & 1))):
        some = pl.ds(pl.multiple_of(part * (2 * LANE), 2 * LANE), 2 * LANE)
        for flip in range(2):
            rows = pl.ds(pl.multiple_of(((dp >> 1) ^ flip) * (2 * LANE), 2 * LANE), 2 * LANE)
            out_ref[rows, some] = ref[flip].astype(F32)


def place(pair, near):
    return pl.pallas_call(
        place_kernel,
        in_specs=[VMEM] * 2,
        out_specs=VMEM,
        out_shape=jax.ShapeDtypeStruct((512, 512), F32),
        compiler_params=pltpu.CompilerParams(vmem_limit_bytes=8 * MIB),
        cost_estimate=FREE,
        name="place",
    )(pair, near)


def reduce_by_axis(layer_input, *args):
    near = xor_permute(layer_input, CORE)
    v0, odd = front(*args)
    odd = odd[:1] > 0.5
    v1 = xor_permute(v0, CORE)
    both = 2 * LANE

    def sums(parts, dtype):
        return partial_sums(parts, dtype, layer_input, near, v0, v1)

    def after_all(*values):
        return lax.optimization_barrier(values)

    def add(*terms):
        total = terms[0]
        for term in terms[1:]:
            total = total + term.astype(F32)
        return total

    def chain(z, y, x):
        return ((z, y, x, 0), (z, y, x, 1))

    def own(z, y, part):
        return ((z, y, 1, part), (z, y, 0, part))

    def parts(*pairs):
        return [tuple(zip(*pair)) for pair in pairs]

    first, second = sums(parts((chain(3, 1, 1), own(1, 1, 0)), (chain(2, 1, 1), own(1, 0, 0))), BF16)
    third, fourth = sums(parts((chain(3, 0, 1), own(1, 1, 1)), (chain(2, 1, 0), own(1, 0, 1))), BF16)
    keep1, keep2 = sums(parts((chain(3, 1, 0), own(0, 1, 0)), (chain(2, 0, 1), own(0, 0, 0))), F32)
    keep3, keep4 = sums(parts((chain(3, 0, 0), own(0, 1, 1)), (chain(2, 0, 0), own(0, 0, 1))), F32)
    side = fourth
    first = routed(first, X, Z1)
    second = routed(second, Y, Z1)
    third = routed(third, X, Z1)
    total1 = add(keep1, first)
    fourth = jnp.where(odd, total1.astype(BF16), fourth)
    second = after_all(second, fourth)[0]
    fourth = routed(fourth, Y, Z1)
    total2 = add(keep2, second)
    fifth = jnp.where(odd, total2, total1).astype(BF16)
    rows, window = inner_swap(after_all(v0, third)[0], v1)
    fifth_sent = fifth
    side = after_all(side, fifth)[0]
    fifth = routed(fifth, X, Y)
    side = routed(side, Y, 0)
    third, fourth = after_all(third, fourth, fifth_sent)[:2]
    total3 = add(keep3, third)
    sixth = jnp.where(odd, add(total3, fourth), total3).astype(BF16)
    window, side, fifth = after_all(window, side, fifth, sixth)[:3]
    window = xor_permute(window, Y)
    sixth = routed(sixth, Z1, Y)
    some = add(total2, fifth)
    rest = add(keep4, jnp.where(odd, side, fourth))
    rest, sixth = after_all(rest, sixth)
    rest = add(rest, sixth)
    last = jnp.where(odd, add(rest, fifth), jnp.concatenate([some[:both], rest[:both]])).astype(BF16)
    last, window = after_all(last, window)
    last = routed(last, Z2, X)
    base = jnp.concatenate([add(some[both:], last[:both]), add(rest[both:], last[both:])])
    mine = jnp.where(odd, last.astype(F32), base)
    crossed = xor_permute(jnp.where(odd, last[:both], base[both:].astype(BF16)), CORE)
    mine = add(jnp.where(odd, mine[both:], mine[:both]), crossed).astype(BF16)
    from_y = xor_permute(mine, Y)
    value_grad = outer_swap(v0, rows, after_all(window, from_y)[0])
    pair = jnp.stack([mine, from_y])
    return place(pair, xor_permute(pair, CORE)), value_grad


def swapped(block, axis, distance):
    count = lax.axis_size(axis)
    route = []
    for low in range(count):
        high = low | 1 << distance
        if high != low and high < count:
            route += [(low, high), (high, low)]
    return lax.ppermute(block, axis, route)


def blend_rows(item, incoming, offset, extent):
    inside = (jnp.arange(CAP) < extent)[:, None]
    chosen = jnp.where(inside, incoming, lax.dynamic_slice_in_dim(item, offset, CAP, 0))
    return lax.dynamic_update_slice_in_dim(item, chosen, offset, 0)


def reduce_by_owner(layer_input, *args):
    swap_start, swap_rows = args[-2:]
    tokens = layer_input.shape[0]
    values = front(*args)[0][:tokens]
    balanced = values
    for level in range(lax.axis_size("dp").bit_length() - 1):
        offset = swap_start[0, level]
        window = lax.dynamic_slice_in_dim(balanced, offset, CAP, 0)
        balanced = blend_rows(balanced, swapped(window, "dp", level), offset, swap_rows[0, level])
    owners = lax.axis_size("fsdp")
    owned = (D + owners - 1) // owners
    padded = jnp.pad(layer_input, ((0, 0), (0, owned * owners - D)))
    arranged = lax.all_to_all(
        padded.reshape(tokens, owners, owned), "fsdp", split_axis=1, concat_axis=0, tiled=True
    )
    block = lax.dot_general(
        arranged.reshape(-1, owned),
        lax.all_gather(values, "fsdp", axis=0, tiled=True),
        (((0,), (0,)), ((), ())),
        preferred_element_type=F32,
    )
    return lax.psum(block, "dp"), balanced


def on_device(layer_input, *args):
    if lax.axis_size("dp") == 4 and lax.axis_size("fsdp") == 8:
        return reduce_by_axis(layer_input, *args)
    return reduce_by_owner(layer_input, *args)


def solution(mesh):
    return jax.shard_map(
        on_device,
        mesh=mesh,
        in_specs=(
            P(("dp", "fsdp"), None),
            P(("dp", "fsdp"), None),
            P(("dp", "fsdp"), None),
            P(("dp", "fsdp"), None),
            P(("dp", "fsdp")),
            P(("dp", "fsdp")),
            P(),
            P(("dp", "fsdp")),
            P(("dp", "fsdp"), None),
            P(("dp", "fsdp"), None),
        ),
        out_specs=(P("fsdp", None), P(("dp", "fsdp"), None)),
        check_vma=False,
    )
```

```python
import functools
import math

import jax
import jax.numpy as jnp
from jax import lax
from jax.experimental import pallas as pl
from jax.experimental.pallas import tpu as pltpu
from jax.sharding import PartitionSpec as P

D = 4096
HD = 128
CAP = 32
HALF = 128
SEG = 16
LANE = 128
INFO = 16
MIB = 1 << 20
FREE = pl.CostEstimate(flops=0, bytes_accessed=0, transcendentals=0)
BF16 = jnp.bfloat16
F32 = jnp.float32

VMEM = pl.BlockSpec(memory_space=pltpu.VMEM)
HBM = pl.BlockSpec(memory_space=pltpu.HBM)


def attend_half(per_group, folded, span, q_ref, k_ref, g_ref, allowed, factor):
    heads = q_ref.shape[1] // HD
    groups = heads // per_group
    scores = [
        lax.dot_general(
            k_ref[span, pl.ds(group * HD, HD)],
            jnp.concatenate(
                [q_ref[span, pl.ds((group * per_group + n) * HD, HD)] for n in range(per_group)], axis=0
            ),
            (((1,), (1,)), ((), ())),
            preferred_element_type=F32,
        )
        for group in range(groups)
    ]
    weighted = [
        (g_ref[span, pl.ds(head * HD, HD)].astype(F32) * factor).astype(BF16) for head in range(heads)
    ]
    if folded:
        block = lax.broadcasted_iota(jnp.int32, (SEG, HALF), 1) // SEG
    probs = []
    for head in range(heads):
        n = head % per_group
        own = scores[head // per_group][:, n * HALF:(n + 1) * HALF]
        if folded:
            own = fold_blocks(own, block)
        own = jnp.where(allowed, own, -1e30)
        expo = jnp.exp2((own - jnp.max(own, axis=0, keepdims=True)) * (HD ** (-0.5) * math.log2(math.e)))
        prob = (expo * (1.0 / jnp.sum(expo, axis=0, keepdims=True))).astype(BF16)
        if folded:
            prob = jnp.concatenate(
                [jnp.where(block == b, prob, jnp.zeros_like(prob)) for b in range(HALF // SEG)], axis=0
            )
        probs.append(prob)
    return [
        jnp.dot(
            jnp.concatenate(probs[head:head + per_group], axis=1),
            jnp.concatenate(weighted[head:head + per_group], axis=0),
            preferred_element_type=F32,
        ).astype(BF16)
        for head in range(0, heads, per_group)
    ]


def fold_blocks(square, block):
    total = square[:SEG]
    for b in range(1, HALF // SEG):
        total = jnp.where(block == b, square[b * SEG:(b + 1) * SEG], total)
    return total


def mask_and_factor(folded, span, loss_ref, exponent_ref, ids_ref, index_ref):
    exponent = exponent_ref[0]
    unscale = jnp.float32(1.0)
    for bit in range(5):
        unscale = unscale * jnp.where((exponent >> bit) & 1 == 1, jnp.float32(2.0 ** -(1 << bit)), 1.0)
    row = lax.broadcasted_iota(jnp.int32, (HALF, HALF), 0)
    col = lax.broadcasted_iota(jnp.int32, (HALF, HALF), 1)
    doc_i = jnp.broadcast_to(ids_ref[:, span], (HALF, HALF))
    allowed = (doc_i == doc_i.T) & (row <= col)
    if folded:
        allowed = fold_blocks(
            jnp.where(allowed, 1, 0), lax.broadcasted_iota(jnp.int32, (SEG, HALF), 1) // SEG
        ) == 1
    index = index_ref[:, span]
    factor = jnp.zeros((1, HALF), F32)
    for entry in range(loss_ref.shape[0]):
        factor = jnp.where(index == entry, loss_ref[entry], factor)
    return allowed, jnp.broadcast_to(factor * unscale, (HALF, HALF)).T


def front_kernel(
    per_group, loss_hbm, exponent_hbm, start_hbm, rows_hbm, q_hbm, k_hbm, g_hbm, ids_hbm, index_hbm, *rest
):
    v_ref, odd_ref, loss_ref, exponent_ref, start_ref, rows_ref, q_ref, k_ref, g_ref, ids_ref, index_ref, sems = rest
    count = 0

    def begin(source, target):
        nonlocal count
        copy = pltpu.make_async_copy(source, target, sems.at[count])
        copy.start()
        count += 1
        return copy

    small = [
        begin(source, target)
        for source, target in (
            (ids_hbm, ids_ref), (index_hbm, index_ref), (loss_hbm, loss_ref), (exponent_hbm, exponent_ref),
            (start_hbm, start_ref), (rows_hbm, rows_ref),
        )
    ]
    groups = k_ref.shape[1] // HD
    wide = per_group * HD
    loads = []
    for half in range(2):
        span = pl.ds(half * HALF, HALF)
        loads.append([
            begin(source.at[span, :], target.at[span, :])
            for source, target in ((q_hbm, q_ref), (k_hbm, k_ref), (g_hbm, g_ref))
        ])
    odd_ref[...] = jnp.broadcast_to((lax.axis_index("dp") & 1).astype(F32), odd_ref.shape)
    for copy in small:
        copy.wait()
    masks = [
        mask_and_factor(half == 1, pl.ds(half * HALF, HALF), loss_ref, exponent_ref, ids_ref, index_ref)
        for half in range(2)
    ]
    info_row = lax.broadcasted_iota(jnp.int32, (INFO, k_ref.shape[1]), 0)
    info = jnp.zeros(info_row.shape, jnp.int32)
    for level in range(min(start_ref.shape[1], INFO // 2)):
        info = jnp.where(info_row == 2 * level, start_ref[0, level], info)
        info = jnp.where(info_row == 2 * level + 1, rows_ref[0, level], info)
    v_ref[pl.ds(2 * HALF, INFO), :] = info.astype(F32).astype(BF16)
    for half in range(2):
        for copy in loads[half]:
            copy.wait()
        span = pl.ds(half * HALF, HALF)
        values = attend_half(per_group, half == 1, span, q_ref, k_ref, g_ref, *masks[half])
        for group, value in enumerate(values):
            v_ref[span, pl.ds(group * HD, HD)] = value


def front(query, key, grad, ids, index, loss, exponent, start, rows):
    tokens, key_width = key.shape
    per_group = query.shape[1] // key_width
    args = [
        loss, exponent, start, rows, query, key, grad, ids.reshape(1, tokens), index.reshape(1, tokens)
    ]
    return pl.pallas_call(
        functools.partial(front_kernel, per_group),
        in_specs=[HBM] * 9,
        out_specs=[VMEM] * 2,
        out_shape=[
            jax.ShapeDtypeStruct((tokens + INFO, key_width), BF16), jax.ShapeDtypeStruct((8, 2 * HALF), F32)
        ],
        scratch_shapes=[
            pltpu.SMEM(loss.shape, F32), pltpu.SMEM(exponent.shape, jnp.int32),
            pltpu.SMEM(start.shape, jnp.int32), pltpu.SMEM(rows.shape, jnp.int32),
            pltpu.VMEM(query.shape, BF16), pltpu.VMEM(key.shape, BF16), pltpu.VMEM(grad.shape, BF16),
            pltpu.VMEM((1, tokens), jnp.int32), pltpu.VMEM((1, tokens), jnp.int32),
            pltpu.SemaphoreType.DMA((12,)),
        ],
        compiler_params=pltpu.CompilerParams(vmem_limit_bytes=24 * MIB),
        cost_estimate=FREE,
        name="front",
    )(*[arg if arg is exponent else pltpu.with_memory_space_constraint(arg, pltpu.HBM) for arg in args])


CORE, Y, X, Z1, Z2 = 8, 16, 1, 2, 4


def routed(value, odd, even):
    owners = lax.axis_size("fsdp")
    count = lax.axis_size("dp") * owners
    return lax.ppermute(
        value, ("dp", "fsdp"), [(i, i ^ (odd if i // owners % 2 else even)) for i in range(count)]
    )


def xor_permute(value, mask):
    return routed(value, mask, mask)


def partial_kernel(parts, own_ref, near_ref, v0_ref, v1_ref, *out_refs):
    dp = lax.axis_index("dp")
    fsdp = lax.axis_index("fsdp")
    odd = dp & 1

    def pick(choices):
        return choices[0] + odd * (choices[1] - choices[0])

    for units, out_ref in zip(parts, out_refs):
        for number, (odd_unit, even_unit) in enumerate(units):
            z, y, x, part = (pick(pair) for pair in zip(even_unit, odd_unit))
            owner = fsdp ^ (z * 2 + x)
            quarter = (dp - odd) ^ (y * 2)
            column = pl.ds(pl.multiple_of(owner * (4 * LANE) + quarter * LANE, 2 * LANE), 2 * LANE)
            some = pl.ds(pl.multiple_of(part * (2 * LANE), 2 * LANE), 2 * LANE)
            total = lax.dot_general(
                jnp.concatenate([own_ref[:, column], near_ref[:, column]], axis=0),
                jnp.concatenate([ref[pl.ds(0, 2 * HALF), some] for ref in (v0_ref, v1_ref)], axis=0),
                (((0,), (0,)), ((), ())),
                preferred_element_type=F32,
            )
            out_ref[pl.ds(number * (2 * LANE), 2 * LANE), :] = total.astype(out_ref.dtype)


def partial_sums(parts, dtype, own, near, v0, v1):
    return pl.pallas_call(
        functools.partial(partial_kernel, parts),
        in_specs=[VMEM] * 4,
        out_specs=[VMEM] * len(parts),
        out_shape=[jax.ShapeDtypeStruct((2 * HALF * len(units), 2 * HALF), dtype) for units in parts],
        compiler_params=pltpu.CompilerParams(vmem_limit_bytes=24 * MIB),
        cost_estimate=FREE,
        name="partial_sums",
    )(own, near, v0, v1)


def inner_swap_kernel(v0_ref, v1_ref, out_ref, window_ref):
    tokens = out_ref.shape[0]
    infos = [ref[pl.ds(tokens, INFO), pl.ds(0, HALF)].astype(F32).astype(jnp.int32) for ref in (v0_ref, v1_ref)]

    def table(device, entry):
        return jnp.broadcast_to(infos[device][entry:entry + 1, :], (HALF, HALF))

    place = lax.broadcasted_iota(jnp.int32, (HALF, HALF), 0) + HALF
    inner = lax.broadcasted_iota(jnp.int32, (HALF, HALF), 1) + HALF
    first = table(0, 0)
    moved = (place >= first) & (place < first + table(0, 1))
    stays = jnp.where(~moved & (place == inner), 1.0, 0.0).astype(BF16)
    comes = jnp.where(moved & (place + table(1, 0) - first == inner), 1.0, 0.0).astype(BF16)
    taken = jnp.where(place - HALF + table(0, 2) == inner, 1.0, 0.0).astype(BF16)[:CAP]
    rows = (
        jnp.dot(stays, v0_ref[pl.ds(HALF, HALF), :], preferred_element_type=F32)
        + jnp.dot(comes, v1_ref[pl.ds(HALF, HALF), :], preferred_element_type=F32)
    ).astype(BF16)
    out_ref[pl.ds(0, HALF), :] = v0_ref[pl.ds(0, HALF), :]
    out_ref[pl.ds(HALF, HALF), :] = rows
    window_ref[...] = jnp.dot(taken, rows, preferred_element_type=F32).astype(BF16)


def inner_swap(v0, v1):
    return pl.pallas_call(
        inner_swap_kernel,
        in_specs=[VMEM] * 2,
        out_specs=[VMEM] * 2,
        out_shape=[jax.ShapeDtypeStruct((2 * HALF, 512), BF16), jax.ShapeDtypeStruct((CAP, 512), BF16)],
        compiler_params=pltpu.CompilerParams(vmem_limit_bytes=8 * MIB),
        cost_estimate=FREE,
        name="inner_swap",
    )(v0, v1)


def outer_swap_kernel(v0_ref, rows_ref, window_ref, out_ref):
    tokens = out_ref.shape[0]
    info = v0_ref[pl.ds(tokens, INFO), pl.ds(0, HALF)].astype(F32).astype(jnp.int32)
    first = jnp.broadcast_to(info[2:3, :], (HALF, HALF))
    extent = jnp.broadcast_to(info[3:4, :], (HALF, HALF))
    place = lax.broadcasted_iota(jnp.int32, (HALF, HALF), 0) + HALF
    inner = lax.broadcasted_iota(jnp.int32, (HALF, HALF), 1)
    moved = (place >= first) & (place < first + extent)
    stays = jnp.where(~moved & (place == inner + HALF), 1.0, 0.0).astype(BF16)
    comes = jnp.where(moved & (place - first == inner), 1.0, 0.0).astype(BF16)[:, :CAP]
    out_ref[pl.ds(0, HALF), :] = rows_ref[pl.ds(0, HALF), :]
    out_ref[pl.ds(HALF, HALF), :] = (
        jnp.dot(stays, rows_ref[pl.ds(HALF, HALF), :], preferred_element_type=F32)
        + jnp.dot(comes, window_ref[...], preferred_element_type=F32)
    ).astype(BF16)


def outer_swap(v0, rows, window):
    return pl.pallas_call(
        outer_swap_kernel,
        in_specs=[VMEM] * 3,
        out_specs=VMEM,
        out_shape=jax.ShapeDtypeStruct(rows.shape, BF16),
        compiler_params=pltpu.CompilerParams(vmem_limit_bytes=8 * MIB),
        cost_estimate=FREE,
        name="outer_swap",
    )(v0, rows, window)


def place_kernel(pair_ref, near_ref, out_ref):
    dp = lax.axis_index("dp")
    for ref, part in ((pair_ref, dp & 1), (near_ref, 1 - (dp & 1))):
        some = pl.ds(pl.multiple_of(part * (2 * LANE), 2 * LANE), 2 * LANE)
        for flip in range(2):
            rows = pl.ds(pl.multiple_of(((dp >> 1) ^ flip) * (2 * LANE), 2 * LANE), 2 * LANE)
            out_ref[rows, some] = ref[flip].astype(F32)


def place(pair, near):
    return pl.pallas_call(
        place_kernel,
        in_specs=[VMEM] * 2,
        out_specs=VMEM,
        out_shape=jax.ShapeDtypeStruct((512, 512), F32),
        compiler_params=pltpu.CompilerParams(vmem_limit_bytes=8 * MIB),
        cost_estimate=FREE,
        name="place",
    )(pair, near)


def fold_kernel(base_ref, arrived_ref, out_ref):
    out_ref[...] = base_ref[...] + arrived_ref[...].astype(F32)


def fold(base, arrived):
    return pl.pallas_call(
        fold_kernel,
        in_specs=[VMEM] * 2,
        out_specs=VMEM,
        out_shape=jax.ShapeDtypeStruct(base.shape, F32),
        compiler_params=pltpu.CompilerParams(vmem_limit_bytes=8 * MIB),
        cost_estimate=pl.CostEstimate(flops=8_000_000_000, bytes_accessed=0, transcendentals=0),
        name="fold",
    )(base, arrived)


def reduce_by_axis(layer_input, *args):
    near = xor_permute(layer_input, CORE)
    v0, odd = front(*args)
    odd = odd[:1] > 0.5
    v1 = xor_permute(v0, CORE)
    both = 2 * LANE

    def sums(parts, dtype):
        return partial_sums(parts, dtype, layer_input, near, v0, v1)

    def after_all(*values):
        return lax.optimization_barrier(values)

    def add(*terms):
        total = terms[0]
        for term in terms[1:]:
            total = total + term.astype(F32)
        return total

    def chain(z, y, x):
        return ((z, y, x, 0), (z, y, x, 1))

    def own(z, y, part):
        return ((z, y, 1, part), (z, y, 0, part))

    def parts(*pairs):
        return [tuple(zip(*pair)) for pair in pairs]

    first, second = sums(parts((chain(3, 1, 1), own(1, 1, 0)), (chain(2, 1, 1), own(1, 1, 1))), BF16)
    third, spare = sums(parts((chain(3, 0, 1), own(1, 0, 0)), (chain(2, 1, 0), own(1, 0, 1))), BF16)
    keep1, keep2 = sums(parts((chain(3, 1, 0), own(0, 1, 0)), (chain(2, 0, 1), own(0, 1, 1))), F32)
    keep3, keep4 = sums(parts((chain(3, 0, 0), own(0, 0, 0)), (chain(2, 0, 0), own(0, 0, 1))), F32)
    first = routed(first, X, Z1)
    second = routed(second, Y, Z1)
    third = routed(third, X, Z1)
    total1 = add(keep1, first)
    fourth = jnp.where(odd, total1.astype(BF16), spare)
    second = after_all(second, fourth)[0]
    fourth = routed(fourth, Y, Z1)
    total2 = add(keep2, second)
    fifth = jnp.where(odd, spare, total2.astype(BF16))
    sixth = jnp.where(odd, total2, total1).astype(BF16)
    rows, window = inner_swap(after_all(v0, spare)[0], v1)
    third, fourth, window = after_all(third, fourth, window, fifth, sixth)[:3]
    fifth = routed(fifth, Y, Y)
    sixth = routed(sixth, X, Y)
    total3 = add(keep3, third)
    joined = add(total3, fourth).astype(BF16)
    fourth, fifth, sixth = after_all(fourth, fifth, sixth, joined)[:3]
    joined = routed(joined, Z1, 0)
    rest = add(keep4, fifth)
    some = add(total3, sixth)
    rest = jnp.where(odd, add(rest, sixth, joined), add(rest, fourth))
    last1 = rest[:both].astype(BF16)
    last2 = jnp.where(odd, rest[both:], some[:both]).astype(BF16)
    window = xor_permute(after_all(window, last1, last2)[0], Y)
    last1 = routed(last1, Z2, X)
    last2 = routed(last2, Z2, X)
    last1, window = after_all(last1, window)
    crossed = xor_permute(jnp.where(odd, last1, add(rest[both:], last1).astype(BF16)), CORE)
    mine = add(fold(jnp.where(odd, 0.0, some[both:]), last2), crossed).astype(BF16)
    from_y = xor_permute(mine, Y)
    value_grad = outer_swap(v0, rows, after_all(window, from_y)[0])
    pair = jnp.stack([mine, from_y])
    return place(pair, xor_permute(pair, CORE)), value_grad


def swapped(block, axis, distance):
    count = lax.axis_size(axis)
    route = []
    for low in range(count):
        high = low | 1 << distance
        if high != low and high < count:
            route += [(low, high), (high, low)]
    return lax.ppermute(block, axis, route)


def blend_rows(item, incoming, offset, extent):
    inside = (jnp.arange(CAP) < extent)[:, None]
    chosen = jnp.where(inside, incoming, lax.dynamic_slice_in_dim(item, offset, CAP, 0))
    return lax.dynamic_update_slice_in_dim(item, chosen, offset, 0)


def reduce_by_owner(layer_input, *args):
    swap_start, swap_rows = args[-2:]
    tokens = layer_input.shape[0]
    values = front(*args)[0][:tokens]
    balanced = values
    for level in range(lax.axis_size("dp").bit_length() - 1):
        offset = swap_start[0, level]
        window = lax.dynamic_slice_in_dim(balanced, offset, CAP, 0)
        balanced = blend_rows(balanced, swapped(window, "dp", level), offset, swap_rows[0, level])
    owners = lax.axis_size("fsdp")
    owned = (D + owners - 1) // owners
    padded = jnp.pad(layer_input, ((0, 0), (0, owned * owners - D)))
    arranged = lax.all_to_all(
        padded.reshape(tokens, owners, owned), "fsdp", split_axis=1, concat_axis=0, tiled=True
    )
    block = lax.dot_general(
        arranged.reshape(-1, owned),
        lax.all_gather(values, "fsdp", axis=0, tiled=True),
        (((0,), (0,)), ((), ())),
        preferred_element_type=F32,
    )
    return lax.psum(block, "dp"), balanced


def on_device(layer_input, *args):
    if lax.axis_size("dp") == 4 and lax.axis_size("fsdp") == 8:
        return reduce_by_axis(layer_input, *args)
    return reduce_by_owner(layer_input, *args)


def solution(mesh):
    return jax.shard_map(
        on_device,
        mesh=mesh,
        in_specs=(
            P(("dp", "fsdp"), None),
            P(("dp", "fsdp"), None),
            P(("dp", "fsdp"), None),
            P(("dp", "fsdp"), None),
            P(("dp", "fsdp")),
            P(("dp", "fsdp")),
            P(),
            P(("dp", "fsdp")),
            P(("dp", "fsdp"), None),
            P(("dp", "fsdp"), None),
        ),
        out_specs=(P("fsdp", None), P(("dp", "fsdp"), None)),
        check_vma=False,
    )
```

```python
import functools
import math

import jax
import jax.numpy as jnp
from jax import lax
from jax.experimental import pallas as pl
from jax.experimental.pallas import tpu as pltpu
from jax.sharding import PartitionSpec as P

D = 4096
HD = 128
CAP = 32
HALF = 128
SEG = 16
LANE = 128
INFO = 16
MIB = 1 << 20
FREE = pl.CostEstimate(flops=0, bytes_accessed=0, transcendentals=0)
BF16 = jnp.bfloat16
F32 = jnp.float32

VMEM = pl.BlockSpec(memory_space=pltpu.VMEM)
HBM = pl.BlockSpec(memory_space=pltpu.HBM)


def attend_half(per_group, folded, span, q_ref, k_ref, g_ref, allowed, factor):
    heads = q_ref.shape[1] // HD
    groups = heads // per_group
    scores = [
        lax.dot_general(
            k_ref[span, pl.ds(group * HD, HD)],
            jnp.concatenate(
                [q_ref[span, pl.ds((group * per_group + n) * HD, HD)] for n in range(per_group)], axis=0
            ),
            (((1,), (1,)), ((), ())),
            preferred_element_type=F32,
        )
        for group in range(groups)
    ]
    weighted = [
        (g_ref[span, pl.ds(head * HD, HD)].astype(F32) * factor).astype(BF16) for head in range(heads)
    ]
    if folded:
        block = lax.broadcasted_iota(jnp.int32, (SEG, HALF), 1) // SEG
    probs = []
    for head in range(heads):
        n = head % per_group
        own = scores[head // per_group][:, n * HALF:(n + 1) * HALF]
        if folded:
            own = fold_blocks(own, block)
        own = jnp.where(allowed, own, -1e30)
        expo = jnp.exp2((own - jnp.max(own, axis=0, keepdims=True)) * (HD ** (-0.5) * math.log2(math.e)))
        prob = (expo * (1.0 / jnp.sum(expo, axis=0, keepdims=True))).astype(BF16)
        if folded:
            prob = jnp.concatenate(
                [jnp.where(block == b, prob, jnp.zeros_like(prob)) for b in range(HALF // SEG)], axis=0
            )
        probs.append(prob)
    return [
        jnp.dot(
            jnp.concatenate(probs[head:head + per_group], axis=1),
            jnp.concatenate(weighted[head:head + per_group], axis=0),
            preferred_element_type=F32,
        ).astype(BF16)
        for head in range(0, heads, per_group)
    ]


def fold_blocks(square, block):
    total = square[:SEG]
    for b in range(1, HALF // SEG):
        total = jnp.where(block == b, square[b * SEG:(b + 1) * SEG], total)
    return total


def mask_and_factor(folded, span, loss_ref, exponent_ref, ids_ref, index_ref):
    exponent = exponent_ref[0]
    unscale = jnp.float32(1.0)
    for bit in range(5):
        unscale = unscale * jnp.where((exponent >> bit) & 1 == 1, jnp.float32(2.0 ** -(1 << bit)), 1.0)
    row = lax.broadcasted_iota(jnp.int32, (HALF, HALF), 0)
    col = lax.broadcasted_iota(jnp.int32, (HALF, HALF), 1)
    doc_i = jnp.broadcast_to(ids_ref[:, span], (HALF, HALF))
    allowed = (doc_i == doc_i.T) & (row <= col)
    if folded:
        allowed = fold_blocks(
            jnp.where(allowed, 1, 0), lax.broadcasted_iota(jnp.int32, (SEG, HALF), 1) // SEG
        ) == 1
    index = index_ref[:, span]
    factor = jnp.zeros((1, HALF), F32)
    for entry in range(loss_ref.shape[0]):
        factor = jnp.where(index == entry, loss_ref[entry], factor)
    return allowed, jnp.broadcast_to(factor * unscale, (HALF, HALF)).T


def front_kernel(
    per_group, loss_hbm, exponent_hbm, start_hbm, rows_hbm, q_hbm, k_hbm, g_hbm, ids_hbm, index_hbm, *rest
):
    v_ref, odd_ref, loss_ref, exponent_ref, start_ref, rows_ref, q_ref, k_ref, g_ref, ids_ref, index_ref, sems = rest
    count = 0

    def begin(source, target):
        nonlocal count
        copy = pltpu.make_async_copy(source, target, sems.at[count])
        copy.start()
        count += 1
        return copy

    small = [
        begin(source, target)
        for source, target in (
            (ids_hbm, ids_ref), (index_hbm, index_ref), (loss_hbm, loss_ref), (exponent_hbm, exponent_ref),
            (start_hbm, start_ref), (rows_hbm, rows_ref),
        )
    ]
    groups = k_ref.shape[1] // HD
    wide = per_group * HD
    loads = []
    for half in range(2):
        span = pl.ds(half * HALF, HALF)
        loads.append([
            begin(source.at[span, :], target.at[span, :])
            for source, target in ((q_hbm, q_ref), (k_hbm, k_ref), (g_hbm, g_ref))
        ])
    odd_ref[...] = jnp.broadcast_to((lax.axis_index("dp") & 1).astype(F32), odd_ref.shape)
    for copy in small:
        copy.wait()
    masks = [
        mask_and_factor(half == 1, pl.ds(half * HALF, HALF), loss_ref, exponent_ref, ids_ref, index_ref)
        for half in range(2)
    ]
    info_row = lax.broadcasted_iota(jnp.int32, (INFO, k_ref.shape[1]), 0)
    info = jnp.zeros(info_row.shape, jnp.int32)
    for level in range(min(start_ref.shape[1], INFO // 2)):
        info = jnp.where(info_row == 2 * level, start_ref[0, level], info)
        info = jnp.where(info_row == 2 * level + 1, rows_ref[0, level], info)
    v_ref[pl.ds(2 * HALF, INFO), :] = info.astype(F32).astype(BF16)
    for half in range(2):
        for copy in loads[half]:
            copy.wait()
        span = pl.ds(half * HALF, HALF)
        values = attend_half(per_group, half == 1, span, q_ref, k_ref, g_ref, *masks[half])
        for group, value in enumerate(values):
            v_ref[span, pl.ds(group * HD, HD)] = value


def front(query, key, grad, ids, index, loss, exponent, start, rows):
    tokens, key_width = key.shape
    per_group = query.shape[1] // key_width
    args = [
        loss, exponent, start, rows, query, key, grad, ids.reshape(1, tokens), index.reshape(1, tokens)
    ]
    return pl.pallas_call(
        functools.partial(front_kernel, per_group),
        in_specs=[HBM] * 9,
        out_specs=[VMEM] * 2,
        out_shape=[
            jax.ShapeDtypeStruct((tokens + INFO, key_width), BF16), jax.ShapeDtypeStruct((8, 2 * HALF), F32)
        ],
        scratch_shapes=[
            pltpu.SMEM(loss.shape, F32), pltpu.SMEM(exponent.shape, jnp.int32),
            pltpu.SMEM(start.shape, jnp.int32), pltpu.SMEM(rows.shape, jnp.int32),
            pltpu.VMEM(query.shape, BF16), pltpu.VMEM(key.shape, BF16), pltpu.VMEM(grad.shape, BF16),
            pltpu.VMEM((1, tokens), jnp.int32), pltpu.VMEM((1, tokens), jnp.int32),
            pltpu.SemaphoreType.DMA((12,)),
        ],
        compiler_params=pltpu.CompilerParams(vmem_limit_bytes=24 * MIB),
        cost_estimate=FREE,
        name="front",
    )(*[arg if arg is exponent else pltpu.with_memory_space_constraint(arg, pltpu.HBM) for arg in args])


CORE, Y, X, Z1, Z2 = 8, 16, 1, 2, 4


def routed(value, odd, even):
    owners = lax.axis_size("fsdp")
    count = lax.axis_size("dp") * owners
    return lax.ppermute(
        value, ("dp", "fsdp"), [(i, i ^ (odd if i // owners % 2 else even)) for i in range(count)]
    )


def xor_permute(value, mask):
    return routed(value, mask, mask)


def partial_kernel(parts, own_ref, near_ref, v0_ref, v1_ref, *out_refs):
    dp = lax.axis_index("dp")
    fsdp = lax.axis_index("fsdp")
    odd = dp & 1

    def pick(choices):
        return choices[0] + odd * (choices[1] - choices[0])

    for units, out_ref in zip(parts, out_refs):
        for number, (odd_unit, even_unit) in enumerate(units):
            z, y, x, part = (pick(pair) for pair in zip(even_unit, odd_unit))
            owner = fsdp ^ (z * 2 + x)
            quarter = (dp - odd) ^ (y * 2)
            column = pl.ds(pl.multiple_of(owner * (4 * LANE) + quarter * LANE, 2 * LANE), 2 * LANE)
            some = pl.ds(pl.multiple_of(part * (2 * LANE), 2 * LANE), 2 * LANE)
            total = lax.dot_general(
                jnp.concatenate([own_ref[:, column], near_ref[:, column]], axis=0),
                jnp.concatenate([ref[pl.ds(0, 2 * HALF), some] for ref in (v0_ref, v1_ref)], axis=0),
                (((0,), (0,)), ((), ())),
                preferred_element_type=F32,
            )
            out_ref[pl.ds(number * (2 * LANE), 2 * LANE), :] = total.astype(out_ref.dtype)


def partial_sums(parts, dtype, own, near, v0, v1):
    return pl.pallas_call(
        functools.partial(partial_kernel, parts),
        in_specs=[VMEM] * 4,
        out_specs=[VMEM] * len(parts),
        out_shape=[jax.ShapeDtypeStruct((2 * HALF * len(units), 2 * HALF), dtype) for units in parts],
        compiler_params=pltpu.CompilerParams(vmem_limit_bytes=24 * MIB),
        cost_estimate=FREE,
        name="partial_sums",
    )(own, near, v0, v1)


def inner_swap_kernel(v0_ref, v1_ref, out_ref, window_ref):
    tokens = out_ref.shape[0]
    infos = [ref[pl.ds(tokens, INFO), pl.ds(0, HALF)].astype(F32).astype(jnp.int32) for ref in (v0_ref, v1_ref)]

    def table(device, entry):
        return jnp.broadcast_to(infos[device][entry:entry + 1, :], (HALF, HALF))

    place = lax.broadcasted_iota(jnp.int32, (HALF, HALF), 0) + HALF
    inner = lax.broadcasted_iota(jnp.int32, (HALF, HALF), 1) + HALF
    first = table(0, 0)
    moved = (place >= first) & (place < first + table(0, 1))
    stays = jnp.where(~moved & (place == inner), 1.0, 0.0).astype(BF16)
    comes = jnp.where(moved & (place + table(1, 0) - first == inner), 1.0, 0.0).astype(BF16)
    taken = jnp.where(place - HALF + table(0, 2) == inner, 1.0, 0.0).astype(BF16)[:CAP]
    rows = (
        jnp.dot(stays, v0_ref[pl.ds(HALF, HALF), :], preferred_element_type=F32)
        + jnp.dot(comes, v1_ref[pl.ds(HALF, HALF), :], preferred_element_type=F32)
    ).astype(BF16)
    out_ref[pl.ds(0, HALF), :] = v0_ref[pl.ds(0, HALF), :]
    out_ref[pl.ds(HALF, HALF), :] = rows
    window_ref[...] = jnp.dot(taken, rows, preferred_element_type=F32).astype(BF16)


def inner_swap(v0, v1):
    return pl.pallas_call(
        inner_swap_kernel,
        in_specs=[VMEM] * 2,
        out_specs=[VMEM] * 2,
        out_shape=[jax.ShapeDtypeStruct((2 * HALF, 512), BF16), jax.ShapeDtypeStruct((CAP, 512), BF16)],
        compiler_params=pltpu.CompilerParams(vmem_limit_bytes=8 * MIB),
        cost_estimate=FREE,
        name="inner_swap",
    )(v0, v1)


def outer_swap_kernel(v0_ref, rows_ref, window_ref, out_ref):
    tokens = out_ref.shape[0]
    info = v0_ref[pl.ds(tokens, INFO), pl.ds(0, HALF)].astype(F32).astype(jnp.int32)
    first = jnp.broadcast_to(info[2:3, :], (HALF, HALF))
    extent = jnp.broadcast_to(info[3:4, :], (HALF, HALF))
    place = lax.broadcasted_iota(jnp.int32, (HALF, HALF), 0) + HALF
    inner = lax.broadcasted_iota(jnp.int32, (HALF, HALF), 1)
    moved = (place >= first) & (place < first + extent)
    stays = jnp.where(~moved & (place == inner + HALF), 1.0, 0.0).astype(BF16)
    comes = jnp.where(moved & (place - first == inner), 1.0, 0.0).astype(BF16)[:, :CAP]
    out_ref[pl.ds(0, HALF), :] = rows_ref[pl.ds(0, HALF), :]
    out_ref[pl.ds(HALF, HALF), :] = (
        jnp.dot(stays, rows_ref[pl.ds(HALF, HALF), :], preferred_element_type=F32)
        + jnp.dot(comes, window_ref[...], preferred_element_type=F32)
    ).astype(BF16)


def outer_swap(v0, rows, window):
    return pl.pallas_call(
        outer_swap_kernel,
        in_specs=[VMEM] * 3,
        out_specs=VMEM,
        out_shape=jax.ShapeDtypeStruct(rows.shape, BF16),
        compiler_params=pltpu.CompilerParams(vmem_limit_bytes=8 * MIB),
        cost_estimate=FREE,
        name="outer_swap",
    )(v0, rows, window)


def place_kernel(pair_ref, near_ref, out_ref):
    dp = lax.axis_index("dp")
    for ref, part in ((pair_ref, dp & 1), (near_ref, 1 - (dp & 1))):
        some = pl.ds(pl.multiple_of(part * (2 * LANE), 2 * LANE), 2 * LANE)
        for flip in range(2):
            rows = pl.ds(pl.multiple_of(((dp >> 1) ^ flip) * (2 * LANE), 2 * LANE), 2 * LANE)
            out_ref[rows, some] = ref[flip].astype(F32)


def place(pair, near):
    return pl.pallas_call(
        place_kernel,
        in_specs=[VMEM] * 2,
        out_specs=VMEM,
        out_shape=jax.ShapeDtypeStruct((512, 512), F32),
        compiler_params=pltpu.CompilerParams(vmem_limit_bytes=8 * MIB),
        cost_estimate=FREE,
        name="place",
    )(pair, near)


def fold_kernel(base_ref, arrived_ref, out_ref):
    out_ref[...] = base_ref[...] + arrived_ref[...].astype(F32)


def fold(base, arrived):
    return pl.pallas_call(
        fold_kernel,
        in_specs=[VMEM] * 2,
        out_specs=VMEM,
        out_shape=jax.ShapeDtypeStruct(base.shape, F32),
        compiler_params=pltpu.CompilerParams(vmem_limit_bytes=8 * MIB),
        cost_estimate=pl.CostEstimate(flops=8_000_000_000, bytes_accessed=0, transcendentals=0),
        name="fold",
    )(base, arrived)


def reduce_by_axis(layer_input, *args):
    near = xor_permute(layer_input, CORE)
    v0, odd = front(*args)
    odd = odd[:1] > 0.5
    v1 = xor_permute(v0, CORE)
    both = 2 * LANE

    def sums(parts, dtype):
        return partial_sums(parts, dtype, layer_input, near, v0, v1)

    def after_all(*values):
        return lax.optimization_barrier(values)

    def add(*terms):
        total = terms[0]
        for term in terms[1:]:
            total = total + term.astype(F32)
        return total

    def chain(z, y, x):
        return ((z, y, x, 0), (z, y, x, 1))

    def own(z, far, part):
        return ((z, far, 1, part), (z, far, 0, part)) if part == 0 else ((z, 1, far, part), (z, 0, far, part))

    def parts(*pairs):
        return [tuple(zip(*pair)) for pair in pairs]

    first, second = sums(parts((chain(3, 1, 1), own(1, 1, 0)), (chain(2, 1, 1), own(1, 1, 1))), BF16)
    third, spare = sums(parts((chain(3, 0, 1), own(1, 0, 0)), (chain(2, 1, 0), own(1, 0, 1))), BF16)
    keep1, keep2 = sums(parts((chain(3, 1, 0), own(0, 1, 0)), (chain(2, 0, 1), own(0, 1, 1))), F32)
    keep3, keep4 = sums(parts((chain(3, 0, 0), own(0, 0, 0)), (chain(2, 0, 0), own(0, 0, 1))), F32)
    first = routed(first, X, Z1)
    second = routed(second, Y, Z1)
    third = routed(third, X, Z1)
    total1 = add(keep1, first)
    fourth = jnp.where(odd, total1.astype(BF16), spare)
    second = after_all(second, fourth)[0]
    fourth = routed(fourth, Y, Z1)
    total2 = add(keep2, second)
    fifth = jnp.where(odd, spare, total2.astype(BF16))
    sixth = jnp.where(odd, total2, total1).astype(BF16)
    rows, window = inner_swap(after_all(v0, spare)[0], v1)
    third, fourth, window = after_all(third, fourth, window, fifth, sixth)[:3]
    fifth = routed(fifth, Y, X)
    sixth = routed(sixth, X, Y)
    total3 = add(keep3, third)
    joined = add(total3, fourth).astype(BF16)
    fourth, fifth, sixth = after_all(fourth, fifth, sixth, joined)[:3]
    joined = routed(joined, Z1, X)
    rest = add(keep4, fifth)
    some = add(total3, sixth)
    rest = jnp.where(odd, add(rest, sixth, joined), add(rest, fourth))
    last1 = rest[:both].astype(BF16)
    last2 = jnp.where(odd, rest[both:], some[:both]).astype(BF16)
    window = xor_permute(after_all(window, last1, last2)[0], Y)
    last1 = routed(last1, Z2, Y)
    last2 = routed(last2, Z2, X)
    last1, window = after_all(last1, window)
    crossed = xor_permute(jnp.where(odd, last1, add(rest[both:], last1).astype(BF16)), CORE)
    mine = add(fold(jnp.where(odd, 0.0, some[both:]), last2), crossed).astype(BF16)
    from_y = xor_permute(mine, Y)
    value_grad = outer_swap(v0, rows, after_all(window, from_y)[0])
    pair = jnp.stack([mine, from_y])
    return place(pair, xor_permute(pair, CORE)), value_grad


def swapped(block, axis, distance):
    count = lax.axis_size(axis)
    route = []
    for low in range(count):
        high = low | 1 << distance
        if high != low and high < count:
            route += [(low, high), (high, low)]
    return lax.ppermute(block, axis, route)


def blend_rows(item, incoming, offset, extent):
    inside = (jnp.arange(CAP) < extent)[:, None]
    chosen = jnp.where(inside, incoming, lax.dynamic_slice_in_dim(item, offset, CAP, 0))
    return lax.dynamic_update_slice_in_dim(item, chosen, offset, 0)


def reduce_by_owner(layer_input, *args):
    swap_start, swap_rows = args[-2:]
    tokens = layer_input.shape[0]
    values = front(*args)[0][:tokens]
    balanced = values
    for level in range(lax.axis_size("dp").bit_length() - 1):
        offset = swap_start[0, level]
        window = lax.dynamic_slice_in_dim(balanced, offset, CAP, 0)
        balanced = blend_rows(balanced, swapped(window, "dp", level), offset, swap_rows[0, level])
    owners = lax.axis_size("fsdp")
    owned = (D + owners - 1) // owners
    padded = jnp.pad(layer_input, ((0, 0), (0, owned * owners - D)))
    arranged = lax.all_to_all(
        padded.reshape(tokens, owners, owned), "fsdp", split_axis=1, concat_axis=0, tiled=True
    )
    block = lax.dot_general(
        arranged.reshape(-1, owned),
        lax.all_gather(values, "fsdp", axis=0, tiled=True),
        (((0,), (0,)), ((), ())),
        preferred_element_type=F32,
    )
    return lax.psum(block, "dp"), balanced


def on_device(layer_input, *args):
    if lax.axis_size("dp") == 4 and lax.axis_size("fsdp") == 8:
        return reduce_by_axis(layer_input, *args)
    return reduce_by_owner(layer_input, *args)


def solution(mesh):
    return jax.shard_map(
        on_device,
        mesh=mesh,
        in_specs=(
            P(("dp", "fsdp"), None),
            P(("dp", "fsdp"), None),
            P(("dp", "fsdp"), None),
            P(("dp", "fsdp"), None),
            P(("dp", "fsdp")),
            P(("dp", "fsdp")),
            P(),
            P(("dp", "fsdp")),
            P(("dp", "fsdp"), None),
            P(("dp", "fsdp"), None),
        ),
        out_specs=(P("fsdp", None), P(("dp", "fsdp"), None)),
        check_vma=False,
    )
```

```python
import functools
import math

import jax
import jax.numpy as jnp
from jax import lax
from jax.experimental import pallas as pl
from jax.experimental.pallas import tpu as pltpu
from jax.sharding import PartitionSpec as P

D = 4096
HD = 128
CAP = 32
HALF = 128
SEG = 16
LANE = 128
INFO = 16
MIB = 1 << 20
FREE = pl.CostEstimate(flops=0, bytes_accessed=0, transcendentals=0)
BF16 = jnp.bfloat16
F32 = jnp.float32

VMEM = pl.BlockSpec(memory_space=pltpu.VMEM)
HBM = pl.BlockSpec(memory_space=pltpu.HBM)


def attend_half(per_group, folded, span, q_ref, k_ref, g_ref, allowed, factor):
    heads = q_ref.shape[1] // HD
    groups = heads // per_group
    scores = [
        lax.dot_general(
            k_ref[span, pl.ds(group * HD, HD)],
            jnp.concatenate(
                [q_ref[span, pl.ds((group * per_group + n) * HD, HD)] for n in range(per_group)], axis=0
            ),
            (((1,), (1,)), ((), ())),
            preferred_element_type=F32,
        )
        for group in range(groups)
    ]
    weighted = [
        (g_ref[span, pl.ds(head * HD, HD)].astype(F32) * factor).astype(BF16) for head in range(heads)
    ]
    if folded:
        block = lax.broadcasted_iota(jnp.int32, (SEG, HALF), 1) // SEG
    probs = []
    for head in range(heads):
        n = head % per_group
        own = scores[head // per_group][:, n * HALF:(n + 1) * HALF]
        if folded:
            own = fold_blocks(own, block)
        own = jnp.where(allowed, own, -1e30)
        expo = jnp.exp2((own - jnp.max(own, axis=0, keepdims=True)) * (HD ** (-0.5) * math.log2(math.e)))
        prob = (expo * (1.0 / jnp.sum(expo, axis=0, keepdims=True))).astype(BF16)
        if folded:
            prob = jnp.concatenate(
                [jnp.where(block == b, prob, jnp.zeros_like(prob)) for b in range(HALF // SEG)], axis=0
            )
        probs.append(prob)
    return [
        jnp.dot(
            jnp.concatenate(probs[head:head + per_group], axis=1),
            jnp.concatenate(weighted[head:head + per_group], axis=0),
            preferred_element_type=F32,
        ).astype(BF16)
        for head in range(0, heads, per_group)
    ]


def fold_blocks(square, block):
    total = square[:SEG]
    for b in range(1, HALF // SEG):
        total = jnp.where(block == b, square[b * SEG:(b + 1) * SEG], total)
    return total


def mask_and_factor(folded, span, loss_ref, exponent_ref, ids_ref, index_ref):
    exponent = exponent_ref[0]
    unscale = jnp.float32(1.0)
    for bit in range(5):
        unscale = unscale * jnp.where((exponent >> bit) & 1 == 1, jnp.float32(2.0 ** -(1 << bit)), 1.0)
    row = lax.broadcasted_iota(jnp.int32, (HALF, HALF), 0)
    col = lax.broadcasted_iota(jnp.int32, (HALF, HALF), 1)
    doc_i = jnp.broadcast_to(ids_ref[:, span], (HALF, HALF))
    allowed = (doc_i == doc_i.T) & (row <= col)
    if folded:
        allowed = fold_blocks(
            jnp.where(allowed, 1, 0), lax.broadcasted_iota(jnp.int32, (SEG, HALF), 1) // SEG
        ) == 1
    index = index_ref[:, span]
    factor = jnp.zeros((1, HALF), F32)
    for entry in range(loss_ref.shape[0]):
        factor = jnp.where(index == entry, loss_ref[entry], factor)
    return allowed, jnp.broadcast_to(factor * unscale, (HALF, HALF)).T


def front_kernel(
    per_group, loss_hbm, exponent_hbm, start_hbm, rows_hbm, q_hbm, k_hbm, g_hbm, ids_hbm, index_hbm, *rest
):
    v_ref, odd_ref, loss_ref, exponent_ref, start_ref, rows_ref, q_ref, k_ref, g_ref, ids_ref, index_ref, sems = rest
    count = 0

    def begin(source, target):
        nonlocal count
        copy = pltpu.make_async_copy(source, target, sems.at[count])
        copy.start()
        count += 1
        return copy

    small = [
        begin(source, target)
        for source, target in (
            (ids_hbm, ids_ref), (index_hbm, index_ref), (loss_hbm, loss_ref), (exponent_hbm, exponent_ref),
            (start_hbm, start_ref), (rows_hbm, rows_ref),
        )
    ]
    groups = k_ref.shape[1] // HD
    wide = per_group * HD
    loads = []
    for half in range(2):
        span = pl.ds(half * HALF, HALF)
        loads.append([
            begin(source.at[span, :], target.at[span, :])
            for source, target in ((q_hbm, q_ref), (k_hbm, k_ref), (g_hbm, g_ref))
        ])
    odd_ref[...] = jnp.broadcast_to((lax.axis_index("dp") & 1).astype(F32), odd_ref.shape)
    for copy in small:
        copy.wait()
    masks = [
        mask_and_factor(half == 1, pl.ds(half * HALF, HALF), loss_ref, exponent_ref, ids_ref, index_ref)
        for half in range(2)
    ]
    info_row = lax.broadcasted_iota(jnp.int32, (INFO, k_ref.shape[1]), 0)
    info = jnp.zeros(info_row.shape, jnp.int32)
    for level in range(min(start_ref.shape[1], INFO // 2)):
        info = jnp.where(info_row == 2 * level, start_ref[0, level], info)
        info = jnp.where(info_row == 2 * level + 1, rows_ref[0, level], info)
    v_ref[pl.ds(2 * HALF, INFO), :] = info.astype(F32).astype(BF16)
    for half in range(2):
        for copy in loads[half]:
            copy.wait()
        span = pl.ds(half * HALF, HALF)
        values = attend_half(per_group, half == 1, span, q_ref, k_ref, g_ref, *masks[half])
        for group, value in enumerate(values):
            v_ref[span, pl.ds(group * HD, HD)] = value


def front(query, key, grad, ids, index, loss, exponent, start, rows):
    tokens, key_width = key.shape
    per_group = query.shape[1] // key_width
    args = [
        loss, exponent, start, rows, query, key, grad, ids.reshape(1, tokens), index.reshape(1, tokens)
    ]
    return pl.pallas_call(
        functools.partial(front_kernel, per_group),
        in_specs=[HBM] * 9,
        out_specs=[VMEM] * 2,
        out_shape=[
            jax.ShapeDtypeStruct((tokens + INFO, key_width), BF16), jax.ShapeDtypeStruct((8, 2 * HALF), F32)
        ],
        scratch_shapes=[
            pltpu.SMEM(loss.shape, F32), pltpu.SMEM(exponent.shape, jnp.int32),
            pltpu.SMEM(start.shape, jnp.int32), pltpu.SMEM(rows.shape, jnp.int32),
            pltpu.VMEM(query.shape, BF16), pltpu.VMEM(key.shape, BF16), pltpu.VMEM(grad.shape, BF16),
            pltpu.VMEM((1, tokens), jnp.int32), pltpu.VMEM((1, tokens), jnp.int32),
            pltpu.SemaphoreType.DMA((12,)),
        ],
        compiler_params=pltpu.CompilerParams(vmem_limit_bytes=24 * MIB),
        cost_estimate=FREE,
        name="front",
    )(*[arg if arg is exponent else pltpu.with_memory_space_constraint(arg, pltpu.HBM) for arg in args])


CORE, Y, X, Z1, Z2 = 8, 16, 1, 2, 4


def routed(value, odd, even):
    owners = lax.axis_size("fsdp")
    count = lax.axis_size("dp") * owners
    return lax.ppermute(
        value, ("dp", "fsdp"), [(i, i ^ (odd if i // owners % 2 else even)) for i in range(count)]
    )


def xor_permute(value, mask):
    return routed(value, mask, mask)


def partial_kernel(parts, own_ref, near_ref, v0_ref, v1_ref, *out_refs):
    dp = lax.axis_index("dp")
    fsdp = lax.axis_index("fsdp")
    odd = dp & 1

    def pick(choices):
        return choices[0] + odd * (choices[1] - choices[0])

    for units, out_ref in zip(parts, out_refs):
        for number, (odd_unit, even_unit) in enumerate(units):
            z, y, x, part = (pick(pair) for pair in zip(even_unit, odd_unit))
            owner = fsdp ^ (z * 2 + x)
            quarter = (dp - odd) ^ (y * 2)
            column = pl.ds(pl.multiple_of(owner * (4 * LANE) + quarter * LANE, 2 * LANE), 2 * LANE)
            some = pl.ds(pl.multiple_of(part * (2 * LANE), 2 * LANE), 2 * LANE)
            total = lax.dot_general(
                jnp.concatenate([own_ref[:, column], near_ref[:, column]], axis=0),
                jnp.concatenate([ref[pl.ds(0, 2 * HALF), some] for ref in (v0_ref, v1_ref)], axis=0),
                (((0,), (0,)), ((), ())),
                preferred_element_type=F32,
            )
            out_ref[pl.ds(number * (2 * LANE), 2 * LANE), :] = total.astype(out_ref.dtype)


def partial_sums(parts, dtype, own, near, v0, v1):
    return pl.pallas_call(
        functools.partial(partial_kernel, parts),
        in_specs=[VMEM] * 4,
        out_specs=[VMEM] * len(parts),
        out_shape=[jax.ShapeDtypeStruct((2 * HALF * len(units), 2 * HALF), dtype) for units in parts],
        compiler_params=pltpu.CompilerParams(vmem_limit_bytes=24 * MIB),
        cost_estimate=FREE,
        name="partial_sums",
    )(own, near, v0, v1)


def inner_swap_kernel(v0_ref, v1_ref, out_ref, window_ref):
    tokens = out_ref.shape[0]
    infos = [ref[pl.ds(tokens, INFO), pl.ds(0, HALF)].astype(F32).astype(jnp.int32) for ref in (v0_ref, v1_ref)]

    def table(device, entry):
        return jnp.broadcast_to(infos[device][entry:entry + 1, :], (HALF, HALF))

    place = lax.broadcasted_iota(jnp.int32, (HALF, HALF), 0) + HALF
    inner = lax.broadcasted_iota(jnp.int32, (HALF, HALF), 1) + HALF
    first = table(0, 0)
    moved = (place >= first) & (place < first + table(0, 1))
    stays = jnp.where(~moved & (place == inner), 1.0, 0.0).astype(BF16)
    comes = jnp.where(moved & (place + table(1, 0) - first == inner), 1.0, 0.0).astype(BF16)
    taken = jnp.where(place - HALF + table(0, 2) == inner, 1.0, 0.0).astype(BF16)[:CAP]
    rows = (
        jnp.dot(stays, v0_ref[pl.ds(HALF, HALF), :], preferred_element_type=F32)
        + jnp.dot(comes, v1_ref[pl.ds(HALF, HALF), :], preferred_element_type=F32)
    ).astype(BF16)
    out_ref[pl.ds(0, HALF), :] = v0_ref[pl.ds(0, HALF), :]
    out_ref[pl.ds(HALF, HALF), :] = rows
    window_ref[...] = jnp.dot(taken, rows, preferred_element_type=F32).astype(BF16)


def inner_swap(v0, v1):
    return pl.pallas_call(
        inner_swap_kernel,
        in_specs=[VMEM] * 2,
        out_specs=[VMEM] * 2,
        out_shape=[jax.ShapeDtypeStruct((2 * HALF, 512), BF16), jax.ShapeDtypeStruct((CAP, 512), BF16)],
        compiler_params=pltpu.CompilerParams(vmem_limit_bytes=8 * MIB),
        cost_estimate=FREE,
        name="inner_swap",
    )(v0, v1)


def outer_swap_kernel(v0_ref, rows_ref, window_ref, out_ref):
    tokens = out_ref.shape[0]
    info = v0_ref[pl.ds(tokens, INFO), pl.ds(0, HALF)].astype(F32).astype(jnp.int32)
    first = jnp.broadcast_to(info[2:3, :], (HALF, HALF))
    extent = jnp.broadcast_to(info[3:4, :], (HALF, HALF))
    place = lax.broadcasted_iota(jnp.int32, (HALF, HALF), 0) + HALF
    inner = lax.broadcasted_iota(jnp.int32, (HALF, HALF), 1)
    moved = (place >= first) & (place < first + extent)
    stays = jnp.where(~moved & (place == inner + HALF), 1.0, 0.0).astype(BF16)
    comes = jnp.where(moved & (place - first == inner), 1.0, 0.0).astype(BF16)[:, :CAP]
    out_ref[pl.ds(0, HALF), :] = rows_ref[pl.ds(0, HALF), :]
    out_ref[pl.ds(HALF, HALF), :] = (
        jnp.dot(stays, rows_ref[pl.ds(HALF, HALF), :], preferred_element_type=F32)
        + jnp.dot(comes, window_ref[...], preferred_element_type=F32)
    ).astype(BF16)


def outer_swap(v0, rows, window):
    return pl.pallas_call(
        outer_swap_kernel,
        in_specs=[VMEM] * 3,
        out_specs=VMEM,
        out_shape=jax.ShapeDtypeStruct(rows.shape, BF16),
        compiler_params=pltpu.CompilerParams(vmem_limit_bytes=8 * MIB),
        cost_estimate=FREE,
        name="outer_swap",
    )(v0, rows, window)


def place_kernel(pair_ref, near_ref, out_ref):
    dp = lax.axis_index("dp")
    for ref, part in ((pair_ref, dp & 1), (near_ref, 1 - (dp & 1))):
        some = pl.ds(pl.multiple_of(part * (2 * LANE), 2 * LANE), 2 * LANE)
        for flip in range(2):
            rows = pl.ds(pl.multiple_of(((dp >> 1) ^ flip) * (2 * LANE), 2 * LANE), 2 * LANE)
            out_ref[rows, some] = ref[flip].astype(F32)


def place(pair, near):
    return pl.pallas_call(
        place_kernel,
        in_specs=[VMEM] * 2,
        out_specs=VMEM,
        out_shape=jax.ShapeDtypeStruct((512, 512), F32),
        compiler_params=pltpu.CompilerParams(vmem_limit_bytes=8 * MIB),
        cost_estimate=FREE,
        name="place",
    )(pair, near)


def fold_kernel(base_ref, arrived_ref, odd_ref, out_ref):
    out_ref[...] = jnp.where(odd_ref[:1, :] > 0.5, arrived_ref[...].astype(F32), base_ref[...])


def fold(base, arrived, odd):
    return pl.pallas_call(
        fold_kernel,
        in_specs=[VMEM] * 3,
        out_specs=VMEM,
        out_shape=jax.ShapeDtypeStruct(base.shape, F32),
        compiler_params=pltpu.CompilerParams(vmem_limit_bytes=8 * MIB),
        cost_estimate=pl.CostEstimate(flops=8_000_000_000, bytes_accessed=0, transcendentals=0),
        name="fold",
    )(base, arrived, odd)


def reduce_by_axis(layer_input, *args):
    near = xor_permute(layer_input, CORE)
    v0, odd_row = front(*args)
    odd = odd_row[:1] > 0.5
    v1 = xor_permute(v0, CORE)
    both = 2 * LANE

    def sums(parts, dtype):
        return partial_sums(parts, dtype, layer_input, near, v0, v1)

    def after_all(*values):
        return lax.optimization_barrier(values)

    def add(*terms):
        total = terms[0]
        for term in terms[1:]:
            total = total + term.astype(F32)
        return total

    def chain(z, y, x):
        return ((z, y, x, 0), (z, y, x, 1))

    def own(z, far, part):
        return ((z, far, 1, part), (z, far, 0, part)) if part == 0 else ((z, 1, far, part), (z, 0, far, part))

    def parts(*pairs):
        return [tuple(zip(*pair)) for pair in pairs]

    first, second = sums(parts((chain(3, 1, 1), own(1, 1, 0)), (chain(2, 1, 1), own(1, 1, 1))), BF16)
    third, spare = sums(parts((chain(3, 0, 1), own(1, 0, 0)), (chain(2, 1, 0), own(1, 0, 1))), BF16)
    keep1, keep2 = sums(parts((chain(3, 1, 0), own(0, 1, 0)), (chain(2, 0, 1), own(0, 1, 1))), F32)
    keep3, keep4 = sums(parts((chain(3, 0, 0), own(0, 0, 0)), (chain(2, 0, 0), own(0, 0, 1))), F32)
    first = routed(first, X, Z1)
    second = routed(second, Y, Z1)
    third = routed(third, X, Z1)
    fourth = add(keep1, first).astype(BF16)
    second = after_all(second, fourth)[0]
    sixth = add(keep2, second).astype(BF16)
    fifth, sixth = after_all(spare, sixth)
    rows, window = inner_swap(after_all(v0, spare)[0], v1)
    fourth = routed(fourth, Y, Y)
    fifth = routed(fifth, Y, Z1)
    third, fourth, window = after_all(third, fourth, window, sixth)[:3]
    sixth = routed(sixth, X, X)
    some = add(keep3, third, fourth)
    joined = some.astype(BF16)
    fifth, sixth = after_all(fifth, sixth, joined)[:2]
    joined = routed(joined, Z1, X)
    rest = add(keep4, fifth, sixth)
    crossing = add(rest, joined)
    last1 = jnp.where(odd, crossing[:both], rest[:both]).astype(BF16)
    last2 = crossing[both:].astype(BF16)
    window = xor_permute(after_all(window, last1, last2)[0], Y)
    last1 = routed(last1, Z2, Y)
    last2 = routed(last2, Z2, X)
    last1, window = after_all(last1, window)
    crossed = xor_permute(jnp.where(odd, last1, add(rest[both:], last1).astype(BF16)), CORE)
    base = fold(add(some[both:], joined[:both]), last2, odd_row)
    mine = add(base, crossed).astype(BF16)
    from_y = xor_permute(mine, Y)
    value_grad = outer_swap(v0, rows, after_all(window, from_y)[0])
    pair = jnp.stack([mine, from_y])
    return place(pair, xor_permute(pair, CORE)), value_grad


def swapped(block, axis, distance):
    count = lax.axis_size(axis)
    route = []
    for low in range(count):
        high = low | 1 << distance
        if high != low and high < count:
            route += [(low, high), (high, low)]
    return lax.ppermute(block, axis, route)


def blend_rows(item, incoming, offset, extent):
    inside = (jnp.arange(CAP) < extent)[:, None]
    chosen = jnp.where(inside, incoming, lax.dynamic_slice_in_dim(item, offset, CAP, 0))
    return lax.dynamic_update_slice_in_dim(item, chosen, offset, 0)


def reduce_by_owner(layer_input, *args):
    swap_start, swap_rows = args[-2:]
    tokens = layer_input.shape[0]
    values = front(*args)[0][:tokens]
    balanced = values
    for level in range(lax.axis_size("dp").bit_length() - 1):
        offset = swap_start[0, level]
        window = lax.dynamic_slice_in_dim(balanced, offset, CAP, 0)
        balanced = blend_rows(balanced, swapped(window, "dp", level), offset, swap_rows[0, level])
    owners = lax.axis_size("fsdp")
    owned = (D + owners - 1) // owners
    padded = jnp.pad(layer_input, ((0, 0), (0, owned * owners - D)))
    arranged = lax.all_to_all(
        padded.reshape(tokens, owners, owned), "fsdp", split_axis=1, concat_axis=0, tiled=True
    )
    block = lax.dot_general(
        arranged.reshape(-1, owned),
        lax.all_gather(values, "fsdp", axis=0, tiled=True),
        (((0,), (0,)), ((), ())),
        preferred_element_type=F32,
    )
    return lax.psum(block, "dp"), balanced


def on_device(layer_input, *args):
    if lax.axis_size("dp") == 4 and lax.axis_size("fsdp") == 8:
        return reduce_by_axis(layer_input, *args)
    return reduce_by_owner(layer_input, *args)


def solution(mesh):
    return jax.shard_map(
        on_device,
        mesh=mesh,
        in_specs=(
            P(("dp", "fsdp"), None),
            P(("dp", "fsdp"), None),
            P(("dp", "fsdp"), None),
            P(("dp", "fsdp"), None),
            P(("dp", "fsdp")),
            P(("dp", "fsdp")),
            P(),
            P(("dp", "fsdp")),
            P(("dp", "fsdp"), None),
            P(("dp", "fsdp"), None),
        ),
        out_specs=(P("fsdp", None), P(("dp", "fsdp"), None)),
        check_vma=False,
    )
```

```python
import functools
import math

import jax
import jax.numpy as jnp
from jax import lax
from jax.experimental import pallas as pl
from jax.experimental.pallas import tpu as pltpu
from jax.sharding import PartitionSpec as P

D = 4096
HD = 128
CAP = 32
HALF = 128
SEG = 16
LANE = 128
INFO = 16
MIB = 1 << 20
FREE = pl.CostEstimate(flops=0, bytes_accessed=0, transcendentals=0)
BF16 = jnp.bfloat16
F32 = jnp.float32

VMEM = pl.BlockSpec(memory_space=pltpu.VMEM)
HBM = pl.BlockSpec(memory_space=pltpu.HBM)


def attend_half(per_group, folded, span, q_ref, k_ref, g_ref, allowed, factor):
    heads = q_ref.shape[1] // HD
    groups = heads // per_group
    scores = [
        lax.dot_general(
            k_ref[span, pl.ds(group * HD, HD)],
            jnp.concatenate(
                [q_ref[span, pl.ds((group * per_group + n) * HD, HD)] for n in range(per_group)], axis=0
            ),
            (((1,), (1,)), ((), ())),
            preferred_element_type=F32,
        )
        for group in range(groups)
    ]
    weighted = [
        (g_ref[span, pl.ds(head * HD, HD)].astype(F32) * factor).astype(BF16) for head in range(heads)
    ]
    if folded:
        block = lax.broadcasted_iota(jnp.int32, (SEG, HALF), 1) // SEG
    probs = []
    for head in range(heads):
        n = head % per_group
        own = scores[head // per_group][:, n * HALF:(n + 1) * HALF]
        if folded:
            own = fold_blocks(own, block)
        own = jnp.where(allowed, own, -1e30)
        expo = jnp.exp2((own - jnp.max(own, axis=0, keepdims=True)) * (HD ** (-0.5) * math.log2(math.e)))
        prob = (expo * (1.0 / jnp.sum(expo, axis=0, keepdims=True))).astype(BF16)
        if folded:
            prob = jnp.concatenate(
                [jnp.where(block == b, prob, jnp.zeros_like(prob)) for b in range(HALF // SEG)], axis=0
            )
        probs.append(prob)
    return [
        jnp.dot(
            jnp.concatenate(probs[head:head + per_group], axis=1),
            jnp.concatenate(weighted[head:head + per_group], axis=0),
            preferred_element_type=F32,
        ).astype(BF16)
        for head in range(0, heads, per_group)
    ]


def fold_blocks(square, block):
    total = square[:SEG]
    for b in range(1, HALF // SEG):
        total = jnp.where(block == b, square[b * SEG:(b + 1) * SEG], total)
    return total


def mask_and_factor(folded, span, loss_ref, exponent_ref, ids_ref, index_ref):
    exponent = exponent_ref[0]
    unscale = jnp.float32(1.0)
    for bit in range(5):
        unscale = unscale * jnp.where((exponent >> bit) & 1 == 1, jnp.float32(2.0 ** -(1 << bit)), 1.0)
    row = lax.broadcasted_iota(jnp.int32, (HALF, HALF), 0)
    col = lax.broadcasted_iota(jnp.int32, (HALF, HALF), 1)
    doc_i = jnp.broadcast_to(ids_ref[:, span], (HALF, HALF))
    allowed = (doc_i == doc_i.T) & (row <= col)
    if folded:
        allowed = fold_blocks(
            jnp.where(allowed, 1, 0), lax.broadcasted_iota(jnp.int32, (SEG, HALF), 1) // SEG
        ) == 1
    index = index_ref[:, span]
    factor = jnp.zeros((1, HALF), F32)
    for entry in range(loss_ref.shape[0]):
        factor = jnp.where(index == entry, loss_ref[entry], factor)
    return allowed, jnp.broadcast_to(factor * unscale, (HALF, HALF)).T


def front_kernel(
    per_group, loss_hbm, exponent_hbm, start_hbm, rows_hbm, q_hbm, k_hbm, g_hbm, ids_hbm, index_hbm, *rest
):
    v_ref, lead_ref, loss_ref, exponent_ref, start_ref, rows_ref, q_ref, k_ref, g_ref, ids_ref, index_ref, sems = rest
    count = 0

    def begin(source, target):
        nonlocal count
        copy = pltpu.make_async_copy(source, target, sems.at[count])
        copy.start()
        count += 1
        return copy

    small = [
        begin(source, target)
        for source, target in (
            (ids_hbm, ids_ref), (index_hbm, index_ref), (loss_hbm, loss_ref), (exponent_hbm, exponent_ref),
            (start_hbm, start_ref), (rows_hbm, rows_ref),
        )
    ]
    groups = k_ref.shape[1] // HD
    wide = per_group * HD
    loads = []
    for half in range(2):
        span = pl.ds(half * HALF, HALF)
        loads.append([
            begin(source.at[span, :], target.at[span, :])
            for source, target in ((q_hbm, q_ref), (k_hbm, k_ref), (g_hbm, g_ref))
        ])
    lead_ref[...] = jnp.broadcast_to((1 - (lax.axis_index("dp") & 1)).astype(F32), lead_ref.shape)
    for copy in small:
        copy.wait()
    masks = [
        mask_and_factor(half == 1, pl.ds(half * HALF, HALF), loss_ref, exponent_ref, ids_ref, index_ref)
        for half in range(2)
    ]
    info_row = lax.broadcasted_iota(jnp.int32, (INFO, k_ref.shape[1]), 0)
    info = jnp.zeros(info_row.shape, jnp.int32)
    for level in range(min(start_ref.shape[1], INFO // 2)):
        info = jnp.where(info_row == 2 * level, start_ref[0, level], info)
        info = jnp.where(info_row == 2 * level + 1, rows_ref[0, level], info)
    v_ref[pl.ds(2 * HALF, INFO), :] = info.astype(F32).astype(BF16)
    for half in range(2):
        for copy in loads[half]:
            copy.wait()
        span = pl.ds(half * HALF, HALF)
        values = attend_half(per_group, half == 1, span, q_ref, k_ref, g_ref, *masks[half])
        for group, value in enumerate(values):
            v_ref[span, pl.ds(group * HD, HD)] = value


def front(query, key, grad, ids, index, loss, exponent, start, rows):
    tokens, key_width = key.shape
    per_group = query.shape[1] // key_width
    args = [
        loss, exponent, start, rows, query, key, grad, ids.reshape(1, tokens), index.reshape(1, tokens)
    ]
    return pl.pallas_call(
        functools.partial(front_kernel, per_group),
        in_specs=[HBM] * 9,
        out_specs=[VMEM] * 2,
        out_shape=[
            jax.ShapeDtypeStruct((tokens + INFO, key_width), BF16), jax.ShapeDtypeStruct((8, 2 * HALF), F32)
        ],
        scratch_shapes=[
            pltpu.SMEM(loss.shape, F32), pltpu.SMEM(exponent.shape, jnp.int32),
            pltpu.SMEM(start.shape, jnp.int32), pltpu.SMEM(rows.shape, jnp.int32),
            pltpu.VMEM(query.shape, BF16), pltpu.VMEM(key.shape, BF16), pltpu.VMEM(grad.shape, BF16),
            pltpu.VMEM((1, tokens), jnp.int32), pltpu.VMEM((1, tokens), jnp.int32),
            pltpu.SemaphoreType.DMA((12,)),
        ],
        compiler_params=pltpu.CompilerParams(vmem_limit_bytes=24 * MIB),
        cost_estimate=FREE,
        name="front",
    )(*[arg if arg is exponent else pltpu.with_memory_space_constraint(arg, pltpu.HBM) for arg in args])


CORE, Y, X, Z1, Z2 = 8, 16, 1, 2, 4


def routed(value, lead, other):
    owners = lax.axis_size("fsdp")
    count = lax.axis_size("dp") * owners
    return lax.ppermute(
        value, ("dp", "fsdp"), [(i, i ^ (other if i // owners % 2 else lead)) for i in range(count)]
    )


def xor_permute(value, mask):
    return routed(value, mask, mask)


def partial_kernel(parts, own_ref, near_ref, v0_ref, v1_ref, *out_refs):
    dp = lax.axis_index("dp")
    fsdp = lax.axis_index("fsdp")
    core = dp & 1

    def pick(choices):
        return choices[0] + core * (choices[1] - choices[0])

    for units, out_ref in zip(parts, out_refs):
        for number, (lead_unit, other_unit) in enumerate(units):
            z, y, x, part = (pick(pair) for pair in zip(lead_unit, other_unit))
            owner = fsdp ^ (z * 2 + x)
            quarter = (dp - core) ^ (y * 2)
            column = pl.ds(pl.multiple_of(owner * (4 * LANE) + quarter * LANE, 2 * LANE), 2 * LANE)
            some = pl.ds(pl.multiple_of(part * (2 * LANE), 2 * LANE), 2 * LANE)
            total = lax.dot_general(
                jnp.concatenate([own_ref[:, column], near_ref[:, column]], axis=0),
                jnp.concatenate([ref[pl.ds(0, 2 * HALF), some] for ref in (v0_ref, v1_ref)], axis=0),
                (((0,), (0,)), ((), ())),
                preferred_element_type=F32,
            )
            out_ref[pl.ds(number * (2 * LANE), 2 * LANE), :] = total.astype(out_ref.dtype)


def partial_sums(parts, dtype, own, near, v0, v1):
    return pl.pallas_call(
        functools.partial(partial_kernel, parts),
        in_specs=[VMEM] * 4,
        out_specs=[VMEM] * len(parts),
        out_shape=[jax.ShapeDtypeStruct((2 * HALF * len(units), 2 * HALF), dtype) for units in parts],
        compiler_params=pltpu.CompilerParams(vmem_limit_bytes=24 * MIB),
        cost_estimate=FREE,
        name="partial_sums",
    )(own, near, v0, v1)


def inner_swap_kernel(v0_ref, v1_ref, out_ref, window_ref):
    tokens = out_ref.shape[0]
    infos = [ref[pl.ds(tokens, INFO), pl.ds(0, HALF)].astype(F32).astype(jnp.int32) for ref in (v0_ref, v1_ref)]

    def table(device, entry):
        return jnp.broadcast_to(infos[device][entry:entry + 1, :], (HALF, HALF))

    place = lax.broadcasted_iota(jnp.int32, (HALF, HALF), 0) + HALF
    inner = lax.broadcasted_iota(jnp.int32, (HALF, HALF), 1) + HALF
    first = table(0, 0)
    moved = (place >= first) & (place < first + table(0, 1))
    stays = jnp.where(~moved & (place == inner), 1.0, 0.0).astype(BF16)
    comes = jnp.where(moved & (place + table(1, 0) - first == inner), 1.0, 0.0).astype(BF16)
    taken = jnp.where(place - HALF + table(0, 2) == inner, 1.0, 0.0).astype(BF16)[:CAP]
    rows = (
        jnp.dot(stays, v0_ref[pl.ds(HALF, HALF), :], preferred_element_type=F32)
        + jnp.dot(comes, v1_ref[pl.ds(HALF, HALF), :], preferred_element_type=F32)
    ).astype(BF16)
    out_ref[pl.ds(0, HALF), :] = v0_ref[pl.ds(0, HALF), :]
    out_ref[pl.ds(HALF, HALF), :] = rows
    window_ref[...] = jnp.dot(taken, rows, preferred_element_type=F32).astype(BF16)


def inner_swap(v0, v1):
    return pl.pallas_call(
        inner_swap_kernel,
        in_specs=[VMEM] * 2,
        out_specs=[VMEM] * 2,
        out_shape=[jax.ShapeDtypeStruct((2 * HALF, 512), BF16), jax.ShapeDtypeStruct((CAP, 512), BF16)],
        compiler_params=pltpu.CompilerParams(vmem_limit_bytes=8 * MIB),
        cost_estimate=FREE,
        name="inner_swap",
    )(v0, v1)


def outer_swap_kernel(v0_ref, rows_ref, window_ref, out_ref):
    tokens = out_ref.shape[0]
    info = v0_ref[pl.ds(tokens, INFO), pl.ds(0, HALF)].astype(F32).astype(jnp.int32)
    first = jnp.broadcast_to(info[2:3, :], (HALF, HALF))
    extent = jnp.broadcast_to(info[3:4, :], (HALF, HALF))
    place = lax.broadcasted_iota(jnp.int32, (HALF, HALF), 0) + HALF
    inner = lax.broadcasted_iota(jnp.int32, (HALF, HALF), 1)
    moved = (place >= first) & (place < first + extent)
    stays = jnp.where(~moved & (place == inner + HALF), 1.0, 0.0).astype(BF16)
    comes = jnp.where(moved & (place - first == inner), 1.0, 0.0).astype(BF16)[:, :CAP]
    out_ref[pl.ds(0, HALF), :] = rows_ref[pl.ds(0, HALF), :]
    out_ref[pl.ds(HALF, HALF), :] = (
        jnp.dot(stays, rows_ref[pl.ds(HALF, HALF), :], preferred_element_type=F32)
        + jnp.dot(comes, window_ref[...], preferred_element_type=F32)
    ).astype(BF16)


def outer_swap(v0, rows, window):
    return pl.pallas_call(
        outer_swap_kernel,
        in_specs=[VMEM] * 3,
        out_specs=VMEM,
        out_shape=jax.ShapeDtypeStruct(rows.shape, BF16),
        compiler_params=pltpu.CompilerParams(vmem_limit_bytes=8 * MIB),
        cost_estimate=FREE,
        name="outer_swap",
    )(v0, rows, window)


def place_kernel(pair_ref, near_ref, out_ref):
    dp = lax.axis_index("dp")
    for ref, part in ((pair_ref, 1 - (dp & 1)), (near_ref, dp & 1)):
        some = pl.ds(pl.multiple_of(part * (2 * LANE), 2 * LANE), 2 * LANE)
        for flip in range(2):
            rows = pl.ds(pl.multiple_of(((dp >> 1) ^ flip) * (2 * LANE), 2 * LANE), 2 * LANE)
            out_ref[rows, some] = ref[flip].astype(F32)


def place(pair, near):
    return pl.pallas_call(
        place_kernel,
        in_specs=[VMEM] * 2,
        out_specs=VMEM,
        out_shape=jax.ShapeDtypeStruct((512, 512), F32),
        compiler_params=pltpu.CompilerParams(vmem_limit_bytes=8 * MIB),
        cost_estimate=FREE,
        name="place",
    )(pair, near)


def fold_kernel(base_ref, arrived_ref, lead_ref, out_ref):
    out_ref[...] = jnp.where(lead_ref[:1, :] > 0.5, arrived_ref[...].astype(F32), base_ref[...])


def fold(base, arrived, odd):
    return pl.pallas_call(
        fold_kernel,
        in_specs=[VMEM] * 3,
        out_specs=VMEM,
        out_shape=jax.ShapeDtypeStruct(base.shape, F32),
        compiler_params=pltpu.CompilerParams(vmem_limit_bytes=8 * MIB),
        cost_estimate=pl.CostEstimate(flops=8_000_000_000, bytes_accessed=0, transcendentals=0),
        name="fold",
    )(base, arrived, odd)


def reduce_by_axis(layer_input, *args):
    near = xor_permute(layer_input, CORE)
    v0, lead_row = front(*args)
    lead = lead_row[:1] > 0.5
    v1 = xor_permute(v0, CORE)
    both = 2 * LANE

    def sums(parts, dtype):
        return partial_sums(parts, dtype, layer_input, near, v0, v1)

    def after_all(*values):
        return lax.optimization_barrier(values)

    def add(*terms):
        total = terms[0]
        for term in terms[1:]:
            total = total + term.astype(F32)
        return total

    def chain(z, y, x):
        return ((z, y, x, 0), (z, y, x, 1))

    def own(z, far, part):
        return ((z, far, 1, part), (z, far, 0, part)) if part == 0 else ((z, 1, far, part), (z, 0, far, part))

    def parts(*pairs):
        return [tuple(zip(*pair)) for pair in pairs]

    first, second = sums(parts((chain(3, 1, 1), own(1, 1, 0)), (chain(2, 1, 1), own(1, 1, 1))), BF16)
    third, spare = sums(parts((chain(3, 0, 1), own(1, 0, 0)), (chain(2, 1, 0), own(1, 0, 1))), BF16)
    keep1, keep2 = sums(parts((chain(3, 1, 0), own(0, 1, 0)), (chain(2, 0, 1), own(0, 1, 1))), F32)
    keep3, keep4 = sums(parts((chain(3, 0, 0), own(0, 0, 0)), (chain(2, 0, 0), own(0, 0, 1))), F32)
    first = routed(first, X, Z1)
    second = routed(second, Y, Z1)
    third = routed(third, X, Z1)
    fourth = add(keep1, first).astype(BF16)
    second = after_all(second, fourth)[0]
    sixth = add(keep2, second).astype(BF16)
    fifth, sixth = after_all(spare, sixth)
    rows, window = inner_swap(after_all(v0, spare)[0], v1)
    fourth = routed(fourth, Y, Y)
    fifth = routed(fifth, Y, Z1)
    third, fourth, window = after_all(third, fourth, window, sixth)[:3]
    sixth = routed(sixth, X, X)
    some = add(keep3, third, fourth)
    joined = some.astype(BF16)
    fifth, sixth = after_all(fifth, sixth, joined)[:2]
    joined = routed(joined, Z1, X)
    rest = add(keep4, fifth, sixth)
    crossing = add(rest, joined)
    last1 = jnp.where(lead, crossing[:both], rest[:both]).astype(BF16)
    last2 = crossing[both:].astype(BF16)
    window = xor_permute(after_all(window, last1, last2)[0], Y)
    last1 = routed(last1, Z2, Y)
    last2 = routed(last2, Z2, X)
    last1, window = after_all(last1, window)
    crossed = xor_permute(jnp.where(lead, last1, add(rest[both:], last1).astype(BF16)), CORE)
    base = fold(add(some[both:], joined[:both]), last2, lead_row)
    mine = add(base, crossed).astype(BF16)
    from_y = xor_permute(mine, Y)
    value_grad = outer_swap(v0, rows, after_all(window, from_y)[0])
    pair = jnp.stack([mine, from_y])
    return place(pair, xor_permute(pair, CORE)), value_grad


def swapped(block, axis, distance):
    count = lax.axis_size(axis)
    route = []
    for low in range(count):
        high = low | 1 << distance
        if high != low and high < count:
            route += [(low, high), (high, low)]
    return lax.ppermute(block, axis, route)


def blend_rows(item, incoming, offset, extent):
    inside = (jnp.arange(CAP) < extent)[:, None]
    chosen = jnp.where(inside, incoming, lax.dynamic_slice_in_dim(item, offset, CAP, 0))
    return lax.dynamic_update_slice_in_dim(item, chosen, offset, 0)


def reduce_by_owner(layer_input, *args):
    swap_start, swap_rows = args[-2:]
    tokens = layer_input.shape[0]
    values = front(*args)[0][:tokens]
    balanced = values
    for level in range(lax.axis_size("dp").bit_length() - 1):
        offset = swap_start[0, level]
        window = lax.dynamic_slice_in_dim(balanced, offset, CAP, 0)
        balanced = blend_rows(balanced, swapped(window, "dp", level), offset, swap_rows[0, level])
    owners = lax.axis_size("fsdp")
    owned = (D + owners - 1) // owners
    padded = jnp.pad(layer_input, ((0, 0), (0, owned * owners - D)))
    arranged = lax.all_to_all(
        padded.reshape(tokens, owners, owned), "fsdp", split_axis=1, concat_axis=0, tiled=True
    )
    block = lax.dot_general(
        arranged.reshape(-1, owned),
        lax.all_gather(values, "fsdp", axis=0, tiled=True),
        (((0,), (0,)), ((), ())),
        preferred_element_type=F32,
    )
    return lax.psum(block, "dp"), balanced


def on_device(layer_input, *args):
    if lax.axis_size("dp") == 4 and lax.axis_size("fsdp") == 8:
        return reduce_by_axis(layer_input, *args)
    return reduce_by_owner(layer_input, *args)


def solution(mesh):
    return jax.shard_map(
        on_device,
        mesh=mesh,
        in_specs=(
            P(("dp", "fsdp"), None),
            P(("dp", "fsdp"), None),
            P(("dp", "fsdp"), None),
            P(("dp", "fsdp"), None),
            P(("dp", "fsdp")),
            P(("dp", "fsdp")),
            P(),
            P(("dp", "fsdp")),
            P(("dp", "fsdp"), None),
            P(("dp", "fsdp"), None),
        ),
        out_specs=(P("fsdp", None), P(("dp", "fsdp"), None)),
        check_vma=False,
    )
```

```python
import functools
import math

import jax
import jax.numpy as jnp
from jax import lax
from jax.experimental import pallas as pl
from jax.experimental.pallas import tpu as pltpu
from jax.sharding import PartitionSpec as P

D = 4096
HD = 128
CAP = 32
HALF = 128
SEG = 16
LANE = 128
INFO = 16
MIB = 1 << 20
FREE = pl.CostEstimate(flops=0, bytes_accessed=0, transcendentals=0)
BF16 = jnp.bfloat16
F32 = jnp.float32

VMEM = pl.BlockSpec(memory_space=pltpu.VMEM)
HBM = pl.BlockSpec(memory_space=pltpu.HBM)


def attend_half(per_group, folded, span, q_ref, k_ref, g_ref, allowed, factor):
    heads = q_ref.shape[1] // HD
    groups = heads // per_group
    scores = [
        lax.dot_general(
            k_ref[span, pl.ds(group * HD, HD)],
            jnp.concatenate(
                [q_ref[span, pl.ds((group * per_group + n) * HD, HD)] for n in range(per_group)], axis=0
            ),
            (((1,), (1,)), ((), ())),
            preferred_element_type=F32,
        )
        for group in range(groups)
    ]
    weighted = [
        (g_ref[span, pl.ds(head * HD, HD)].astype(F32) * factor).astype(BF16) for head in range(heads)
    ]
    if folded:
        block = lax.broadcasted_iota(jnp.int32, (SEG, HALF), 1) // SEG
    probs = []
    for head in range(heads):
        n = head % per_group
        own = scores[head // per_group][:, n * HALF:(n + 1) * HALF]
        if folded:
            own = fold_blocks(own, block)
        own = jnp.where(allowed, own, -1e30)
        expo = jnp.exp2((own - jnp.max(own, axis=0, keepdims=True)) * (HD ** (-0.5) * math.log2(math.e)))
        prob = (expo * (1.0 / jnp.sum(expo, axis=0, keepdims=True))).astype(BF16)
        if folded:
            prob = jnp.concatenate(
                [jnp.where(block == b, prob, jnp.zeros_like(prob)) for b in range(HALF // SEG)], axis=0
            )
        probs.append(prob)
    return [
        jnp.dot(
            jnp.concatenate(probs[head:head + per_group], axis=1),
            jnp.concatenate(weighted[head:head + per_group], axis=0),
            preferred_element_type=F32,
        ).astype(BF16)
        for head in range(0, heads, per_group)
    ]


def fold_blocks(square, block):
    total = square[:SEG]
    for b in range(1, HALF // SEG):
        total = jnp.where(block == b, square[b * SEG:(b + 1) * SEG], total)
    return total


def mask_and_factor(folded, span, loss_ref, exponent_ref, ids_ref, index_ref):
    exponent = exponent_ref[0]
    unscale = jnp.float32(1.0)
    for bit in range(5):
        unscale = unscale * jnp.where((exponent >> bit) & 1 == 1, jnp.float32(2.0 ** -(1 << bit)), 1.0)
    row = lax.broadcasted_iota(jnp.int32, (HALF, HALF), 0)
    col = lax.broadcasted_iota(jnp.int32, (HALF, HALF), 1)
    doc_i = jnp.broadcast_to(ids_ref[:, span], (HALF, HALF))
    allowed = (doc_i == doc_i.T) & (row <= col)
    if folded:
        allowed = fold_blocks(
            jnp.where(allowed, 1, 0), lax.broadcasted_iota(jnp.int32, (SEG, HALF), 1) // SEG
        ) == 1
    index = index_ref[:, span]
    factor = jnp.zeros((1, HALF), F32)
    for entry in range(loss_ref.shape[0]):
        factor = jnp.where(index == entry, loss_ref[entry], factor)
    return allowed, jnp.broadcast_to(factor * unscale, (HALF, HALF)).T


def front_kernel(
    per_group, loss_hbm, exponent_hbm, start_hbm, rows_hbm, q_hbm, k_hbm, g_hbm, ids_hbm, index_hbm, *rest
):
    v_ref, loss_ref, exponent_ref, start_ref, rows_ref, q_ref, k_ref, g_ref, ids_ref, index_ref, sems = rest
    count = 0

    def begin(source, target):
        nonlocal count
        copy = pltpu.make_async_copy(source, target, sems.at[count])
        copy.start()
        count += 1
        return copy

    small = [
        begin(source, target)
        for source, target in (
            (ids_hbm, ids_ref), (index_hbm, index_ref), (loss_hbm, loss_ref), (exponent_hbm, exponent_ref),
            (start_hbm, start_ref), (rows_hbm, rows_ref),
        )
    ]
    groups = k_ref.shape[1] // HD
    wide = per_group * HD
    loads = []
    for half in range(2):
        span = pl.ds(half * HALF, HALF)
        loads.append([
            begin(source.at[span, :], target.at[span, :])
            for source, target in ((q_hbm, q_ref), (k_hbm, k_ref), (g_hbm, g_ref))
        ])
    for copy in small:
        copy.wait()
    masks = [
        mask_and_factor(half == 1, pl.ds(half * HALF, HALF), loss_ref, exponent_ref, ids_ref, index_ref)
        for half in range(2)
    ]
    info_row = lax.broadcasted_iota(jnp.int32, (INFO, k_ref.shape[1]), 0)
    info = jnp.zeros(info_row.shape, jnp.int32)
    for level in range(min(start_ref.shape[1], INFO // 2)):
        info = jnp.where(info_row == 2 * level, start_ref[0, level], info)
        info = jnp.where(info_row == 2 * level + 1, rows_ref[0, level], info)
    v_ref[pl.ds(2 * HALF, INFO), :] = info.astype(F32).astype(BF16)
    for half in range(2):
        for copy in loads[half]:
            copy.wait()
        span = pl.ds(half * HALF, HALF)
        values = attend_half(per_group, half == 1, span, q_ref, k_ref, g_ref, *masks[half])
        for group, value in enumerate(values):
            v_ref[span, pl.ds(group * HD, HD)] = value


def front(query, key, grad, ids, index, loss, exponent, start, rows):
    tokens, key_width = key.shape
    per_group = query.shape[1] // key_width
    args = [
        loss, exponent, start, rows, query, key, grad, ids.reshape(1, tokens), index.reshape(1, tokens)
    ]
    return pl.pallas_call(
        functools.partial(front_kernel, per_group),
        in_specs=[HBM] * 9,
        out_specs=VMEM,
        out_shape=jax.ShapeDtypeStruct((tokens + INFO, key_width), BF16),
        scratch_shapes=[
            pltpu.SMEM(loss.shape, F32), pltpu.SMEM(exponent.shape, jnp.int32),
            pltpu.SMEM(start.shape, jnp.int32), pltpu.SMEM(rows.shape, jnp.int32),
            pltpu.VMEM(query.shape, BF16), pltpu.VMEM(key.shape, BF16), pltpu.VMEM(grad.shape, BF16),
            pltpu.VMEM((1, tokens), jnp.int32), pltpu.VMEM((1, tokens), jnp.int32),
            pltpu.SemaphoreType.DMA((12,)),
        ],
        compiler_params=pltpu.CompilerParams(vmem_limit_bytes=24 * MIB),
        cost_estimate=FREE,
        name="front",
    )(*[arg if arg is exponent else pltpu.with_memory_space_constraint(arg, pltpu.HBM) for arg in args])


CORE, Y, X, Z1, Z2 = 8, 16, 1, 2, 4


def xor_permute(value, mask):
    count = lax.axis_size("dp") * lax.axis_size("fsdp")
    return lax.ppermute(value, ("dp", "fsdp"), [(i, i ^ mask) for i in range(count)])


def partial_kernel(parts, own_ref, near_ref, v0_ref, v1_ref, *out_refs):
    dp = lax.axis_index("dp")
    fsdp = lax.axis_index("fsdp")
    loaded = {}

    def block(z, y, x):
        if (z, y, x) not in loaded:
            owner = fsdp ^ (z << 1 | x)
            column = pl.multiple_of(owner * (4 * LANE) + (dp ^ (y << 1)) * LANE, LANE)
            loaded[z, y, x] = jnp.concatenate([ref[:, pl.ds(column, LANE)] for ref in (own_ref, near_ref)], axis=0)
        return loaded[z, y, x]

    for (blocks, start, width), out_ref in zip(parts, out_refs):
        v = jnp.concatenate([ref[pl.ds(0, 2 * HALF), pl.ds(start, width)] for ref in (v0_ref, v1_ref)], axis=0)
        total = lax.dot_general(
            jnp.concatenate([block(*place) for place in blocks], axis=1), v, (((0,), (0,)), ((), ())),
            preferred_element_type=F32,
        )
        out_ref[...] = total.astype(out_ref.dtype)


def partial_sums(parts, dtype, own, near, v0, v1):
    return pl.pallas_call(
        functools.partial(partial_kernel, parts),
        in_specs=[VMEM] * 4,
        out_specs=[VMEM] * len(parts),
        out_shape=[jax.ShapeDtypeStruct((len(blocks) * LANE, width), dtype) for blocks, _, width in parts],
        compiler_params=pltpu.CompilerParams(vmem_limit_bytes=24 * MIB),
        cost_estimate=FREE,
        name="partial_sums",
    )(own, near, v0, v1)


def inner_swap_kernel(v0_ref, v1_ref, out_ref, window_ref):
    tokens = out_ref.shape[0]
    infos = [ref[pl.ds(tokens, INFO), pl.ds(0, HALF)].astype(F32).astype(jnp.int32) for ref in (v0_ref, v1_ref)]

    def table(device, entry):
        return jnp.broadcast_to(infos[device][entry:entry + 1, :], (HALF, HALF))

    place = lax.broadcasted_iota(jnp.int32, (HALF, HALF), 0) + HALF
    inner = lax.broadcasted_iota(jnp.int32, (HALF, HALF), 1) + HALF
    first = table(0, 0)
    moved = (place >= first) & (place < first + table(0, 1))
    stays = jnp.where(~moved & (place == inner), 1.0, 0.0).astype(BF16)
    comes = jnp.where(moved & (place + table(1, 0) - first == inner), 1.0, 0.0).astype(BF16)
    taken = jnp.where(place - HALF + table(0, 2) == inner, 1.0, 0.0).astype(BF16)[:CAP]
    rows = (
        jnp.dot(stays, v0_ref[pl.ds(HALF, HALF), :], preferred_element_type=F32)
        + jnp.dot(comes, v1_ref[pl.ds(HALF, HALF), :], preferred_element_type=F32)
    ).astype(BF16)
    out_ref[pl.ds(0, HALF), :] = v0_ref[pl.ds(0, HALF), :]
    out_ref[pl.ds(HALF, HALF), :] = rows
    window_ref[...] = jnp.dot(taken, rows, preferred_element_type=F32).astype(BF16)


def inner_swap(v0, v1):
    return pl.pallas_call(
        inner_swap_kernel,
        in_specs=[VMEM] * 2,
        out_specs=[VMEM] * 2,
        out_shape=[jax.ShapeDtypeStruct((2 * HALF, 512), BF16), jax.ShapeDtypeStruct((CAP, 512), BF16)],
        compiler_params=pltpu.CompilerParams(vmem_limit_bytes=8 * MIB),
        cost_estimate=FREE,
        name="inner_swap",
    )(v0, v1)


def outer_swap_kernel(v0_ref, rows_ref, window_ref, out_ref):
    tokens = out_ref.shape[0]
    info = v0_ref[pl.ds(tokens, INFO), pl.ds(0, HALF)].astype(F32).astype(jnp.int32)
    first = jnp.broadcast_to(info[2:3, :], (HALF, HALF))
    extent = jnp.broadcast_to(info[3:4, :], (HALF, HALF))
    place = lax.broadcasted_iota(jnp.int32, (HALF, HALF), 0) + HALF
    inner = lax.broadcasted_iota(jnp.int32, (HALF, HALF), 1)
    moved = (place >= first) & (place < first + extent)
    stays = jnp.where(~moved & (place == inner + HALF), 1.0, 0.0).astype(BF16)
    comes = jnp.where(moved & (place - first == inner), 1.0, 0.0).astype(BF16)[:, :CAP]
    out_ref[pl.ds(0, HALF), :] = rows_ref[pl.ds(0, HALF), :]
    out_ref[pl.ds(HALF, HALF), :] = (
        jnp.dot(stays, rows_ref[pl.ds(HALF, HALF), :], preferred_element_type=F32)
        + jnp.dot(comes, window_ref[...], preferred_element_type=F32)
    ).astype(BF16)


def outer_swap(v0, rows, window):
    return pl.pallas_call(
        outer_swap_kernel,
        in_specs=[VMEM] * 3,
        out_specs=VMEM,
        out_shape=jax.ShapeDtypeStruct(rows.shape, BF16),
        compiler_params=pltpu.CompilerParams(vmem_limit_bytes=8 * MIB),
        cost_estimate=FREE,
        name="outer_swap",
    )(v0, rows, window)


def place_kernel(core, pair_ref, *rest):
    *_, out_ref, wide, sems = rest
    copies = []
    for y in range(2):
        wide[y] = pair_ref[y].astype(F32)
        row = pl.multiple_of((lax.axis_index("dp") ^ (y << 1 | core)) * LANE, LANE)
        copies.append(pltpu.make_async_copy(wide.at[y], out_ref.at[pl.ds(row, LANE), :], sems.at[y]))
        copies[-1].start()
    for copy in copies:
        copy.wait()


def place(core, pair, *placed):
    return pl.pallas_call(
        functools.partial(place_kernel, core),
        in_specs=[VMEM] + [HBM] * len(placed),
        out_specs=HBM,
        out_shape=jax.ShapeDtypeStruct((512, 512), F32),
        scratch_shapes=[pltpu.VMEM((2, LANE, 512), F32), pltpu.SemaphoreType.DMA((2,))],
        input_output_aliases={1: 0} if placed else {},
        compiler_params=pltpu.CompilerParams(vmem_limit_bytes=8 * MIB),
        cost_estimate=FREE,
        name="place",
    )(pair, *placed)


def fold_kernel(base_ref, arrived_ref, out_ref):
    out_ref[...] = base_ref[...] + arrived_ref[...].astype(F32)


def fold(base, arrived):
    return pl.pallas_call(
        fold_kernel,
        in_specs=[VMEM] * 2,
        out_specs=VMEM,
        out_shape=jax.ShapeDtypeStruct(base.shape, F32),
        compiler_params=pltpu.CompilerParams(vmem_limit_bytes=8 * MIB),
        cost_estimate=pl.CostEstimate(flops=6_000_000_000, bytes_accessed=0, transcendentals=0),
        name="fold",
    )(base, arrived)


def reduce_by_axis(layer_input, *args):
    near = xor_permute(layer_input, CORE)
    v0 = front(*args)
    v1 = xor_permute(v0, CORE)

    def sums(parts, dtype, v=v0):
        return partial_sums(parts, dtype, layer_input, near, v, v1)

    def after_all(*values):
        return lax.optimization_barrier(values)

    def add(*terms):
        total = terms[0]
        for term in terms[1:]:
            total = total + term.astype(F32)
        return total

    first_b, = sums([(((3, 1, 1), (3, 0, 1)), 0, 512)], BF16)
    first_a, = sums([(((2, 1, 1), (2, 1, 0)), 0, 512)], BF16)
    every = ((1, 1), (1, 0), (0, 1), (0, 0))
    pair_some, = sums([(tuple((1, *at) for at in every), 0, 256)], BF16)
    pair_rest, = sums([(tuple((1, *at) for at in every), 256, 256)], BF16, after_all(v0, pair_some)[0])
    keep_b, keep_a = sums([(((3, 1, 0), (3, 0, 0)), 0, 512), (((2, 0, 1), (2, 0, 0)), 0, 512)], F32)
    own_some, own_rest = sums([(tuple((0, *at) for at in every), start, 256) for start in (0, 256)], F32)
    first_b = xor_permute(first_b, X)
    first_a = xor_permute(first_a, Y)
    pair_sent = pair_rest
    pair_some = xor_permute(pair_some, Z1)
    pair_rest = xor_permute(pair_rest, Z1)
    on_b = add(keep_b[:LANE], first_b[:LANE]).astype(BF16)
    rows, window = inner_swap(after_all(v0, pair_sent)[0], v1)
    window = xor_permute(after_all(window, on_b)[0], Y)
    on_b = xor_permute(on_b, Y)
    on_a = xor_permute(add(keep_a[:LANE], first_a[:LANE]).astype(BF16), X)
    z3 = add(keep_b[LANE:], first_b[LANE:], on_b).astype(BF16)
    pair_some, window = after_all(pair_some, window, z3)[:2]
    z3 = xor_permute(z3, Z1)
    z2 = add(keep_a[LANE:], first_a[LANE:], on_a, z3).astype(BF16)

    some = add(own_some, pair_some)
    some_in = xor_permute(some[:2 * LANE].astype(BF16), Y)
    rest = add(own_rest, after_all(pair_rest, some)[0])
    rest_far, rest_y, rest_x, rest_own = (rest[row:row + LANE] for row in range(0, 4 * LANE, LANE))
    rest_in = xor_permute(jnp.concatenate([rest_far, rest_x]).astype(BF16), X)
    some_in = after_all(some_in, z2)[0]
    z2 = xor_permute(z2, Z2)
    some_on = add(some[2 * LANE:3 * LANE], some_in[:LANE]).astype(BF16)
    rest_in = after_all(rest_in, some_on)[0]
    some_on = xor_permute(some_on, X)
    rest_on = xor_permute(add(rest_y, rest_in[:LANE]).astype(BF16), Y)
    base = jnp.concatenate([add(some[3 * LANE:], some_in[LANE:]), add(rest_own, rest_in[LANE:])], axis=1)
    mine = add(fold(base, z2), jnp.concatenate([some_on, rest_on], axis=1)).astype(BF16)
    from_y = xor_permute(mine, Y)
    value_grad = outer_swap(v0, rows, after_all(window, mine)[0])
    from_y, value_grad = after_all(from_y, value_grad)
    pair = jnp.stack([mine, from_y])
    near_pair = xor_permute(pair, CORE)
    half = place(0, pair)
    near_pair, half = after_all(near_pair, half)
    return place(1, near_pair, half), value_grad


def swapped(block, axis, distance):
    count = lax.axis_size(axis)
    route = []
    for low in range(count):
        high = low | 1 << distance
        if high != low and high < count:
            route += [(low, high), (high, low)]
    return lax.ppermute(block, axis, route)


def blend_rows(item, incoming, offset, extent):
    inside = (jnp.arange(CAP) < extent)[:, None]
    chosen = jnp.where(inside, incoming, lax.dynamic_slice_in_dim(item, offset, CAP, 0))
    return lax.dynamic_update_slice_in_dim(item, chosen, offset, 0)


def reduce_by_owner(layer_input, *args):
    swap_start, swap_rows = args[-2:]
    tokens = layer_input.shape[0]
    values = front(*args)[:tokens]
    balanced = values
    for level in range(lax.axis_size("dp").bit_length() - 1):
        offset = swap_start[0, level]
        window = lax.dynamic_slice_in_dim(balanced, offset, CAP, 0)
        balanced = blend_rows(balanced, swapped(window, "dp", level), offset, swap_rows[0, level])
    owners = lax.axis_size("fsdp")
    owned = (D + owners - 1) // owners
    padded = jnp.pad(layer_input, ((0, 0), (0, owned * owners - D)))
    arranged = lax.all_to_all(
        padded.reshape(tokens, owners, owned), "fsdp", split_axis=1, concat_axis=0, tiled=True
    )
    block = lax.dot_general(
        arranged.reshape(-1, owned),
        lax.all_gather(values, "fsdp", axis=0, tiled=True),
        (((0,), (0,)), ((), ())),
        preferred_element_type=F32,
    )
    return lax.psum(block, "dp"), balanced


def on_device(layer_input, *args):
    if lax.axis_size("dp") == 4 and lax.axis_size("fsdp") == 8:
        return reduce_by_axis(layer_input, *args)
    return reduce_by_owner(layer_input, *args)


def solution(mesh):
    return jax.shard_map(
        on_device,
        mesh=mesh,
        in_specs=(
            P(("dp", "fsdp"), None),
            P(("dp", "fsdp"), None),
            P(("dp", "fsdp"), None),
            P(("dp", "fsdp"), None),
            P(("dp", "fsdp")),
            P(("dp", "fsdp")),
            P(),
            P(("dp", "fsdp")),
            P(("dp", "fsdp"), None),
            P(("dp", "fsdp"), None),
        ),
        out_specs=(P("fsdp", None), P(("dp", "fsdp"), None)),
        check_vma=False,
    )
```

```python
import functools
import math

import jax
import jax.numpy as jnp
from jax import lax
from jax.experimental import pallas as pl
from jax.experimental.pallas import tpu as pltpu
from jax.sharding import PartitionSpec as P

D = 4096
HD = 128
CAP = 32
HALF = 128
SEG = 16
LANE = 128
INFO = 16
MIB = 1 << 20
FREE = pl.CostEstimate(flops=0, bytes_accessed=0, transcendentals=0)
BF16 = jnp.bfloat16
F32 = jnp.float32

VMEM = pl.BlockSpec(memory_space=pltpu.VMEM)
HBM = pl.BlockSpec(memory_space=pltpu.HBM)


def attend_half(per_group, folded, span, q_ref, k_ref, g_ref, allowed, factor):
    heads = q_ref.shape[1] // HD
    groups = heads // per_group
    scores = [
        lax.dot_general(
            k_ref[span, pl.ds(group * HD, HD)],
            jnp.concatenate(
                [q_ref[span, pl.ds((group * per_group + n) * HD, HD)] for n in range(per_group)], axis=0
            ),
            (((1,), (1,)), ((), ())),
            preferred_element_type=F32,
        )
        for group in range(groups)
    ]
    weighted = [
        (g_ref[span, pl.ds(head * HD, HD)].astype(F32) * factor).astype(BF16) for head in range(heads)
    ]
    if folded:
        block = lax.broadcasted_iota(jnp.int32, (SEG, HALF), 1) // SEG
    probs = []
    for head in range(heads):
        n = head % per_group
        own = scores[head // per_group][:, n * HALF:(n + 1) * HALF]
        if folded:
            own = fold_blocks(own, block)
        own = jnp.where(allowed, own, -1e30)
        expo = jnp.exp2((own - jnp.max(own, axis=0, keepdims=True)) * (HD ** (-0.5) * math.log2(math.e)))
        prob = (expo * (1.0 / jnp.sum(expo, axis=0, keepdims=True))).astype(BF16)
        if folded:
            prob = jnp.concatenate(
                [jnp.where(block == b, prob, jnp.zeros_like(prob)) for b in range(HALF // SEG)], axis=0
            )
        probs.append(prob)
    return [
        jnp.dot(
            jnp.concatenate(probs[head:head + per_group], axis=1),
            jnp.concatenate(weighted[head:head + per_group], axis=0),
            preferred_element_type=F32,
        ).astype(BF16)
        for head in range(0, heads, per_group)
    ]


def fold_blocks(square, block):
    total = square[:SEG]
    for b in range(1, HALF // SEG):
        total = jnp.where(block == b, square[b * SEG:(b + 1) * SEG], total)
    return total


def mask_and_factor(folded, span, loss_ref, exponent_ref, ids_ref, index_ref):
    exponent = exponent_ref[0]
    unscale = jnp.float32(1.0)
    for bit in range(5):
        unscale = unscale * jnp.where((exponent >> bit) & 1 == 1, jnp.float32(2.0 ** -(1 << bit)), 1.0)
    row = lax.broadcasted_iota(jnp.int32, (HALF, HALF), 0)
    col = lax.broadcasted_iota(jnp.int32, (HALF, HALF), 1)
    doc_i = jnp.broadcast_to(ids_ref[:, span], (HALF, HALF))
    allowed = (doc_i == doc_i.T) & (row <= col)
    if folded:
        allowed = fold_blocks(
            jnp.where(allowed, 1, 0), lax.broadcasted_iota(jnp.int32, (SEG, HALF), 1) // SEG
        ) == 1
    index = index_ref[:, span]
    factor = jnp.zeros((1, HALF), F32)
    for entry in range(loss_ref.shape[0]):
        factor = jnp.where(index == entry, loss_ref[entry], factor)
    return allowed, jnp.broadcast_to(factor * unscale, (HALF, HALF)).T


def front_kernel(
    per_group, loss_hbm, exponent_hbm, start_hbm, rows_hbm, q_hbm, k_hbm, g_hbm, ids_hbm, index_hbm, *rest
):
    v_ref, loss_ref, exponent_ref, start_ref, rows_ref, q_ref, k_ref, g_ref, ids_ref, index_ref, sems = rest
    count = 0

    def begin(source, target):
        nonlocal count
        copy = pltpu.make_async_copy(source, target, sems.at[count])
        copy.start()
        count += 1
        return copy

    small = [
        begin(source, target)
        for source, target in (
            (ids_hbm, ids_ref), (index_hbm, index_ref), (loss_hbm, loss_ref), (exponent_hbm, exponent_ref),
            (start_hbm, start_ref), (rows_hbm, rows_ref),
        )
    ]
    groups = k_ref.shape[1] // HD
    wide = per_group * HD
    loads = []
    for half in range(2):
        span = pl.ds(half * HALF, HALF)
        loads.append([
            begin(source.at[span, :], target.at[span, :])
            for source, target in ((q_hbm, q_ref), (k_hbm, k_ref), (g_hbm, g_ref))
        ])
    for copy in small:
        copy.wait()
    masks = [
        mask_and_factor(half == 1, pl.ds(half * HALF, HALF), loss_ref, exponent_ref, ids_ref, index_ref)
        for half in range(2)
    ]
    info_row = lax.broadcasted_iota(jnp.int32, (INFO, k_ref.shape[1]), 0)
    info = jnp.zeros(info_row.shape, jnp.int32)
    for level in range(min(start_ref.shape[1], INFO // 2)):
        info = jnp.where(info_row == 2 * level, start_ref[0, level], info)
        info = jnp.where(info_row == 2 * level + 1, rows_ref[0, level], info)
    v_ref[pl.ds(2 * HALF, INFO), :] = info.astype(F32).astype(BF16)
    for half in range(2):
        for copy in loads[half]:
            copy.wait()
        span = pl.ds(half * HALF, HALF)
        values = attend_half(per_group, half == 1, span, q_ref, k_ref, g_ref, *masks[half])
        for group, value in enumerate(values):
            v_ref[span, pl.ds(group * HD, HD)] = value


def front(query, key, grad, ids, index, loss, exponent, start, rows):
    tokens, key_width = key.shape
    per_group = query.shape[1] // key_width
    args = [
        loss, exponent, start, rows, query, key, grad, ids.reshape(1, tokens), index.reshape(1, tokens)
    ]
    return pl.pallas_call(
        functools.partial(front_kernel, per_group),
        in_specs=[HBM] * 9,
        out_specs=VMEM,
        out_shape=jax.ShapeDtypeStruct((tokens + INFO, key_width), BF16),
        scratch_shapes=[
            pltpu.SMEM(loss.shape, F32), pltpu.SMEM(exponent.shape, jnp.int32),
            pltpu.SMEM(start.shape, jnp.int32), pltpu.SMEM(rows.shape, jnp.int32),
            pltpu.VMEM(query.shape, BF16), pltpu.VMEM(key.shape, BF16), pltpu.VMEM(grad.shape, BF16),
            pltpu.VMEM((1, tokens), jnp.int32), pltpu.VMEM((1, tokens), jnp.int32),
            pltpu.SemaphoreType.DMA((12,)),
        ],
        compiler_params=pltpu.CompilerParams(vmem_limit_bytes=24 * MIB),
        cost_estimate=FREE,
        name="front",
    )(*[arg if arg is exponent else pltpu.with_memory_space_constraint(arg, pltpu.HBM) for arg in args])


CORE, Y, X, Z1, Z2 = 8, 16, 1, 2, 4


def xor_permute(value, mask):
    count = lax.axis_size("dp") * lax.axis_size("fsdp")
    return lax.ppermute(value, ("dp", "fsdp"), [(i, i ^ mask) for i in range(count)])


def partial_kernel(parts, own_ref, near_ref, v0_ref, v1_ref, *out_refs):
    dp = lax.axis_index("dp")
    fsdp = lax.axis_index("fsdp")
    loaded = {}

    def block(z, y, x):
        if (z, y, x) not in loaded:
            owner = fsdp ^ (z << 1 | x)
            column = pl.multiple_of(owner * (4 * LANE) + (dp ^ (y << 1)) * LANE, LANE)
            loaded[z, y, x] = jnp.concatenate([ref[:, pl.ds(column, LANE)] for ref in (own_ref, near_ref)], axis=0)
        return loaded[z, y, x]

    for (blocks, start, width), out_ref in zip(parts, out_refs):
        v = jnp.concatenate([ref[pl.ds(0, 2 * HALF), pl.ds(start, width)] for ref in (v0_ref, v1_ref)], axis=0)
        total = lax.dot_general(
            jnp.concatenate([block(*place) for place in blocks], axis=1), v, (((0,), (0,)), ((), ())),
            preferred_element_type=F32,
        )
        out_ref[...] = total.astype(out_ref.dtype)


def partial_sums(parts, dtype, own, near, v0, v1):
    return pl.pallas_call(
        functools.partial(partial_kernel, parts),
        in_specs=[VMEM] * 4,
        out_specs=[VMEM] * len(parts),
        out_shape=[jax.ShapeDtypeStruct((len(blocks) * LANE, width), dtype) for blocks, _, width in parts],
        compiler_params=pltpu.CompilerParams(vmem_limit_bytes=24 * MIB),
        cost_estimate=FREE,
        name="partial_sums",
    )(own, near, v0, v1)


def inner_swap_kernel(v0_ref, v1_ref, out_ref, window_ref):
    tokens = out_ref.shape[0]
    infos = [ref[pl.ds(tokens, INFO), pl.ds(0, HALF)].astype(F32).astype(jnp.int32) for ref in (v0_ref, v1_ref)]

    def table(device, entry):
        return jnp.broadcast_to(infos[device][entry:entry + 1, :], (HALF, HALF))

    place = lax.broadcasted_iota(jnp.int32, (HALF, HALF), 0) + HALF
    inner = lax.broadcasted_iota(jnp.int32, (HALF, HALF), 1) + HALF
    first = table(0, 0)
    moved = (place >= first) & (place < first + table(0, 1))
    stays = jnp.where(~moved & (place == inner), 1.0, 0.0).astype(BF16)
    comes = jnp.where(moved & (place + table(1, 0) - first == inner), 1.0, 0.0).astype(BF16)
    taken = jnp.where(place - HALF + table(0, 2) == inner, 1.0, 0.0).astype(BF16)[:CAP]
    rows = (
        jnp.dot(stays, v0_ref[pl.ds(HALF, HALF), :], preferred_element_type=F32)
        + jnp.dot(comes, v1_ref[pl.ds(HALF, HALF), :], preferred_element_type=F32)
    ).astype(BF16)
    out_ref[pl.ds(0, HALF), :] = v0_ref[pl.ds(0, HALF), :]
    out_ref[pl.ds(HALF, HALF), :] = rows
    window_ref[...] = jnp.dot(taken, rows, preferred_element_type=F32).astype(BF16)


def inner_swap(v0, v1):
    return pl.pallas_call(
        inner_swap_kernel,
        in_specs=[VMEM] * 2,
        out_specs=[VMEM] * 2,
        out_shape=[jax.ShapeDtypeStruct((2 * HALF, 512), BF16), jax.ShapeDtypeStruct((CAP, 512), BF16)],
        compiler_params=pltpu.CompilerParams(vmem_limit_bytes=8 * MIB),
        cost_estimate=FREE,
        name="inner_swap",
    )(v0, v1)


def outer_swap_kernel(v0_ref, rows_ref, window_ref, out_ref):
    tokens = out_ref.shape[0]
    info = v0_ref[pl.ds(tokens, INFO), pl.ds(0, HALF)].astype(F32).astype(jnp.int32)
    first = jnp.broadcast_to(info[2:3, :], (HALF, HALF))
    extent = jnp.broadcast_to(info[3:4, :], (HALF, HALF))
    place = lax.broadcasted_iota(jnp.int32, (HALF, HALF), 0) + HALF
    inner = lax.broadcasted_iota(jnp.int32, (HALF, HALF), 1)
    moved = (place >= first) & (place < first + extent)
    stays = jnp.where(~moved & (place == inner + HALF), 1.0, 0.0).astype(BF16)
    comes = jnp.where(moved & (place - first == inner), 1.0, 0.0).astype(BF16)[:, :CAP]
    out_ref[pl.ds(0, HALF), :] = rows_ref[pl.ds(0, HALF), :]
    out_ref[pl.ds(HALF, HALF), :] = (
        jnp.dot(stays, rows_ref[pl.ds(HALF, HALF), :], preferred_element_type=F32)
        + jnp.dot(comes, window_ref[...], preferred_element_type=F32)
    ).astype(BF16)


def outer_swap(v0, rows, window):
    return pl.pallas_call(
        outer_swap_kernel,
        in_specs=[VMEM] * 3,
        out_specs=VMEM,
        out_shape=jax.ShapeDtypeStruct(rows.shape, BF16),
        compiler_params=pltpu.CompilerParams(vmem_limit_bytes=8 * MIB),
        cost_estimate=FREE,
        name="outer_swap",
    )(v0, rows, window)


def place_kernel(core, pair_ref, *rest):
    *_, out_ref, wide, sems = rest
    copies = []
    for y in range(2):
        wide[y] = pair_ref[y].astype(F32)
        row = pl.multiple_of((lax.axis_index("dp") ^ (y << 1 | core)) * LANE, LANE)
        copies.append(pltpu.make_async_copy(wide.at[y], out_ref.at[pl.ds(row, LANE), :], sems.at[y]))
        copies[-1].start()
    for copy in copies:
        copy.wait()


def place(core, pair, *placed):
    return pl.pallas_call(
        functools.partial(place_kernel, core),
        in_specs=[VMEM] + [HBM] * len(placed),
        out_specs=HBM,
        out_shape=jax.ShapeDtypeStruct((512, 512), F32),
        scratch_shapes=[pltpu.VMEM((2, LANE, 512), F32), pltpu.SemaphoreType.DMA((2,))],
        input_output_aliases={1: 0} if placed else {},
        compiler_params=pltpu.CompilerParams(vmem_limit_bytes=8 * MIB),
        cost_estimate=FREE,
        name="place",
    )(pair, *placed)


def fold_kernel(base_ref, arrived_ref, out_ref):
    out_ref[...] = base_ref[...] + arrived_ref[...].astype(F32)


def fold(base, arrived):
    return pl.pallas_call(
        fold_kernel,
        in_specs=[VMEM] * 2,
        out_specs=VMEM,
        out_shape=jax.ShapeDtypeStruct(base.shape, F32),
        compiler_params=pltpu.CompilerParams(vmem_limit_bytes=8 * MIB),
        cost_estimate=pl.CostEstimate(flops=6_000_000_000, bytes_accessed=0, transcendentals=0),
        name="fold",
    )(base, arrived)


def reduce_by_axis(layer_input, *args):
    near = xor_permute(layer_input, CORE)
    v0 = front(*args)
    v1 = xor_permute(v0, CORE)

    def sums(parts, dtype, v=v0):
        return partial_sums(parts, dtype, layer_input, near, v, v1)

    def after_all(*values):
        return lax.optimization_barrier(values)

    def add(*terms):
        total = terms[0]
        for term in terms[1:]:
            total = total + term.astype(F32)
        return total

    far_b, = sums([(((3, 1, 1),), 0, 512)], BF16)
    first_a, = sums([(((2, 1, 1), (2, 1, 0)), 0, 512)], BF16)
    every = ((1, 1), (1, 0), (0, 1), (0, 0))
    side_b, pair_some = sums([(((3, 0, 1),), 0, 512), (tuple((1, *at) for at in every[:3]), 0, 256)], BF16)
    pair_rest, pair_own = sums(
        [(tuple((1, *at) for at in every[:3]), 256, 256), (((1, 0, 0),), 0, 512)], BF16, after_all(v0, pair_some)[0]
    )
    keep_b, keep_a = sums([(((3, 1, 0), (3, 0, 0)), 0, 512), (((2, 0, 1), (2, 0, 0)), 0, 512)], F32)
    own_some, own_rest = sums([(tuple((0, *at) for at in every), start, 256) for start in (0, 256)], F32)
    far_b = xor_permute(far_b, X)
    side_b = xor_permute(side_b, X)
    first_a = xor_permute(first_a, Y)
    pair_sent = pair_rest
    pair_some = xor_permute(pair_some, Z1)
    pair_rest = xor_permute(pair_rest, Z1)
    on_b = add(keep_b[:LANE], far_b).astype(BF16)
    rows, window = inner_swap(after_all(v0, pair_sent)[0], v1)
    window = xor_permute(after_all(window, on_b)[0], Y)
    on_b = xor_permute(on_b, Y)
    on_a = xor_permute(add(keep_a[:LANE], first_a[:LANE]).astype(BF16), X)
    z3 = add(keep_b[LANE:], side_b, on_b).astype(BF16)
    pair_some, window, pair_own = after_all(pair_some, window, pair_own, z3)[:3]
    z3 = xor_permute(z3, Z1)
    pair_own = xor_permute(pair_own, Z1)
    z2 = add(keep_a[LANE:], first_a[LANE:], on_a, z3).astype(BF16)

    some = add(own_some[:3 * LANE], pair_some)
    some_in = xor_permute(some[:2 * LANE].astype(BF16), Y)
    rest = add(own_rest[:3 * LANE], after_all(pair_rest, some)[0])
    rest_far, rest_y, rest_x = (rest[row:row + LANE] for row in range(0, 3 * LANE, LANE))
    rest_in = xor_permute(jnp.concatenate([rest_far, rest_x]).astype(BF16), X)
    some_in = after_all(some_in, z2)[0]
    z2 = xor_permute(z2, Z2)
    some_on = add(some[2 * LANE:], some_in[:LANE]).astype(BF16)
    rest_in = after_all(rest_in, some_on)[0]
    some_on = xor_permute(some_on, X)
    rest_on = xor_permute(add(rest_y, rest_in[:LANE]).astype(BF16), Y)
    base = jnp.concatenate([
        add(own_some[3 * LANE:], pair_own[:, :256], some_in[LANE:]),
        add(own_rest[3 * LANE:], pair_own[:, 256:], rest_in[LANE:]),
    ], axis=1)
    mine = add(fold(base, z2), jnp.concatenate([some_on, rest_on], axis=1)).astype(BF16)
    from_y = xor_permute(mine, Y)
    value_grad = outer_swap(v0, rows, after_all(window, mine)[0])
    from_y, value_grad = after_all(from_y, value_grad)
    pair = jnp.stack([mine, from_y])
    near_pair = xor_permute(pair, CORE)
    half = place(0, pair)
    near_pair, half = after_all(near_pair, half)
    return place(1, near_pair, half), value_grad


def swapped(block, axis, distance):
    count = lax.axis_size(axis)
    route = []
    for low in range(count):
        high = low | 1 << distance
        if high != low and high < count:
            route += [(low, high), (high, low)]
    return lax.ppermute(block, axis, route)


def blend_rows(item, incoming, offset, extent):
    inside = (jnp.arange(CAP) < extent)[:, None]
    chosen = jnp.where(inside, incoming, lax.dynamic_slice_in_dim(item, offset, CAP, 0))
    return lax.dynamic_update_slice_in_dim(item, chosen, offset, 0)


def reduce_by_owner(layer_input, *args):
    swap_start, swap_rows = args[-2:]
    tokens = layer_input.shape[0]
    values = front(*args)[:tokens]
    balanced = values
    for level in range(lax.axis_size("dp").bit_length() - 1):
        offset = swap_start[0, level]
        window = lax.dynamic_slice_in_dim(balanced, offset, CAP, 0)
        balanced = blend_rows(balanced, swapped(window, "dp", level), offset, swap_rows[0, level])
    owners = lax.axis_size("fsdp")
    owned = (D + owners - 1) // owners
    padded = jnp.pad(layer_input, ((0, 0), (0, owned * owners - D)))
    arranged = lax.all_to_all(
        padded.reshape(tokens, owners, owned), "fsdp", split_axis=1, concat_axis=0, tiled=True
    )
    block = lax.dot_general(
        arranged.reshape(-1, owned),
        lax.all_gather(values, "fsdp", axis=0, tiled=True),
        (((0,), (0,)), ((), ())),
        preferred_element_type=F32,
    )
    return lax.psum(block, "dp"), balanced


def on_device(layer_input, *args):
    if lax.axis_size("dp") == 4 and lax.axis_size("fsdp") == 8:
        return reduce_by_axis(layer_input, *args)
    return reduce_by_owner(layer_input, *args)


def solution(mesh):
    return jax.shard_map(
        on_device,
        mesh=mesh,
        in_specs=(
            P(("dp", "fsdp"), None),
            P(("dp", "fsdp"), None),
            P(("dp", "fsdp"), None),
            P(("dp", "fsdp"), None),
            P(("dp", "fsdp")),
            P(("dp", "fsdp")),
            P(),
            P(("dp", "fsdp")),
            P(("dp", "fsdp"), None),
            P(("dp", "fsdp"), None),
        ),
        out_specs=(P("fsdp", None), P(("dp", "fsdp"), None)),
        check_vma=False,
    )
```

```python
import functools
import math

import jax
import jax.numpy as jnp
from jax import lax
from jax.experimental import pallas as pl
from jax.experimental.pallas import tpu as pltpu
from jax.sharding import PartitionSpec as P

D = 4096
HD = 128
CAP = 32
HALF = 128
SEG = 16
LANE = 128
INFO = 16
MIB = 1 << 20
FREE = pl.CostEstimate(flops=0, bytes_accessed=0, transcendentals=0)
BF16 = jnp.bfloat16
F32 = jnp.float32

VMEM = pl.BlockSpec(memory_space=pltpu.VMEM)
HBM = pl.BlockSpec(memory_space=pltpu.HBM)


def attend_half(per_group, folded, span, q_ref, k_ref, g_ref, allowed, factor):
    heads = q_ref.shape[1] // HD
    groups = heads // per_group
    scores = [
        lax.dot_general(
            k_ref[span, pl.ds(group * HD, HD)],
            jnp.concatenate(
                [q_ref[span, pl.ds((group * per_group + n) * HD, HD)] for n in range(per_group)], axis=0
            ),
            (((1,), (1,)), ((), ())),
            preferred_element_type=F32,
        )
        for group in range(groups)
    ]
    weighted = [
        (g_ref[span, pl.ds(head * HD, HD)].astype(F32) * factor).astype(BF16) for head in range(heads)
    ]
    if folded:
        block = lax.broadcasted_iota(jnp.int32, (SEG, HALF), 1) // SEG
    probs = []
    for head in range(heads):
        n = head % per_group
        own = scores[head // per_group][:, n * HALF:(n + 1) * HALF]
        if folded:
            own = fold_blocks(own, block)
        own = jnp.where(allowed, own, -1e30)
        expo = jnp.exp2((own - jnp.max(own, axis=0, keepdims=True)) * (HD ** (-0.5) * math.log2(math.e)))
        prob = (expo * (1.0 / jnp.sum(expo, axis=0, keepdims=True))).astype(BF16)
        if folded:
            prob = jnp.concatenate(
                [jnp.where(block == b, prob, jnp.zeros_like(prob)) for b in range(HALF // SEG)], axis=0
            )
        probs.append(prob)
    return [
        jnp.dot(
            jnp.concatenate(probs[head:head + per_group], axis=1),
            jnp.concatenate(weighted[head:head + per_group], axis=0),
            preferred_element_type=F32,
        ).astype(BF16)
        for head in range(0, heads, per_group)
    ]


def fold_blocks(square, block):
    total = square[:SEG]
    for b in range(1, HALF // SEG):
        total = jnp.where(block == b, square[b * SEG:(b + 1) * SEG], total)
    return total


def mask_and_factor(folded, span, loss_ref, exponent_ref, ids_ref, index_ref):
    exponent = exponent_ref[0]
    unscale = jnp.float32(1.0)
    for bit in range(5):
        unscale = unscale * jnp.where((exponent >> bit) & 1 == 1, jnp.float32(2.0 ** -(1 << bit)), 1.0)
    row = lax.broadcasted_iota(jnp.int32, (HALF, HALF), 0)
    col = lax.broadcasted_iota(jnp.int32, (HALF, HALF), 1)
    doc_i = jnp.broadcast_to(ids_ref[:, span], (HALF, HALF))
    allowed = (doc_i == doc_i.T) & (row <= col)
    if folded:
        allowed = fold_blocks(
            jnp.where(allowed, 1, 0), lax.broadcasted_iota(jnp.int32, (SEG, HALF), 1) // SEG
        ) == 1
    index = index_ref[:, span]
    factor = jnp.zeros((1, HALF), F32)
    for entry in range(loss_ref.shape[0]):
        factor = jnp.where(index == entry, loss_ref[entry], factor)
    return allowed, jnp.broadcast_to(factor * unscale, (HALF, HALF)).T


def front_kernel(
    per_group, loss_hbm, exponent_hbm, start_hbm, rows_hbm, q_hbm, k_hbm, g_hbm, ids_hbm, index_hbm, *rest
):
    v_ref, loss_ref, exponent_ref, start_ref, rows_ref, q_ref, k_ref, g_ref, ids_ref, index_ref, sems = rest
    count = 0

    def begin(source, target):
        nonlocal count
        copy = pltpu.make_async_copy(source, target, sems.at[count])
        copy.start()
        count += 1
        return copy

    small = [
        begin(source, target)
        for source, target in (
            (ids_hbm, ids_ref), (index_hbm, index_ref), (loss_hbm, loss_ref), (exponent_hbm, exponent_ref),
            (start_hbm, start_ref), (rows_hbm, rows_ref),
        )
    ]
    groups = k_ref.shape[1] // HD
    wide = per_group * HD
    loads = []
    for half in range(2):
        span = pl.ds(half * HALF, HALF)
        loads.append([
            begin(source.at[span, :], target.at[span, :])
            for source, target in ((q_hbm, q_ref), (k_hbm, k_ref), (g_hbm, g_ref))
        ])
    for copy in small:
        copy.wait()
    masks = [
        mask_and_factor(half == 1, pl.ds(half * HALF, HALF), loss_ref, exponent_ref, ids_ref, index_ref)
        for half in range(2)
    ]
    info_row = lax.broadcasted_iota(jnp.int32, (INFO, k_ref.shape[1]), 0)
    info = jnp.zeros(info_row.shape, jnp.int32)
    for level in range(min(start_ref.shape[1], INFO // 2)):
        info = jnp.where(info_row == 2 * level, start_ref[0, level], info)
        info = jnp.where(info_row == 2 * level + 1, rows_ref[0, level], info)
    v_ref[pl.ds(2 * HALF, INFO), :] = info.astype(F32).astype(BF16)
    for half in range(2):
        for copy in loads[half]:
            copy.wait()
        span = pl.ds(half * HALF, HALF)
        values = attend_half(per_group, half == 1, span, q_ref, k_ref, g_ref, *masks[half])
        for group, value in enumerate(values):
            v_ref[span, pl.ds(group * HD, HD)] = value


def front(query, key, grad, ids, index, loss, exponent, start, rows):
    tokens, key_width = key.shape
    per_group = query.shape[1] // key_width
    args = [
        loss, exponent, start, rows, query, key, grad, ids.reshape(1, tokens), index.reshape(1, tokens)
    ]
    return pl.pallas_call(
        functools.partial(front_kernel, per_group),
        in_specs=[HBM] * 9,
        out_specs=VMEM,
        out_shape=jax.ShapeDtypeStruct((tokens + INFO, key_width), BF16),
        scratch_shapes=[
            pltpu.SMEM(loss.shape, F32), pltpu.SMEM(exponent.shape, jnp.int32),
            pltpu.SMEM(start.shape, jnp.int32), pltpu.SMEM(rows.shape, jnp.int32),
            pltpu.VMEM(query.shape, BF16), pltpu.VMEM(key.shape, BF16), pltpu.VMEM(grad.shape, BF16),
            pltpu.VMEM((1, tokens), jnp.int32), pltpu.VMEM((1, tokens), jnp.int32),
            pltpu.SemaphoreType.DMA((12,)),
        ],
        compiler_params=pltpu.CompilerParams(vmem_limit_bytes=24 * MIB),
        cost_estimate=FREE,
        name="front",
    )(*[arg if arg is exponent else pltpu.with_memory_space_constraint(arg, pltpu.HBM) for arg in args])


CORE, Y, X, Z1, Z2 = 8, 16, 1, 2, 4


def xor_permute(value, mask):
    count = lax.axis_size("dp") * lax.axis_size("fsdp")
    return lax.ppermute(value, ("dp", "fsdp"), [(i, i ^ mask) for i in range(count)])


def partial_kernel(parts, own_ref, near_ref, v0_ref, v1_ref, *out_refs):
    dp = lax.axis_index("dp")
    fsdp = lax.axis_index("fsdp")
    loaded = {}

    def block(z, y, x):
        if (z, y, x) not in loaded:
            owner = fsdp ^ (z << 1 | x)
            column = pl.multiple_of(owner * (4 * LANE) + (dp ^ (y << 1)) * LANE, LANE)
            loaded[z, y, x] = jnp.concatenate([ref[:, pl.ds(column, LANE)] for ref in (own_ref, near_ref)], axis=0)
        return loaded[z, y, x]

    for (blocks, start, width), out_ref in zip(parts, out_refs):
        v = jnp.concatenate([ref[pl.ds(0, 2 * HALF), pl.ds(start, width)] for ref in (v0_ref, v1_ref)], axis=0)
        total = lax.dot_general(
            jnp.concatenate([block(*place) for place in blocks], axis=1), v, (((0,), (0,)), ((), ())),
            preferred_element_type=F32,
        )
        out_ref[...] = total.astype(out_ref.dtype)


def partial_sums(parts, dtype, own, near, v0, v1):
    return pl.pallas_call(
        functools.partial(partial_kernel, parts),
        in_specs=[VMEM] * 4,
        out_specs=[VMEM] * len(parts),
        out_shape=[jax.ShapeDtypeStruct((len(blocks) * LANE, width), dtype) for blocks, _, width in parts],
        compiler_params=pltpu.CompilerParams(vmem_limit_bytes=24 * MIB),
        cost_estimate=FREE,
        name="partial_sums",
    )(own, near, v0, v1)


def inner_swap_kernel(v0_ref, v1_ref, out_ref, window_ref):
    tokens = out_ref.shape[0]
    infos = [ref[pl.ds(tokens, INFO), pl.ds(0, HALF)].astype(F32).astype(jnp.int32) for ref in (v0_ref, v1_ref)]

    def table(device, entry):
        return jnp.broadcast_to(infos[device][entry:entry + 1, :], (HALF, HALF))

    place = lax.broadcasted_iota(jnp.int32, (HALF, HALF), 0) + HALF
    inner = lax.broadcasted_iota(jnp.int32, (HALF, HALF), 1) + HALF
    first = table(0, 0)
    moved = (place >= first) & (place < first + table(0, 1))
    stays = jnp.where(~moved & (place == inner), 1.0, 0.0).astype(BF16)
    comes = jnp.where(moved & (place + table(1, 0) - first == inner), 1.0, 0.0).astype(BF16)
    taken = jnp.where(place - HALF + table(0, 2) == inner, 1.0, 0.0).astype(BF16)[:CAP]
    rows = (
        jnp.dot(stays, v0_ref[pl.ds(HALF, HALF), :], preferred_element_type=F32)
        + jnp.dot(comes, v1_ref[pl.ds(HALF, HALF), :], preferred_element_type=F32)
    ).astype(BF16)
    out_ref[pl.ds(0, HALF), :] = v0_ref[pl.ds(0, HALF), :]
    out_ref[pl.ds(HALF, HALF), :] = rows
    window_ref[...] = jnp.dot(taken, rows, preferred_element_type=F32).astype(BF16)


def inner_swap(v0, v1):
    return pl.pallas_call(
        inner_swap_kernel,
        in_specs=[VMEM] * 2,
        out_specs=[VMEM] * 2,
        out_shape=[jax.ShapeDtypeStruct((2 * HALF, 512), BF16), jax.ShapeDtypeStruct((CAP, 512), BF16)],
        compiler_params=pltpu.CompilerParams(vmem_limit_bytes=8 * MIB),
        cost_estimate=FREE,
        name="inner_swap",
    )(v0, v1)


def outer_swap_kernel(v0_ref, rows_ref, window_ref, out_ref):
    tokens = out_ref.shape[0]
    info = v0_ref[pl.ds(tokens, INFO), pl.ds(0, HALF)].astype(F32).astype(jnp.int32)
    first = jnp.broadcast_to(info[2:3, :], (HALF, HALF))
    extent = jnp.broadcast_to(info[3:4, :], (HALF, HALF))
    place = lax.broadcasted_iota(jnp.int32, (HALF, HALF), 0) + HALF
    inner = lax.broadcasted_iota(jnp.int32, (HALF, HALF), 1)
    moved = (place >= first) & (place < first + extent)
    stays = jnp.where(~moved & (place == inner + HALF), 1.0, 0.0).astype(BF16)
    comes = jnp.where(moved & (place - first == inner), 1.0, 0.0).astype(BF16)[:, :CAP]
    out_ref[pl.ds(0, HALF), :] = rows_ref[pl.ds(0, HALF), :]
    out_ref[pl.ds(HALF, HALF), :] = (
        jnp.dot(stays, rows_ref[pl.ds(HALF, HALF), :], preferred_element_type=F32)
        + jnp.dot(comes, window_ref[...], preferred_element_type=F32)
    ).astype(BF16)


def outer_swap(v0, rows, window):
    return pl.pallas_call(
        outer_swap_kernel,
        in_specs=[VMEM] * 3,
        out_specs=VMEM,
        out_shape=jax.ShapeDtypeStruct(rows.shape, BF16),
        compiler_params=pltpu.CompilerParams(vmem_limit_bytes=8 * MIB),
        cost_estimate=FREE,
        name="outer_swap",
    )(v0, rows, window)


def place_kernel(core, pair_ref, *rest):
    *_, out_ref, wide, sems = rest
    copies = []
    for y in range(2):
        wide[y] = pair_ref[y].astype(F32)
        row = pl.multiple_of((lax.axis_index("dp") ^ (y << 1 | core)) * LANE, LANE)
        copies.append(pltpu.make_async_copy(wide.at[y], out_ref.at[pl.ds(row, LANE), :], sems.at[y]))
        copies[-1].start()
    for copy in copies:
        copy.wait()


def place(core, pair, *placed):
    return pl.pallas_call(
        functools.partial(place_kernel, core),
        in_specs=[VMEM] + [HBM] * len(placed),
        out_specs=HBM,
        out_shape=jax.ShapeDtypeStruct((512, 512), F32),
        scratch_shapes=[pltpu.VMEM((2, LANE, 512), F32), pltpu.SemaphoreType.DMA((2,))],
        input_output_aliases={1: 0} if placed else {},
        compiler_params=pltpu.CompilerParams(vmem_limit_bytes=8 * MIB),
        cost_estimate=FREE,
        name="place",
    )(pair, *placed)


def fold_kernel(base_ref, arrived_ref, out_ref):
    out_ref[...] = base_ref[...] + arrived_ref[...].astype(F32)


def fold(base, arrived):
    return pl.pallas_call(
        fold_kernel,
        in_specs=[VMEM] * 2,
        out_specs=VMEM,
        out_shape=jax.ShapeDtypeStruct(base.shape, F32),
        compiler_params=pltpu.CompilerParams(vmem_limit_bytes=8 * MIB),
        cost_estimate=pl.CostEstimate(flops=6_000_000_000, bytes_accessed=0, transcendentals=0),
        name="fold",
    )(base, arrived)


def reduce_by_axis(layer_input, *args):
    near = xor_permute(layer_input, CORE)
    v0 = front(*args)
    v1 = xor_permute(v0, CORE)

    def sums(parts, dtype, v=v0):
        return partial_sums(parts, dtype, layer_input, near, v, v1)

    def after_all(*values):
        return lax.optimization_barrier(values)

    def add(*terms):
        total = terms[0]
        for term in terms[1:]:
            total = total + term.astype(F32)
        return total

    far_b, = sums([(((3, 1, 1),), 0, 512)], BF16)
    far_a, = sums([(((2, 1, 1),), 0, 512)], BF16)
    every = ((1, 1), (1, 0), (0, 1), (0, 0))
    side_b, pair_some = sums([(((3, 0, 1),), 0, 512), (tuple((1, *at) for at in every[:3]), 0, 256)], BF16)
    pair_rest, side_a = sums(
        [(tuple((1, *at) for at in every[:3]), 256, 256), (((2, 1, 0),), 0, 512)], BF16, after_all(v0, pair_some)[0]
    )
    keep_b, keep_a = sums([(((3, 1, 0), (3, 0, 0)), 0, 512), (((2, 0, 1), (2, 0, 0)), 0, 512)], F32)
    far_b = xor_permute(far_b, X)
    side_b = xor_permute(side_b, X)
    far_a = xor_permute(far_a, Y)
    pair_some = xor_permute(pair_some, Z1)
    pair_rest = xor_permute(pair_rest, Z1)
    far_b, far_a = after_all(far_b, far_a)
    on_b = add(keep_b[:LANE], far_b).astype(BF16)
    v0_late = after_all(v0, on_b)[0]
    rows, window = inner_swap(v0_late, v1)
    own_some, own_rest = sums([(tuple((0, *at) for at in every), start, 256) for start in (0, 256)], F32, v0_late)
    pair_own, = sums([(((1, 0, 0),), 0, 512)], BF16, v0_late)
    on_b = xor_permute(on_b, Y)
    side_a = xor_permute(jnp.concatenate([side_a, window]), Y)
    side_a, window = side_a[:LANE], side_a[LANE:]
    on_a = xor_permute(add(keep_a[:LANE], far_a).astype(BF16), X)
    z3 = add(keep_b[LANE:], side_b, on_b).astype(BF16)
    pair_some, pair_own = after_all(pair_some, pair_own, z3)[:2]
    z3 = xor_permute(z3, Z1)
    pair_own = xor_permute(pair_own, Z1)
    z2 = add(keep_a[LANE:], side_a, on_a, z3).astype(BF16)

    some = add(own_some[:3 * LANE], pair_some)
    some_in = xor_permute(some[:2 * LANE].astype(BF16), Y)
    rest = add(own_rest[:3 * LANE], after_all(pair_rest, some)[0])
    rest_far, rest_y, rest_x = (rest[row:row + LANE] for row in range(0, 3 * LANE, LANE))
    rest_in = xor_permute(jnp.concatenate([rest_far, rest_x]).astype(BF16), X)
    some_in = after_all(some_in, z2)[0]
    z2 = xor_permute(z2, Z2)
    some_on = add(some[2 * LANE:], some_in[:LANE]).astype(BF16)
    rest_in = after_all(rest_in, some_on)[0]
    some_on = xor_permute(some_on, X)
    rest_on = xor_permute(add(rest_y, rest_in[:LANE]).astype(BF16), Y)
    base = jnp.concatenate([
        add(own_some[3 * LANE:], pair_own[:, :256], some_in[LANE:]),
        add(own_rest[3 * LANE:], pair_own[:, 256:], rest_in[LANE:]),
    ], axis=1)
    mine = add(fold(base, z2), jnp.concatenate([some_on, rest_on], axis=1)).astype(BF16)
    from_y = xor_permute(mine, Y)
    value_grad = outer_swap(v0, rows, after_all(window, mine)[0])
    from_y, value_grad = after_all(from_y, value_grad)
    pair = jnp.stack([mine, from_y])
    near_pair = xor_permute(pair, CORE)
    half = place(0, pair)
    near_pair, half = after_all(near_pair, half)
    return place(1, near_pair, half), value_grad


def swapped(block, axis, distance):
    count = lax.axis_size(axis)
    route = []
    for low in range(count):
        high = low | 1 << distance
        if high != low and high < count:
            route += [(low, high), (high, low)]
    return lax.ppermute(block, axis, route)


def blend_rows(item, incoming, offset, extent):
    inside = (jnp.arange(CAP) < extent)[:, None]
    chosen = jnp.where(inside, incoming, lax.dynamic_slice_in_dim(item, offset, CAP, 0))
    return lax.dynamic_update_slice_in_dim(item, chosen, offset, 0)


def reduce_by_owner(layer_input, *args):
    swap_start, swap_rows = args[-2:]
    tokens = layer_input.shape[0]
    values = front(*args)[:tokens]
    balanced = values
    for level in range(lax.axis_size("dp").bit_length() - 1):
        offset = swap_start[0, level]
        window = lax.dynamic_slice_in_dim(balanced, offset, CAP, 0)
        balanced = blend_rows(balanced, swapped(window, "dp", level), offset, swap_rows[0, level])
    owners = lax.axis_size("fsdp")
    owned = (D + owners - 1) // owners
    padded = jnp.pad(layer_input, ((0, 0), (0, owned * owners - D)))
    arranged = lax.all_to_all(
        padded.reshape(tokens, owners, owned), "fsdp", split_axis=1, concat_axis=0, tiled=True
    )
    block = lax.dot_general(
        arranged.reshape(-1, owned),
        lax.all_gather(values, "fsdp", axis=0, tiled=True),
        (((0,), (0,)), ((), ())),
        preferred_element_type=F32,
    )
    return lax.psum(block, "dp"), balanced


def on_device(layer_input, *args):
    if lax.axis_size("dp") == 4 and lax.axis_size("fsdp") == 8:
        return reduce_by_axis(layer_input, *args)
    return reduce_by_owner(layer_input, *args)


def solution(mesh):
    return jax.shard_map(
        on_device,
        mesh=mesh,
        in_specs=(
            P(("dp", "fsdp"), None),
            P(("dp", "fsdp"), None),
            P(("dp", "fsdp"), None),
            P(("dp", "fsdp"), None),
            P(("dp", "fsdp")),
            P(("dp", "fsdp")),
            P(),
            P(("dp", "fsdp")),
            P(("dp", "fsdp"), None),
            P(("dp", "fsdp"), None),
        ),
        out_specs=(P("fsdp", None), P(("dp", "fsdp"), None)),
        check_vma=False,
    )
```

```python
import functools
import math

import jax
import jax.numpy as jnp
from jax import lax
from jax.experimental import pallas as pl
from jax.experimental.pallas import tpu as pltpu
from jax.sharding import PartitionSpec as P

D = 4096
HD = 128
CAP = 32
HALF = 128
SEG = 16
LANE = 128
INFO = 16
MIB = 1 << 20
FREE = pl.CostEstimate(flops=0, bytes_accessed=0, transcendentals=0)
BF16 = jnp.bfloat16
F32 = jnp.float32

VMEM = pl.BlockSpec(memory_space=pltpu.VMEM)
HBM = pl.BlockSpec(memory_space=pltpu.HBM)


def attend_half(per_group, folded, span, q_ref, k_ref, g_ref, allowed, factor):
    heads = q_ref.shape[1] // HD
    groups = heads // per_group
    scores = [
        lax.dot_general(
            k_ref[span, pl.ds(group * HD, HD)],
            jnp.concatenate(
                [q_ref[span, pl.ds((group * per_group + n) * HD, HD)] for n in range(per_group)], axis=0
            ),
            (((1,), (1,)), ((), ())),
            preferred_element_type=F32,
        )
        for group in range(groups)
    ]
    weighted = [
        (g_ref[span, pl.ds(head * HD, HD)].astype(F32) * factor).astype(BF16) for head in range(heads)
    ]
    if folded:
        block = lax.broadcasted_iota(jnp.int32, (SEG, HALF), 1) // SEG
    probs = []
    for head in range(heads):
        n = head % per_group
        own = scores[head // per_group][:, n * HALF:(n + 1) * HALF]
        if folded:
            own = fold_blocks(own, block)
        own = jnp.where(allowed, own, -1e30)
        expo = jnp.exp2((own - jnp.max(own, axis=0, keepdims=True)) * (HD ** (-0.5) * math.log2(math.e)))
        prob = (expo * (1.0 / jnp.sum(expo, axis=0, keepdims=True))).astype(BF16)
        if folded:
            prob = jnp.concatenate(
                [jnp.where(block == b, prob, jnp.zeros_like(prob)) for b in range(HALF // SEG)], axis=0
            )
        probs.append(prob)
    return [
        jnp.dot(
            jnp.concatenate(probs[head:head + per_group], axis=1),
            jnp.concatenate(weighted[head:head + per_group], axis=0),
            preferred_element_type=F32,
        ).astype(BF16)
        for head in range(0, heads, per_group)
    ]


def fold_blocks(square, block):
    total = square[:SEG]
    for b in range(1, HALF // SEG):
        total = jnp.where(block == b, square[b * SEG:(b + 1) * SEG], total)
    return total


def mask_and_factor(folded, span, loss_ref, exponent_ref, ids_ref, index_ref):
    exponent = exponent_ref[0]
    unscale = jnp.float32(1.0)
    for bit in range(5):
        unscale = unscale * jnp.where((exponent >> bit) & 1 == 1, jnp.float32(2.0 ** -(1 << bit)), 1.0)
    row = lax.broadcasted_iota(jnp.int32, (HALF, HALF), 0)
    col = lax.broadcasted_iota(jnp.int32, (HALF, HALF), 1)
    doc_i = jnp.broadcast_to(ids_ref[:, span], (HALF, HALF))
    allowed = (doc_i == doc_i.T) & (row <= col)
    if folded:
        allowed = fold_blocks(
            jnp.where(allowed, 1, 0), lax.broadcasted_iota(jnp.int32, (SEG, HALF), 1) // SEG
        ) == 1
    index = index_ref[:, span]
    factor = jnp.zeros((1, HALF), F32)
    for entry in range(loss_ref.shape[0]):
        factor = jnp.where(index == entry, loss_ref[entry], factor)
    return allowed, jnp.broadcast_to(factor * unscale, (HALF, HALF)).T


def front_kernel(
    per_group, loss_hbm, exponent_hbm, start_hbm, rows_hbm, q_hbm, k_hbm, g_hbm, ids_hbm, index_hbm, *rest
):
    v_ref, loss_ref, exponent_ref, start_ref, rows_ref, q_ref, k_ref, g_ref, ids_ref, index_ref, sems = rest
    count = 0

    def begin(source, target):
        nonlocal count
        copy = pltpu.make_async_copy(source, target, sems.at[count])
        copy.start()
        count += 1
        return copy

    small = [
        begin(source, target)
        for source, target in (
            (ids_hbm, ids_ref), (index_hbm, index_ref), (loss_hbm, loss_ref), (exponent_hbm, exponent_ref),
            (start_hbm, start_ref), (rows_hbm, rows_ref),
        )
    ]
    groups = k_ref.shape[1] // HD
    wide = per_group * HD
    loads = []
    for half in range(2):
        span = pl.ds(half * HALF, HALF)
        loads.append([
            begin(source.at[span, :], target.at[span, :])
            for source, target in ((q_hbm, q_ref), (k_hbm, k_ref), (g_hbm, g_ref))
        ])
    for copy in small:
        copy.wait()
    masks = [
        mask_and_factor(half == 1, pl.ds(half * HALF, HALF), loss_ref, exponent_ref, ids_ref, index_ref)
        for half in range(2)
    ]
    info_row = lax.broadcasted_iota(jnp.int32, (INFO, k_ref.shape[1]), 0)
    info = jnp.zeros(info_row.shape, jnp.int32)
    for level in range(min(start_ref.shape[1], INFO // 2)):
        info = jnp.where(info_row == 2 * level, start_ref[0, level], info)
        info = jnp.where(info_row == 2 * level + 1, rows_ref[0, level], info)
    v_ref[pl.ds(2 * HALF, INFO), :] = info.astype(F32).astype(BF16)
    for half in range(2):
        for copy in loads[half]:
            copy.wait()
        span = pl.ds(half * HALF, HALF)
        values = attend_half(per_group, half == 1, span, q_ref, k_ref, g_ref, *masks[half])
        for group, value in enumerate(values):
            v_ref[span, pl.ds(group * HD, HD)] = value


def front(query, key, grad, ids, index, loss, exponent, start, rows):
    tokens, key_width = key.shape
    per_group = query.shape[1] // key_width
    args = [
        loss, exponent, start, rows, query, key, grad, ids.reshape(1, tokens), index.reshape(1, tokens)
    ]
    return pl.pallas_call(
        functools.partial(front_kernel, per_group),
        in_specs=[HBM] * 9,
        out_specs=VMEM,
        out_shape=jax.ShapeDtypeStruct((tokens + INFO, key_width), BF16),
        scratch_shapes=[
            pltpu.SMEM(loss.shape, F32), pltpu.SMEM(exponent.shape, jnp.int32),
            pltpu.SMEM(start.shape, jnp.int32), pltpu.SMEM(rows.shape, jnp.int32),
            pltpu.VMEM(query.shape, BF16), pltpu.VMEM(key.shape, BF16), pltpu.VMEM(grad.shape, BF16),
            pltpu.VMEM((1, tokens), jnp.int32), pltpu.VMEM((1, tokens), jnp.int32),
            pltpu.SemaphoreType.DMA((12,)),
        ],
        compiler_params=pltpu.CompilerParams(vmem_limit_bytes=24 * MIB),
        cost_estimate=FREE,
        name="front",
    )(*[arg if arg is exponent else pltpu.with_memory_space_constraint(arg, pltpu.HBM) for arg in args])


CORE, Y, X, Z1, Z2 = 8, 16, 1, 2, 4


def xor_permute(value, mask):
    count = lax.axis_size("dp") * lax.axis_size("fsdp")
    return lax.ppermute(value, ("dp", "fsdp"), [(i, i ^ mask) for i in range(count)])


def partial_kernel(parts, own_ref, near_ref, v0_ref, v1_ref, *out_refs):
    dp = lax.axis_index("dp")
    fsdp = lax.axis_index("fsdp")
    loaded = {}

    def block(z, y, x):
        if (z, y, x) not in loaded:
            owner = fsdp ^ (z << 1 | x)
            column = pl.multiple_of(owner * (4 * LANE) + (dp ^ (y << 1)) * LANE, LANE)
            loaded[z, y, x] = jnp.concatenate([ref[:, pl.ds(column, LANE)] for ref in (own_ref, near_ref)], axis=0)
        return loaded[z, y, x]

    for (blocks, start, width), out_ref in zip(parts, out_refs):
        v = jnp.concatenate([ref[pl.ds(0, 2 * HALF), pl.ds(start, width)] for ref in (v0_ref, v1_ref)], axis=0)
        total = lax.dot_general(
            jnp.concatenate([block(*place) for place in blocks], axis=1), v, (((0,), (0,)), ((), ())),
            preferred_element_type=F32,
        )
        out_ref[...] = total.astype(out_ref.dtype)


def partial_sums(parts, dtype, own, near, v0, v1):
    return pl.pallas_call(
        functools.partial(partial_kernel, parts),
        in_specs=[VMEM] * 4,
        out_specs=[VMEM] * len(parts),
        out_shape=[jax.ShapeDtypeStruct((len(blocks) * LANE, width), dtype) for blocks, _, width in parts],
        compiler_params=pltpu.CompilerParams(vmem_limit_bytes=24 * MIB),
        cost_estimate=FREE,
        name="partial_sums",
    )(own, near, v0, v1)


def inner_swap_kernel(v0_ref, v1_ref, out_ref, window_ref):
    tokens = out_ref.shape[0]
    infos = [ref[pl.ds(tokens, INFO), pl.ds(0, HALF)].astype(F32).astype(jnp.int32) for ref in (v0_ref, v1_ref)]

    def table(device, entry):
        return jnp.broadcast_to(infos[device][entry:entry + 1, :], (HALF, HALF))

    place = lax.broadcasted_iota(jnp.int32, (HALF, HALF), 0) + HALF
    inner = lax.broadcasted_iota(jnp.int32, (HALF, HALF), 1) + HALF
    first = table(0, 0)
    moved = (place >= first) & (place < first + table(0, 1))
    stays = jnp.where(~moved & (place == inner), 1.0, 0.0).astype(BF16)
    comes = jnp.where(moved & (place + table(1, 0) - first == inner), 1.0, 0.0).astype(BF16)
    taken = jnp.where(place - HALF + table(0, 2) == inner, 1.0, 0.0).astype(BF16)[:CAP]
    rows = (
        jnp.dot(stays, v0_ref[pl.ds(HALF, HALF), :], preferred_element_type=F32)
        + jnp.dot(comes, v1_ref[pl.ds(HALF, HALF), :], preferred_element_type=F32)
    ).astype(BF16)
    out_ref[pl.ds(0, HALF), :] = v0_ref[pl.ds(0, HALF), :]
    out_ref[pl.ds(HALF, HALF), :] = rows
    window_ref[...] = jnp.dot(taken, rows, preferred_element_type=F32).astype(BF16)


def inner_swap(v0, v1):
    return pl.pallas_call(
        inner_swap_kernel,
        in_specs=[VMEM] * 2,
        out_specs=[VMEM] * 2,
        out_shape=[jax.ShapeDtypeStruct((2 * HALF, 512), BF16), jax.ShapeDtypeStruct((CAP, 512), BF16)],
        compiler_params=pltpu.CompilerParams(vmem_limit_bytes=8 * MIB),
        cost_estimate=FREE,
        name="inner_swap",
    )(v0, v1)


def outer_swap_kernel(v0_ref, rows_ref, window_ref, out_ref):
    tokens = out_ref.shape[0]
    info = v0_ref[pl.ds(tokens, INFO), pl.ds(0, HALF)].astype(F32).astype(jnp.int32)
    first = jnp.broadcast_to(info[2:3, :], (HALF, HALF))
    extent = jnp.broadcast_to(info[3:4, :], (HALF, HALF))
    place = lax.broadcasted_iota(jnp.int32, (HALF, HALF), 0) + HALF
    inner = lax.broadcasted_iota(jnp.int32, (HALF, HALF), 1)
    moved = (place >= first) & (place < first + extent)
    stays = jnp.where(~moved & (place == inner + HALF), 1.0, 0.0).astype(BF16)
    comes = jnp.where(moved & (place - first == inner), 1.0, 0.0).astype(BF16)[:, :CAP]
    out_ref[pl.ds(0, HALF), :] = rows_ref[pl.ds(0, HALF), :]
    out_ref[pl.ds(HALF, HALF), :] = (
        jnp.dot(stays, rows_ref[pl.ds(HALF, HALF), :], preferred_element_type=F32)
        + jnp.dot(comes, window_ref[...], preferred_element_type=F32)
    ).astype(BF16)


def outer_swap(v0, rows, window):
    return pl.pallas_call(
        outer_swap_kernel,
        in_specs=[VMEM] * 3,
        out_specs=VMEM,
        out_shape=jax.ShapeDtypeStruct(rows.shape, BF16),
        compiler_params=pltpu.CompilerParams(vmem_limit_bytes=8 * MIB),
        cost_estimate=FREE,
        name="outer_swap",
    )(v0, rows, window)


def place_kernel(core, pair_ref, *rest):
    *_, out_ref, wide, sems = rest
    copies = []
    for y in range(2):
        wide[y] = pair_ref[y].astype(F32)
        row = pl.multiple_of((lax.axis_index("dp") ^ (y << 1 | core)) * LANE, LANE)
        copies.append(pltpu.make_async_copy(wide.at[y], out_ref.at[pl.ds(row, LANE), :], sems.at[y]))
        copies[-1].start()
    for copy in copies:
        copy.wait()


def place(core, pair, *placed):
    return pl.pallas_call(
        functools.partial(place_kernel, core),
        in_specs=[VMEM] + [HBM] * len(placed),
        out_specs=HBM,
        out_shape=jax.ShapeDtypeStruct((512, 512), F32),
        scratch_shapes=[pltpu.VMEM((2, LANE, 512), F32), pltpu.SemaphoreType.DMA((2,))],
        input_output_aliases={1: 0} if placed else {},
        compiler_params=pltpu.CompilerParams(vmem_limit_bytes=8 * MIB),
        cost_estimate=FREE,
        name="place",
    )(pair, *placed)


def fold_kernel(base_ref, arrived_ref, out_ref):
    out_ref[...] = base_ref[...] + arrived_ref[...].astype(F32)


def fold(base, arrived):
    return pl.pallas_call(
        fold_kernel,
        in_specs=[VMEM] * 2,
        out_specs=VMEM,
        out_shape=jax.ShapeDtypeStruct(base.shape, F32),
        compiler_params=pltpu.CompilerParams(vmem_limit_bytes=8 * MIB),
        cost_estimate=pl.CostEstimate(flops=6_000_000_000, bytes_accessed=0, transcendentals=0),
        name="fold",
    )(base, arrived)


def reduce_by_axis(layer_input, *args):
    near = xor_permute(layer_input, CORE)
    v0 = front(*args)
    v1 = xor_permute(v0, CORE)

    def sums(parts, dtype, v=v0):
        return partial_sums(parts, dtype, layer_input, near, v, v1)

    def after_all(*values):
        return lax.optimization_barrier(values)

    def add(*terms):
        total = terms[0]
        for term in terms[1:]:
            total = total + term.astype(F32)
        return total

    far_b, = sums([(((3, 1, 1),), 0, 512)], BF16)
    far_a, = sums([(((2, 1, 1),), 0, 512)], BF16)
    every = ((1, 1), (1, 0), (0, 1), (0, 0))
    side_b, pair_some = sums([(((3, 0, 1),), 0, 512), (tuple((1, *at) for at in every[:3]), 0, 256)], BF16)
    pair_rest, side_a = sums(
        [(tuple((1, *at) for at in every[:3]), 256, 256), (((2, 1, 0),), 0, 512)], BF16, after_all(v0, pair_some)[0]
    )
    keep_b, keep_a = sums([(((3, 1, 0), (3, 0, 0)), 0, 512), (((2, 0, 1), (2, 0, 0)), 0, 512)], F32)
    far_b = xor_permute(far_b, X)
    side_b = xor_permute(side_b, X)
    far_a = xor_permute(far_a, Y)
    pair_some = xor_permute(pair_some, Z1)
    pair_rest = xor_permute(pair_rest, Z1)
    far_b, far_a = after_all(far_b, far_a)
    on_b = add(keep_b[:LANE], far_b).astype(BF16)
    v0_late = after_all(v0, on_b)[0]
    rows, window = inner_swap(v0_late, v1)
    own_some, own_rest = sums([(tuple((0, *at) for at in every), start, 256) for start in (0, 256)], F32, v0_late)
    pair_own, = sums([(((1, 0, 0),), 0, 512)], BF16, v0_late)
    on_b = xor_permute(on_b, Y)
    on_a = xor_permute(add(keep_a[:LANE], far_a).astype(BF16), X)
    z3 = add(keep_b[LANE:], side_b, on_b).astype(BF16)
    side_a = after_all(jnp.concatenate([side_a, window]), z3)[0]
    side_a = xor_permute(side_a, Y)
    side_a, window = side_a[:LANE], side_a[LANE:]
    pair_some, pair_own = after_all(pair_some, pair_own, z3)[:2]
    z3 = xor_permute(z3, Z1)
    pair_own = xor_permute(pair_own, Z1)
    z2 = add(keep_a[LANE:], side_a, on_a, z3).astype(BF16)

    some = add(own_some[:3 * LANE], pair_some)
    some_in = xor_permute(some[:2 * LANE].astype(BF16), Y)
    rest = add(own_rest[:3 * LANE], after_all(pair_rest, some)[0])
    rest_far, rest_y, rest_x = (rest[row:row + LANE] for row in range(0, 3 * LANE, LANE))
    rest_in = xor_permute(jnp.concatenate([rest_far, rest_x]).astype(BF16), X)
    some_in = after_all(some_in, z2)[0]
    z2 = xor_permute(z2, Z2)
    some_on = add(some[2 * LANE:], some_in[:LANE]).astype(BF16)
    rest_in = after_all(rest_in, some_on)[0]
    some_on = xor_permute(some_on, X)
    rest_on = xor_permute(add(rest_y, rest_in[:LANE]).astype(BF16), Y)
    base = jnp.concatenate([
        add(own_some[3 * LANE:], pair_own[:, :256], some_in[LANE:]),
        add(own_rest[3 * LANE:], pair_own[:, 256:], rest_in[LANE:]),
    ], axis=1)
    mine = add(fold(base, z2), jnp.concatenate([some_on, rest_on], axis=1)).astype(BF16)
    from_y = xor_permute(mine, Y)
    value_grad = outer_swap(v0, rows, after_all(window, mine)[0])
    from_y, value_grad = after_all(from_y, value_grad)
    pair = jnp.stack([mine, from_y])
    near_pair = xor_permute(pair, CORE)
    half = place(0, pair)
    near_pair, half = after_all(near_pair, half)
    return place(1, near_pair, half), value_grad


def swapped(block, axis, distance):
    count = lax.axis_size(axis)
    route = []
    for low in range(count):
        high = low | 1 << distance
        if high != low and high < count:
            route += [(low, high), (high, low)]
    return lax.ppermute(block, axis, route)


def blend_rows(item, incoming, offset, extent):
    inside = (jnp.arange(CAP) < extent)[:, None]
    chosen = jnp.where(inside, incoming, lax.dynamic_slice_in_dim(item, offset, CAP, 0))
    return lax.dynamic_update_slice_in_dim(item, chosen, offset, 0)


def reduce_by_owner(layer_input, *args):
    swap_start, swap_rows = args[-2:]
    tokens = layer_input.shape[0]
    values = front(*args)[:tokens]
    balanced = values
    for level in range(lax.axis_size("dp").bit_length() - 1):
        offset = swap_start[0, level]
        window = lax.dynamic_slice_in_dim(balanced, offset, CAP, 0)
        balanced = blend_rows(balanced, swapped(window, "dp", level), offset, swap_rows[0, level])
    owners = lax.axis_size("fsdp")
    owned = (D + owners - 1) // owners
    padded = jnp.pad(layer_input, ((0, 0), (0, owned * owners - D)))
    arranged = lax.all_to_all(
        padded.reshape(tokens, owners, owned), "fsdp", split_axis=1, concat_axis=0, tiled=True
    )
    block = lax.dot_general(
        arranged.reshape(-1, owned),
        lax.all_gather(values, "fsdp", axis=0, tiled=True),
        (((0,), (0,)), ((), ())),
        preferred_element_type=F32,
    )
    return lax.psum(block, "dp"), balanced


def on_device(layer_input, *args):
    if lax.axis_size("dp") == 4 and lax.axis_size("fsdp") == 8:
        return reduce_by_axis(layer_input, *args)
    return reduce_by_owner(layer_input, *args)


def solution(mesh):
    return jax.shard_map(
        on_device,
        mesh=mesh,
        in_specs=(
            P(("dp", "fsdp"), None),
            P(("dp", "fsdp"), None),
            P(("dp", "fsdp"), None),
            P(("dp", "fsdp"), None),
            P(("dp", "fsdp")),
            P(("dp", "fsdp")),
            P(),
            P(("dp", "fsdp")),
            P(("dp", "fsdp"), None),
            P(("dp", "fsdp"), None),
        ),
        out_specs=(P("fsdp", None), P(("dp", "fsdp"), None)),
        check_vma=False,
    )
```

```python
import functools
import math

import jax
import jax.numpy as jnp
from jax import lax
from jax.experimental import pallas as pl
from jax.experimental.pallas import tpu as pltpu
from jax.sharding import PartitionSpec as P

D = 4096
HD = 128
CAP = 32
HALF = 128
SEG = 16
LANE = 128
INFO = 16
MIB = 1 << 20
FREE = pl.CostEstimate(flops=0, bytes_accessed=0, transcendentals=0)
BF16 = jnp.bfloat16
F32 = jnp.float32

VMEM = pl.BlockSpec(memory_space=pltpu.VMEM)
HBM = pl.BlockSpec(memory_space=pltpu.HBM)


def attend_half(per_group, folded, span, q_ref, k_ref, g_ref, allowed, factor):
    heads = q_ref.shape[1] // HD
    groups = heads // per_group
    scores = [
        lax.dot_general(
            k_ref[span, pl.ds(group * HD, HD)],
            jnp.concatenate(
                [q_ref[span, pl.ds((group * per_group + n) * HD, HD)] for n in range(per_group)], axis=0
            ),
            (((1,), (1,)), ((), ())),
            preferred_element_type=F32,
        )
        for group in range(groups)
    ]
    weighted = [
        (g_ref[span, pl.ds(head * HD, HD)].astype(F32) * factor).astype(BF16) for head in range(heads)
    ]
    if folded:
        block = lax.broadcasted_iota(jnp.int32, (SEG, HALF), 1) // SEG
    probs = []
    for head in range(heads):
        n = head % per_group
        own = scores[head // per_group][:, n * HALF:(n + 1) * HALF]
        if folded:
            own = fold_blocks(own, block)
        own = jnp.where(allowed, own, -1e30)
        expo = jnp.exp2((own - jnp.max(own, axis=0, keepdims=True)) * (HD ** (-0.5) * math.log2(math.e)))
        prob = (expo * (1.0 / jnp.sum(expo, axis=0, keepdims=True))).astype(BF16)
        if folded:
            prob = jnp.concatenate(
                [jnp.where(block == b, prob, jnp.zeros_like(prob)) for b in range(HALF // SEG)], axis=0
            )
        probs.append(prob)
    return [
        jnp.dot(
            jnp.concatenate(probs[head:head + per_group], axis=1),
            jnp.concatenate(weighted[head:head + per_group], axis=0),
            preferred_element_type=F32,
        ).astype(BF16)
        for head in range(0, heads, per_group)
    ]


def fold_blocks(square, block):
    total = square[:SEG]
    for b in range(1, HALF // SEG):
        total = jnp.where(block == b, square[b * SEG:(b + 1) * SEG], total)
    return total


def mask_and_factor(folded, span, loss_ref, exponent_ref, ids_ref, index_ref):
    exponent = exponent_ref[0]
    unscale = jnp.float32(1.0)
    for bit in range(5):
        unscale = unscale * jnp.where((exponent >> bit) & 1 == 1, jnp.float32(2.0 ** -(1 << bit)), 1.0)
    row = lax.broadcasted_iota(jnp.int32, (HALF, HALF), 0)
    col = lax.broadcasted_iota(jnp.int32, (HALF, HALF), 1)
    doc_i = jnp.broadcast_to(ids_ref[:, span], (HALF, HALF))
    allowed = (doc_i == doc_i.T) & (row <= col)
    if folded:
        allowed = fold_blocks(
            jnp.where(allowed, 1, 0), lax.broadcasted_iota(jnp.int32, (SEG, HALF), 1) // SEG
        ) == 1
    index = index_ref[:, span]
    factor = jnp.zeros((1, HALF), F32)
    for entry in range(loss_ref.shape[0]):
        factor = jnp.where(index == entry, loss_ref[entry], factor)
    return allowed, jnp.broadcast_to(factor * unscale, (HALF, HALF)).T


def front_kernel(
    per_group, loss_hbm, exponent_hbm, start_hbm, rows_hbm, q_hbm, k_hbm, g_hbm, ids_hbm, index_hbm, *rest
):
    v_ref, loss_ref, exponent_ref, start_ref, rows_ref, q_ref, k_ref, g_ref, ids_ref, index_ref, sems = rest
    count = 0

    def begin(source, target):
        nonlocal count
        copy = pltpu.make_async_copy(source, target, sems.at[count])
        copy.start()
        count += 1
        return copy

    small = [
        begin(source, target)
        for source, target in (
            (ids_hbm, ids_ref), (index_hbm, index_ref), (loss_hbm, loss_ref), (exponent_hbm, exponent_ref),
            (start_hbm, start_ref), (rows_hbm, rows_ref),
        )
    ]
    groups = k_ref.shape[1] // HD
    wide = per_group * HD
    loads = []
    for half in range(2):
        span = pl.ds(half * HALF, HALF)
        loads.append([
            begin(source.at[span, :], target.at[span, :])
            for source, target in ((q_hbm, q_ref), (k_hbm, k_ref), (g_hbm, g_ref))
        ])
    for copy in small:
        copy.wait()
    masks = [
        mask_and_factor(half == 1, pl.ds(half * HALF, HALF), loss_ref, exponent_ref, ids_ref, index_ref)
        for half in range(2)
    ]
    info_row = lax.broadcasted_iota(jnp.int32, (INFO, k_ref.shape[1]), 0)
    info = jnp.zeros(info_row.shape, jnp.int32)
    for level in range(min(start_ref.shape[1], INFO // 2)):
        info = jnp.where(info_row == 2 * level, start_ref[0, level], info)
        info = jnp.where(info_row == 2 * level + 1, rows_ref[0, level], info)
    v_ref[pl.ds(2 * HALF, INFO), :] = info.astype(F32).astype(BF16)
    for half in range(2):
        for copy in loads[half]:
            copy.wait()
        span = pl.ds(half * HALF, HALF)
        values = attend_half(per_group, half == 1, span, q_ref, k_ref, g_ref, *masks[half])
        for group, value in enumerate(values):
            v_ref[span, pl.ds(group * HD, HD)] = value


def front(query, key, grad, ids, index, loss, exponent, start, rows):
    tokens, key_width = key.shape
    per_group = query.shape[1] // key_width
    args = [
        loss, exponent, start, rows, query, key, grad, ids.reshape(1, tokens), index.reshape(1, tokens)
    ]
    return pl.pallas_call(
        functools.partial(front_kernel, per_group),
        in_specs=[HBM] * 9,
        out_specs=VMEM,
        out_shape=jax.ShapeDtypeStruct((tokens + INFO, key_width), BF16),
        scratch_shapes=[
            pltpu.SMEM(loss.shape, F32), pltpu.SMEM(exponent.shape, jnp.int32),
            pltpu.SMEM(start.shape, jnp.int32), pltpu.SMEM(rows.shape, jnp.int32),
            pltpu.VMEM(query.shape, BF16), pltpu.VMEM(key.shape, BF16), pltpu.VMEM(grad.shape, BF16),
            pltpu.VMEM((1, tokens), jnp.int32), pltpu.VMEM((1, tokens), jnp.int32),
            pltpu.SemaphoreType.DMA((12,)),
        ],
        compiler_params=pltpu.CompilerParams(vmem_limit_bytes=24 * MIB),
        cost_estimate=FREE,
        name="front",
    )(*[arg if arg is exponent else pltpu.with_memory_space_constraint(arg, pltpu.HBM) for arg in args])


CORE, Y, X, Z1, Z2 = 8, 16, 1, 2, 4


def xor_permute(value, mask):
    count = lax.axis_size("dp") * lax.axis_size("fsdp")
    return lax.ppermute(value, ("dp", "fsdp"), [(i, i ^ mask) for i in range(count)])


def partial_kernel(parts, own_ref, near_ref, v0_ref, v1_ref, *out_refs):
    dp = lax.axis_index("dp")
    fsdp = lax.axis_index("fsdp")
    loaded = {}

    def block(z, y, x):
        if (z, y, x) not in loaded:
            owner = fsdp ^ (z << 1 | x)
            column = pl.multiple_of(owner * (4 * LANE) + (dp ^ (y << 1)) * LANE, LANE)
            loaded[z, y, x] = jnp.concatenate([ref[:, pl.ds(column, LANE)] for ref in (own_ref, near_ref)], axis=0)
        return loaded[z, y, x]

    for (blocks, start, width), out_ref in zip(parts, out_refs):
        v = jnp.concatenate([ref[pl.ds(0, 2 * HALF), pl.ds(start, width)] for ref in (v0_ref, v1_ref)], axis=0)
        total = lax.dot_general(
            jnp.concatenate([block(*place) for place in blocks], axis=1), v, (((0,), (0,)), ((), ())),
            preferred_element_type=F32,
        )
        out_ref[...] = total.astype(out_ref.dtype)


def partial_sums(parts, dtype, own, near, v0, v1):
    return pl.pallas_call(
        functools.partial(partial_kernel, parts),
        in_specs=[VMEM] * 4,
        out_specs=[VMEM] * len(parts),
        out_shape=[jax.ShapeDtypeStruct((len(blocks) * LANE, width), dtype) for blocks, _, width in parts],
        compiler_params=pltpu.CompilerParams(vmem_limit_bytes=24 * MIB),
        cost_estimate=FREE,
        name="partial_sums",
    )(own, near, v0, v1)


def inner_swap_kernel(v0_ref, v1_ref, out_ref, window_ref):
    tokens = out_ref.shape[0]
    infos = [ref[pl.ds(tokens, INFO), pl.ds(0, HALF)].astype(F32).astype(jnp.int32) for ref in (v0_ref, v1_ref)]

    def table(device, entry):
        return jnp.broadcast_to(infos[device][entry:entry + 1, :], (HALF, HALF))

    place = lax.broadcasted_iota(jnp.int32, (HALF, HALF), 0) + HALF
    inner = lax.broadcasted_iota(jnp.int32, (HALF, HALF), 1) + HALF
    first = table(0, 0)
    moved = (place >= first) & (place < first + table(0, 1))
    stays = jnp.where(~moved & (place == inner), 1.0, 0.0).astype(BF16)
    comes = jnp.where(moved & (place + table(1, 0) - first == inner), 1.0, 0.0).astype(BF16)
    taken = jnp.where(place - HALF + table(0, 2) == inner, 1.0, 0.0).astype(BF16)[:CAP]
    rows = (
        jnp.dot(stays, v0_ref[pl.ds(HALF, HALF), :], preferred_element_type=F32)
        + jnp.dot(comes, v1_ref[pl.ds(HALF, HALF), :], preferred_element_type=F32)
    ).astype(BF16)
    out_ref[pl.ds(0, HALF), :] = v0_ref[pl.ds(0, HALF), :]
    out_ref[pl.ds(HALF, HALF), :] = rows
    window_ref[...] = jnp.dot(taken, rows, preferred_element_type=F32).astype(BF16)


def inner_swap(v0, v1):
    return pl.pallas_call(
        inner_swap_kernel,
        in_specs=[VMEM] * 2,
        out_specs=[VMEM] * 2,
        out_shape=[jax.ShapeDtypeStruct((2 * HALF, 512), BF16), jax.ShapeDtypeStruct((CAP, 512), BF16)],
        compiler_params=pltpu.CompilerParams(vmem_limit_bytes=8 * MIB),
        cost_estimate=FREE,
        name="inner_swap",
    )(v0, v1)


def outer_swap_kernel(v0_ref, rows_ref, window_ref, out_ref):
    tokens = out_ref.shape[0]
    info = v0_ref[pl.ds(tokens, INFO), pl.ds(0, HALF)].astype(F32).astype(jnp.int32)
    first = jnp.broadcast_to(info[2:3, :], (HALF, HALF))
    extent = jnp.broadcast_to(info[3:4, :], (HALF, HALF))
    place = lax.broadcasted_iota(jnp.int32, (HALF, HALF), 0) + HALF
    inner = lax.broadcasted_iota(jnp.int32, (HALF, HALF), 1)
    moved = (place >= first) & (place < first + extent)
    stays = jnp.where(~moved & (place == inner + HALF), 1.0, 0.0).astype(BF16)
    comes = jnp.where(moved & (place - first == inner), 1.0, 0.0).astype(BF16)[:, :CAP]
    out_ref[pl.ds(0, HALF), :] = rows_ref[pl.ds(0, HALF), :]
    out_ref[pl.ds(HALF, HALF), :] = (
        jnp.dot(stays, rows_ref[pl.ds(HALF, HALF), :], preferred_element_type=F32)
        + jnp.dot(comes, window_ref[...], preferred_element_type=F32)
    ).astype(BF16)


def outer_swap(v0, rows, window):
    return pl.pallas_call(
        outer_swap_kernel,
        in_specs=[VMEM] * 3,
        out_specs=VMEM,
        out_shape=jax.ShapeDtypeStruct(rows.shape, BF16),
        compiler_params=pltpu.CompilerParams(vmem_limit_bytes=8 * MIB),
        cost_estimate=FREE,
        name="outer_swap",
    )(v0, rows, window)


def place_kernel(core, pair_ref, *rest):
    *_, out_ref, wide, sems = rest
    copies = []
    for y in range(2):
        wide[y] = pair_ref[y].astype(F32)
        row = pl.multiple_of((lax.axis_index("dp") ^ (y << 1 | core)) * LANE, LANE)
        copies.append(pltpu.make_async_copy(wide.at[y], out_ref.at[pl.ds(row, LANE), :], sems.at[y]))
        copies[-1].start()
    for copy in copies:
        copy.wait()


def place(core, pair, *placed):
    return pl.pallas_call(
        functools.partial(place_kernel, core),
        in_specs=[VMEM] + [HBM] * len(placed),
        out_specs=HBM,
        out_shape=jax.ShapeDtypeStruct((512, 512), F32),
        scratch_shapes=[pltpu.VMEM((2, LANE, 512), F32), pltpu.SemaphoreType.DMA((2,))],
        input_output_aliases={1: 0} if placed else {},
        compiler_params=pltpu.CompilerParams(vmem_limit_bytes=8 * MIB),
        cost_estimate=FREE,
        name="place",
    )(pair, *placed)


def fold_kernel(base_ref, arrived_ref, out_ref):
    out_ref[...] = base_ref[...] + arrived_ref[...].astype(F32)


def fold(base, arrived):
    return pl.pallas_call(
        fold_kernel,
        in_specs=[VMEM] * 2,
        out_specs=VMEM,
        out_shape=jax.ShapeDtypeStruct(base.shape, F32),
        compiler_params=pltpu.CompilerParams(vmem_limit_bytes=8 * MIB),
        cost_estimate=pl.CostEstimate(flops=6_000_000_000, bytes_accessed=0, transcendentals=0),
        name="fold",
    )(base, arrived)


def reduce_by_axis(layer_input, *args):
    near = xor_permute(layer_input, CORE)
    v0 = front(*args)
    v1 = xor_permute(v0, CORE)

    def sums(parts, dtype, v=v0):
        return partial_sums(parts, dtype, layer_input, near, v, v1)

    def after_all(*values):
        return lax.optimization_barrier(values)

    def add(*terms):
        total = terms[0]
        for term in terms[1:]:
            total = total + term.astype(F32)
        return total

    far_b, = sums([(((3, 1, 1),), 0, 512)], BF16)
    far_a, = sums([(((2, 1, 1),), 0, 512)], BF16)
    every = ((1, 1), (1, 0), (0, 1), (0, 0))
    side_b, pair_some = sums([(((3, 0, 1),), 0, 512), (tuple((1, *at) for at in every[:3]), 0, 256)], BF16)
    pair_rest, side_a = sums(
        [(tuple((1, *at) for at in every[:3]), 256, 256), (((2, 1, 0),), 0, 512)], BF16, after_all(v0, pair_some)[0]
    )
    keep_b, keep_a = sums([(((3, 1, 0), (3, 0, 0)), 0, 512), (((2, 0, 1), (2, 0, 0)), 0, 512)], F32)
    far_b = xor_permute(far_b, X)
    side_b = xor_permute(side_b, X)
    far_a = xor_permute(far_a, Y)
    pair_some = xor_permute(pair_some, Z1)
    pair_rest = xor_permute(pair_rest, Z1)
    far_b, far_a = after_all(far_b, far_a)
    on_b = add(keep_b[:LANE], far_b).astype(BF16)
    v0_late = after_all(v0, on_b)[0]
    rows, window = inner_swap(v0_late, v1)
    own_some, own_rest = sums([(tuple((0, *at) for at in every), start, 256) for start in (0, 256)], F32, v0_late)
    pair_own, = sums([(((1, 0, 0),), 0, 512)], BF16, v0_late)
    on_b = xor_permute(on_b, Y)
    on_a = xor_permute(add(keep_a[:LANE], far_a).astype(BF16), X)
    z3 = add(keep_b[LANE:], side_b, on_b).astype(BF16)
    side_a = xor_permute(after_all(jnp.concatenate([side_a, window]), own_some)[0], Y)
    side_a, window = side_a[:LANE], side_a[LANE:]
    pair_some = after_all(pair_some, z3)[0]
    z3 = xor_permute(z3, Z1)
    z2 = add(keep_a[LANE:], side_a, on_a, z3).astype(BF16)

    some = add(own_some[:3 * LANE], pair_some)
    some_in = xor_permute(some[:2 * LANE].astype(BF16), Y)
    rest = add(own_rest[:3 * LANE], after_all(pair_rest, some)[0])
    rest_far, rest_y, rest_x = (rest[row:row + LANE] for row in range(0, 3 * LANE, LANE))
    rest_in = xor_permute(jnp.concatenate([rest_far, rest_x]).astype(BF16), X)
    some_in, pair_own = after_all(some_in, pair_own, z2)[:2]
    z2 = xor_permute(z2, Z2)
    pair_own = xor_permute(pair_own, Z1)
    some_on = add(some[2 * LANE:], some_in[:LANE]).astype(BF16)
    rest_in = after_all(rest_in, some_on)[0]
    some_on = xor_permute(some_on, X)
    rest_on = add(rest_y, rest_in[:LANE]).astype(BF16)
    pair_own = after_all(pair_own, rest_on)[0]
    rest_on = xor_permute(rest_on, Y)
    base = jnp.concatenate([
        add(own_some[3 * LANE:], pair_own[:, :256], some_in[LANE:]),
        add(own_rest[3 * LANE:], pair_own[:, 256:], rest_in[LANE:]),
    ], axis=1)
    mine = add(fold(base, z2), jnp.concatenate([some_on, rest_on], axis=1)).astype(BF16)
    from_y = xor_permute(mine, Y)
    value_grad = outer_swap(v0, rows, after_all(window, mine)[0])
    from_y, value_grad = after_all(from_y, value_grad)
    pair = jnp.stack([mine, from_y])
    near_pair = xor_permute(pair, CORE)
    half = place(0, pair)
    near_pair, half = after_all(near_pair, half)
    return place(1, near_pair, half), value_grad


def swapped(block, axis, distance):
    count = lax.axis_size(axis)
    route = []
    for low in range(count):
        high = low | 1 << distance
        if high != low and high < count:
            route += [(low, high), (high, low)]
    return lax.ppermute(block, axis, route)


def blend_rows(item, incoming, offset, extent):
    inside = (jnp.arange(CAP) < extent)[:, None]
    chosen = jnp.where(inside, incoming, lax.dynamic_slice_in_dim(item, offset, CAP, 0))
    return lax.dynamic_update_slice_in_dim(item, chosen, offset, 0)


def reduce_by_owner(layer_input, *args):
    swap_start, swap_rows = args[-2:]
    tokens = layer_input.shape[0]
    values = front(*args)[:tokens]
    balanced = values
    for level in range(lax.axis_size("dp").bit_length() - 1):
        offset = swap_start[0, level]
        window = lax.dynamic_slice_in_dim(balanced, offset, CAP, 0)
        balanced = blend_rows(balanced, swapped(window, "dp", level), offset, swap_rows[0, level])
    owners = lax.axis_size("fsdp")
    owned = (D + owners - 1) // owners
    padded = jnp.pad(layer_input, ((0, 0), (0, owned * owners - D)))
    arranged = lax.all_to_all(
        padded.reshape(tokens, owners, owned), "fsdp", split_axis=1, concat_axis=0, tiled=True
    )
    block = lax.dot_general(
        arranged.reshape(-1, owned),
        lax.all_gather(values, "fsdp", axis=0, tiled=True),
        (((0,), (0,)), ((), ())),
        preferred_element_type=F32,
    )
    return lax.psum(block, "dp"), balanced


def on_device(layer_input, *args):
    if lax.axis_size("dp") == 4 and lax.axis_size("fsdp") == 8:
        return reduce_by_axis(layer_input, *args)
    return reduce_by_owner(layer_input, *args)


def solution(mesh):
    return jax.shard_map(
        on_device,
        mesh=mesh,
        in_specs=(
            P(("dp", "fsdp"), None),
            P(("dp", "fsdp"), None),
            P(("dp", "fsdp"), None),
            P(("dp", "fsdp"), None),
            P(("dp", "fsdp")),
            P(("dp", "fsdp")),
            P(),
            P(("dp", "fsdp")),
            P(("dp", "fsdp"), None),
            P(("dp", "fsdp"), None),
        ),
        out_specs=(P("fsdp", None), P(("dp", "fsdp"), None)),
        check_vma=False,
    )
```

```python
import functools
import math

import jax
import jax.numpy as jnp
from jax import lax
from jax.experimental import pallas as pl
from jax.experimental.pallas import tpu as pltpu
from jax.sharding import PartitionSpec as P

D = 4096
HD = 128
CAP = 32
HALF = 128
SEG = 16
LANE = 128
INFO = 16
MIB = 1 << 20
FREE = pl.CostEstimate(flops=0, bytes_accessed=0, transcendentals=0)
BF16 = jnp.bfloat16
F32 = jnp.float32

VMEM = pl.BlockSpec(memory_space=pltpu.VMEM)
HBM = pl.BlockSpec(memory_space=pltpu.HBM)


def attend_half(per_group, folded, span, q_ref, k_ref, g_ref, allowed, factor):
    heads = q_ref.shape[1] // HD
    groups = heads // per_group
    scores = [
        lax.dot_general(
            k_ref[span, pl.ds(group * HD, HD)],
            jnp.concatenate(
                [q_ref[span, pl.ds((group * per_group + n) * HD, HD)] for n in range(per_group)], axis=0
            ),
            (((1,), (1,)), ((), ())),
            preferred_element_type=F32,
        )
        for group in range(groups)
    ]
    weighted = [
        (g_ref[span, pl.ds(head * HD, HD)].astype(F32) * factor).astype(BF16) for head in range(heads)
    ]
    if folded:
        block = lax.broadcasted_iota(jnp.int32, (SEG, HALF), 1) // SEG
    probs = []
    for head in range(heads):
        n = head % per_group
        own = scores[head // per_group][:, n * HALF:(n + 1) * HALF]
        if folded:
            own = fold_blocks(own, block)
        own = jnp.where(allowed, own, -1e30)
        expo = jnp.exp2((own - jnp.max(own, axis=0, keepdims=True)) * (HD ** (-0.5) * math.log2(math.e)))
        prob = (expo * (1.0 / jnp.sum(expo, axis=0, keepdims=True))).astype(BF16)
        if folded:
            prob = jnp.concatenate(
                [jnp.where(block == b, prob, jnp.zeros_like(prob)) for b in range(HALF // SEG)], axis=0
            )
        probs.append(prob)
    return [
        jnp.dot(
            jnp.concatenate(probs[head:head + per_group], axis=1),
            jnp.concatenate(weighted[head:head + per_group], axis=0),
            preferred_element_type=F32,
        ).astype(BF16)
        for head in range(0, heads, per_group)
    ]


def fold_blocks(square, block):
    total = square[:SEG]
    for b in range(1, HALF // SEG):
        total = jnp.where(block == b, square[b * SEG:(b + 1) * SEG], total)
    return total


def mask_and_factor(folded, span, loss_ref, exponent_ref, ids_ref, index_ref):
    exponent = exponent_ref[0]
    unscale = jnp.float32(1.0)
    for bit in range(5):
        unscale = unscale * jnp.where((exponent >> bit) & 1 == 1, jnp.float32(2.0 ** -(1 << bit)), 1.0)
    row = lax.broadcasted_iota(jnp.int32, (HALF, HALF), 0)
    col = lax.broadcasted_iota(jnp.int32, (HALF, HALF), 1)
    doc_i = jnp.broadcast_to(ids_ref[:, span], (HALF, HALF))
    allowed = (doc_i == doc_i.T) & (row <= col)
    if folded:
        allowed = fold_blocks(
            jnp.where(allowed, 1, 0), lax.broadcasted_iota(jnp.int32, (SEG, HALF), 1) // SEG
        ) == 1
    index = index_ref[:, span]
    factor = jnp.zeros((1, HALF), F32)
    for entry in range(loss_ref.shape[0]):
        factor = jnp.where(index == entry, loss_ref[entry], factor)
    return allowed, jnp.broadcast_to(factor * unscale, (HALF, HALF)).T


def front_kernel(
    per_group, loss_hbm, exponent_hbm, start_hbm, rows_hbm, q_hbm, k_hbm, g_hbm, ids_hbm, index_hbm, *rest
):
    v_ref, loss_ref, exponent_ref, start_ref, rows_ref, q_ref, k_ref, g_ref, ids_ref, index_ref, sems = rest
    count = 0

    def begin(source, target):
        nonlocal count
        copy = pltpu.make_async_copy(source, target, sems.at[count])
        copy.start()
        count += 1
        return copy

    small = [
        begin(source, target)
        for source, target in (
            (ids_hbm, ids_ref), (index_hbm, index_ref), (loss_hbm, loss_ref), (exponent_hbm, exponent_ref),
            (start_hbm, start_ref), (rows_hbm, rows_ref),
        )
    ]
    groups = k_ref.shape[1] // HD
    wide = per_group * HD
    loads = []
    for half in range(2):
        span = pl.ds(half * HALF, HALF)
        loads.append([
            begin(source.at[span, :], target.at[span, :])
            for source, target in ((q_hbm, q_ref), (k_hbm, k_ref), (g_hbm, g_ref))
        ])
    for copy in small:
        copy.wait()
    masks = [
        mask_and_factor(half == 1, pl.ds(half * HALF, HALF), loss_ref, exponent_ref, ids_ref, index_ref)
        for half in range(2)
    ]
    info_row = lax.broadcasted_iota(jnp.int32, (INFO, k_ref.shape[1]), 0)
    info = jnp.zeros(info_row.shape, jnp.int32)
    for level in range(min(start_ref.shape[1], INFO // 2)):
        info = jnp.where(info_row == 2 * level, start_ref[0, level], info)
        info = jnp.where(info_row == 2 * level + 1, rows_ref[0, level], info)
    v_ref[pl.ds(2 * HALF, INFO), :] = info.astype(F32).astype(BF16)
    for half in range(2):
        for copy in loads[half]:
            copy.wait()
        span = pl.ds(half * HALF, HALF)
        values = attend_half(per_group, half == 1, span, q_ref, k_ref, g_ref, *masks[half])
        for group, value in enumerate(values):
            v_ref[span, pl.ds(group * HD, HD)] = value


def front(query, key, grad, ids, index, loss, exponent, start, rows):
    tokens, key_width = key.shape
    per_group = query.shape[1] // key_width
    args = [
        loss, exponent, start, rows, query, key, grad, ids.reshape(1, tokens), index.reshape(1, tokens)
    ]
    return pl.pallas_call(
        functools.partial(front_kernel, per_group),
        in_specs=[HBM] * 9,
        out_specs=VMEM,
        out_shape=jax.ShapeDtypeStruct((tokens + INFO, key_width), BF16),
        scratch_shapes=[
            pltpu.SMEM(loss.shape, F32), pltpu.SMEM(exponent.shape, jnp.int32),
            pltpu.SMEM(start.shape, jnp.int32), pltpu.SMEM(rows.shape, jnp.int32),
            pltpu.VMEM(query.shape, BF16), pltpu.VMEM(key.shape, BF16), pltpu.VMEM(grad.shape, BF16),
            pltpu.VMEM((1, tokens), jnp.int32), pltpu.VMEM((1, tokens), jnp.int32),
            pltpu.SemaphoreType.DMA((12,)),
        ],
        compiler_params=pltpu.CompilerParams(vmem_limit_bytes=24 * MIB),
        cost_estimate=FREE,
        name="front",
    )(*[arg if arg is exponent else pltpu.with_memory_space_constraint(arg, pltpu.HBM) for arg in args])


CORE, Y, X, Z1, Z2 = 8, 16, 1, 2, 4


def xor_permute(value, mask):
    count = lax.axis_size("dp") * lax.axis_size("fsdp")
    return lax.ppermute(value, ("dp", "fsdp"), [(i, i ^ mask) for i in range(count)])


def partial_kernel(parts, own_ref, near_ref, v0_ref, v1_ref, *out_refs):
    dp = lax.axis_index("dp")
    fsdp = lax.axis_index("fsdp")
    loaded = {}

    def block(z, y, x):
        if (z, y, x) not in loaded:
            owner = fsdp ^ (z << 1 | x)
            column = pl.multiple_of(owner * (4 * LANE) + (dp ^ (y << 1)) * LANE, LANE)
            loaded[z, y, x] = jnp.concatenate([ref[:, pl.ds(column, LANE)] for ref in (own_ref, near_ref)], axis=0)
        return loaded[z, y, x]

    for (blocks, start, width), out_ref in zip(parts, out_refs):
        v = jnp.concatenate([ref[pl.ds(0, 2 * HALF), pl.ds(start, width)] for ref in (v0_ref, v1_ref)], axis=0)
        total = lax.dot_general(
            jnp.concatenate([block(*place) for place in blocks], axis=1), v, (((0,), (0,)), ((), ())),
            preferred_element_type=F32,
        )
        out_ref[...] = total.astype(out_ref.dtype)


def partial_sums(parts, dtype, own, near, v0, v1):
    return pl.pallas_call(
        functools.partial(partial_kernel, parts),
        in_specs=[VMEM] * 4,
        out_specs=[VMEM] * len(parts),
        out_shape=[jax.ShapeDtypeStruct((len(blocks) * LANE, width), dtype) for blocks, _, width in parts],
        compiler_params=pltpu.CompilerParams(vmem_limit_bytes=24 * MIB),
        cost_estimate=FREE,
        name="partial_sums",
    )(own, near, v0, v1)


def inner_swap_kernel(v0_ref, v1_ref, out_ref, window_ref):
    tokens = out_ref.shape[0]
    infos = [ref[pl.ds(tokens, INFO), pl.ds(0, HALF)].astype(F32).astype(jnp.int32) for ref in (v0_ref, v1_ref)]

    def table(device, entry):
        return jnp.broadcast_to(infos[device][entry:entry + 1, :], (HALF, HALF))

    place = lax.broadcasted_iota(jnp.int32, (HALF, HALF), 0) + HALF
    inner = lax.broadcasted_iota(jnp.int32, (HALF, HALF), 1) + HALF
    first = table(0, 0)
    moved = (place >= first) & (place < first + table(0, 1))
    stays = jnp.where(~moved & (place == inner), 1.0, 0.0).astype(BF16)
    comes = jnp.where(moved & (place + table(1, 0) - first == inner), 1.0, 0.0).astype(BF16)
    taken = jnp.where(place - HALF + table(0, 2) == inner, 1.0, 0.0).astype(BF16)[:CAP]
    rows = (
        jnp.dot(stays, v0_ref[pl.ds(HALF, HALF), :], preferred_element_type=F32)
        + jnp.dot(comes, v1_ref[pl.ds(HALF, HALF), :], preferred_element_type=F32)
    ).astype(BF16)
    out_ref[pl.ds(0, HALF), :] = v0_ref[pl.ds(0, HALF), :]
    out_ref[pl.ds(HALF, HALF), :] = rows
    window_ref[...] = jnp.dot(taken, rows, preferred_element_type=F32).astype(BF16)


def inner_swap(v0, v1):
    return pl.pallas_call(
        inner_swap_kernel,
        in_specs=[VMEM] * 2,
        out_specs=[VMEM] * 2,
        out_shape=[jax.ShapeDtypeStruct((2 * HALF, 512), BF16), jax.ShapeDtypeStruct((CAP, 512), BF16)],
        compiler_params=pltpu.CompilerParams(vmem_limit_bytes=8 * MIB),
        cost_estimate=FREE,
        name="inner_swap",
    )(v0, v1)


def outer_swap_kernel(v0_ref, rows_ref, window_ref, out_ref):
    tokens = out_ref.shape[0]
    info = v0_ref[pl.ds(tokens, INFO), pl.ds(0, HALF)].astype(F32).astype(jnp.int32)
    first = jnp.broadcast_to(info[2:3, :], (HALF, HALF))
    extent = jnp.broadcast_to(info[3:4, :], (HALF, HALF))
    place = lax.broadcasted_iota(jnp.int32, (HALF, HALF), 0) + HALF
    inner = lax.broadcasted_iota(jnp.int32, (HALF, HALF), 1)
    moved = (place >= first) & (place < first + extent)
    stays = jnp.where(~moved & (place == inner + HALF), 1.0, 0.0).astype(BF16)
    comes = jnp.where(moved & (place - first == inner), 1.0, 0.0).astype(BF16)[:, :CAP]
    out_ref[pl.ds(0, HALF), :] = rows_ref[pl.ds(0, HALF), :]
    out_ref[pl.ds(HALF, HALF), :] = (
        jnp.dot(stays, rows_ref[pl.ds(HALF, HALF), :], preferred_element_type=F32)
        + jnp.dot(comes, window_ref[...], preferred_element_type=F32)
    ).astype(BF16)


def outer_swap(v0, rows, window):
    return pl.pallas_call(
        outer_swap_kernel,
        in_specs=[VMEM] * 3,
        out_specs=VMEM,
        out_shape=jax.ShapeDtypeStruct(rows.shape, BF16),
        compiler_params=pltpu.CompilerParams(vmem_limit_bytes=8 * MIB),
        cost_estimate=FREE,
        name="outer_swap",
    )(v0, rows, window)


def place_kernel(core, pair_ref, *rest):
    *_, out_ref, wide, sems = rest
    copies = []
    for y in range(2):
        wide[y] = pair_ref[y].astype(F32)
        row = pl.multiple_of((lax.axis_index("dp") ^ (y << 1 | core)) * LANE, LANE)
        copies.append(pltpu.make_async_copy(wide.at[y], out_ref.at[pl.ds(row, LANE), :], sems.at[y]))
        copies[-1].start()
    for copy in copies:
        copy.wait()


def place(core, pair, *placed):
    return pl.pallas_call(
        functools.partial(place_kernel, core),
        in_specs=[VMEM] + [HBM] * len(placed),
        out_specs=HBM,
        out_shape=jax.ShapeDtypeStruct((512, 512), F32),
        scratch_shapes=[pltpu.VMEM((2, LANE, 512), F32), pltpu.SemaphoreType.DMA((2,))],
        input_output_aliases={1: 0} if placed else {},
        compiler_params=pltpu.CompilerParams(vmem_limit_bytes=8 * MIB),
        cost_estimate=FREE,
        name="place",
    )(pair, *placed)


def fold_kernel(base_ref, arrived_ref, out_ref):
    out_ref[...] = base_ref[...] + arrived_ref[...].astype(F32)


def fold(base, arrived):
    return pl.pallas_call(
        fold_kernel,
        in_specs=[VMEM] * 2,
        out_specs=VMEM,
        out_shape=jax.ShapeDtypeStruct(base.shape, F32),
        compiler_params=pltpu.CompilerParams(vmem_limit_bytes=8 * MIB),
        cost_estimate=pl.CostEstimate(flops=6_000_000_000, bytes_accessed=0, transcendentals=0),
        name="fold",
    )(base, arrived)


def reduce_by_axis(layer_input, *args):
    near = xor_permute(layer_input, CORE)
    v0 = front(*args)
    v1 = xor_permute(v0, CORE)

    def sums(parts, dtype, v=v0):
        return partial_sums(parts, dtype, layer_input, near, v, v1)

    def after_all(*values):
        return lax.optimization_barrier(values)

    def add(*terms):
        total = terms[0]
        for term in terms[1:]:
            total = total + term.astype(F32)
        return total

    far_b, = sums([(((3, 1, 1),), 0, 512)], BF16)
    far_a, = sums([(((2, 1, 1),), 0, 512)], BF16)
    every = ((1, 1), (1, 0), (0, 1), (0, 0))
    side_b, pair_some = sums([(((3, 0, 1),), 0, 512), (tuple((1, *at) for at in every[:3]), 0, 256)], BF16)
    pair_rest, side_a = sums(
        [(tuple((1, *at) for at in every[:3]), 256, 256), (((2, 1, 0),), 0, 512)], BF16, after_all(v0, pair_some)[0]
    )
    keep_b, keep_a = sums([(((3, 1, 0), (3, 0, 0)), 0, 512), (((2, 0, 1), (2, 0, 0)), 0, 512)], F32)
    far_b = xor_permute(far_b, X)
    side_b = xor_permute(side_b, X)
    far_a = xor_permute(far_a, Y)
    pair_some = xor_permute(pair_some, Z1)
    pair_rest = xor_permute(pair_rest, Z1)
    far_b, far_a = after_all(far_b, far_a)
    on_b = add(keep_b[:LANE], far_b).astype(BF16)
    v0_late = after_all(v0, on_b)[0]
    rows, window = inner_swap(v0_late, v1)
    own_some, own_rest = sums([(tuple((0, *at) for at in every), start, 256) for start in (0, 256)], F32, v0_late)
    pair_own, = sums([(((1, 0, 0),), 0, 512)], BF16, v0_late)
    on_b = xor_permute(on_b, Y)
    on_a = xor_permute(add(keep_a[:LANE], far_a).astype(BF16), X)
    z3 = add(keep_b[LANE:], side_b, on_b).astype(BF16)
    side_a = xor_permute(after_all(jnp.concatenate([side_a, window]), own_some)[0], Y)
    side_a, window = side_a[:LANE], side_a[LANE:]
    pair_some = after_all(pair_some, z3)[0]
    z3 = xor_permute(z3, Z1)
    z2 = add(keep_a[LANE:], side_a, on_a, z3).astype(BF16)

    some = add(own_some[:3 * LANE], pair_some)
    some_far, some_y, some_x = (some[row:row + LANE] for row in range(0, 3 * LANE, LANE))
    some_in = xor_permute(jnp.concatenate([some_far, some_x]).astype(BF16), X)
    rest = add(own_rest[:3 * LANE], after_all(pair_rest, some)[0])
    rest_in = xor_permute(rest[:2 * LANE].astype(BF16), Y)
    some_in, pair_own = after_all(some_in, pair_own, z2)[:2]
    z2 = xor_permute(z2, Z2)
    pair_own = xor_permute(pair_own, Z1)
    some_on = add(some_y, some_in[:LANE]).astype(BF16)
    rest_in = after_all(rest_in, some_on)[0]
    some_on = xor_permute(some_on, Y)
    rest_on = add(rest[2 * LANE:], rest_in[:LANE]).astype(BF16)
    pair_own = after_all(pair_own, rest_on)[0]
    rest_on = xor_permute(rest_on, X)
    base = jnp.concatenate([
        add(own_some[3 * LANE:], pair_own[:, :256], some_in[LANE:]),
        add(own_rest[3 * LANE:], pair_own[:, 256:], rest_in[LANE:]),
    ], axis=1)
    mine = add(fold(base, z2), jnp.concatenate([some_on, rest_on], axis=1)).astype(BF16)
    from_y = xor_permute(mine, Y)
    value_grad = outer_swap(v0, rows, after_all(window, mine)[0])
    from_y, value_grad = after_all(from_y, value_grad)
    pair = jnp.stack([mine, from_y])
    near_pair = xor_permute(pair, CORE)
    half = place(0, pair)
    near_pair, half = after_all(near_pair, half)
    return place(1, near_pair, half), value_grad


def swapped(block, axis, distance):
    count = lax.axis_size(axis)
    route = []
    for low in range(count):
        high = low | 1 << distance
        if high != low and high < count:
            route += [(low, high), (high, low)]
    return lax.ppermute(block, axis, route)


def blend_rows(item, incoming, offset, extent):
    inside = (jnp.arange(CAP) < extent)[:, None]
    chosen = jnp.where(inside, incoming, lax.dynamic_slice_in_dim(item, offset, CAP, 0))
    return lax.dynamic_update_slice_in_dim(item, chosen, offset, 0)


def reduce_by_owner(layer_input, *args):
    swap_start, swap_rows = args[-2:]
    tokens = layer_input.shape[0]
    values = front(*args)[:tokens]
    balanced = values
    for level in range(lax.axis_size("dp").bit_length() - 1):
        offset = swap_start[0, level]
        window = lax.dynamic_slice_in_dim(balanced, offset, CAP, 0)
        balanced = blend_rows(balanced, swapped(window, "dp", level), offset, swap_rows[0, level])
    owners = lax.axis_size("fsdp")
    owned = (D + owners - 1) // owners
    padded = jnp.pad(layer_input, ((0, 0), (0, owned * owners - D)))
    arranged = lax.all_to_all(
        padded.reshape(tokens, owners, owned), "fsdp", split_axis=1, concat_axis=0, tiled=True
    )
    block = lax.dot_general(
        arranged.reshape(-1, owned),
        lax.all_gather(values, "fsdp", axis=0, tiled=True),
        (((0,), (0,)), ((), ())),
        preferred_element_type=F32,
    )
    return lax.psum(block, "dp"), balanced


def on_device(layer_input, *args):
    if lax.axis_size("dp") == 4 and lax.axis_size("fsdp") == 8:
        return reduce_by_axis(layer_input, *args)
    return reduce_by_owner(layer_input, *args)


def solution(mesh):
    return jax.shard_map(
        on_device,
        mesh=mesh,
        in_specs=(
            P(("dp", "fsdp"), None),
            P(("dp", "fsdp"), None),
            P(("dp", "fsdp"), None),
            P(("dp", "fsdp"), None),
            P(("dp", "fsdp")),
            P(("dp", "fsdp")),
            P(),
            P(("dp", "fsdp")),
            P(("dp", "fsdp"), None),
            P(("dp", "fsdp"), None),
        ),
        out_specs=(P("fsdp", None), P(("dp", "fsdp"), None)),
        check_vma=False,
    )
```

```python
import functools
import math

import jax
import jax.numpy as jnp
from jax import lax
from jax.experimental import pallas as pl
from jax.experimental.pallas import tpu as pltpu
from jax.sharding import PartitionSpec as P

D = 4096
HD = 128
CAP = 32
HALF = 128
SEG = 16
LANE = 128
INFO = 16
MIB = 1 << 20
FREE = pl.CostEstimate(flops=0, bytes_accessed=0, transcendentals=0)
BF16 = jnp.bfloat16
F32 = jnp.float32

VMEM = pl.BlockSpec(memory_space=pltpu.VMEM)
HBM = pl.BlockSpec(memory_space=pltpu.HBM)


def attend_half(per_group, folded, span, q_ref, k_ref, g_ref, allowed, factor):
    heads = q_ref.shape[1] // HD
    groups = heads // per_group
    scores = [
        lax.dot_general(
            k_ref[span, pl.ds(group * HD, HD)],
            jnp.concatenate(
                [q_ref[span, pl.ds((group * per_group + n) * HD, HD)] for n in range(per_group)], axis=0
            ),
            (((1,), (1,)), ((), ())),
            preferred_element_type=F32,
        )
        for group in range(groups)
    ]
    weighted = [
        (g_ref[span, pl.ds(head * HD, HD)].astype(F32) * factor).astype(BF16) for head in range(heads)
    ]
    if folded:
        block = lax.broadcasted_iota(jnp.int32, (SEG, HALF), 1) // SEG
    probs = []
    for head in range(heads):
        n = head % per_group
        own = scores[head // per_group][:, n * HALF:(n + 1) * HALF]
        if folded:
            own = fold_blocks(own, block)
        own = jnp.where(allowed, own, -1e30)
        expo = jnp.exp2((own - jnp.max(own, axis=0, keepdims=True)) * (HD ** (-0.5) * math.log2(math.e)))
        prob = (expo * (1.0 / jnp.sum(expo, axis=0, keepdims=True))).astype(BF16)
        if folded:
            prob = jnp.concatenate(
                [jnp.where(block == b, prob, jnp.zeros_like(prob)) for b in range(HALF // SEG)], axis=0
            )
        probs.append(prob)
    return [
        jnp.dot(
            jnp.concatenate(probs[head:head + per_group], axis=1),
            jnp.concatenate(weighted[head:head + per_group], axis=0),
            preferred_element_type=F32,
        ).astype(BF16)
        for head in range(0, heads, per_group)
    ]


def fold_blocks(square, block):
    total = square[:SEG]
    for b in range(1, HALF // SEG):
        total = jnp.where(block == b, square[b * SEG:(b + 1) * SEG], total)
    return total


def mask_and_factor(folded, span, loss_ref, exponent_ref, ids_ref, index_ref):
    exponent = exponent_ref[0]
    unscale = jnp.float32(1.0)
    for bit in range(5):
        unscale = unscale * jnp.where((exponent >> bit) & 1 == 1, jnp.float32(2.0 ** -(1 << bit)), 1.0)
    row = lax.broadcasted_iota(jnp.int32, (HALF, HALF), 0)
    col = lax.broadcasted_iota(jnp.int32, (HALF, HALF), 1)
    doc_i = jnp.broadcast_to(ids_ref[:, span], (HALF, HALF))
    allowed = (doc_i == doc_i.T) & (row <= col)
    if folded:
        allowed = fold_blocks(
            jnp.where(allowed, 1, 0), lax.broadcasted_iota(jnp.int32, (SEG, HALF), 1) // SEG
        ) == 1
    index = index_ref[:, span]
    factor = jnp.zeros((1, HALF), F32)
    for entry in range(loss_ref.shape[0]):
        factor = jnp.where(index == entry, loss_ref[entry], factor)
    return allowed, jnp.broadcast_to(factor * unscale, (HALF, HALF)).T


def front_kernel(
    per_group, loss_hbm, exponent_hbm, start_hbm, rows_hbm, q_hbm, k_hbm, g_hbm, ids_hbm, index_hbm, *rest
):
    v_ref, loss_ref, exponent_ref, start_ref, rows_ref, q_ref, k_ref, g_ref, ids_ref, index_ref, sems = rest
    count = 0

    def begin(source, target):
        nonlocal count
        copy = pltpu.make_async_copy(source, target, sems.at[count])
        copy.start()
        count += 1
        return copy

    small = [
        begin(source, target)
        for source, target in (
            (ids_hbm, ids_ref), (index_hbm, index_ref), (loss_hbm, loss_ref), (exponent_hbm, exponent_ref),
            (start_hbm, start_ref), (rows_hbm, rows_ref),
        )
    ]
    groups = k_ref.shape[1] // HD
    wide = per_group * HD
    loads = []
    for half in range(2):
        span = pl.ds(half * HALF, HALF)
        loads.append([
            begin(source.at[span, :], target.at[span, :])
            for source, target in ((q_hbm, q_ref), (k_hbm, k_ref), (g_hbm, g_ref))
        ])
    for copy in small:
        copy.wait()
    masks = [
        mask_and_factor(half == 1, pl.ds(half * HALF, HALF), loss_ref, exponent_ref, ids_ref, index_ref)
        for half in range(2)
    ]
    info_row = lax.broadcasted_iota(jnp.int32, (INFO, k_ref.shape[1]), 0)
    info = jnp.zeros(info_row.shape, jnp.int32)
    for level in range(min(start_ref.shape[1], INFO // 2)):
        info = jnp.where(info_row == 2 * level, start_ref[0, level], info)
        info = jnp.where(info_row == 2 * level + 1, rows_ref[0, level], info)
    v_ref[pl.ds(2 * HALF, INFO), :] = info.astype(F32).astype(BF16)
    for half in range(2):
        for copy in loads[half]:
            copy.wait()
        span = pl.ds(half * HALF, HALF)
        values = attend_half(per_group, half == 1, span, q_ref, k_ref, g_ref, *masks[half])
        for group, value in enumerate(values):
            v_ref[span, pl.ds(group * HD, HD)] = value


def front(query, key, grad, ids, index, loss, exponent, start, rows):
    tokens, key_width = key.shape
    per_group = query.shape[1] // key_width
    args = [
        loss, exponent, start, rows, query, key, grad, ids.reshape(1, tokens), index.reshape(1, tokens)
    ]
    return pl.pallas_call(
        functools.partial(front_kernel, per_group),
        in_specs=[HBM] * 9,
        out_specs=VMEM,
        out_shape=jax.ShapeDtypeStruct((tokens + INFO, key_width), BF16),
        scratch_shapes=[
            pltpu.SMEM(loss.shape, F32), pltpu.SMEM(exponent.shape, jnp.int32),
            pltpu.SMEM(start.shape, jnp.int32), pltpu.SMEM(rows.shape, jnp.int32),
            pltpu.VMEM(query.shape, BF16), pltpu.VMEM(key.shape, BF16), pltpu.VMEM(grad.shape, BF16),
            pltpu.VMEM((1, tokens), jnp.int32), pltpu.VMEM((1, tokens), jnp.int32),
            pltpu.SemaphoreType.DMA((12,)),
        ],
        compiler_params=pltpu.CompilerParams(vmem_limit_bytes=24 * MIB),
        cost_estimate=FREE,
        name="front",
    )(*[arg if arg is exponent else pltpu.with_memory_space_constraint(arg, pltpu.HBM) for arg in args])


CORE, Y, X, Z1, Z2 = 8, 16, 1, 2, 4


def xor_permute(value, mask):
    count = lax.axis_size("dp") * lax.axis_size("fsdp")
    return lax.ppermute(value, ("dp", "fsdp"), [(i, i ^ mask) for i in range(count)])


def partial_kernel(parts, own_ref, near_ref, v0_ref, v1_ref, *out_refs):
    dp = lax.axis_index("dp")
    fsdp = lax.axis_index("fsdp")
    loaded = {}

    def block(z, y, x):
        if (z, y, x) not in loaded:
            owner = fsdp ^ (z << 1 | x)
            column = pl.multiple_of(owner * (4 * LANE) + (dp ^ (y << 1)) * LANE, LANE)
            loaded[z, y, x] = jnp.concatenate([ref[:, pl.ds(column, LANE)] for ref in (own_ref, near_ref)], axis=0)
        return loaded[z, y, x]

    for (blocks, start, width), out_ref in zip(parts, out_refs):
        v = jnp.concatenate([ref[pl.ds(0, 2 * HALF), pl.ds(start, width)] for ref in (v0_ref, v1_ref)], axis=0)
        total = lax.dot_general(
            jnp.concatenate([block(*place) for place in blocks], axis=1), v, (((0,), (0,)), ((), ())),
            preferred_element_type=F32,
        )
        out_ref[...] = total.astype(out_ref.dtype)


def partial_sums(parts, dtype, own, near, v0, v1):
    return pl.pallas_call(
        functools.partial(partial_kernel, parts),
        in_specs=[VMEM] * 4,
        out_specs=[VMEM] * len(parts),
        out_shape=[jax.ShapeDtypeStruct((len(blocks) * LANE, width), dtype) for blocks, _, width in parts],
        compiler_params=pltpu.CompilerParams(vmem_limit_bytes=24 * MIB),
        cost_estimate=FREE,
        name="partial_sums",
    )(own, near, v0, v1)


def inner_swap_kernel(v0_ref, v1_ref, out_ref, window_ref):
    tokens = out_ref.shape[0]
    infos = [ref[pl.ds(tokens, INFO), pl.ds(0, HALF)].astype(F32).astype(jnp.int32) for ref in (v0_ref, v1_ref)]

    def table(device, entry):
        return jnp.broadcast_to(infos[device][entry:entry + 1, :], (HALF, HALF))

    place = lax.broadcasted_iota(jnp.int32, (HALF, HALF), 0) + HALF
    inner = lax.broadcasted_iota(jnp.int32, (HALF, HALF), 1) + HALF
    first = table(0, 0)
    moved = (place >= first) & (place < first + table(0, 1))
    stays = jnp.where(~moved & (place == inner), 1.0, 0.0).astype(BF16)
    comes = jnp.where(moved & (place + table(1, 0) - first == inner), 1.0, 0.0).astype(BF16)
    taken = jnp.where(place - HALF + table(0, 2) == inner, 1.0, 0.0).astype(BF16)[:CAP]
    rows = (
        jnp.dot(stays, v0_ref[pl.ds(HALF, HALF), :], preferred_element_type=F32)
        + jnp.dot(comes, v1_ref[pl.ds(HALF, HALF), :], preferred_element_type=F32)
    ).astype(BF16)
    out_ref[pl.ds(0, HALF), :] = v0_ref[pl.ds(0, HALF), :]
    out_ref[pl.ds(HALF, HALF), :] = rows
    window_ref[...] = jnp.dot(taken, rows, preferred_element_type=F32).astype(BF16)


def inner_swap(v0, v1):
    return pl.pallas_call(
        inner_swap_kernel,
        in_specs=[VMEM] * 2,
        out_specs=[VMEM] * 2,
        out_shape=[jax.ShapeDtypeStruct((2 * HALF, 512), BF16), jax.ShapeDtypeStruct((CAP, 512), BF16)],
        compiler_params=pltpu.CompilerParams(vmem_limit_bytes=8 * MIB),
        cost_estimate=FREE,
        name="inner_swap",
    )(v0, v1)


def outer_swap_kernel(v0_ref, rows_ref, window_ref, out_ref):
    tokens = out_ref.shape[0]
    info = v0_ref[pl.ds(tokens, INFO), pl.ds(0, HALF)].astype(F32).astype(jnp.int32)
    first = jnp.broadcast_to(info[2:3, :], (HALF, HALF))
    extent = jnp.broadcast_to(info[3:4, :], (HALF, HALF))
    place = lax.broadcasted_iota(jnp.int32, (HALF, HALF), 0) + HALF
    inner = lax.broadcasted_iota(jnp.int32, (HALF, HALF), 1)
    moved = (place >= first) & (place < first + extent)
    stays = jnp.where(~moved & (place == inner + HALF), 1.0, 0.0).astype(BF16)
    comes = jnp.where(moved & (place - first == inner), 1.0, 0.0).astype(BF16)[:, :CAP]
    out_ref[pl.ds(0, HALF), :] = rows_ref[pl.ds(0, HALF), :]
    out_ref[pl.ds(HALF, HALF), :] = (
        jnp.dot(stays, rows_ref[pl.ds(HALF, HALF), :], preferred_element_type=F32)
        + jnp.dot(comes, window_ref[...], preferred_element_type=F32)
    ).astype(BF16)


def outer_swap(v0, rows, window):
    return pl.pallas_call(
        outer_swap_kernel,
        in_specs=[VMEM] * 3,
        out_specs=VMEM,
        out_shape=jax.ShapeDtypeStruct(rows.shape, BF16),
        compiler_params=pltpu.CompilerParams(vmem_limit_bytes=8 * MIB),
        cost_estimate=FREE,
        name="outer_swap",
    )(v0, rows, window)


def place_kernel(core, pair_ref, *rest):
    *_, out_ref, wide, sems = rest
    copies = []
    for y in range(2):
        wide[y] = pair_ref[y].astype(F32)
        row = pl.multiple_of((lax.axis_index("dp") ^ (y << 1 | core)) * LANE, LANE)
        copies.append(pltpu.make_async_copy(wide.at[y], out_ref.at[pl.ds(row, LANE), :], sems.at[y]))
        copies[-1].start()
    for copy in copies:
        copy.wait()


def place(core, pair, *placed):
    return pl.pallas_call(
        functools.partial(place_kernel, core),
        in_specs=[VMEM] + [HBM] * len(placed),
        out_specs=HBM,
        out_shape=jax.ShapeDtypeStruct((512, 512), F32),
        scratch_shapes=[pltpu.VMEM((2, LANE, 512), F32), pltpu.SemaphoreType.DMA((2,))],
        input_output_aliases={1: 0} if placed else {},
        compiler_params=pltpu.CompilerParams(vmem_limit_bytes=8 * MIB),
        cost_estimate=FREE,
        name="place",
    )(pair, *placed)


def fold_kernel(base_ref, arrived_ref, out_ref):
    out_ref[...] = base_ref[...] + arrived_ref[...].astype(F32)


def fold(base, arrived):
    return pl.pallas_call(
        fold_kernel,
        in_specs=[VMEM] * 2,
        out_specs=VMEM,
        out_shape=jax.ShapeDtypeStruct(base.shape, F32),
        compiler_params=pltpu.CompilerParams(vmem_limit_bytes=8 * MIB),
        cost_estimate=pl.CostEstimate(flops=6_000_000_000, bytes_accessed=0, transcendentals=0),
        name="fold",
    )(base, arrived)


def reduce_by_axis(layer_input, *args):
    near = xor_permute(layer_input, CORE)
    v0 = front(*args)
    v1 = xor_permute(v0, CORE)

    def sums(parts, dtype, v=v0):
        return partial_sums(parts, dtype, layer_input, near, v, v1)

    def after_all(*values):
        return lax.optimization_barrier(values)

    def add(*terms):
        total = terms[0]
        for term in terms[1:]:
            total = total + term.astype(F32)
        return total

    far_b, = sums([(((3, 1, 1),), 0, 512)], BF16)
    far_a, = sums([(((2, 1, 1),), 0, 512)], BF16)
    every = ((1, 1), (1, 0), (0, 1), (0, 0))
    side_b, pair_some = sums([(((3, 0, 1),), 0, 512), (tuple((1, *at) for at in every[:3]), 0, 256)], BF16)
    pair_rest, side_a = sums(
        [(tuple((1, *at) for at in every[:3]), 256, 256), (((2, 1, 0),), 0, 512)], BF16, after_all(v0, pair_some)[0]
    )
    keep_b, keep_a = sums([(((3, 1, 0), (3, 0, 0)), 0, 512), (((2, 0, 1), (2, 0, 0)), 0, 512)], F32)
    far_b = xor_permute(far_b, X)
    side_b = xor_permute(side_b, X)
    far_a = xor_permute(far_a, Y)
    pair_some = xor_permute(pair_some, Z1)
    pair_rest = xor_permute(pair_rest, Z1)
    far_b, far_a = after_all(far_b, far_a)
    on_b = add(keep_b[:LANE], far_b).astype(BF16)
    v0_late = after_all(v0, on_b)[0]
    rows, window = inner_swap(v0_late, v1)
    own_some, own_rest = sums([(tuple((0, *at) for at in every), start, 256) for start in (0, 256)], F32, v0_late)
    pair_own, = sums([(((1, 0, 0),), 0, 512)], BF16, v0_late)
    on_b = xor_permute(on_b, Y)
    on_a = xor_permute(add(keep_a[:LANE], far_a).astype(BF16), X)
    z3 = add(keep_b[LANE:], side_b, on_b).astype(BF16)
    side_a = xor_permute(after_all(jnp.concatenate([side_a, window]), own_some)[0], Y)
    side_a, window = side_a[:LANE], side_a[LANE:]
    pair_some, pair_own = after_all(pair_some, pair_own, z3)[:2]
    z3 = xor_permute(z3, Z1)
    pair_own = xor_permute(pair_own, Z1)
    z2 = add(keep_a[LANE:], side_a, on_a, z3).astype(BF16)

    some = add(own_some[:3 * LANE], pair_some)
    some_far, some_y, some_x = (some[row:row + LANE] for row in range(0, 3 * LANE, LANE))
    some_in = xor_permute(jnp.concatenate([some_far, some_x]).astype(BF16), X)
    rest = add(own_rest[:3 * LANE], after_all(pair_rest, some)[0])
    rest_in = xor_permute(rest[:2 * LANE].astype(BF16), Y)
    some_in = after_all(some_in, z2)[0]
    z2 = xor_permute(z2, Z2)
    some_on = add(some_y, some_in[:LANE]).astype(BF16)
    rest_in = after_all(rest_in, some_on)[0]
    some_on = xor_permute(some_on, Y)
    rest_on = add(rest[2 * LANE:], rest_in[:LANE]).astype(BF16)
    rest_on = xor_permute(rest_on, X)
    base = jnp.concatenate([
        add(own_some[3 * LANE:], pair_own[:, :256], some_in[LANE:]),
        add(own_rest[3 * LANE:], pair_own[:, 256:], rest_in[LANE:]),
    ], axis=1)
    mine = add(fold(base, z2), jnp.concatenate([some_on, rest_on], axis=1)).astype(BF16)
    from_y = xor_permute(mine, Y)
    value_grad = outer_swap(v0, rows, after_all(window, mine)[0])
    from_y, value_grad = after_all(from_y, value_grad)
    pair = jnp.stack([mine, from_y])
    near_pair = xor_permute(pair, CORE)
    half = place(0, pair)
    near_pair, half = after_all(near_pair, half)
    return place(1, near_pair, half), value_grad


def swapped(block, axis, distance):
    count = lax.axis_size(axis)
    route = []
    for low in range(count):
        high = low | 1 << distance
        if high != low and high < count:
            route += [(low, high), (high, low)]
    return lax.ppermute(block, axis, route)


def blend_rows(item, incoming, offset, extent):
    inside = (jnp.arange(CAP) < extent)[:, None]
    chosen = jnp.where(inside, incoming, lax.dynamic_slice_in_dim(item, offset, CAP, 0))
    return lax.dynamic_update_slice_in_dim(item, chosen, offset, 0)


def reduce_by_owner(layer_input, *args):
    swap_start, swap_rows = args[-2:]
    tokens = layer_input.shape[0]
    values = front(*args)[:tokens]
    balanced = values
    for level in range(lax.axis_size("dp").bit_length() - 1):
        offset = swap_start[0, level]
        window = lax.dynamic_slice_in_dim(balanced, offset, CAP, 0)
        balanced = blend_rows(balanced, swapped(window, "dp", level), offset, swap_rows[0, level])
    owners = lax.axis_size("fsdp")
    owned = (D + owners - 1) // owners
    padded = jnp.pad(layer_input, ((0, 0), (0, owned * owners - D)))
    arranged = lax.all_to_all(
        padded.reshape(tokens, owners, owned), "fsdp", split_axis=1, concat_axis=0, tiled=True
    )
    block = lax.dot_general(
        arranged.reshape(-1, owned),
        lax.all_gather(values, "fsdp", axis=0, tiled=True),
        (((0,), (0,)), ((), ())),
        preferred_element_type=F32,
    )
    return lax.psum(block, "dp"), balanced


def on_device(layer_input, *args):
    if lax.axis_size("dp") == 4 and lax.axis_size("fsdp") == 8:
        return reduce_by_axis(layer_input, *args)
    return reduce_by_owner(layer_input, *args)


def solution(mesh):
    return jax.shard_map(
        on_device,
        mesh=mesh,
        in_specs=(
            P(("dp", "fsdp"), None),
            P(("dp", "fsdp"), None),
            P(("dp", "fsdp"), None),
            P(("dp", "fsdp"), None),
            P(("dp", "fsdp")),
            P(("dp", "fsdp")),
            P(),
            P(("dp", "fsdp")),
            P(("dp", "fsdp"), None),
            P(("dp", "fsdp"), None),
        ),
        out_specs=(P("fsdp", None), P(("dp", "fsdp"), None)),
        check_vma=False,
    )
```

```python
import functools
import math

import jax
import jax.numpy as jnp
from jax import lax
from jax.experimental import pallas as pl
from jax.experimental.pallas import tpu as pltpu
from jax.sharding import PartitionSpec as P

D = 4096
HD = 128
CAP = 32
HALF = 128
SEG = 16
LANE = 128
INFO = 16
MIB = 1 << 20
FREE = pl.CostEstimate(flops=0, bytes_accessed=0, transcendentals=0)
BF16 = jnp.bfloat16
F32 = jnp.float32

VMEM = pl.BlockSpec(memory_space=pltpu.VMEM)
HBM = pl.BlockSpec(memory_space=pltpu.HBM)


def attend_half(per_group, folded, span, q_ref, k_ref, g_ref, allowed, factor):
    heads = q_ref.shape[1] // HD
    groups = heads // per_group
    scores = [
        lax.dot_general(
            k_ref[span, pl.ds(group * HD, HD)],
            jnp.concatenate(
                [q_ref[span, pl.ds((group * per_group + n) * HD, HD)] for n in range(per_group)], axis=0
            ),
            (((1,), (1,)), ((), ())),
            preferred_element_type=F32,
        )
        for group in range(groups)
    ]
    weighted = [
        (g_ref[span, pl.ds(head * HD, HD)].astype(F32) * factor).astype(BF16) for head in range(heads)
    ]
    if folded:
        block = lax.broadcasted_iota(jnp.int32, (SEG, HALF), 1) // SEG
    probs = []
    for head in range(heads):
        n = head % per_group
        own = scores[head // per_group][:, n * HALF:(n + 1) * HALF]
        if folded:
            own = fold_blocks(own, block)
        own = jnp.where(allowed, own, -1e30)
        expo = jnp.exp2((own - jnp.max(own, axis=0, keepdims=True)) * (HD ** (-0.5) * math.log2(math.e)))
        prob = (expo * (1.0 / jnp.sum(expo, axis=0, keepdims=True))).astype(BF16)
        if folded:
            prob = jnp.concatenate(
                [jnp.where(block == b, prob, jnp.zeros_like(prob)) for b in range(HALF // SEG)], axis=0
            )
        probs.append(prob)
    return [
        jnp.dot(
            jnp.concatenate(probs[head:head + per_group], axis=1),
            jnp.concatenate(weighted[head:head + per_group], axis=0),
            preferred_element_type=F32,
        ).astype(BF16)
        for head in range(0, heads, per_group)
    ]


def fold_blocks(square, block):
    total = square[:SEG]
    for b in range(1, HALF // SEG):
        total = jnp.where(block == b, square[b * SEG:(b + 1) * SEG], total)
    return total


def mask_and_factor(folded, span, loss_ref, exponent_ref, ids_ref, index_ref):
    exponent = exponent_ref[0]
    unscale = jnp.float32(1.0)
    for bit in range(5):
        unscale = unscale * jnp.where((exponent >> bit) & 1 == 1, jnp.float32(2.0 ** -(1 << bit)), 1.0)
    row = lax.broadcasted_iota(jnp.int32, (HALF, HALF), 0)
    col = lax.broadcasted_iota(jnp.int32, (HALF, HALF), 1)
    doc_i = jnp.broadcast_to(ids_ref[:, span], (HALF, HALF))
    allowed = (doc_i == doc_i.T) & (row <= col)
    if folded:
        allowed = fold_blocks(
            jnp.where(allowed, 1, 0), lax.broadcasted_iota(jnp.int32, (SEG, HALF), 1) // SEG
        ) == 1
    index = index_ref[:, span]
    factor = jnp.zeros((1, HALF), F32)
    for entry in range(loss_ref.shape[0]):
        factor = jnp.where(index == entry, loss_ref[entry], factor)
    return allowed, jnp.broadcast_to(factor * unscale, (HALF, HALF)).T


def front_kernel(
    per_group, loss_hbm, exponent_hbm, start_hbm, rows_hbm, q_hbm, k_hbm, g_hbm, ids_hbm, index_hbm, *rest
):
    v_ref, loss_ref, exponent_ref, start_ref, rows_ref, q_ref, k_ref, g_ref, ids_ref, index_ref, sems = rest
    count = 0

    def begin(source, target):
        nonlocal count
        copy = pltpu.make_async_copy(source, target, sems.at[count])
        copy.start()
        count += 1
        return copy

    small = [
        begin(source, target)
        for source, target in (
            (ids_hbm, ids_ref), (index_hbm, index_ref), (loss_hbm, loss_ref), (exponent_hbm, exponent_ref),
            (start_hbm, start_ref), (rows_hbm, rows_ref),
        )
    ]
    groups = k_ref.shape[1] // HD
    wide = per_group * HD
    loads = []
    for half in range(2):
        span = pl.ds(half * HALF, HALF)
        loads.append([
            begin(source.at[span, :], target.at[span, :])
            for source, target in ((q_hbm, q_ref), (k_hbm, k_ref), (g_hbm, g_ref))
        ])
    for copy in small:
        copy.wait()
    masks = [
        mask_and_factor(half == 1, pl.ds(half * HALF, HALF), loss_ref, exponent_ref, ids_ref, index_ref)
        for half in range(2)
    ]
    info_row = lax.broadcasted_iota(jnp.int32, (INFO, k_ref.shape[1]), 0)
    info = jnp.zeros(info_row.shape, jnp.int32)
    for level in range(min(start_ref.shape[1], INFO // 2)):
        info = jnp.where(info_row == 2 * level, start_ref[0, level], info)
        info = jnp.where(info_row == 2 * level + 1, rows_ref[0, level], info)
    v_ref[pl.ds(2 * HALF, INFO), :] = info.astype(F32).astype(BF16)
    for half in range(2):
        for copy in loads[half]:
            copy.wait()
        span = pl.ds(half * HALF, HALF)
        values = attend_half(per_group, half == 1, span, q_ref, k_ref, g_ref, *masks[half])
        for group, value in enumerate(values):
            v_ref[span, pl.ds(group * HD, HD)] = value


def front(query, key, grad, ids, index, loss, exponent, start, rows):
    tokens, key_width = key.shape
    per_group = query.shape[1] // key_width
    args = [
        loss, exponent, start, rows, query, key, grad, ids.reshape(1, tokens), index.reshape(1, tokens)
    ]
    return pl.pallas_call(
        functools.partial(front_kernel, per_group),
        in_specs=[HBM] * 9,
        out_specs=VMEM,
        out_shape=jax.ShapeDtypeStruct((tokens + INFO, key_width), BF16),
        scratch_shapes=[
            pltpu.SMEM(loss.shape, F32), pltpu.SMEM(exponent.shape, jnp.int32),
            pltpu.SMEM(start.shape, jnp.int32), pltpu.SMEM(rows.shape, jnp.int32),
            pltpu.VMEM(query.shape, BF16), pltpu.VMEM(key.shape, BF16), pltpu.VMEM(grad.shape, BF16),
            pltpu.VMEM((1, tokens), jnp.int32), pltpu.VMEM((1, tokens), jnp.int32),
            pltpu.SemaphoreType.DMA((12,)),
        ],
        compiler_params=pltpu.CompilerParams(vmem_limit_bytes=24 * MIB),
        cost_estimate=FREE,
        name="front",
    )(*[arg if arg is exponent else pltpu.with_memory_space_constraint(arg, pltpu.HBM) for arg in args])


CORE, Y, X, Z1, Z2 = 8, 16, 1, 2, 4


def xor_permute(value, mask):
    count = lax.axis_size("dp") * lax.axis_size("fsdp")
    return lax.ppermute(value, ("dp", "fsdp"), [(i, i ^ mask) for i in range(count)])


def partial_kernel(parts, own_ref, near_ref, v0_ref, v1_ref, *out_refs):
    dp = lax.axis_index("dp")
    fsdp = lax.axis_index("fsdp")
    loaded = {}

    def block(z, y, x):
        if (z, y, x) not in loaded:
            owner = fsdp ^ (z << 1 | x)
            column = pl.multiple_of(owner * (4 * LANE) + (dp ^ (y << 1)) * LANE, LANE)
            loaded[z, y, x] = jnp.concatenate([ref[:, pl.ds(column, LANE)] for ref in (own_ref, near_ref)], axis=0)
        return loaded[z, y, x]

    for (blocks, start, width), out_ref in zip(parts, out_refs):
        v = jnp.concatenate([ref[pl.ds(0, 2 * HALF), pl.ds(start, width)] for ref in (v0_ref, v1_ref)], axis=0)
        total = lax.dot_general(
            jnp.concatenate([block(*place) for place in blocks], axis=1), v, (((0,), (0,)), ((), ())),
            preferred_element_type=F32,
        )
        out_ref[...] = total.astype(out_ref.dtype)


def partial_sums(parts, dtype, own, near, v0, v1):
    return pl.pallas_call(
        functools.partial(partial_kernel, parts),
        in_specs=[VMEM] * 4,
        out_specs=[VMEM] * len(parts),
        out_shape=[jax.ShapeDtypeStruct((len(blocks) * LANE, width), dtype) for blocks, _, width in parts],
        compiler_params=pltpu.CompilerParams(vmem_limit_bytes=24 * MIB),
        cost_estimate=FREE,
        name="partial_sums",
    )(own, near, v0, v1)


def inner_swap_kernel(v0_ref, v1_ref, out_ref, window_ref):
    tokens = out_ref.shape[0]
    infos = [ref[pl.ds(tokens, INFO), pl.ds(0, HALF)].astype(F32).astype(jnp.int32) for ref in (v0_ref, v1_ref)]

    def table(device, entry):
        return jnp.broadcast_to(infos[device][entry:entry + 1, :], (HALF, HALF))

    place = lax.broadcasted_iota(jnp.int32, (HALF, HALF), 0) + HALF
    inner = lax.broadcasted_iota(jnp.int32, (HALF, HALF), 1) + HALF
    first = table(0, 0)
    moved = (place >= first) & (place < first + table(0, 1))
    stays = jnp.where(~moved & (place == inner), 1.0, 0.0).astype(BF16)
    comes = jnp.where(moved & (place + table(1, 0) - first == inner), 1.0, 0.0).astype(BF16)
    taken = jnp.where(place - HALF + table(0, 2) == inner, 1.0, 0.0).astype(BF16)[:CAP]
    rows = (
        jnp.dot(stays, v0_ref[pl.ds(HALF, HALF), :], preferred_element_type=F32)
        + jnp.dot(comes, v1_ref[pl.ds(HALF, HALF), :], preferred_element_type=F32)
    ).astype(BF16)
    out_ref[pl.ds(0, HALF), :] = v0_ref[pl.ds(0, HALF), :]
    out_ref[pl.ds(HALF, HALF), :] = rows
    window_ref[...] = jnp.dot(taken, rows, preferred_element_type=F32).astype(BF16)


def inner_swap(v0, v1):
    return pl.pallas_call(
        inner_swap_kernel,
        in_specs=[VMEM] * 2,
        out_specs=[VMEM] * 2,
        out_shape=[jax.ShapeDtypeStruct((2 * HALF, 512), BF16), jax.ShapeDtypeStruct((CAP, 512), BF16)],
        compiler_params=pltpu.CompilerParams(vmem_limit_bytes=8 * MIB),
        cost_estimate=FREE,
        name="inner_swap",
    )(v0, v1)


def outer_swap_kernel(v0_ref, rows_ref, window_ref, out_ref):
    tokens = out_ref.shape[0]
    info = v0_ref[pl.ds(tokens, INFO), pl.ds(0, HALF)].astype(F32).astype(jnp.int32)
    first = jnp.broadcast_to(info[2:3, :], (HALF, HALF))
    extent = jnp.broadcast_to(info[3:4, :], (HALF, HALF))
    place = lax.broadcasted_iota(jnp.int32, (HALF, HALF), 0) + HALF
    inner = lax.broadcasted_iota(jnp.int32, (HALF, HALF), 1)
    moved = (place >= first) & (place < first + extent)
    stays = jnp.where(~moved & (place == inner + HALF), 1.0, 0.0).astype(BF16)
    comes = jnp.where(moved & (place - first == inner), 1.0, 0.0).astype(BF16)[:, :CAP]
    out_ref[pl.ds(0, HALF), :] = rows_ref[pl.ds(0, HALF), :]
    out_ref[pl.ds(HALF, HALF), :] = (
        jnp.dot(stays, rows_ref[pl.ds(HALF, HALF), :], preferred_element_type=F32)
        + jnp.dot(comes, window_ref[...], preferred_element_type=F32)
    ).astype(BF16)


def outer_swap(v0, rows, window):
    return pl.pallas_call(
        outer_swap_kernel,
        in_specs=[VMEM] * 3,
        out_specs=VMEM,
        out_shape=jax.ShapeDtypeStruct(rows.shape, BF16),
        compiler_params=pltpu.CompilerParams(vmem_limit_bytes=8 * MIB),
        cost_estimate=FREE,
        name="outer_swap",
    )(v0, rows, window)


def place_kernel(core, pair_ref, *rest):
    *_, out_ref, wide, sems = rest
    copies = []
    for y in range(2):
        wide[y] = pair_ref[y].astype(F32)
        row = pl.multiple_of((lax.axis_index("dp") ^ (y << 1 | core)) * LANE, LANE)
        copies.append(pltpu.make_async_copy(wide.at[y], out_ref.at[pl.ds(row, LANE), :], sems.at[y]))
        copies[-1].start()
    for copy in copies:
        copy.wait()


def place(core, pair, *placed):
    return pl.pallas_call(
        functools.partial(place_kernel, core),
        in_specs=[VMEM] + [HBM] * len(placed),
        out_specs=HBM,
        out_shape=jax.ShapeDtypeStruct((512, 512), F32),
        scratch_shapes=[pltpu.VMEM((2, LANE, 512), F32), pltpu.SemaphoreType.DMA((2,))],
        input_output_aliases={1: 0} if placed else {},
        compiler_params=pltpu.CompilerParams(vmem_limit_bytes=8 * MIB),
        cost_estimate=FREE,
        name="place",
    )(pair, *placed)


def fold_kernel(base_ref, arrived_ref, out_ref):
    out_ref[...] = base_ref[...] + arrived_ref[...].astype(F32)


def fold(base, arrived):
    return pl.pallas_call(
        fold_kernel,
        in_specs=[VMEM] * 2,
        out_specs=VMEM,
        out_shape=jax.ShapeDtypeStruct(base.shape, F32),
        compiler_params=pltpu.CompilerParams(vmem_limit_bytes=8 * MIB),
        cost_estimate=pl.CostEstimate(flops=6_000_000_000, bytes_accessed=0, transcendentals=0),
        name="fold",
    )(base, arrived)


def reduce_by_axis(layer_input, *args):
    near = xor_permute(layer_input, CORE)
    v0 = front(*args)
    v1 = xor_permute(v0, CORE)

    def sums(parts, dtype, v=v0):
        return partial_sums(parts, dtype, layer_input, near, v, v1)

    def after_all(*values):
        return lax.optimization_barrier(values)

    def add(*terms):
        total = terms[0]
        for term in terms[1:]:
            total = total + term.astype(F32)
        return total

    far_b, = sums([(((3, 1, 1),), 0, 512)], BF16)
    first_a, = sums([(((2, 1, 1), (2, 1, 0)), 0, 512)], BF16)
    every = ((1, 1), (1, 0), (0, 1), (0, 0))
    side_b, pair_some = sums([(((3, 0, 1),), 0, 512), (tuple((1, *at) for at in every[:3]), 0, 256)], BF16)
    pair_rest, pair_own = sums(
        [(tuple((1, *at) for at in every[:3]), 256, 256), (((1, 0, 0),), 0, 512)], BF16, after_all(v0, pair_some)[0]
    )
    keep_b, keep_a = sums([(((3, 1, 0), (3, 0, 0)), 0, 512), (((2, 0, 1), (2, 0, 0)), 0, 512)], F32)
    own_some, own_rest = sums([(tuple((0, *at) for at in every), start, 256) for start in (0, 256)], F32)
    far_b = xor_permute(far_b, X)
    side_b = xor_permute(side_b, X)
    first_a = xor_permute(first_a, Y)
    pair_sent = pair_rest
    pair_some = xor_permute(pair_some, Z1)
    pair_rest = xor_permute(pair_rest, Z1)
    on_b = add(keep_b[:LANE], far_b).astype(BF16)
    rows, window = inner_swap(after_all(v0, pair_sent)[0], v1)
    window = xor_permute(after_all(window, on_b)[0], Y)
    on_b = xor_permute(on_b, Y)
    on_a = xor_permute(add(keep_a[:LANE], first_a[:LANE]).astype(BF16), X)
    z3 = add(keep_b[LANE:], side_b, on_b).astype(BF16)
    pair_some, window = after_all(pair_some, window, z3)[:2]
    z3 = xor_permute(z3, Z1)
    z2 = add(keep_a[LANE:], first_a[LANE:], on_a, z3).astype(BF16)

    some = add(own_some[:3 * LANE], pair_some)
    some_in = xor_permute(some[:2 * LANE].astype(BF16), Y)
    rest = add(own_rest[:3 * LANE], after_all(pair_rest, some)[0])
    rest_far, rest_y, rest_x = (rest[row:row + LANE] for row in range(0, 3 * LANE, LANE))
    rest_in = xor_permute(jnp.concatenate([rest_far, rest_x]).astype(BF16), X)
    some_in, pair_own = after_all(some_in, pair_own, z2)[:2]
    z2 = xor_permute(z2, Z2)
    pair_own = xor_permute(pair_own, Z1)
    some_on = add(some[2 * LANE:], some_in[:LANE]).astype(BF16)
    rest_in = after_all(rest_in, some_on)[0]
    some_on = xor_permute(some_on, X)
    rest_on = xor_permute(add(rest_y, rest_in[:LANE]).astype(BF16), Y)
    base = jnp.concatenate([
        add(own_some[3 * LANE:], pair_own[:, :256], some_in[LANE:]),
        add(own_rest[3 * LANE:], pair_own[:, 256:], rest_in[LANE:]),
    ], axis=1)
    mine = add(fold(base, z2), jnp.concatenate([some_on, rest_on], axis=1)).astype(BF16)
    from_y = xor_permute(mine, Y)
    value_grad = outer_swap(v0, rows, after_all(window, mine)[0])
    from_y, value_grad = after_all(from_y, value_grad)
    pair = jnp.stack([mine, from_y])
    near_pair = xor_permute(pair, CORE)
    half = place(0, pair)
    near_pair, half = after_all(near_pair, half)
    return place(1, near_pair, half), value_grad


def swapped(block, axis, distance):
    count = lax.axis_size(axis)
    route = []
    for low in range(count):
        high = low | 1 << distance
        if high != low and high < count:
            route += [(low, high), (high, low)]
    return lax.ppermute(block, axis, route)


def blend_rows(item, incoming, offset, extent):
    inside = (jnp.arange(CAP) < extent)[:, None]
    chosen = jnp.where(inside, incoming, lax.dynamic_slice_in_dim(item, offset, CAP, 0))
    return lax.dynamic_update_slice_in_dim(item, chosen, offset, 0)


def reduce_by_owner(layer_input, *args):
    swap_start, swap_rows = args[-2:]
    tokens = layer_input.shape[0]
    values = front(*args)[:tokens]
    balanced = values
    for level in range(lax.axis_size("dp").bit_length() - 1):
        offset = swap_start[0, level]
        window = lax.dynamic_slice_in_dim(balanced, offset, CAP, 0)
        balanced = blend_rows(balanced, swapped(window, "dp", level), offset, swap_rows[0, level])
    owners = lax.axis_size("fsdp")
    owned = (D + owners - 1) // owners
    padded = jnp.pad(layer_input, ((0, 0), (0, owned * owners - D)))
    arranged = lax.all_to_all(
        padded.reshape(tokens, owners, owned), "fsdp", split_axis=1, concat_axis=0, tiled=True
    )
    block = lax.dot_general(
        arranged.reshape(-1, owned),
        lax.all_gather(values, "fsdp", axis=0, tiled=True),
        (((0,), (0,)), ((), ())),
        preferred_element_type=F32,
    )
    return lax.psum(block, "dp"), balanced


def on_device(layer_input, *args):
    if lax.axis_size("dp") == 4 and lax.axis_size("fsdp") == 8:
        return reduce_by_axis(layer_input, *args)
    return reduce_by_owner(layer_input, *args)


def solution(mesh):
    return jax.shard_map(
        on_device,
        mesh=mesh,
        in_specs=(
            P(("dp", "fsdp"), None),
            P(("dp", "fsdp"), None),
            P(("dp", "fsdp"), None),
            P(("dp", "fsdp"), None),
            P(("dp", "fsdp")),
            P(("dp", "fsdp")),
            P(),
            P(("dp", "fsdp")),
            P(("dp", "fsdp"), None),
            P(("dp", "fsdp"), None),
        ),
        out_specs=(P("fsdp", None), P(("dp", "fsdp"), None)),
        check_vma=False,
    )
```

```python
import functools
import math

import jax
import jax.numpy as jnp
from jax import lax
from jax.experimental import pallas as pl
from jax.experimental.pallas import tpu as pltpu
from jax.sharding import PartitionSpec as P

D = 4096
HD = 128
CAP = 32
HALF = 128
SEG = 16
LANE = 128
INFO = 16
MIB = 1 << 20
FREE = pl.CostEstimate(flops=0, bytes_accessed=0, transcendentals=0)
BF16 = jnp.bfloat16
F32 = jnp.float32

VMEM = pl.BlockSpec(memory_space=pltpu.VMEM)
HBM = pl.BlockSpec(memory_space=pltpu.HBM)


def attend_half(per_group, folded, span, q_ref, k_ref, g_ref, allowed, factor):
    heads = q_ref.shape[1] // HD
    groups = heads // per_group
    scores = [
        lax.dot_general(
            k_ref[span, pl.ds(group * HD, HD)],
            jnp.concatenate(
                [q_ref[span, pl.ds((group * per_group + n) * HD, HD)] for n in range(per_group)], axis=0
            ),
            (((1,), (1,)), ((), ())),
            preferred_element_type=F32,
        )
        for group in range(groups)
    ]
    weighted = [
        (g_ref[span, pl.ds(head * HD, HD)].astype(F32) * factor).astype(BF16) for head in range(heads)
    ]
    if folded:
        block = lax.broadcasted_iota(jnp.int32, (SEG, HALF), 1) // SEG
    probs = []
    for head in range(heads):
        n = head % per_group
        own = scores[head // per_group][:, n * HALF:(n + 1) * HALF]
        if folded:
            own = fold_blocks(own, block)
        own = jnp.where(allowed, own, -1e30)
        expo = jnp.exp2((own - jnp.max(own, axis=0, keepdims=True)) * (HD ** (-0.5) * math.log2(math.e)))
        prob = (expo * (1.0 / jnp.sum(expo, axis=0, keepdims=True))).astype(BF16)
        if folded:
            prob = jnp.concatenate(
                [jnp.where(block == b, prob, jnp.zeros_like(prob)) for b in range(HALF // SEG)], axis=0
            )
        probs.append(prob)
    return [
        jnp.dot(
            jnp.concatenate(probs[head:head + per_group], axis=1),
            jnp.concatenate(weighted[head:head + per_group], axis=0),
            preferred_element_type=F32,
        ).astype(BF16)
        for head in range(0, heads, per_group)
    ]


def fold_blocks(square, block):
    total = square[:SEG]
    for b in range(1, HALF // SEG):
        total = jnp.where(block == b, square[b * SEG:(b + 1) * SEG], total)
    return total


def mask_and_factor(folded, span, loss_ref, exponent_ref, ids_ref, index_ref):
    exponent = exponent_ref[0]
    unscale = jnp.float32(1.0)
    for bit in range(5):
        unscale = unscale * jnp.where((exponent >> bit) & 1 == 1, jnp.float32(2.0 ** -(1 << bit)), 1.0)
    row = lax.broadcasted_iota(jnp.int32, (HALF, HALF), 0)
    col = lax.broadcasted_iota(jnp.int32, (HALF, HALF), 1)
    doc_i = jnp.broadcast_to(ids_ref[:, span], (HALF, HALF))
    allowed = (doc_i == doc_i.T) & (row <= col)
    if folded:
        allowed = fold_blocks(
            jnp.where(allowed, 1, 0), lax.broadcasted_iota(jnp.int32, (SEG, HALF), 1) // SEG
        ) == 1
    index = index_ref[:, span]
    factor = jnp.zeros((1, HALF), F32)
    for entry in range(loss_ref.shape[0]):
        factor = jnp.where(index == entry, loss_ref[entry], factor)
    return allowed, jnp.broadcast_to(factor * unscale, (HALF, HALF)).T


def front_kernel(
    per_group, loss_hbm, exponent_hbm, start_hbm, rows_hbm, q_hbm, k_hbm, g_hbm, ids_hbm, index_hbm, *rest
):
    v_ref, loss_ref, exponent_ref, start_ref, rows_ref, q_ref, k_ref, g_ref, ids_ref, index_ref, sems = rest
    count = 0

    def begin(source, target):
        nonlocal count
        copy = pltpu.make_async_copy(source, target, sems.at[count])
        copy.start()
        count += 1
        return copy

    small = [
        begin(source, target)
        for source, target in (
            (ids_hbm, ids_ref), (index_hbm, index_ref), (loss_hbm, loss_ref), (exponent_hbm, exponent_ref),
            (start_hbm, start_ref), (rows_hbm, rows_ref),
        )
    ]
    groups = k_ref.shape[1] // HD
    wide = per_group * HD
    loads = []
    for half in range(2):
        span = pl.ds(half * HALF, HALF)
        loads.append([
            begin(source.at[span, :], target.at[span, :])
            for source, target in ((q_hbm, q_ref), (k_hbm, k_ref), (g_hbm, g_ref))
        ])
    for copy in small:
        copy.wait()
    masks = [
        mask_and_factor(half == 1, pl.ds(half * HALF, HALF), loss_ref, exponent_ref, ids_ref, index_ref)
        for half in range(2)
    ]
    info_row = lax.broadcasted_iota(jnp.int32, (INFO, k_ref.shape[1]), 0)
    info = jnp.zeros(info_row.shape, jnp.int32)
    for level in range(min(start_ref.shape[1], INFO // 2)):
        info = jnp.where(info_row == 2 * level, start_ref[0, level], info)
        info = jnp.where(info_row == 2 * level + 1, rows_ref[0, level], info)
    v_ref[pl.ds(2 * HALF, INFO), :] = info.astype(F32).astype(BF16)
    for half in range(2):
        for copy in loads[half]:
            copy.wait()
        span = pl.ds(half * HALF, HALF)
        values = attend_half(per_group, half == 1, span, q_ref, k_ref, g_ref, *masks[half])
        for group, value in enumerate(values):
            v_ref[span, pl.ds(group * HD, HD)] = value


def front(query, key, grad, ids, index, loss, exponent, start, rows):
    tokens, key_width = key.shape
    per_group = query.shape[1] // key_width
    args = [
        loss, exponent, start, rows, query, key, grad, ids.reshape(1, tokens), index.reshape(1, tokens)
    ]
    return pl.pallas_call(
        functools.partial(front_kernel, per_group),
        in_specs=[HBM] * 9,
        out_specs=VMEM,
        out_shape=jax.ShapeDtypeStruct((tokens + INFO, key_width), BF16),
        scratch_shapes=[
            pltpu.SMEM(loss.shape, F32), pltpu.SMEM(exponent.shape, jnp.int32),
            pltpu.SMEM(start.shape, jnp.int32), pltpu.SMEM(rows.shape, jnp.int32),
            pltpu.VMEM(query.shape, BF16), pltpu.VMEM(key.shape, BF16), pltpu.VMEM(grad.shape, BF16),
            pltpu.VMEM((1, tokens), jnp.int32), pltpu.VMEM((1, tokens), jnp.int32),
            pltpu.SemaphoreType.DMA((12,)),
        ],
        compiler_params=pltpu.CompilerParams(vmem_limit_bytes=24 * MIB),
        cost_estimate=FREE,
        name="front",
    )(*[arg if arg is exponent else pltpu.with_memory_space_constraint(arg, pltpu.HBM) for arg in args])


CORE, Y, X, Z1, Z2 = 8, 16, 1, 2, 4


def xor_permute(value, mask):
    count = lax.axis_size("dp") * lax.axis_size("fsdp")
    return lax.ppermute(value, ("dp", "fsdp"), [(i, i ^ mask) for i in range(count)])


def partial_kernel(parts, own_ref, near_ref, v0_ref, v1_ref, *out_refs):
    dp = lax.axis_index("dp")
    fsdp = lax.axis_index("fsdp")
    loaded = {}

    def block(z, y, x):
        if (z, y, x) not in loaded:
            owner = fsdp ^ (z << 1 | x)
            column = pl.multiple_of(owner * (4 * LANE) + (dp ^ (y << 1)) * LANE, LANE)
            loaded[z, y, x] = jnp.concatenate([ref[:, pl.ds(column, LANE)] for ref in (own_ref, near_ref)], axis=0)
        return loaded[z, y, x]

    for (blocks, start, width), out_ref in zip(parts, out_refs):
        v = jnp.concatenate([ref[pl.ds(0, 2 * HALF), pl.ds(start, width)] for ref in (v0_ref, v1_ref)], axis=0)
        total = lax.dot_general(
            jnp.concatenate([block(*place) for place in blocks], axis=1), v, (((0,), (0,)), ((), ())),
            preferred_element_type=F32,
        )
        out_ref[...] = total.astype(out_ref.dtype)


def partial_sums(parts, dtype, own, near, v0, v1):
    return pl.pallas_call(
        functools.partial(partial_kernel, parts),
        in_specs=[VMEM] * 4,
        out_specs=[VMEM] * len(parts),
        out_shape=[jax.ShapeDtypeStruct((len(blocks) * LANE, width), dtype) for blocks, _, width in parts],
        compiler_params=pltpu.CompilerParams(vmem_limit_bytes=24 * MIB),
        cost_estimate=FREE,
        name="partial_sums",
    )(own, near, v0, v1)


def inner_swap_kernel(v0_ref, v1_ref, out_ref, window_ref):
    tokens = out_ref.shape[0]
    infos = [ref[pl.ds(tokens, INFO), pl.ds(0, HALF)].astype(F32).astype(jnp.int32) for ref in (v0_ref, v1_ref)]

    def table(device, entry):
        return jnp.broadcast_to(infos[device][entry:entry + 1, :], (HALF, HALF))

    place = lax.broadcasted_iota(jnp.int32, (HALF, HALF), 0) + HALF
    inner = lax.broadcasted_iota(jnp.int32, (HALF, HALF), 1) + HALF
    first = table(0, 0)
    moved = (place >= first) & (place < first + table(0, 1))
    stays = jnp.where(~moved & (place == inner), 1.0, 0.0).astype(BF16)
    comes = jnp.where(moved & (place + table(1, 0) - first == inner), 1.0, 0.0).astype(BF16)
    taken = jnp.where(place - HALF + table(0, 2) == inner, 1.0, 0.0).astype(BF16)[:CAP]
    rows = (
        jnp.dot(stays, v0_ref[pl.ds(HALF, HALF), :], preferred_element_type=F32)
        + jnp.dot(comes, v1_ref[pl.ds(HALF, HALF), :], preferred_element_type=F32)
    ).astype(BF16)
    out_ref[pl.ds(0, HALF), :] = v0_ref[pl.ds(0, HALF), :]
    out_ref[pl.ds(HALF, HALF), :] = rows
    window_ref[...] = jnp.dot(taken, rows, preferred_element_type=F32).astype(BF16)


def inner_swap(v0, v1):
    return pl.pallas_call(
        inner_swap_kernel,
        in_specs=[VMEM] * 2,
        out_specs=[VMEM] * 2,
        out_shape=[jax.ShapeDtypeStruct((2 * HALF, 512), BF16), jax.ShapeDtypeStruct((CAP, 512), BF16)],
        compiler_params=pltpu.CompilerParams(vmem_limit_bytes=8 * MIB),
        cost_estimate=FREE,
        name="inner_swap",
    )(v0, v1)


def outer_swap_kernel(v0_ref, rows_ref, window_ref, out_ref):
    tokens = out_ref.shape[0]
    info = v0_ref[pl.ds(tokens, INFO), pl.ds(0, HALF)].astype(F32).astype(jnp.int32)
    first = jnp.broadcast_to(info[2:3, :], (HALF, HALF))
    extent = jnp.broadcast_to(info[3:4, :], (HALF, HALF))
    place = lax.broadcasted_iota(jnp.int32, (HALF, HALF), 0) + HALF
    inner = lax.broadcasted_iota(jnp.int32, (HALF, HALF), 1)
    moved = (place >= first) & (place < first + extent)
    stays = jnp.where(~moved & (place == inner + HALF), 1.0, 0.0).astype(BF16)
    comes = jnp.where(moved & (place - first == inner), 1.0, 0.0).astype(BF16)[:, :CAP]
    out_ref[pl.ds(0, HALF), :] = rows_ref[pl.ds(0, HALF), :]
    out_ref[pl.ds(HALF, HALF), :] = (
        jnp.dot(stays, rows_ref[pl.ds(HALF, HALF), :], preferred_element_type=F32)
        + jnp.dot(comes, window_ref[...], preferred_element_type=F32)
    ).astype(BF16)


def outer_swap(v0, rows, window):
    return pl.pallas_call(
        outer_swap_kernel,
        in_specs=[VMEM] * 3,
        out_specs=VMEM,
        out_shape=jax.ShapeDtypeStruct(rows.shape, BF16),
        compiler_params=pltpu.CompilerParams(vmem_limit_bytes=8 * MIB),
        cost_estimate=FREE,
        name="outer_swap",
    )(v0, rows, window)


def place_kernel(core, pair_ref, *rest):
    *_, out_ref, wide, sems = rest
    copies = []
    for y in range(2):
        wide[y] = pair_ref[y].astype(F32)
        row = pl.multiple_of((lax.axis_index("dp") ^ (y << 1 | core)) * LANE, LANE)
        copies.append(pltpu.make_async_copy(wide.at[y], out_ref.at[pl.ds(row, LANE), :], sems.at[y]))
        copies[-1].start()
    for copy in copies:
        copy.wait()


def place(core, pair, *placed):
    return pl.pallas_call(
        functools.partial(place_kernel, core),
        in_specs=[VMEM] + [HBM] * len(placed),
        out_specs=HBM,
        out_shape=jax.ShapeDtypeStruct((512, 512), F32),
        scratch_shapes=[pltpu.VMEM((2, LANE, 512), F32), pltpu.SemaphoreType.DMA((2,))],
        input_output_aliases={1: 0} if placed else {},
        compiler_params=pltpu.CompilerParams(vmem_limit_bytes=8 * MIB),
        cost_estimate=FREE,
        name="place",
    )(pair, *placed)


def fold_kernel(base_ref, arrived_ref, out_ref):
    out_ref[...] = base_ref[...] + arrived_ref[...].astype(F32)


def fold(base, arrived):
    return pl.pallas_call(
        fold_kernel,
        in_specs=[VMEM] * 2,
        out_specs=VMEM,
        out_shape=jax.ShapeDtypeStruct(base.shape, F32),
        compiler_params=pltpu.CompilerParams(vmem_limit_bytes=8 * MIB),
        cost_estimate=pl.CostEstimate(flops=6_000_000_000, bytes_accessed=0, transcendentals=0),
        name="fold",
    )(base, arrived)


def reduce_by_axis(layer_input, *args):
    near = xor_permute(layer_input, CORE)
    v0 = front(*args)
    v1 = xor_permute(v0, CORE)

    def sums(parts, dtype, v=v0):
        return partial_sums(parts, dtype, layer_input, near, v, v1)

    def after_all(*values):
        return lax.optimization_barrier(values)

    def add(*terms):
        total = terms[0]
        for term in terms[1:]:
            total = total + term.astype(F32)
        return total

    far_b, = sums([(((3, 1, 1),), 0, 512)], BF16)
    far_a, = sums([(((2, 1, 1),), 0, 512)], BF16)
    every = ((1, 1), (1, 0), (0, 1), (0, 0))
    side_b, pair_some = sums([(((3, 0, 1),), 0, 512), (tuple((1, *at) for at in every[:3]), 0, 256)], BF16)
    pair_rest, side_a = sums(
        [(tuple((1, *at) for at in every[:3]), 256, 256), (((2, 1, 0),), 0, 512)], BF16, after_all(v0, pair_some)[0]
    )
    keep_b, keep_a = sums([(((3, 1, 0), (3, 0, 0)), 0, 512), (((2, 0, 1), (2, 0, 0)), 0, 512)], F32)
    far_b = xor_permute(far_b, X)
    side_b = xor_permute(side_b, X)
    far_a = xor_permute(far_a, Y)
    pair_some = xor_permute(pair_some, Z1)
    pair_rest = xor_permute(pair_rest, Z1)
    far_b, far_a = after_all(far_b, far_a)
    on_b = add(keep_b[:LANE], far_b).astype(BF16)
    v0_late = after_all(v0, on_b)[0]
    rows, window = inner_swap(v0_late, v1)
    own_some, own_rest = sums([(tuple((0, *at) for at in every), start, 256) for start in (0, 256)], F32, v0_late)
    pair_own, = sums([(((1, 0, 0),), 0, 512)], BF16, v0_late)
    on_b = xor_permute(on_b, Y)
    on_a = xor_permute(add(keep_a[:LANE], far_a).astype(BF16), X)
    z3 = add(keep_b[LANE:], side_b, on_b).astype(BF16)
    side_a = xor_permute(after_all(jnp.concatenate([side_a, window]), own_some)[0], Y)
    side_a, window = side_a[:LANE], side_a[LANE:]
    pair_some = after_all(pair_some, z3)[0]
    z3 = xor_permute(z3, Z1)
    z2 = add(keep_a[LANE:], side_a, on_a, z3).astype(BF16)

    some = add(own_some[:3 * LANE], pair_some)
    some_in = xor_permute(some[:2 * LANE].astype(BF16), Y)
    rest = add(own_rest[:3 * LANE], after_all(pair_rest, some)[0])
    rest_far, rest_y, rest_x = (rest[row:row + LANE] for row in range(0, 3 * LANE, LANE))
    rest_in = xor_permute(jnp.concatenate([rest_far, rest_x]).astype(BF16), X)
    some_in = after_all(some_in, z2)[0]
    z2 = xor_permute(z2, Z2)
    some_on = add(some[2 * LANE:], some_in[:LANE]).astype(BF16)
    rest_in = after_all(rest_in, some_on)[0]
    some_on = xor_permute(some_on, X)
    rest_on = add(rest_y, rest_in[:LANE]).astype(BF16)
    pair_own = xor_permute(after_all(pair_own, rest_on)[0], Z1)
    rest_on = xor_permute(rest_on, Y)
    base = jnp.concatenate([
        add(own_some[3 * LANE:], some_in[LANE:]),
        add(own_rest[3 * LANE:], rest_in[LANE:]),
    ], axis=1)
    mine = add(fold(base, z2), jnp.concatenate([some_on, rest_on], axis=1), pair_own).astype(BF16)
    from_y = xor_permute(mine, Y)
    value_grad = outer_swap(v0, rows, after_all(window, mine)[0])
    from_y, value_grad = after_all(from_y, value_grad)
    pair = jnp.stack([mine, from_y])
    near_pair = xor_permute(pair, CORE)
    half = place(0, pair)
    near_pair, half = after_all(near_pair, half)
    return place(1, near_pair, half), value_grad


def swapped(block, axis, distance):
    count = lax.axis_size(axis)
    route = []
    for low in range(count):
        high = low | 1 << distance
        if high != low and high < count:
            route += [(low, high), (high, low)]
    return lax.ppermute(block, axis, route)


def blend_rows(item, incoming, offset, extent):
    inside = (jnp.arange(CAP) < extent)[:, None]
    chosen = jnp.where(inside, incoming, lax.dynamic_slice_in_dim(item, offset, CAP, 0))
    return lax.dynamic_update_slice_in_dim(item, chosen, offset, 0)


def reduce_by_owner(layer_input, *args):
    swap_start, swap_rows = args[-2:]
    tokens = layer_input.shape[0]
    values = front(*args)[:tokens]
    balanced = values
    for level in range(lax.axis_size("dp").bit_length() - 1):
        offset = swap_start[0, level]
        window = lax.dynamic_slice_in_dim(balanced, offset, CAP, 0)
        balanced = blend_rows(balanced, swapped(window, "dp", level), offset, swap_rows[0, level])
    owners = lax.axis_size("fsdp")
    owned = (D + owners - 1) // owners
    padded = jnp.pad(layer_input, ((0, 0), (0, owned * owners - D)))
    arranged = lax.all_to_all(
        padded.reshape(tokens, owners, owned), "fsdp", split_axis=1, concat_axis=0, tiled=True
    )
    block = lax.dot_general(
        arranged.reshape(-1, owned),
        lax.all_gather(values, "fsdp", axis=0, tiled=True),
        (((0,), (0,)), ((), ())),
        preferred_element_type=F32,
    )
    return lax.psum(block, "dp"), balanced


def on_device(layer_input, *args):
    if lax.axis_size("dp") == 4 and lax.axis_size("fsdp") == 8:
        return reduce_by_axis(layer_input, *args)
    return reduce_by_owner(layer_input, *args)


def solution(mesh):
    return jax.shard_map(
        on_device,
        mesh=mesh,
        in_specs=(
            P(("dp", "fsdp"), None),
            P(("dp", "fsdp"), None),
            P(("dp", "fsdp"), None),
            P(("dp", "fsdp"), None),
            P(("dp", "fsdp")),
            P(("dp", "fsdp")),
            P(),
            P(("dp", "fsdp")),
            P(("dp", "fsdp"), None),
            P(("dp", "fsdp"), None),
        ),
        out_specs=(P("fsdp", None), P(("dp", "fsdp"), None)),
        check_vma=False,
    )
```
